32 devices in a mesh: gather: 8 (over z, core), tm: 4 (over y, x).
Axes of the slice: x: 2, y: 2, z: 4, core: 2. Of those that a mesh axis runs over, the one named last changes fastest.
Arguments:
- records: bfloat16 [8, 4, 80, 512], P('gather', None, None, 'tm'), may hold values from -6 to 6
- lift_weight: bfloat16 [32, 4], replicated, may hold values from -3 to 3
- lift_bias: float32 [32], replicated, may hold values from -2.5 to 2.5
- conv_weight: bfloat16 [4, 32, 32, 3, 3], replicated, may hold values from -0.375 to 0.375
- conv_bias: float32 [4, 32], replicated, may hold values from -1.5 to 1.5
- out_weight: bfloat16 [4, 32], replicated, may hold values from -1 to 1
- live_count: int32 [8], replicated, may hold values from 40 to 80, as said below
- trace_node: int32 [8, 80], replicated, may hold values from 0 to 79, as said below
- node_owner: int32 [80], replicated, may hold values from 0 to 7, as said below
Outputs:
- deblended: float32 [8, 4, 80, 512], P(None, None, 'gather', 'tm')
The draws below stay inside these ranges and needn't reach their ends.
Inputs may be any that keep to these rules, and one draw needn't show every extreme that they name: `live_count`: some shot gather has all 80 traces live. `trace_node`: each row holds every node once; its first live_count slots hold consecutive nodes in rising order, and the others continue from there cyclically. `node_owner`: every index of gather owns 10 or 9 nodes, and some owns 10.
All inputs are finite; a program needn't handle non-finite values.
Results may differ from the reference program's by a relative error of at most 0.0039.
Values may be sent and summed in bfloat16 or wider, within the bound.
No kernel may reach another device: no remote copies, remote signals or barrier semaphores. Data moves between devices by JAX's collectives and lax.ppermute only.
A program may use at most 64 MiB of HBM per device.

```python
import jax
import jax.numpy as jnp
from jax import lax

C = 32
COMPS = 4
NODES = 80
LAYERS = 2
HOLDERS = 8
SHOTS = 8
TIME = 512
NODE_CAP = 10
NODE_SLOTS = 80


def shot_layout(key):
    base = jax.random.fold_in(key, 5)
    first_key, second_key, third_key = jax.random.split(base, 3)
    live = jax.random.randint(first_key, (SHOTS,), NODES // 2, NODES + 1)
    full_shot = jax.random.randint(second_key, (), 0, SHOTS)
    live = jnp.where(jnp.arange(SHOTS) == full_shot, NODES, live).astype(jnp.int32)
    start = jax.random.randint(third_key, (SHOTS,), 0, NODES - live + 1)
    nodes = (start[:, None] + jnp.arange(NODES)[None, :]) % NODES
    return (live, nodes.astype(jnp.int32))


def draw_live_count(key, part):
    return shot_layout(key)[0]


def draw_trace_node(key, part):
    return shot_layout(key)[1]


def draw_node_owner(key, part):
    order = jax.random.permutation(jax.random.fold_in(key, 9), NODES)
    return (order % HOLDERS).astype(jnp.int32)


def steps_of(key, shape, cuts, smallest, high):
    def one(dim, blocks):
        draws = jax.random.uniform(jax.random.fold_in(jax.random.fold_in(key, 6), dim), (blocks,), jnp.float32, smallest / len(cuts), high / len(cuts))
        return jnp.repeat(jnp.exp(draws), shape[dim] // blocks).reshape((-1,) + (1,) * (len(shape) - dim - 1))

    factor_of = one(*cuts[0])
    for cut in cuts[1:]:
        factor_of = factor_of * one(*cut)
    return factor_of


def bell_draw(rng, shape, width, bound, shards=(), kind=jnp.bfloat16):
    drawn = jax.random.normal(rng, shape, jnp.float32) * width
    if len(shards) > 0:
        drawn = steps_of(rng, shape, shards, -0.22, 0.18) * drawn
    return jnp.clip(drawn, min=-bound, max=bound).astype(kind)


def setup_inputs(seed: int = 0) -> dict:
    seeds = jax.random.split(jax.random.key(seed), 10)
    return {
        "records": bell_draw(seeds[0], (SHOTS, COMPS, NODES, TIME), 1.0, 6.0, ((0, 8), (3, 4))),
        "lift_weight": bell_draw(seeds[1], (C, COMPS), COMPS ** -0.5, 3.0),
        "lift_bias": bell_draw(seeds[2], (C,), 0.5, 2.5, (), jnp.float32),
        "conv_weight": bell_draw(seeds[3], (2 * LAYERS, C, C, 3, 3), (9 * C) ** -0.5, 0.375),
        "conv_bias": bell_draw(seeds[4], (2 * LAYERS, C), 0.3, 1.5, (), jnp.float32),
        "out_weight": bell_draw(seeds[5], (COMPS, C), C ** -0.5, 1.0),
        "live_count": draw_live_count(jax.random.fold_in(seeds[9], 71), 0),
        "trace_node": draw_trace_node(jax.random.fold_in(seeds[9], 71), 0),
        "node_owner": draw_node_owner(jax.random.fold_in(seeds[9], 71), 0),
    }


def dilated(field, kernel, dilation_factor):
    return lax.conv_general_dilated(field.astype(jnp.float32), kernel.astype(jnp.float32), (1, 1), ((dilation_factor, dilation_factor), (dilation_factor, dilation_factor)), rhs_dilation=(dilation_factor, dilation_factor), dimension_numbers=("NCHW", "OIHW", "NCHW"), precision=lax.Precision.HIGHEST, preferred_element_type=jnp.float32)


def residual_layer(field, kernel, bias_row, dilation_factor, keep_mask):
    summed = dilated(field, kernel, dilation_factor) + bias_row[None, :, None, None]
    return ((field.astype(jnp.float32) + jnp.maximum(summed, 0.0)) * keep_mask).astype(jnp.bfloat16)


def reference(records, lift_weight, lift_bias, conv_weight, conv_bias, out_weight, live_count, trace_node, node_owner):
    positions = jnp.arange(NODES, dtype=jnp.int32)
    same_owner = node_owner[:, None] == node_owner[None, :]
    earlier = positions[None, :] < positions[:, None]
    ranks = jnp.sum((same_owner & earlier).astype(jnp.int32), axis=1).astype(jnp.int32)
    slot_of_node = (node_owner * NODE_CAP + ranks).astype(jnp.int32)
    slot_table = slot_of_node[trace_node].astype(jnp.int32)
    live_table = positions[None, :] < live_count[:, None]
    lift_f = lift_weight.astype(jnp.float32)

    def shot_pass(inputs):
        record_block, live_row, slot_row = inputs
        keep_mask = live_row.astype(jnp.float32)[None, None, :, None]
        mixed = jnp.einsum("ck,kjt->cjt", lift_f, record_block.astype(jnp.float32), precision=lax.Precision.HIGHEST)
        hidden_state = ((mixed[None] + lift_bias[None, :, None, None]) * keep_mask).astype(jnp.bfloat16)
        for depth_level in range(LAYERS):
            hidden_state = residual_layer(hidden_state, conv_weight[depth_level], conv_bias[depth_level], 4 ** depth_level, keep_mask)
        placed = jnp.zeros((NODE_SLOTS, C, TIME), jnp.bfloat16).at[slot_row].set(jnp.transpose(hidden_state[0], (1, 0, 2)))
        live_records = record_block * live_row.astype(jnp.bfloat16)[None, :, None]
        placed_records = jnp.zeros((NODE_SLOTS, COMPS, TIME), jnp.bfloat16).at[slot_row].set(jnp.transpose(live_records, (1, 0, 2)))
        return placed, placed_records

    receiver_hidden, recv_records = lax.map(shot_pass, (records, live_table, slot_table))
    recv_live = jnp.zeros((SHOTS, NODE_SLOTS), jnp.float32).at[jnp.arange(SHOTS)[:, None], slot_table].set(live_table.astype(jnp.float32))
    out_f = out_weight.astype(jnp.float32)

    def node_pass(slot_index):
        gathered = lax.dynamic_index_in_dim(receiver_hidden, slot_index, axis=1, keepdims=False)
        rec_slot = lax.dynamic_index_in_dim(recv_records, slot_index, axis=1, keepdims=False)
        live_col = lax.dynamic_index_in_dim(recv_live, slot_index, axis=1, keepdims=False)
        keep_mask = live_col[None, None, :, None]
        hidden_state = jnp.transpose(gathered, (1, 0, 2))[None]
        for depth_level in range(LAYERS):
            hidden_state = residual_layer(hidden_state, conv_weight[LAYERS + depth_level], conv_bias[LAYERS + depth_level], 2 * 4 ** depth_level, keep_mask)
        noise = jnp.einsum("kc,cst->skt", out_f, hidden_state[0].astype(jnp.float32), precision=lax.Precision.HIGHEST)
        return (rec_slot.astype(jnp.float32) + noise) * live_col[:, None, None]

    per_slot = lax.map(node_pass, jnp.arange(NODE_SLOTS, dtype=jnp.int32))
    return jnp.transpose(per_slot, (1, 2, 0, 3))
```

```python
import functools
import itertools

import jax
import jax.numpy as jnp
from jax import lax
from jax.experimental import pallas as pl
from jax.experimental.pallas import tpu as pltpu
from jax.sharding import PartitionSpec as P

F32 = jnp.float32
BF16 = jnp.bfloat16
CH = 32
CORES = 2
COMPS = 4
GROUP = 8
LANES = GROUP * CH
HALO = 16
QUAD = 4
HALF = QUAD * CH
KROWS = 128
PARTS = QUAD * COMPS + 2 * QUAD


def iota(shape, dim):
    return lax.broadcasted_iota(jnp.int32, shape, dim)


def dot(a, b):
    return jnp.dot(a, b, preferred_element_type=F32)


def dot_t(a, b):
    return lax.dot_general(a, b, (((1,), (1,)), ((), ())), preferred_element_type=F32)


def onehot(cond):
    return cond.astype(F32).astype(BF16)


def band_links(dilation, offset):
    return [
        a
        for a in range(3)
        if any(s + GROUP * offset == t + (a - 1) * dilation for s in range(GROUP) for t in range(GROUP))
    ]


def split3(value):
    terms = []
    for _ in range(3):
        term = value.astype(BF16)
        terms.append(term)
        value = value - term.astype(F32)
    return terms


def shot_of(place_ref, n, shots):
    planes = shots // CORES
    plane = place_ref[0] // CORES
    core = place_ref[0] - CORES * plane
    return CORES * (plane ^ (n % planes)) + (core if n < planes else 1 - core)


def couple_of(place_ref, relative):
    return (place_ref[0] // (2 * CORES)) ^ relative


def table_kernel(dils, slots, place_ref, live_ref, trace_ref, owner_ref, pick_ref, keep_ref):
    shots, rows, nodes = pick_ref.shape
    split = round_up(6 * slots, 16)
    me = place_ref[0]

    mine = (owner_ref[...] == me).astype(F32)
    before = onehot(iota((nodes, nodes), 0) < iota((nodes, nodes), 1))
    rank = dot(jnp.broadcast_to(mine, (8, nodes)).astype(BF16), before)[0:1, :]
    node_ids = iota((1, nodes), 1).astype(F32)

    def nodes_of(slot_index):
        held = jnp.where((rank == slot_index.astype(F32)) & (mine > 0.5), 1.0, 0.0)
        node = jnp.sum(held * node_ids, axis=1, keepdims=True)
        there = jnp.sum(held, axis=1, keepdims=True)
        return jnp.where(there > 0.5, node, -1.0e6).astype(jnp.int32)

    row_id = iota((rows, nodes), 0)
    late = row_id >= split
    row_id = jnp.where(late, row_id - split, row_id)
    tap = jnp.zeros((rows, nodes), jnp.int32)
    for m in range(1, 7):
        tap = tap + (row_id >= m * slots).astype(jnp.int32)
    second = (tap >= 3).astype(jnp.int32)
    shift = dils[0] * (tap - 3 * second - 1) + jnp.where(late, 0, dils[1] * (2 * second - 1))
    target = nodes_of(row_id - slots * tap)
    target = jnp.where(tap >= jnp.where(late, 3, 6), -1000000, target + shift)

    node_lane = iota((rows, nodes), 1)
    for n in range(shots):
        s = shot_of(place_ref, n, shots)
        pick_ref[n] = onehot((node_lane == target - trace_ref[s, 0]) & (node_lane < live_ref[s]))

    slot_rows = keep_ref.shape[2]
    own_node = nodes_of(iota((slot_rows, nodes), 0))
    shot_lane = iota((slot_rows, HALF), 1) >> 5
    for c in range(shots // QUAD):
        base = QUAD * couple_of(place_ref, c)
        for b in range(3):
            first = jnp.zeros((slot_rows, HALF), jnp.int32)
            count = jnp.zeros((slot_rows, HALF), jnp.int32)
            for w in range(QUAD):
                at = shot_lane == (w if b == 1 else w ^ 2)
                first = jnp.where(at, trace_ref[base + w, 0], first)
                count = jnp.where(at, live_ref[base + w], count)
            trace = own_node + dils[1] * (b - 1) - first
            keep_ref[c, b] = ((trace >= 0) & (trace < count)).astype(F32)


def fetch(sources, places, sems):
    copies = [pltpu.make_async_copy(a, b, sems.at[n]) for n, (a, b) in enumerate(zip(sources, places))]
    for copy in copies:
        copy.start()
    for copy in copies:
        copy.wait()
    return places


def prep_kernel(dils, slots, place_ref, *refs):
    w0_ref, w1_ref, w2_ref, wide_bias_ref, shift_ref, pick_ref, keep_ref = refs[7:14]
    live_ref, trace_ref, cw_ref, lift_ref, lift_bias_ref, bias_ref, owner_ref = fetch(
        refs[:7], refs[14:21], refs[21]
    )
    table_kernel(dils, slots, place_ref, live_ref, trace_ref, owner_ref, pick_ref, keep_ref)

    rows8 = [lift_ref[...].astype(F32)] + [term.astype(F32) for term in split3(lift_bias_ref[...])]
    table = jnp.concatenate(rows8 + [jnp.zeros((1, CH), F32)], axis=0).astype(BF16)
    data_rows = 3 * QUAD * COMPS
    r8 = iota((KROWS, 8), 0)
    part = jnp.where(r8 < data_rows, r8 & (COMPS - 1), COMPS + ((r8 >> 2) & 3))
    values = dot(onehot((part == iota((KROWS, 8), 1)) & (r8 < 2 * data_rows)), table).astype(BF16)
    wide = iota((CH, 2 * LANES), 1)
    spread = onehot(iota((CH, 2 * LANES), 0) == (wide & 31))
    rr = iota((KROWS, 2 * LANES), 0)
    cc = iota((KROWS, 2 * LANES), 1)
    row_node = jnp.where(rr < data_rows, rr >> 4, (rr - data_rows) >> 4)
    row_shot = jnp.where(rr < data_rows, rr >> 2, rr) & (QUAD - 1)
    place = (cc >> 6) & 3
    node = jnp.where((cc >= LANES) & (place < 2), 1 - place, place)
    same = (row_node == node) & (row_shot == 2 * (cc >> 8) + ((cc >> 5) & 1)) & (rr < 2 * data_rows)
    w0_ref[...] = jnp.where(same & (place < 3), dot(values, spread), 0.0).astype(BF16)

    widen = onehot((iota((LANES, CH), 0) & 31) == iota((LANES, CH), 1))
    kr = iota((LANES, LANES), 0)
    kc = iota((LANES, LANES), 1)
    same_shot = ((kr >> 5) & 1) == ((kc >> 5) & 1)
    sr = iota((3 * CH, LANES), 0)
    sc = iota((3 * CH, LANES), 1)
    for layer, ref, odd_taps in ((0, w1_ref, (1, 0, 2, 3)), (1, w2_ref, (1, 0, 3, 2))):
        base = 3 * layer
        tall = [
            dot_t(widen, cw_ref[(base + a) * 3 * CH : (base + a + 1) * 3 * CH, :]).astype(BF16)
            for a in range(3)
        ]
        for odd, (k_taps, n_taps) in enumerate((((0, 1, 2, 3), (0, 1, 3, 2)), (odd_taps, (1, 0, 2, 3)))):
            place = sum(jnp.where((sc >> 6) == y, n_taps[y], 0) for y in range(4))
            spread2 = onehot(((sr >> 5) == place) & ((sr & 31) == (sc & 31)))
            total = jnp.zeros((LANES, LANES), F32)
            for x in range(4):
                if k_taps[x] < 3:
                    total = jnp.where(((kr >> 6) == x) & same_shot, dot(tall[k_taps[x]], spread2), total)
            ref[odd] = total.astype(BF16)

    span = shift_ref.shape[0]
    window = span - 2 * HALO
    source = iota(shift_ref.shape, 0)
    source = jnp.where(source < window + HALO, source, source + window // 2 - HALO)
    shift_ref[...] = onehot(iota(shift_ref.shape, 1) == source)

    tile = onehot(iota((CH, LANES), 0) == (iota((CH, LANES), 1) & 31))
    wide_bias_ref[...] = sum(dot(term, tile) for term in split3(bias_ref[...]))


def band_kernel(dils, blocks, place_ref, *refs):
    b3_ref, b4_ref, ow_ref = refs[2:5]
    cw_ref, out_w_ref = fetch(refs[:2], refs[5:7], refs[7])
    widen = onehot((iota((LANES, CH), 0) & 31) == iota((LANES, CH), 1))

    er = iota((3 * CH, 3 * LANES), 0)
    ec = iota((3 * CH, 3 * LANES), 1)
    spread3 = onehot(((er >> 5) == (ec >> 8)) & ((er & 31) == (ec & 31)))
    row_lane = iota((LANES, 3 * LANES), 0)
    col_lane = iota((LANES, 3 * LANES), 1) & (LANES - 1)

    def shots_in(lane, block):
        couple = jnp.where(lane < HALF, couple_of(place_ref, 2 * block), couple_of(place_ref, 2 * block + 1))
        return QUAD * couple + ((lane >> 5) & (QUAD - 1))

    def expanded(layer, a):
        base = ((layer - 2) * 3 + a) * 3 * CH
        return dot(dot_t(widen, cw_ref[base : base + 3 * CH, :]).astype(BF16), spread3)

    for layer, ref in ((2, b3_ref), (3, b4_ref)):
        linked_taps = band_links(dils[layer], 0) if blocks == 1 else range(3)
        for out_block in range(blocks):
            for in_block in range(blocks):
                total = jnp.zeros((LANES, 3 * LANES), F32)
                for a in linked_taps:
                    reach = shots_in(col_lane, out_block) + (a - 1) * dils[layer]
                    total = total + jnp.where(shots_in(row_lane, in_block) == reach, expanded(layer, a), 0.0)
                for e in range(3):
                    ref[out_block * blocks + in_block, e * LANES : (e + 1) * LANES, :] = total[
                        :, e * LANES : (e + 1) * LANES
                    ].astype(BF16)

    rows = GROUP * COMPS
    pick = onehot((iota((rows, COMPS), 0) & (COMPS - 1)) == iota((rows, COMPS), 1))
    mine = dot(pick, out_w_ref[...]).astype(BF16)
    tile = onehot(iota((CH, LANES), 0) == (iota((CH, LANES), 1) & 31))
    same = (iota((rows, LANES), 0) >> 2) == (iota((rows, LANES), 1) >> 5)
    ow_ref[...] = jnp.where(same, dot(mine, tile), 0.0).astype(BF16)


def round_up(value, unit):
    return -(-value // unit) * unit


def shifted(value, dilation):
    span = value.shape[0]
    return jnp.concatenate(
        [
            pltpu.roll(value, dilation, axis=0).astype(BF16),
            value.astype(BF16),
            pltpu.roll(value, span - dilation, axis=0).astype(BF16),
        ],
        axis=1,
    )


class Shots:
    def __init__(
        self, dils, windows, step, couple, place_ref, recs, pick_ref, keep_ref, w0_ref, w1_ref, w2_ref,
        bias_ref, shift_ref, part_ref, x2_ref, rec_out_ref,
    ):
        self.dils, self.step, self.couple = dils, step, couple
        self.keep_ref, self.w0_ref, self.w1_ref, self.w2_ref = keep_ref, w0_ref, w1_ref, w2_ref
        self.bias_ref, self.shift_ref, self.x2_ref = bias_ref, shift_ref, x2_ref
        shots, rows, nodes = pick_ref.shape
        planes = shots // CORES
        self.slots = slots = x2_ref.shape[0]
        self.window = window = part_ref.shape[-1]
        self.rows, self.split = part_ref.shape[2], round_up(6 * slots, 16)
        self.span = window + 2 * HALO
        at = place_ref[1]
        self.right_ok = (at < windows - 1).astype(F32)
        self.left_ok = (at > 0).astype(F32)
        self.low_half = iota((self.span, HALF), 1) < CH * CORES

        lane = iota((nodes, 2 * window), 1)
        all_ok = jnp.where(
            lane < window, 1.0, jnp.where(lane < window + window // 2, self.right_ok, self.left_ok)
        ).astype(BF16)

        def put(part, swapped, value):
            for half in range(2):
                lanes = value[:, half * window : (half + 1) * window]
                part_ref[half, part, 0 : self.split] = lanes[0 : self.split]
                part_ref[half, swapped, self.split : rows] = lanes[self.split : rows]

        for x, rec_ref in enumerate(recs):
            n = 2 * couple + x % 2 + (planes if x >= 2 else 0)
            within = shot_of(place_ref, n, shots) & (QUAD - 1)
            edge = rec_ref[COMPS].astype(F32)
            for k in range(COMPS):
                turned = edge if k == 0 else pltpu.roll(edge, window - HALO * k, axis=1)
                both = jnp.concatenate([rec_ref[k], turned.astype(BF16)], axis=1)
                put(within * COMPS + k, (within ^ 2) * COMPS + k, dot(pick_ref[n], both))
            alive = dot(pick_ref[n], all_ok)
            for copy in range(2):
                first = QUAD * COMPS + QUAD * copy
                put(first + within, first + (within ^ 2), alive)

        self.half_rows = part_ref.shape[1] * self.rows
        self.part2 = part_ref.reshape(2 * self.half_rows, window)
        for q in range(slots):
            first = self.split + slots + q
            for half in range(2):
                pair = self.part2[pl.ds(first + (1 - half) * 8 * self.rows, 8, stride=self.rows), :]
                rec_out_ref[q, half * 8 : (half + 1) * 8] = pair

    def inside(self, value):
        w = self.window
        return jnp.concatenate(
            [value[0:w], value[w : w + HALO] * self.right_ok, value[w + HALO :] * self.left_ok], axis=0
        )

    def item_rows(self, q, b):
        start = (3 * (b // 2) * self.slots if b != 1 else self.split) + q
        halves = []
        for half in range(2):
            base = half * self.half_rows + start
            flags = base + QUAD * COMPS * self.rows
            pieces = [
                self.part2[pl.ds(base + a * self.slots, QUAD * COMPS, stride=self.rows), :] for a in range(3)
            ]
            for a in range(3):
                alive = self.part2[pl.ds(flags + a * self.slots, 2 * QUAD, stride=self.rows), :]
                pieces += [alive, alive]
            pieces.append(jnp.zeros((KROWS - 6 * QUAD * COMPS, self.window), F32))
            halves.append(jnp.concatenate(pieces, axis=0).astype(BF16))
        return jnp.concatenate(halves, axis=1)

    def items(self, group):
        return [(group * self.step + i, b) for i in range(self.step) for b in range(3)]

    def first_inputs(self, group):
        items = self.items(group)
        lhs = []
        for n in range(0, len(items), 2):
            some = jnp.concatenate([self.item_rows(q, b) for q, b in items[n : n + 2]], axis=0)
            moved = dot_t(self.shift_ref[...], some).astype(BF16)
            lhs += [moved[:, m : m + KROWS] for m in range(0, moved.shape[1], KROWS)]
        lifted = dot(jnp.concatenate(lhs, axis=0), self.w0_ref[...]).astype(BF16)
        return lifted[:, 0:LANES], lifted[:, LANES:]

    def taps_added(self, even, odd, dilation):
        mid = jnp.where(self.low_half, odd[:, 0:HALF], even[:, 0:HALF])
        late = jnp.where(self.low_half, odd[:, HALF:], even[:, HALF:])
        early = pltpu.roll(jnp.where(self.low_half, even[:, 0:HALF], odd[:, 0:HALF]), HALF // 2, axis=1)
        return (
            pltpu.roll(early, dilation, axis=0) + mid + pltpu.roll(late, self.span - dilation, axis=0)
        )

    def first_layer(self, group, even, odd):
        y_even, y_odd = dot(even, self.w1_ref[0]), dot(odd, self.w1_ref[1])
        x1 = []
        for n, (q, b) in enumerate(self.items(group)):
            at = slice(n * self.span, (n + 1) * self.span)
            old = jnp.where(self.low_half, odd[at, 0:HALF].astype(F32), even[at, 0:HALF].astype(F32))
            total = self.taps_added(y_even[at], y_odd[at], self.dils[0])
            new = jnp.maximum(total + self.bias_ref[0:1, 0:HALF], 0.0)
            x1.append(self.inside((old + new) * self.keep_ref[self.couple, b, q : q + 1, :]))
        even, odd, own = [], [], []
        for i in range(self.step):
            t0, t1, t2 = x1[3 * i : 3 * i + 3]
            t2 = t2.astype(BF16)
            even.append(jnp.concatenate([jnp.where(self.low_half, t0, t1).astype(BF16), t2], axis=1))
            odd.append(jnp.concatenate([jnp.where(self.low_half, t1, t0).astype(BF16), t2], axis=1))
            own.append(t1.astype(BF16))
        return jnp.concatenate(even, axis=0), jnp.concatenate(odd, axis=0), own

    def second_layer(self, group, even, odd, own):
        even, odd = dot(even, self.w2_ref[0]), dot(odd, self.w2_ref[1])
        for i in range(self.step):
            q = group * self.step + i
            at = slice(i * self.span, (i + 1) * self.span)
            total = self.taps_added(even[at], odd[at], self.dils[1])
            new = jnp.maximum(total + self.bias_ref[1:2, 0:HALF], 0.0)
            x2 = (own[i].astype(F32) + new) * self.keep_ref[self.couple, 1, q : q + 1, :]
            self.x2_ref[q] = shifted(self.inside(x2), self.dils[2])


def staged(work):
    inputs, middle = {}, {}
    for t in range(len(work) + 2):
        if t < len(work):
            stage, group = work[t]
            inputs[t] = stage.first_inputs(group)
        if 0 <= t - 1 < len(work):
            stage, group = work[t - 1]
            middle[t - 1] = stage.first_layer(group, *inputs.pop(t - 1))
        if 0 <= t - 2:
            stage, group = work[t - 2]
            stage.second_layer(group, *middle.pop(t - 2))
        yield t


def near_kernel(dils, windows, step, place_ref, *refs):
    pick_ref, keep_ref, w0_ref, w1_ref, w2_ref, bias_ref, shift_ref = refs[:7]
    x2_ref, rec_out_ref, part_ref = refs[7 + QUAD :]
    stage = Shots(
        dils, windows, step, 0, place_ref, refs[7 : 7 + QUAD], pick_ref, keep_ref, w0_ref, w1_ref, w2_ref,
        bias_ref, shift_ref, part_ref, x2_ref, rec_out_ref,
    )
    for _ in staged([(stage, group) for group in range(x2_ref.shape[0] // step)]):
        pass


def main_kernel(dils, windows, step, near, place_ref, *refs):
    shots = refs[0].shape[0]
    couples = shots // QUAD
    pick_ref, keep_ref, w0_ref, w1_ref, w2_ref, b3_ref, b4_ref, ow_ref, bias_ref, shift_ref = refs[:10]
    refs = refs[10:]
    rec_refs, refs = refs[: QUAD * (couples - near)], refs[QUAD * (couples - near) :]
    done_refs, refs = refs[: 2 * near], refs[2 * near :]
    out_ref, part_ref, x2_all, rec_all, x3_ref = refs
    blocks = couples // 2
    slots, window = out_ref.shape[1], out_ref.shape[3]
    span = window + 2 * HALO
    right_ok = (place_ref[1] < windows - 1).astype(F32)
    left_ok = (place_ref[1] > 0).astype(F32)

    stages = []
    x2_refs, rec_refs_out = list(done_refs[0::2]), list(done_refs[1::2])
    for c in range(near, couples):
        x2_refs.append(x2_all.at[c - near])
        rec_refs_out.append(rec_all.at[c - near])
        stages.append(
            Shots(
                dils, windows, step, c, place_ref, rec_refs[QUAD * (c - near) : QUAD * (c - near + 1)],
                pick_ref, keep_ref, w0_ref, w1_ref, w2_ref, bias_ref, shift_ref, part_ref.at[c - near],
                x2_refs[-1], rec_refs_out[-1],
            )
        )

    def receiver_layer(parts_of, weights, layer, block, group, out_rows):
        y = None
        for other in range(blocks):
            term = dot(jnp.concatenate(parts_of(other), axis=0), weights[block * blocks + other])
            y = term if y is None else y + term
        results = []
        for i, part in enumerate(parts_of(block)):
            q = group * step + i
            keep = jnp.concatenate([keep_ref[2 * block + c, 1, q : q + 1, :] for c in range(2)], axis=1)
            old = part[:, LANES : 2 * LANES].astype(F32)
            new = jnp.maximum(y[i * out_rows : (i + 1) * out_rows] + bias_ref[layer : layer + 1, :], 0.0)
            results.append((old + new) * keep)
        return results

    def third_layer(group):
        def parts_of(block):
            return [
                jnp.concatenate(
                    [
                        x2_refs[2 * block + c][group * step + i, :, e * HALF : (e + 1) * HALF]
                        for e in range(3)
                        for c in range(2)
                    ],
                    axis=1,
                )
                for i in range(step)
            ]

        for block in range(blocks):
            for i, value in enumerate(receiver_layer(parts_of, b3_ref, 2, block, group, span)):
                value = jnp.concatenate(
                    [
                        value[0:window],
                        value[window : window + HALO] * right_ok,
                        value[window + HALO :] * left_ok,
                    ],
                    axis=0,
                )
                x3_ref[block, group * step + i] = shifted(value, dils[3])[0:window]

    def last_layer(group):
        def parts_of(block):
            return [x3_ref[block, group * step + i] for i in range(step)]

        for block in range(blocks):
            for i, value in enumerate(receiver_layer(parts_of, b4_ref, 3, block, group, window)):
                q = group * step + i
                noise = dot_t(ow_ref[...], value.astype(BF16))
                record = jnp.concatenate([rec_refs_out[2 * block + c][q] for c in range(2)], axis=0)
                done = (record + noise).reshape(GROUP, COMPS, window)
                for c in range(2):
                    first = QUAD * couple_of(place_ref, 2 * block + c)
                    out_ref[pl.ds(first, QUAD), q] = done[c * QUAD : (c + 1) * QUAD]

    groups = slots // step
    work = [(stage, group) for group in range(groups) for stage in stages]
    lag = len(stages)
    for t in itertools.chain(staged(work), range(len(work) + 2, len(work) + 2 + 2 * lag)):
        done, rest = divmod(t - 2, lag)
        if rest == 0 and 0 <= done - 1 < groups:
            third_layer(done - 1)
        if rest == 0 and 0 <= done - 2 < groups:
            last_layer(done - 2)


def divisor(value, limit):
    return max(d for d in range(1, limit + 1) if value % d == 0)


def body(
    records,
    lift_weight,
    lift_bias,
    conv_weight,
    conv_bias,
    out_weight,
    live_count,
    trace_node,
    node_owner,
):
    _, comps, nodes, window = records.shape
    holders = lax.axis_size("gather")
    windows = lax.axis_size("tm")
    shots = holders * records.shape[0]
    couples = shots // QUAD
    blocks = couples // 2
    slots = (nodes + holders - 1) // holders
    dils = (1, 4, 2, 8)
    rows = round_up(6 * slots, 16) + round_up(3 * slots, 16)
    span = window + 2 * HALO

    planes = holders // CORES
    vmem = pl.BlockSpec(memory_space=pltpu.VMEM)
    smem = pl.BlockSpec(memory_space=pltpu.SMEM)
    hbm = pl.BlockSpec(memory_space=pltpu.HBM)
    like = jax.ShapeDtypeStruct

    def after(value, other):
        return lax.optimization_barrier((value, other))[0]

    def kernel(function, operands, specs, outs, scratch, limit, flops, name):
        return pl.pallas_call(
            function,
            out_shape=outs,
            in_specs=[smem] + specs,
            out_specs=jax.tree.map(lambda _: vmem, outs),
            scratch_shapes=scratch,
            compiler_params=pltpu.CompilerParams(vmem_limit_bytes=limit << 20),
            cost_estimate=pl.CostEstimate(flops=flops, bytes_accessed=1 << 10, transcendentals=0),
            name=name,
        )(place, *operands)

    def fetching(function, raw, memories, outs, name):
        scratch = [memory(a.shape, a.dtype) for memory, a in zip(memories, raw)]
        scratch.append(pltpu.SemaphoreType.DMA((len(raw),)))
        return kernel(function, raw, [hbm] * len(raw), outs, scratch, 16, 10**5, name)

    place = jnp.stack([lax.axis_index("gather"), lax.axis_index("tm")]).astype(jnp.int32)
    taps = jnp.transpose(conv_weight, (0, 3, 4, 1, 2)).reshape(2, -1, CH)

    own = records[0]
    even = lax.axis_index("tm") % 2 == 0
    pack = lambda part: jnp.transpose(part, (1, 0, 2)).reshape(nodes, comps * HALO)
    first, last = pack(own[:, :, :HALO]), pack(own[:, :, window - HALO :])
    got = []
    for begin in range(2):
        pairs = [(w, w + 1) for w in range(begin, windows - 1, 2)]
        pairs += [(b, a) for a, b in pairs]
        got.append(lax.ppermute(jnp.where(even == (begin == 0), last, first), "tm", pairs))
    right, left = jnp.where(even, got[0], got[1]), jnp.where(even, got[1], got[0])
    sent = jnp.concatenate([own, jnp.concatenate([right, left], axis=1)[None]], axis=0)

    w0, w1, w2, wide_bias, shift, pick, keep = fetching(
        functools.partial(prep_kernel, dils, slots),
        (live_count, trace_node, taps[0], jnp.transpose(lift_weight), lift_bias[None, :], conv_bias)
        + (node_owner[None, :],),
        [pltpu.SMEM] * 2 + [pltpu.VMEM] * 5,
        (
            like((KROWS, 2 * LANES), BF16),
            like((2, LANES, LANES), BF16),
            like((2, LANES, LANES), BF16),
            like((conv_bias.shape[0], LANES), F32),
            like((span, 2 * window), BF16),
            like((shots, rows, nodes), BF16),
            like((couples, 3, 16, HALF), F32),
        ),
        "weights",
    )
    sent = after(sent, wide_bias)

    def exchanged(block, distance):
        return lax.ppermute(block, "gather", [(g, g ^ distance) for g in range(holders)])

    near_blocks = [sent] + [exchanged(sent, d) for d in (CORES, 1, CORES + 1)]
    far = [exchanged(sent, CORES * r) for r in range(2, planes)]

    b3, b4, ow = fetching(
        functools.partial(band_kernel, dils, blocks),
        (taps[1], out_weight),
        [pltpu.VMEM] * 2,
        (
            like((blocks * blocks, 3 * LANES, LANES), BF16),
            like((blocks * blocks, 3 * LANES, LANES), BF16),
            like((GROUP * COMPS, LANES), BF16),
        ),
        "bands",
    )

    step = divisor(slots, 2)
    row_stride = round_up(rows, 16) + 8
    x2 = like((slots, span, 3 * HALF), BF16)
    held = like((slots, QUAD * COMPS, window), F32)
    parts = (2, PARTS, row_stride, window)
    operands = [after(pick, ow), keep, w0, w1, w2, wide_bias, shift, *near_blocks]
    near = kernel(
        functools.partial(near_kernel, dils, windows, step),
        operands,
        [vmem] * len(operands),
        (x2, held),
        [pltpu.VMEM(parts, F32)],
        24,
        10**5,
        "near",
    )

    operands = [pick, keep, w0, w1, w2, b3, b4, ow, wide_bias, shift]
    for r in range(0, len(far), 2):
        operands += far[r : r + 2] + [exchanged(after(block, near[1]), 1) for block in far[r : r + 2]]
    operands += near
    out = kernel(
        functools.partial(main_kernel, dils, windows, step, 1),
        operands,
        [vmem] * len(operands),
        like((shots, slots, comps, window), F32),
        [
            pltpu.VMEM((couples - 1, *parts), F32),
            pltpu.VMEM((couples - 1, *x2.shape), BF16),
            pltpu.VMEM((couples - 1, *held.shape), F32),
            pltpu.VMEM((blocks, slots, window, 3 * LANES), BF16),
        ],
        36,
        4 * 10**9,
        "layers",
    )
    return jnp.transpose(out, (0, 2, 1, 3))


def solution(mesh):
    return jax.shard_map(
        body,
        mesh=mesh,
        in_specs=(P("gather", None, None, "tm"), P(), P(), P(), P(), P(), P(), P(), P()),
        out_specs=P(None, None, "gather", "tm"),
        check_vma=False,
    )
```

```python
import functools
import itertools

import jax
import jax.numpy as jnp
from jax import lax
from jax.experimental import pallas as pl
from jax.experimental.pallas import tpu as pltpu
from jax.sharding import PartitionSpec as P

F32 = jnp.float32
BF16 = jnp.bfloat16
CH = 32
CORES = 2
COMPS = 4
GROUP = 8
LANES = GROUP * CH
HALO = 16
QUAD = 4
HALF = QUAD * CH
KROWS = 128
PARTS = QUAD * COMPS + 2 * QUAD


def iota(shape, dim):
    return lax.broadcasted_iota(jnp.int32, shape, dim)


def dot(a, b):
    return jnp.dot(a, b, preferred_element_type=F32)


def dot_t(a, b):
    return lax.dot_general(a, b, (((1,), (1,)), ((), ())), preferred_element_type=F32)


def onehot(cond):
    return cond.astype(F32).astype(BF16)


def band_links(dilation, offset):
    return [
        a
        for a in range(3)
        if any(s + GROUP * offset == t + (a - 1) * dilation for s in range(GROUP) for t in range(GROUP))
    ]


def split3(value):
    terms = []
    for _ in range(3):
        term = value.astype(BF16)
        terms.append(term)
        value = value - term.astype(F32)
    return terms


def shot_of(place_ref, n, shots):
    planes = shots // CORES
    plane = place_ref[0] // CORES
    core = place_ref[0] - CORES * plane
    return CORES * (plane ^ (n % planes)) + (core if n < planes else 1 - core)


def couple_of(place_ref, relative):
    return (place_ref[0] // (2 * CORES)) ^ relative


def table_kernel(dils, slots, place_ref, live_ref, trace_ref, owner_ref, pick_ref, keep_ref):
    shots, rows, nodes = pick_ref.shape
    split = round_up(6 * slots, 16)
    me = place_ref[0]

    mine = (owner_ref[...] == me).astype(F32)
    before = onehot(iota((nodes, nodes), 0) < iota((nodes, nodes), 1))
    rank = dot(jnp.broadcast_to(mine, (8, nodes)).astype(BF16), before)[0:1, :]
    node_ids = iota((1, nodes), 1).astype(F32)

    def nodes_of(slot_index):
        held = jnp.where((rank == slot_index.astype(F32)) & (mine > 0.5), 1.0, 0.0)
        node = jnp.sum(held * node_ids, axis=1, keepdims=True)
        there = jnp.sum(held, axis=1, keepdims=True)
        return jnp.where(there > 0.5, node, -1.0e6).astype(jnp.int32)

    row_id = iota((rows, nodes), 0)
    late = row_id >= split
    row_id = jnp.where(late, row_id - split, row_id)
    tap = jnp.zeros((rows, nodes), jnp.int32)
    for m in range(1, 7):
        tap = tap + (row_id >= m * slots).astype(jnp.int32)
    second = (tap >= 3).astype(jnp.int32)
    shift = dils[0] * (tap - 3 * second - 1) + jnp.where(late, 0, dils[1] * (2 * second - 1))
    target = nodes_of(row_id - slots * tap)
    target = jnp.where(tap >= jnp.where(late, 3, 6), -1000000, target + shift)

    node_lane = iota((rows, nodes), 1)
    for n in range(shots):
        s = shot_of(place_ref, n, shots)
        pick_ref[n] = onehot((node_lane == target - trace_ref[s, 0]) & (node_lane < live_ref[s]))

    slot_rows = keep_ref.shape[2]
    own_node = nodes_of(iota((slot_rows, nodes), 0))
    shot_lane = iota((slot_rows, HALF), 1) >> 5
    for c in range(shots // QUAD):
        base = QUAD * couple_of(place_ref, c)
        for b in range(3):
            first = jnp.zeros((slot_rows, HALF), jnp.int32)
            count = jnp.zeros((slot_rows, HALF), jnp.int32)
            for w in range(QUAD):
                at = shot_lane == (w if b == 1 else w ^ 2)
                first = jnp.where(at, trace_ref[base + w, 0], first)
                count = jnp.where(at, live_ref[base + w], count)
            trace = own_node + dils[1] * (b - 1) - first
            keep_ref[c, b] = ((trace >= 0) & (trace < count)).astype(F32)


def fetch(sources, places, sems):
    copies = [pltpu.make_async_copy(a, b, sems.at[n]) for n, (a, b) in enumerate(zip(sources, places))]
    for copy in copies:
        copy.start()
    for copy in copies:
        copy.wait()
    return places


def prep_kernel(dils, slots, place_ref, *refs):
    w0_ref, w1_ref, w2_ref, wide_bias_ref, shift_ref, pick_ref, keep_ref = refs[7:14]
    live_ref, trace_ref, cw_ref, lift_ref, lift_bias_ref, bias_ref, owner_ref = fetch(
        refs[:7], refs[14:21], refs[21]
    )
    table_kernel(dils, slots, place_ref, live_ref, trace_ref, owner_ref, pick_ref, keep_ref)

    rows8 = [lift_ref[...].astype(F32)] + [term.astype(F32) for term in split3(lift_bias_ref[...])]
    table = jnp.concatenate(rows8 + [jnp.zeros((1, CH), F32)], axis=0).astype(BF16)
    data_rows = 3 * QUAD * COMPS
    r8 = iota((KROWS, 8), 0)
    part = jnp.where(r8 < data_rows, r8 & (COMPS - 1), COMPS + ((r8 >> 2) & 3))
    values = dot(onehot((part == iota((KROWS, 8), 1)) & (r8 < 2 * data_rows)), table).astype(BF16)
    wide = iota((CH, 2 * LANES), 1)
    spread = onehot(iota((CH, 2 * LANES), 0) == (wide & 31))
    rr = iota((KROWS, 2 * LANES), 0)
    cc = iota((KROWS, 2 * LANES), 1)
    row_node = jnp.where(rr < data_rows, rr >> 4, (rr - data_rows) >> 4)
    row_shot = jnp.where(rr < data_rows, rr >> 2, rr) & (QUAD - 1)
    place = (cc >> 6) & 3
    node = jnp.where((cc >= LANES) & (place < 2), 1 - place, place)
    same = (row_node == node) & (row_shot == 2 * (cc >> 8) + ((cc >> 5) & 1)) & (rr < 2 * data_rows)
    w0_ref[...] = jnp.where(same & (place < 3), dot(values, spread), 0.0).astype(BF16)

    widen = onehot((iota((LANES, CH), 0) & 31) == iota((LANES, CH), 1))
    kr = iota((LANES, LANES), 0)
    kc = iota((LANES, LANES), 1)
    same_shot = ((kr >> 5) & 1) == ((kc >> 5) & 1)
    sr = iota((3 * CH, LANES), 0)
    sc = iota((3 * CH, LANES), 1)
    for layer, ref, odd_taps in ((0, w1_ref, (1, 0, 2, 3)), (1, w2_ref, (1, 0, 3, 2))):
        base = 3 * layer
        tall = [
            dot_t(widen, cw_ref[(base + a) * 3 * CH : (base + a + 1) * 3 * CH, :]).astype(BF16)
            for a in range(3)
        ]
        for odd, (k_taps, n_taps) in enumerate((((0, 1, 2, 3), (0, 1, 3, 2)), (odd_taps, (1, 0, 2, 3)))):
            place = sum(jnp.where((sc >> 6) == y, n_taps[y], 0) for y in range(4))
            spread2 = onehot(((sr >> 5) == place) & ((sr & 31) == (sc & 31)))
            total = jnp.zeros((LANES, LANES), F32)
            for x in range(4):
                if k_taps[x] < 3:
                    total = jnp.where(((kr >> 6) == x) & same_shot, dot(tall[k_taps[x]], spread2), total)
            ref[odd] = total.astype(BF16)

    span = shift_ref.shape[0]
    window = span - 2 * HALO
    source = iota(shift_ref.shape, 0)
    source = jnp.where(source < window + HALO, source, source + window // 2 - HALO)
    shift_ref[...] = onehot(iota(shift_ref.shape, 1) == source)

    tile = onehot(iota((CH, LANES), 0) == (iota((CH, LANES), 1) & 31))
    wide_bias_ref[...] = sum(dot(term, tile) for term in split3(bias_ref[...]))


def band_kernel(dils, blocks, place_ref, *refs):
    b3_ref, b4_ref, ow_ref = refs[2:5]
    cw_ref, out_w_ref = fetch(refs[:2], refs[5:7], refs[7])
    widen = onehot((iota((LANES, CH), 0) & 31) == iota((LANES, CH), 1))

    er = iota((3 * CH, 3 * LANES), 0)
    ec = iota((3 * CH, 3 * LANES), 1)
    spread3 = onehot(((er >> 5) == (ec >> 8)) & ((er & 31) == (ec & 31)))
    row_lane = iota((LANES, 3 * LANES), 0)
    col_lane = iota((LANES, 3 * LANES), 1) & (LANES - 1)

    def shots_in(lane, block):
        couple = jnp.where(lane < HALF, couple_of(place_ref, 2 * block), couple_of(place_ref, 2 * block + 1))
        return QUAD * couple + ((lane >> 5) & (QUAD - 1))

    def expanded(layer, a):
        base = ((layer - 2) * 3 + a) * 3 * CH
        return dot(dot_t(widen, cw_ref[base : base + 3 * CH, :]).astype(BF16), spread3)

    for layer, ref in ((2, b3_ref), (3, b4_ref)):
        linked_taps = band_links(dils[layer], 0) if blocks == 1 else range(3)
        for out_block in range(blocks):
            for in_block in range(blocks):
                total = jnp.zeros((LANES, 3 * LANES), F32)
                for a in linked_taps:
                    reach = shots_in(col_lane, out_block) + (a - 1) * dils[layer]
                    total = total + jnp.where(shots_in(row_lane, in_block) == reach, expanded(layer, a), 0.0)
                for e in range(3):
                    ref[out_block * blocks + in_block, e * LANES : (e + 1) * LANES, :] = total[
                        :, e * LANES : (e + 1) * LANES
                    ].astype(BF16)

    rows = GROUP * COMPS
    pick = onehot((iota((rows, COMPS), 0) & (COMPS - 1)) == iota((rows, COMPS), 1))
    mine = dot(pick, out_w_ref[...]).astype(BF16)
    tile = onehot(iota((CH, LANES), 0) == (iota((CH, LANES), 1) & 31))
    same = (iota((rows, LANES), 0) >> 2) == (iota((rows, LANES), 1) >> 5)
    ow_ref[...] = jnp.where(same, dot(mine, tile), 0.0).astype(BF16)


def round_up(value, unit):
    return -(-value // unit) * unit


def shifted(value, dilation):
    span = value.shape[0]
    return jnp.concatenate(
        [
            pltpu.roll(value, dilation, axis=0).astype(BF16),
            value.astype(BF16),
            pltpu.roll(value, span - dilation, axis=0).astype(BF16),
        ],
        axis=1,
    )


class Shots:
    def __init__(
        self, dils, windows, step, couple, place_ref, recs, pick_ref, keep_ref, w0_ref, w1_ref, w2_ref,
        bias_ref, shift_ref, part_ref, x2_ref, rec_out_ref,
    ):
        self.dils, self.step, self.couple = dils, step, couple
        self.keep_ref, self.w0_ref, self.w1_ref, self.w2_ref = keep_ref, w0_ref, w1_ref, w2_ref
        self.bias_ref, self.shift_ref, self.x2_ref = bias_ref, shift_ref, x2_ref
        shots, rows, nodes = pick_ref.shape
        planes = shots // CORES
        self.slots = slots = x2_ref.shape[0]
        self.window = window = part_ref.shape[-1]
        self.rows, self.split = part_ref.shape[2], round_up(6 * slots, 16)
        self.span = window + 2 * HALO
        at = place_ref[1]
        self.right_ok = (at < windows - 1).astype(F32)
        self.left_ok = (at > 0).astype(F32)
        self.low_half = iota((self.span, HALF), 1) < CH * CORES

        lane = iota((nodes, 2 * window), 1)
        all_ok = jnp.where(
            lane < window, 1.0, jnp.where(lane < window + window // 2, self.right_ok, self.left_ok)
        ).astype(BF16)

        def put(part, swapped, value):
            for half in range(2):
                lanes = value[:, half * window : (half + 1) * window]
                part_ref[half, part, 0 : self.split] = lanes[0 : self.split]
                part_ref[half, swapped, self.split : rows] = lanes[self.split : rows]

        for x, rec_ref in enumerate(recs):
            n = 2 * couple + x % 2 + (planes if x >= 2 else 0)
            within = shot_of(place_ref, n, shots) & (QUAD - 1)
            edge = rec_ref[COMPS].astype(F32)
            for k in range(COMPS):
                turned = edge if k == 0 else pltpu.roll(edge, window - HALO * k, axis=1)
                both = jnp.concatenate([rec_ref[k], turned.astype(BF16)], axis=1)
                put(within * COMPS + k, (within ^ 2) * COMPS + k, dot(pick_ref[n], both))
            alive = dot(pick_ref[n], all_ok)
            for copy in range(2):
                first = QUAD * COMPS + QUAD * copy
                put(first + within, first + (within ^ 2), alive)

        self.half_rows = part_ref.shape[1] * self.rows
        self.part2 = part_ref.reshape(2 * self.half_rows, window)
        for q in range(slots):
            first = self.split + slots + q
            for half in range(2):
                pair = self.part2[pl.ds(first + (1 - half) * 8 * self.rows, 8, stride=self.rows), :]
                rec_out_ref[q, half * 8 : (half + 1) * 8] = pair

    def inside(self, value):
        w = self.window
        return jnp.concatenate(
            [value[0:w], value[w : w + HALO] * self.right_ok, value[w + HALO :] * self.left_ok], axis=0
        )

    def item_rows(self, q, b):
        start = (3 * (b // 2) * self.slots if b != 1 else self.split) + q
        halves = []
        for half in range(2):
            base = half * self.half_rows + start
            flags = base + QUAD * COMPS * self.rows
            pieces = [
                self.part2[pl.ds(base + a * self.slots, QUAD * COMPS, stride=self.rows), :] for a in range(3)
            ]
            for a in range(3):
                alive = self.part2[pl.ds(flags + a * self.slots, 2 * QUAD, stride=self.rows), :]
                pieces += [alive, alive]
            pieces.append(jnp.zeros((KROWS - 6 * QUAD * COMPS, self.window), F32))
            halves.append(jnp.concatenate(pieces, axis=0).astype(BF16))
        return jnp.concatenate(halves, axis=1)

    def items(self, group):
        return [(group * self.step + i, b) for i in range(self.step) for b in range(3)]

    def first_inputs(self, group):
        items = self.items(group)
        lhs = []
        for n in range(0, len(items), 2):
            some = jnp.concatenate([self.item_rows(q, b) for q, b in items[n : n + 2]], axis=0)
            moved = dot_t(self.shift_ref[...], some).astype(BF16)
            lhs += [moved[:, m : m + KROWS] for m in range(0, moved.shape[1], KROWS)]
        lifted = dot(jnp.concatenate(lhs, axis=0), self.w0_ref[...]).astype(BF16)
        return lifted[:, 0:LANES], lifted[:, LANES:]

    def taps_added(self, even, odd, dilation):
        mid = jnp.where(self.low_half, odd[:, 0:HALF], even[:, 0:HALF])
        late = jnp.where(self.low_half, odd[:, HALF:], even[:, HALF:])
        early = pltpu.roll(jnp.where(self.low_half, even[:, 0:HALF], odd[:, 0:HALF]), HALF // 2, axis=1)
        return (
            pltpu.roll(early, dilation, axis=0) + mid + pltpu.roll(late, self.span - dilation, axis=0)
        )

    def first_layer(self, group, even, odd):
        y_even, y_odd = dot(even, self.w1_ref[0]), dot(odd, self.w1_ref[1])
        x1 = []
        for n, (q, b) in enumerate(self.items(group)):
            at = slice(n * self.span, (n + 1) * self.span)
            old = jnp.where(self.low_half, odd[at, 0:HALF].astype(F32), even[at, 0:HALF].astype(F32))
            total = self.taps_added(y_even[at], y_odd[at], self.dils[0])
            new = jnp.maximum(total + self.bias_ref[0:1, 0:HALF], 0.0)
            x1.append(self.inside((old + new) * self.keep_ref[self.couple, b, q : q + 1, :]))
        even, odd, own = [], [], []
        for i in range(self.step):
            t0, t1, t2 = x1[3 * i : 3 * i + 3]
            t2 = t2.astype(BF16)
            even.append(jnp.concatenate([jnp.where(self.low_half, t0, t1).astype(BF16), t2], axis=1))
            odd.append(jnp.concatenate([jnp.where(self.low_half, t1, t0).astype(BF16), t2], axis=1))
            own.append(t1.astype(BF16))
        return jnp.concatenate(even, axis=0), jnp.concatenate(odd, axis=0), own

    def second_layer(self, group, even, odd, own):
        even, odd = dot(even, self.w2_ref[0]), dot(odd, self.w2_ref[1])
        for i in range(self.step):
            q = group * self.step + i
            at = slice(i * self.span, (i + 1) * self.span)
            total = self.taps_added(even[at], odd[at], self.dils[1])
            new = jnp.maximum(total + self.bias_ref[1:2, 0:HALF], 0.0)
            x2 = (own[i].astype(F32) + new) * self.keep_ref[self.couple, 1, q : q + 1, :]
            self.x2_ref[q] = shifted(self.inside(x2), self.dils[2])


def staged(work):
    inputs, middle = {}, {}
    for t in range(len(work) + 2):
        if t < len(work):
            stage, group = work[t]
            inputs[t] = stage.first_inputs(group)
        if 0 <= t - 1 < len(work):
            stage, group = work[t - 1]
            middle[t - 1] = stage.first_layer(group, *inputs.pop(t - 1))
        if 0 <= t - 2:
            stage, group = work[t - 2]
            stage.second_layer(group, *middle.pop(t - 2))
        yield t


def near_kernel(dils, windows, step, place_ref, *refs):
    pick_ref, keep_ref, w0_ref, w1_ref, w2_ref, bias_ref, shift_ref = refs[:7]
    x2_ref, rec_out_ref, part_ref = refs[7 + QUAD :]
    stage = Shots(
        dils, windows, step, 0, place_ref, refs[7 : 7 + QUAD], pick_ref, keep_ref, w0_ref, w1_ref, w2_ref,
        bias_ref, shift_ref, part_ref, x2_ref, rec_out_ref,
    )
    for _ in staged([(stage, group) for group in range(x2_ref.shape[0] // step)]):
        pass


def main_kernel(dils, windows, step, near, place_ref, *refs):
    shots = refs[0].shape[0]
    couples = shots // QUAD
    pick_ref, keep_ref, w0_ref, w1_ref, w2_ref, b3_ref, b4_ref, ow_ref, bias_ref, shift_ref = refs[:10]
    refs = refs[10:]
    rec_refs, refs = refs[: QUAD * (couples - near)], refs[QUAD * (couples - near) :]
    done_refs, refs = refs[: 2 * near], refs[2 * near :]
    out_ref, part_ref, x2_all, rec_all, x3_ref = refs
    blocks = couples // 2
    slots, window = out_ref.shape[1], out_ref.shape[3]
    span = window + 2 * HALO
    right_ok = (place_ref[1] < windows - 1).astype(F32)
    left_ok = (place_ref[1] > 0).astype(F32)

    stages = []
    x2_refs, rec_refs_out = list(done_refs[0::2]), list(done_refs[1::2])
    for c in range(near, couples):
        x2_refs.append(x2_all.at[c - near])
        rec_refs_out.append(rec_all.at[c - near])
        stages.append(
            Shots(
                dils, windows, step, c, place_ref, rec_refs[QUAD * (c - near) : QUAD * (c - near + 1)],
                pick_ref, keep_ref, w0_ref, w1_ref, w2_ref, bias_ref, shift_ref, part_ref.at[c - near],
                x2_refs[-1], rec_refs_out[-1],
            )
        )

    def receiver_layer(parts_of, weights, layer, block, group, out_rows):
        y = None
        for other in range(blocks):
            term = dot(jnp.concatenate(parts_of(other), axis=0), weights[block * blocks + other])
            y = term if y is None else y + term
        results = []
        for i, part in enumerate(parts_of(block)):
            q = group * step + i
            keep = jnp.concatenate([keep_ref[2 * block + c, 1, q : q + 1, :] for c in range(2)], axis=1)
            old = part[:, LANES : 2 * LANES].astype(F32)
            new = jnp.maximum(y[i * out_rows : (i + 1) * out_rows] + bias_ref[layer : layer + 1, :], 0.0)
            results.append((old + new) * keep)
        return results

    def third_layer(group):
        def parts_of(block):
            return [
                jnp.concatenate(
                    [
                        x2_refs[2 * block + c][group * step + i, :, e * HALF : (e + 1) * HALF]
                        for e in range(3)
                        for c in range(2)
                    ],
                    axis=1,
                )
                for i in range(step)
            ]

        for block in range(blocks):
            for i, value in enumerate(receiver_layer(parts_of, b3_ref, 2, block, group, span)):
                value = jnp.concatenate(
                    [
                        value[0:window],
                        value[window : window + HALO] * right_ok,
                        value[window + HALO :] * left_ok,
                    ],
                    axis=0,
                )
                x3_ref[block, group * step + i] = shifted(value, dils[3])[0:window]

    def last_layer(group):
        def parts_of(block):
            return [x3_ref[block, group * step + i] for i in range(step)]

        for block in range(blocks):
            for i, value in enumerate(receiver_layer(parts_of, b4_ref, 3, block, group, window)):
                q = group * step + i
                noise = dot_t(ow_ref[...], value.astype(BF16))
                record = jnp.concatenate([rec_refs_out[2 * block + c][q] for c in range(2)], axis=0)
                done = (record + noise).reshape(GROUP, COMPS, window)
                for c in range(2):
                    first = QUAD * couple_of(place_ref, 2 * block + c)
                    out_ref[pl.ds(first, QUAD), q] = done[c * QUAD : (c + 1) * QUAD]

    groups = slots // step
    work = [(stage, group) for group in range(groups) for stage in stages]
    lag = len(stages)
    for t in itertools.chain(staged(work), range(len(work) + 2, len(work) + 2 + 2 * lag)):
        done, rest = divmod(t - 2, lag)
        if rest == 0 and 0 <= done - 1 < groups:
            third_layer(done - 1)
        if rest == 0 and 0 <= done - 2 < groups:
            last_layer(done - 2)


def divisor(value, limit):
    return max(d for d in range(1, limit + 1) if value % d == 0)


def body(
    records,
    lift_weight,
    lift_bias,
    conv_weight,
    conv_bias,
    out_weight,
    live_count,
    trace_node,
    node_owner,
):
    _, comps, nodes, window = records.shape
    holders = lax.axis_size("gather")
    windows = lax.axis_size("tm")
    shots = holders * records.shape[0]
    couples = shots // QUAD
    blocks = couples // 2
    slots = (nodes + holders - 1) // holders
    dils = (1, 4, 2, 8)
    rows = round_up(6 * slots, 16) + round_up(3 * slots, 16)
    span = window + 2 * HALO

    planes = holders // CORES
    vmem = pl.BlockSpec(memory_space=pltpu.VMEM)
    smem = pl.BlockSpec(memory_space=pltpu.SMEM)
    hbm = pl.BlockSpec(memory_space=pltpu.HBM)
    like = jax.ShapeDtypeStruct

    def after(value, other):
        return lax.optimization_barrier((value, other))[0]

    def kernel(function, operands, specs, outs, scratch, limit, flops, name):
        return pl.pallas_call(
            function,
            out_shape=outs,
            in_specs=[smem] + specs,
            out_specs=jax.tree.map(lambda _: vmem, outs),
            scratch_shapes=scratch,
            compiler_params=pltpu.CompilerParams(vmem_limit_bytes=limit << 20),
            cost_estimate=pl.CostEstimate(flops=flops, bytes_accessed=1 << 10, transcendentals=0),
            name=name,
        )(place, *operands)

    def fetching(function, raw, memories, outs, name):
        scratch = [memory(a.shape, a.dtype) for memory, a in zip(memories, raw)]
        scratch.append(pltpu.SemaphoreType.DMA((len(raw),)))
        return kernel(function, raw, [hbm] * len(raw), outs, scratch, 16, 10**5, name)

    place = jnp.stack([lax.axis_index("gather"), lax.axis_index("tm")]).astype(jnp.int32)
    taps = jnp.transpose(conv_weight, (0, 3, 4, 1, 2)).reshape(2, -1, CH)

    own = records[0]
    even = lax.axis_index("tm") % 2 == 0
    pack = lambda part: jnp.transpose(part, (1, 0, 2)).reshape(nodes, comps * HALO)
    first, last = pack(own[:, :, :HALO]), pack(own[:, :, window - HALO :])
    got = []
    for begin in range(2):
        pairs = [(w, w + 1) for w in range(begin, windows - 1, 2)]
        pairs += [(b, a) for a, b in pairs]
        got.append(lax.ppermute(jnp.where(even == (begin == 0), last, first), "tm", pairs))
    right, left = jnp.where(even, got[0], got[1]), jnp.where(even, got[1], got[0])
    sent = jnp.concatenate([own, jnp.concatenate([right, left], axis=1)[None]], axis=0)

    w0, w1, w2, wide_bias, shift, pick, keep = fetching(
        functools.partial(prep_kernel, dils, slots),
        (live_count, trace_node, taps[0], jnp.transpose(lift_weight), lift_bias[None, :], conv_bias)
        + (node_owner[None, :],),
        [pltpu.SMEM] * 2 + [pltpu.VMEM] * 5,
        (
            like((KROWS, 2 * LANES), BF16),
            like((2, LANES, LANES), BF16),
            like((2, LANES, LANES), BF16),
            like((conv_bias.shape[0], LANES), F32),
            like((span, 2 * window), BF16),
            like((shots, rows, nodes), BF16),
            like((couples, 3, 16, HALF), F32),
        ),
        "weights",
    )
    sent = after(sent, wide_bias)

    def exchanged(block, distance):
        return lax.ppermute(block, "gather", [(g, g ^ distance) for g in range(holders)])

    near_blocks = [sent] + [exchanged(sent, d) for d in (CORES, 1, CORES + 1)]
    far = [exchanged(sent, CORES * r) for r in range(2, planes)]

    b3, b4, ow = fetching(
        functools.partial(band_kernel, dils, blocks),
        (taps[1], out_weight),
        [pltpu.VMEM] * 2,
        (
            like((blocks * blocks, 3 * LANES, LANES), BF16),
            like((blocks * blocks, 3 * LANES, LANES), BF16),
            like((GROUP * COMPS, LANES), BF16),
        ),
        "bands",
    )

    step = 1
    row_stride = round_up(rows, 16) + 8
    x2 = like((slots, span, 3 * HALF), BF16)
    held = like((slots, QUAD * COMPS, window), F32)
    parts = (2, PARTS, row_stride, window)
    operands = [pick, keep, w0, w1, w2, wide_bias, shift, *near_blocks]
    near = kernel(
        functools.partial(near_kernel, dils, windows, step),
        operands,
        [vmem] * len(operands),
        (x2, held),
        [pltpu.VMEM(parts, F32)],
        24,
        10**5,
        "near",
    )

    operands = [pick, keep, w0, w1, w2, b3, b4, ow, wide_bias, shift]
    for r in range(0, len(far), 2):
        operands += far[r : r + 2] + [exchanged(after(block, near[1]), 1) for block in far[r : r + 2]]
    operands += near
    out = kernel(
        functools.partial(main_kernel, dils, windows, step, 1),
        operands,
        [vmem] * len(operands),
        like((shots, slots, comps, window), F32),
        [
            pltpu.VMEM((couples - 1, *parts), F32),
            pltpu.VMEM((couples - 1, *x2.shape), BF16),
            pltpu.VMEM((couples - 1, *held.shape), F32),
            pltpu.VMEM((blocks, slots, window, 3 * LANES), BF16),
        ],
        36,
        4 * 10**9,
        "layers",
    )
    return jnp.transpose(out, (0, 2, 1, 3))


def solution(mesh):
    return jax.shard_map(
        body,
        mesh=mesh,
        in_specs=(P("gather", None, None, "tm"), P(), P(), P(), P(), P(), P(), P(), P()),
        out_specs=P(None, None, "gather", "tm"),
        check_vma=False,
    )
```

```python
import functools
import itertools

import jax
import jax.numpy as jnp
from jax import lax
from jax.experimental import pallas as pl
from jax.experimental.pallas import tpu as pltpu
from jax.sharding import PartitionSpec as P

F32 = jnp.float32
BF16 = jnp.bfloat16
CH = 32
CORES = 2
COMPS = 4
GROUP = 8
LANES = GROUP * CH
HALO = 16
QUAD = 4
HALF = QUAD * CH
KROWS = 128
PARTS = QUAD * COMPS + 2 * QUAD


def iota(shape, dim):
    return lax.broadcasted_iota(jnp.int32, shape, dim)


def dot(a, b):
    return jnp.dot(a, b, preferred_element_type=F32)


def dot_t(a, b):
    return lax.dot_general(a, b, (((1,), (1,)), ((), ())), preferred_element_type=F32)


def onehot(cond):
    return cond.astype(F32).astype(BF16)


def band_links(dilation, offset):
    return [
        a
        for a in range(3)
        if any(s + GROUP * offset == t + (a - 1) * dilation for s in range(GROUP) for t in range(GROUP))
    ]


def split3(value):
    terms = []
    for _ in range(3):
        term = value.astype(BF16)
        terms.append(term)
        value = value - term.astype(F32)
    return terms


def shot_of(place_ref, n, shots):
    planes = shots // CORES
    plane = place_ref[0] // CORES
    core = place_ref[0] - CORES * plane
    return CORES * (plane ^ (n % planes)) + (core if n < planes else 1 - core)


def couple_of(place_ref, relative):
    return (place_ref[0] // (2 * CORES)) ^ relative


def table_kernel(dils, slots, place_ref, live_ref, trace_ref, owner_ref, pick_ref, keep_ref):
    shots, rows, nodes = pick_ref.shape
    split = round_up(6 * slots, 16)
    me = place_ref[0]

    mine = (owner_ref[...] == me).astype(F32)
    before = onehot(iota((nodes, nodes), 0) < iota((nodes, nodes), 1))
    rank = dot(jnp.broadcast_to(mine, (8, nodes)).astype(BF16), before)[0:1, :]
    node_ids = iota((1, nodes), 1).astype(F32)

    def nodes_of(slot_index):
        held = jnp.where((rank == slot_index.astype(F32)) & (mine > 0.5), 1.0, 0.0)
        node = jnp.sum(held * node_ids, axis=1, keepdims=True)
        there = jnp.sum(held, axis=1, keepdims=True)
        return jnp.where(there > 0.5, node, -1.0e6).astype(jnp.int32)

    row_id = iota((rows, nodes), 0)
    late = row_id >= split
    row_id = jnp.where(late, row_id - split, row_id)
    tap = jnp.zeros((rows, nodes), jnp.int32)
    for m in range(1, 7):
        tap = tap + (row_id >= m * slots).astype(jnp.int32)
    second = (tap >= 3).astype(jnp.int32)
    shift = dils[0] * (tap - 3 * second - 1) + jnp.where(late, 0, dils[1] * (2 * second - 1))
    target = nodes_of(row_id - slots * tap)
    target = jnp.where(tap >= jnp.where(late, 3, 6), -1000000, target + shift)

    node_lane = iota((rows, nodes), 1)
    for n in range(shots):
        s = shot_of(place_ref, n, shots)
        pick_ref[n] = onehot((node_lane == target - trace_ref[s, 0]) & (node_lane < live_ref[s]))

    slot_rows = keep_ref.shape[2]
    own_node = nodes_of(iota((slot_rows, nodes), 0))
    shot_lane = iota((slot_rows, HALF), 1) >> 5
    for c in range(shots // QUAD):
        base = QUAD * couple_of(place_ref, c)
        for b in range(3):
            first = jnp.zeros((slot_rows, HALF), jnp.int32)
            count = jnp.zeros((slot_rows, HALF), jnp.int32)
            for w in range(QUAD):
                at = shot_lane == (w if b == 1 else w ^ 2)
                first = jnp.where(at, trace_ref[base + w, 0], first)
                count = jnp.where(at, live_ref[base + w], count)
            trace = own_node + dils[1] * (b - 1) - first
            keep_ref[c, b] = ((trace >= 0) & (trace < count)).astype(F32)


def fetch(sources, places, sems):
    copies = [pltpu.make_async_copy(a, b, sems.at[n]) for n, (a, b) in enumerate(zip(sources, places))]
    for copy in copies:
        copy.start()
    for copy in copies:
        copy.wait()
    return places


def prep_kernel(dils, slots, place_ref, *refs):
    w0_ref, w1_ref, w2_ref, wide_bias_ref, shift_ref, pick_ref, keep_ref = refs[7:14]
    half = refs[2].shape[0] // 2
    live_ref, trace_ref, cw_ref, lift_ref, lift_bias_ref, bias_ref, owner_ref = fetch(
        (*refs[:2], refs[2].at[0:half], *refs[3:7]), refs[14:21], refs[21]
    )
    table_kernel(dils, slots, place_ref, live_ref, trace_ref, owner_ref, pick_ref, keep_ref)

    rows8 = [lift_ref[...].astype(F32)] + [term.astype(F32) for term in split3(lift_bias_ref[...])]
    table = jnp.concatenate(rows8 + [jnp.zeros((1, CH), F32)], axis=0).astype(BF16)
    data_rows = 3 * QUAD * COMPS
    r8 = iota((KROWS, 8), 0)
    part = jnp.where(r8 < data_rows, r8 & (COMPS - 1), COMPS + ((r8 >> 2) & 3))
    values = dot(onehot((part == iota((KROWS, 8), 1)) & (r8 < 2 * data_rows)), table).astype(BF16)
    wide = iota((CH, 2 * LANES), 1)
    spread = onehot(iota((CH, 2 * LANES), 0) == (wide & 31))
    rr = iota((KROWS, 2 * LANES), 0)
    cc = iota((KROWS, 2 * LANES), 1)
    row_node = jnp.where(rr < data_rows, rr >> 4, (rr - data_rows) >> 4)
    row_shot = jnp.where(rr < data_rows, rr >> 2, rr) & (QUAD - 1)
    place = (cc >> 6) & 3
    node = jnp.where((cc >= LANES) & (place < 2), 1 - place, place)
    same = (row_node == node) & (row_shot == 2 * (cc >> 8) + ((cc >> 5) & 1)) & (rr < 2 * data_rows)
    w0_ref[...] = jnp.where(same & (place < 3), dot(values, spread), 0.0).astype(BF16)

    widen = onehot((iota((LANES, CH), 0) & 31) == iota((LANES, CH), 1))
    kr = iota((LANES, LANES), 0)
    kc = iota((LANES, LANES), 1)
    same_shot = ((kr >> 5) & 1) == ((kc >> 5) & 1)
    sr = iota((3 * CH, LANES), 0)
    sc = iota((3 * CH, LANES), 1)
    for layer, ref, odd_taps in ((0, w1_ref, (1, 0, 2, 3)), (1, w2_ref, (1, 0, 3, 2))):
        base = 3 * layer
        tall = [
            dot_t(widen, cw_ref[(base + a) * 3 * CH : (base + a + 1) * 3 * CH, :]).astype(BF16)
            for a in range(3)
        ]
        for odd, (k_taps, n_taps) in enumerate((((0, 1, 2, 3), (0, 1, 3, 2)), (odd_taps, (1, 0, 2, 3)))):
            place = sum(jnp.where((sc >> 6) == y, n_taps[y], 0) for y in range(4))
            spread2 = onehot(((sr >> 5) == place) & ((sr & 31) == (sc & 31)))
            total = jnp.zeros((LANES, LANES), F32)
            for x in range(4):
                if k_taps[x] < 3:
                    total = jnp.where(((kr >> 6) == x) & same_shot, dot(tall[k_taps[x]], spread2), total)
            ref[odd] = total.astype(BF16)

    span = shift_ref.shape[0]
    window = span - 2 * HALO
    source = iota(shift_ref.shape, 0)
    source = jnp.where(source < window + HALO, source, source + window // 2 - HALO)
    shift_ref[...] = onehot(iota(shift_ref.shape, 1) == source)

    tile = onehot(iota((CH, LANES), 0) == (iota((CH, LANES), 1) & 31))
    wide_bias_ref[...] = sum(dot(term, tile) for term in split3(bias_ref[...]))


def band_kernel(dils, blocks, place_ref, *refs):
    b3_ref, b4_ref, ow_ref = refs[2:5]
    half = refs[0].shape[0] // 2
    cw_ref, out_w_ref = fetch((refs[0].at[half : 2 * half], refs[1]), refs[5:7], refs[7])
    widen = onehot((iota((LANES, CH), 0) & 31) == iota((LANES, CH), 1))

    er = iota((3 * CH, 3 * LANES), 0)
    ec = iota((3 * CH, 3 * LANES), 1)
    spread3 = onehot(((er >> 5) == (ec >> 8)) & ((er & 31) == (ec & 31)))
    row_lane = iota((LANES, 3 * LANES), 0)
    col_lane = iota((LANES, 3 * LANES), 1) & (LANES - 1)

    def shots_in(lane, block):
        couple = jnp.where(lane < HALF, couple_of(place_ref, 2 * block), couple_of(place_ref, 2 * block + 1))
        return QUAD * couple + ((lane >> 5) & (QUAD - 1))

    def expanded(layer, a):
        base = ((layer - 2) * 3 + a) * 3 * CH
        return dot(dot_t(widen, cw_ref[base : base + 3 * CH, :]).astype(BF16), spread3)

    for layer, ref in ((2, b3_ref), (3, b4_ref)):
        linked_taps = band_links(dils[layer], 0) if blocks == 1 else range(3)
        for out_block in range(blocks):
            for in_block in range(blocks):
                total = jnp.zeros((LANES, 3 * LANES), F32)
                for a in linked_taps:
                    reach = shots_in(col_lane, out_block) + (a - 1) * dils[layer]
                    total = total + jnp.where(shots_in(row_lane, in_block) == reach, expanded(layer, a), 0.0)
                for e in range(3):
                    ref[out_block * blocks + in_block, e * LANES : (e + 1) * LANES, :] = total[
                        :, e * LANES : (e + 1) * LANES
                    ].astype(BF16)

    rows = GROUP * COMPS
    pick = onehot((iota((rows, COMPS), 0) & (COMPS - 1)) == iota((rows, COMPS), 1))
    mine = dot(pick, out_w_ref[...]).astype(BF16)
    tile = onehot(iota((CH, LANES), 0) == (iota((CH, LANES), 1) & 31))
    same = (iota((rows, LANES), 0) >> 2) == (iota((rows, LANES), 1) >> 5)
    ow_ref[...] = jnp.where(same, dot(mine, tile), 0.0).astype(BF16)


def round_up(value, unit):
    return -(-value // unit) * unit


def shifted(value, dilation):
    span = value.shape[0]
    return jnp.concatenate(
        [
            pltpu.roll(value, dilation, axis=0).astype(BF16),
            value.astype(BF16),
            pltpu.roll(value, span - dilation, axis=0).astype(BF16),
        ],
        axis=1,
    )


class Shots:
    def __init__(
        self, dils, windows, step, couple, place_ref, recs, pick_ref, keep_ref, w0_ref, w1_ref, w2_ref,
        bias_ref, shift_ref, part_ref, x2_ref, rec_out_ref,
    ):
        self.dils, self.step, self.couple = dils, step, couple
        self.keep_ref, self.w0_ref, self.w1_ref, self.w2_ref = keep_ref, w0_ref, w1_ref, w2_ref
        self.bias_ref, self.shift_ref, self.x2_ref = bias_ref, shift_ref, x2_ref
        shots, rows, nodes = pick_ref.shape
        planes = shots // CORES
        self.slots = slots = x2_ref.shape[0]
        self.window = window = part_ref.shape[-1]
        self.rows, self.split = part_ref.shape[2], round_up(6 * slots, 16)
        self.span = window + 2 * HALO
        at = place_ref[1]
        self.right_ok = (at < windows - 1).astype(F32)
        self.left_ok = (at > 0).astype(F32)
        self.low_half = iota((self.span, HALF), 1) < CH * CORES

        lane = iota((nodes, 2 * window), 1)
        all_ok = jnp.where(
            lane < window, 1.0, jnp.where(lane < window + window // 2, self.right_ok, self.left_ok)
        ).astype(BF16)

        def put(part, swapped, value):
            for half in range(2):
                lanes = value[:, half * window : (half + 1) * window]
                part_ref[half, part, 0 : self.split] = lanes[0 : self.split]
                part_ref[half, swapped, self.split : rows] = lanes[self.split : rows]

        for x, rec_ref in enumerate(recs):
            n = 2 * couple + x % 2 + (planes if x >= 2 else 0)
            within = shot_of(place_ref, n, shots) & (QUAD - 1)
            edge = rec_ref[COMPS].astype(F32)
            for k in range(COMPS):
                turned = edge if k == 0 else pltpu.roll(edge, window - HALO * k, axis=1)
                both = jnp.concatenate([rec_ref[k], turned.astype(BF16)], axis=1)
                put(within * COMPS + k, (within ^ 2) * COMPS + k, dot(pick_ref[n], both))
            alive = dot(pick_ref[n], all_ok)
            for copy in range(2):
                first = QUAD * COMPS + QUAD * copy
                put(first + within, first + (within ^ 2), alive)

        self.half_rows = part_ref.shape[1] * self.rows
        self.part2 = part_ref.reshape(2 * self.half_rows, window)
        for q in range(slots):
            first = self.split + slots + q
            for half in range(2):
                pair = self.part2[pl.ds(first + (1 - half) * 8 * self.rows, 8, stride=self.rows), :]
                rec_out_ref[q, half * 8 : (half + 1) * 8] = pair

    def inside(self, value):
        w = self.window
        return jnp.concatenate(
            [value[0:w], value[w : w + HALO] * self.right_ok, value[w + HALO :] * self.left_ok], axis=0
        )

    def item_rows(self, q, b):
        start = (3 * (b // 2) * self.slots if b != 1 else self.split) + q
        halves = []
        for half in range(2):
            base = half * self.half_rows + start
            flags = base + QUAD * COMPS * self.rows
            pieces = [
                self.part2[pl.ds(base + a * self.slots, QUAD * COMPS, stride=self.rows), :] for a in range(3)
            ]
            for a in range(3):
                alive = self.part2[pl.ds(flags + a * self.slots, 2 * QUAD, stride=self.rows), :]
                pieces += [alive, alive]
            pieces.append(jnp.zeros((KROWS - 6 * QUAD * COMPS, self.window), F32))
            halves.append(jnp.concatenate(pieces, axis=0).astype(BF16))
        return jnp.concatenate(halves, axis=1)

    def items(self, group):
        return [(group * self.step + i, b) for i in range(self.step) for b in range(3)]

    def first_inputs(self, group):
        items = self.items(group)
        lhs = []
        for n in range(0, len(items), 2):
            some = jnp.concatenate([self.item_rows(q, b) for q, b in items[n : n + 2]], axis=0)
            moved = dot_t(self.shift_ref[...], some).astype(BF16)
            lhs += [moved[:, m : m + KROWS] for m in range(0, moved.shape[1], KROWS)]
        lifted = dot(jnp.concatenate(lhs, axis=0), self.w0_ref[...]).astype(BF16)
        return lifted[:, 0:LANES], lifted[:, LANES:]

    def taps_added(self, even, odd, dilation):
        mid = jnp.where(self.low_half, odd[:, 0:HALF], even[:, 0:HALF])
        late = jnp.where(self.low_half, odd[:, HALF:], even[:, HALF:])
        early = pltpu.roll(jnp.where(self.low_half, even[:, 0:HALF], odd[:, 0:HALF]), HALF // 2, axis=1)
        return (
            pltpu.roll(early, dilation, axis=0) + mid + pltpu.roll(late, self.span - dilation, axis=0)
        )

    def first_layer(self, group, even, odd):
        y_even, y_odd = dot(even, self.w1_ref[0]), dot(odd, self.w1_ref[1])
        x1 = []
        for n, (q, b) in enumerate(self.items(group)):
            at = slice(n * self.span, (n + 1) * self.span)
            old = jnp.where(self.low_half, odd[at, 0:HALF].astype(F32), even[at, 0:HALF].astype(F32))
            total = self.taps_added(y_even[at], y_odd[at], self.dils[0])
            new = jnp.maximum(total + self.bias_ref[0:1, 0:HALF], 0.0)
            x1.append(self.inside((old + new) * self.keep_ref[self.couple, b, q : q + 1, :]))
        even, odd, own = [], [], []
        for i in range(self.step):
            t0, t1, t2 = x1[3 * i : 3 * i + 3]
            t2 = t2.astype(BF16)
            even.append(jnp.concatenate([jnp.where(self.low_half, t0, t1).astype(BF16), t2], axis=1))
            odd.append(jnp.concatenate([jnp.where(self.low_half, t1, t0).astype(BF16), t2], axis=1))
            own.append(t1.astype(BF16))
        return jnp.concatenate(even, axis=0), jnp.concatenate(odd, axis=0), own

    def second_layer(self, group, even, odd, own):
        even, odd = dot(even, self.w2_ref[0]), dot(odd, self.w2_ref[1])
        for i in range(self.step):
            q = group * self.step + i
            at = slice(i * self.span, (i + 1) * self.span)
            total = self.taps_added(even[at], odd[at], self.dils[1])
            new = jnp.maximum(total + self.bias_ref[1:2, 0:HALF], 0.0)
            x2 = (own[i].astype(F32) + new) * self.keep_ref[self.couple, 1, q : q + 1, :]
            self.x2_ref[q] = shifted(self.inside(x2), self.dils[2])


def staged(work):
    inputs, middle = {}, {}
    for t in range(len(work) + 2):
        if t < len(work):
            stage, group = work[t]
            inputs[t] = stage.first_inputs(group)
        if 0 <= t - 1 < len(work):
            stage, group = work[t - 1]
            middle[t - 1] = stage.first_layer(group, *inputs.pop(t - 1))
        if 0 <= t - 2:
            stage, group = work[t - 2]
            stage.second_layer(group, *middle.pop(t - 2))
        yield t


def near_kernel(dils, windows, step, place_ref, *refs):
    pick_ref, keep_ref, w0_ref, w1_ref, w2_ref, bias_ref, shift_ref = refs[:7]
    x2_ref, rec_out_ref, part_ref = refs[7 + QUAD :]
    stage = Shots(
        dils, windows, step, 0, place_ref, refs[7 : 7 + QUAD], pick_ref, keep_ref, w0_ref, w1_ref, w2_ref,
        bias_ref, shift_ref, part_ref, x2_ref, rec_out_ref,
    )
    for _ in staged([(stage, group) for group in range(x2_ref.shape[0] // step)]):
        pass


def main_kernel(dils, windows, step, near, place_ref, *refs):
    shots = refs[0].shape[0]
    couples = shots // QUAD
    pick_ref, keep_ref, w0_ref, w1_ref, w2_ref, b3_ref, b4_ref, ow_ref, bias_ref, shift_ref = refs[:10]
    refs = refs[10:]
    rec_refs, refs = refs[: QUAD * (couples - near)], refs[QUAD * (couples - near) :]
    done_refs, refs = refs[: 2 * near], refs[2 * near :]
    out_ref, part_ref, x2_all, rec_all, x3_ref = refs
    blocks = couples // 2
    slots, window = out_ref.shape[1], out_ref.shape[3]
    span = window + 2 * HALO
    right_ok = (place_ref[1] < windows - 1).astype(F32)
    left_ok = (place_ref[1] > 0).astype(F32)

    stages = []
    x2_refs, rec_refs_out = list(done_refs[0::2]), list(done_refs[1::2])
    for c in range(near, couples):
        x2_refs.append(x2_all.at[c - near])
        rec_refs_out.append(rec_all.at[c - near])
        stages.append(
            Shots(
                dils, windows, step, c, place_ref, rec_refs[QUAD * (c - near) : QUAD * (c - near + 1)],
                pick_ref, keep_ref, w0_ref, w1_ref, w2_ref, bias_ref, shift_ref, part_ref.at[c - near],
                x2_refs[-1], rec_refs_out[-1],
            )
        )

    def receiver_layer(parts_of, weights, layer, block, group, out_rows):
        y = None
        for other in range(blocks):
            term = dot(jnp.concatenate(parts_of(other), axis=0), weights[block * blocks + other])
            y = term if y is None else y + term
        results = []
        for i, part in enumerate(parts_of(block)):
            q = group * step + i
            keep = jnp.concatenate([keep_ref[2 * block + c, 1, q : q + 1, :] for c in range(2)], axis=1)
            old = part[:, LANES : 2 * LANES].astype(F32)
            new = jnp.maximum(y[i * out_rows : (i + 1) * out_rows] + bias_ref[layer : layer + 1, :], 0.0)
            results.append((old + new) * keep)
        return results

    def third_layer(group):
        def parts_of(block):
            return [
                jnp.concatenate(
                    [
                        x2_refs[2 * block + c][group * step + i, :, e * HALF : (e + 1) * HALF]
                        for e in range(3)
                        for c in range(2)
                    ],
                    axis=1,
                )
                for i in range(step)
            ]

        for block in range(blocks):
            for i, value in enumerate(receiver_layer(parts_of, b3_ref, 2, block, group, span)):
                value = jnp.concatenate(
                    [
                        value[0:window],
                        value[window : window + HALO] * right_ok,
                        value[window + HALO :] * left_ok,
                    ],
                    axis=0,
                )
                x3_ref[block, group * step + i] = shifted(value, dils[3])[0:window]

    def last_layer(group):
        def parts_of(block):
            return [x3_ref[block, group * step + i] for i in range(step)]

        for block in range(blocks):
            for i, value in enumerate(receiver_layer(parts_of, b4_ref, 3, block, group, window)):
                q = group * step + i
                noise = dot_t(ow_ref[...], value.astype(BF16))
                record = jnp.concatenate([rec_refs_out[2 * block + c][q] for c in range(2)], axis=0)
                done = (record + noise).reshape(GROUP, COMPS, window)
                for c in range(2):
                    first = QUAD * couple_of(place_ref, 2 * block + c)
                    out_ref[pl.ds(first, QUAD), q] = done[c * QUAD : (c + 1) * QUAD]

    groups = slots // step
    work = [(stage, group) for group in range(groups) for stage in stages]
    lag = len(stages)
    for t in itertools.chain(staged(work), range(len(work) + 2, len(work) + 2 + 2 * lag)):
        done, rest = divmod(t - 2, lag)
        if rest == 0 and 0 <= done - 1 < groups:
            third_layer(done - 1)
        if rest == 0 and 0 <= done - 2 < groups:
            last_layer(done - 2)


def divisor(value, limit):
    return max(d for d in range(1, limit + 1) if value % d == 0)


def body(
    records,
    lift_weight,
    lift_bias,
    conv_weight,
    conv_bias,
    out_weight,
    live_count,
    trace_node,
    node_owner,
):
    _, comps, nodes, window = records.shape
    holders = lax.axis_size("gather")
    windows = lax.axis_size("tm")
    shots = holders * records.shape[0]
    couples = shots // QUAD
    blocks = couples // 2
    slots = (nodes + holders - 1) // holders
    dils = (1, 4, 2, 8)
    rows = round_up(6 * slots, 16) + round_up(3 * slots, 16)
    span = window + 2 * HALO

    planes = holders // CORES
    vmem = pl.BlockSpec(memory_space=pltpu.VMEM)
    smem = pl.BlockSpec(memory_space=pltpu.SMEM)
    hbm = pl.BlockSpec(memory_space=pltpu.HBM)
    like = jax.ShapeDtypeStruct

    def after(value, other):
        return lax.optimization_barrier((value, other))[0]

    def kernel(function, operands, specs, outs, scratch, limit, flops, name):
        return pl.pallas_call(
            function,
            out_shape=outs,
            in_specs=[smem] + specs,
            out_specs=jax.tree.map(lambda _: vmem, outs),
            scratch_shapes=scratch,
            compiler_params=pltpu.CompilerParams(vmem_limit_bytes=limit << 20),
            cost_estimate=pl.CostEstimate(flops=flops, bytes_accessed=1 << 10, transcendentals=0),
            name=name,
        )(place, *operands)

    def fetching(function, raw, memories, outs, name):
        shapes = [(a.shape[0] // 2, CH) if a is taps else a.shape for a in raw]
        scratch = [memory(shape, a.dtype) for memory, shape, a in zip(memories, shapes, raw)]
        scratch.append(pltpu.SemaphoreType.DMA((len(raw),)))
        return kernel(function, raw, [hbm] * len(raw), outs, scratch, 16, 10**5, name)

    place = jnp.stack([lax.axis_index("gather"), lax.axis_index("tm")]).astype(jnp.int32)
    taps = jnp.transpose(conv_weight, (0, 3, 4, 1, 2)).reshape(-1, CH)

    own = records[0]
    even = lax.axis_index("tm") % 2 == 0
    pack = lambda part: jnp.transpose(part, (1, 0, 2)).reshape(nodes, comps * HALO)
    first, last = pack(own[:, :, :HALO]), pack(own[:, :, window - HALO :])
    got = []
    for begin in range(2):
        pairs = [(w, w + 1) for w in range(begin, windows - 1, 2)]
        pairs += [(b, a) for a, b in pairs]
        got.append(lax.ppermute(jnp.where(even == (begin == 0), last, first), "tm", pairs))
    right, left = jnp.where(even, got[0], got[1]), jnp.where(even, got[1], got[0])
    sent = jnp.concatenate([own, jnp.concatenate([right, left], axis=1)[None]], axis=0)

    w0, w1, w2, wide_bias, shift, pick, keep = fetching(
        functools.partial(prep_kernel, dils, slots),
        (live_count, trace_node, taps, jnp.transpose(lift_weight), lift_bias[None, :], conv_bias)
        + (node_owner[None, :],),
        [pltpu.SMEM] * 2 + [pltpu.VMEM] * 5,
        (
            like((KROWS, 2 * LANES), BF16),
            like((2, LANES, LANES), BF16),
            like((2, LANES, LANES), BF16),
            like((conv_bias.shape[0], LANES), F32),
            like((span, 2 * window), BF16),
            like((shots, rows, nodes), BF16),
            like((couples, 3, 16, HALF), F32),
        ),
        "weights",
    )
    sent = after(sent, wide_bias)

    def exchanged(block, distance):
        return lax.ppermute(block, "gather", [(g, g ^ distance) for g in range(holders)])

    near_blocks = [sent] + [exchanged(sent, d) for d in (CORES, 1, CORES + 1)]
    far = [exchanged(sent, CORES * r) for r in range(2, planes)]

    b3, b4, ow = fetching(
        functools.partial(band_kernel, dils, blocks),
        (taps, out_weight),
        [pltpu.VMEM] * 2,
        (
            like((blocks * blocks, 3 * LANES, LANES), BF16),
            like((blocks * blocks, 3 * LANES, LANES), BF16),
            like((GROUP * COMPS, LANES), BF16),
        ),
        "bands",
    )

    step = divisor(slots, 5)
    row_stride = round_up(rows, 16) + 8
    x2 = like((slots, span, 3 * HALF), BF16)
    held = like((slots, QUAD * COMPS, window), F32)
    parts = (2, PARTS, row_stride, window)
    operands = [after(pick, ow), keep, w0, w1, w2, wide_bias, shift, *near_blocks]
    near = kernel(
        functools.partial(near_kernel, dils, windows, step),
        operands,
        [vmem] * len(operands),
        (x2, held),
        [pltpu.VMEM(parts, F32)],
        24,
        10**5,
        "near",
    )

    operands = [pick, keep, w0, w1, w2, b3, b4, ow, wide_bias, shift]
    for r in range(0, len(far), 2):
        operands += far[r : r + 2] + [exchanged(after(block, near[1]), 1) for block in far[r : r + 2]]
    operands += near
    out = kernel(
        functools.partial(main_kernel, dils, windows, step, 1),
        operands,
        [vmem] * len(operands),
        like((shots, slots, comps, window), F32),
        [
            pltpu.VMEM((couples - 1, *parts), F32),
            pltpu.VMEM((couples - 1, *x2.shape), BF16),
            pltpu.VMEM((couples - 1, *held.shape), F32),
            pltpu.VMEM((blocks, slots, window, 3 * LANES), BF16),
        ],
        36,
        4 * 10**9,
        "layers",
    )
    return jnp.transpose(out, (0, 2, 1, 3))


def solution(mesh):
    return jax.shard_map(
        body,
        mesh=mesh,
        in_specs=(P("gather", None, None, "tm"), P(), P(), P(), P(), P(), P(), P(), P()),
        out_specs=P(None, None, "gather", "tm"),
        check_vma=False,
    )
```

```python
import functools
import itertools

import jax
import jax.numpy as jnp
from jax import lax
from jax.experimental import pallas as pl
from jax.experimental.pallas import tpu as pltpu
from jax.sharding import PartitionSpec as P

F32 = jnp.float32
BF16 = jnp.bfloat16
CH = 32
CORES = 2
COMPS = 4
GROUP = 8
LANES = GROUP * CH
HALO = 16
QUAD = 4
HALF = QUAD * CH
KROWS = 128
PARTS = QUAD * COMPS + 2 * QUAD


def iota(shape, dim):
    return lax.broadcasted_iota(jnp.int32, shape, dim)


def dot(a, b):
    return jnp.dot(a, b, preferred_element_type=F32)


def dot_t(a, b):
    return lax.dot_general(a, b, (((1,), (1,)), ((), ())), preferred_element_type=F32)


def onehot(cond):
    return cond.astype(F32).astype(BF16)


def band_links(dilation, offset):
    return [
        a
        for a in range(3)
        if any(s + GROUP * offset == t + (a - 1) * dilation for s in range(GROUP) for t in range(GROUP))
    ]


def split3(value):
    terms = []
    for _ in range(3):
        term = value.astype(BF16)
        terms.append(term)
        value = value - term.astype(F32)
    return terms


def shot_of(place_ref, n, shots):
    planes = shots // CORES
    plane = place_ref[0] // CORES
    core = place_ref[0] - CORES * plane
    return CORES * (plane ^ (n % planes)) + (core if n < planes else 1 - core)


def couple_of(place_ref, relative):
    return (place_ref[0] // (2 * CORES)) ^ relative


def table_kernel(dils, slots, place_ref, live_ref, trace_ref, owner_ref, pick_ref, keep_ref):
    shots, rows, nodes = pick_ref.shape
    split = round_up(6 * slots, 16)
    me = place_ref[0]

    mine = (owner_ref[...] == me).astype(F32)
    before = onehot(iota((nodes, nodes), 0) < iota((nodes, nodes), 1))
    rank = dot(jnp.broadcast_to(mine, (8, nodes)).astype(BF16), before)[0:1, :]
    node_ids = iota((1, nodes), 1).astype(F32)

    def nodes_of(slot_index):
        held = jnp.where((rank == slot_index.astype(F32)) & (mine > 0.5), 1.0, 0.0)
        node = jnp.sum(held * node_ids, axis=1, keepdims=True)
        there = jnp.sum(held, axis=1, keepdims=True)
        return jnp.where(there > 0.5, node, -1.0e6).astype(jnp.int32)

    row_id = iota((rows, nodes), 0)
    late = row_id >= split
    row_id = jnp.where(late, row_id - split, row_id)
    tap = jnp.zeros((rows, nodes), jnp.int32)
    for m in range(1, 7):
        tap = tap + (row_id >= m * slots).astype(jnp.int32)
    second = (tap >= 3).astype(jnp.int32)
    shift = dils[0] * (tap - 3 * second - 1) + jnp.where(late, 0, dils[1] * (2 * second - 1))
    target = nodes_of(row_id - slots * tap)
    target = jnp.where(tap >= jnp.where(late, 3, 6), -1000000, target + shift)

    node_lane = iota((rows, nodes), 1)
    for n in range(shots):
        s = shot_of(place_ref, n, shots)
        pick_ref[n] = onehot((node_lane == target - trace_ref[s, 0]) & (node_lane < live_ref[s]))

    slot_rows = keep_ref.shape[2]
    own_node = nodes_of(iota((slot_rows, nodes), 0))
    shot_lane = iota((slot_rows, HALF), 1) >> 5
    for c in range(shots // QUAD):
        base = QUAD * couple_of(place_ref, c)
        for b in range(3):
            first = jnp.zeros((slot_rows, HALF), jnp.int32)
            count = jnp.zeros((slot_rows, HALF), jnp.int32)
            for w in range(QUAD):
                at = shot_lane == (w if b == 1 else w ^ 2)
                first = jnp.where(at, trace_ref[base + w, 0], first)
                count = jnp.where(at, live_ref[base + w], count)
            trace = own_node + dils[1] * (b - 1) - first
            keep_ref[c, b] = ((trace >= 0) & (trace < count)).astype(F32)


def fetch(sources, places, sems):
    copies = [pltpu.make_async_copy(a, b, sems.at[n]) for n, (a, b) in enumerate(zip(sources, places))]
    for copy in copies:
        copy.start()
    for copy in copies:
        copy.wait()
    return places


def prep_kernel(dils, slots, place_ref, *refs):
    w0_ref, w1_ref, w2_ref, wide_bias_ref, shift_ref, pick_ref, keep_ref = refs[7:14]
    half = refs[2].shape[0] // 2
    live_ref, trace_ref, cw_ref, lift_ref, lift_bias_ref, bias_ref, owner_ref = fetch(
        (*refs[:2], refs[2].at[0:half], *refs[3:7]), refs[14:21], refs[21]
    )
    table_kernel(dils, slots, place_ref, live_ref, trace_ref, owner_ref, pick_ref, keep_ref)

    rows8 = [lift_ref[...].astype(F32)] + [term.astype(F32) for term in split3(lift_bias_ref[...])]
    table = jnp.concatenate(rows8 + [jnp.zeros((1, CH), F32)], axis=0).astype(BF16)
    data_rows = 3 * QUAD * COMPS
    r8 = iota((KROWS, 8), 0)
    part = jnp.where(r8 < data_rows, r8 & (COMPS - 1), COMPS + ((r8 >> 2) & 3))
    values = dot(onehot((part == iota((KROWS, 8), 1)) & (r8 < 2 * data_rows)), table).astype(BF16)
    wide = iota((CH, 2 * LANES), 1)
    spread = onehot(iota((CH, 2 * LANES), 0) == (wide & 31))
    rr = iota((KROWS, 2 * LANES), 0)
    cc = iota((KROWS, 2 * LANES), 1)
    row_node = jnp.where(rr < data_rows, rr >> 4, (rr - data_rows) >> 4)
    row_shot = jnp.where(rr < data_rows, rr >> 2, rr) & (QUAD - 1)
    place = (cc >> 6) & 3
    node = jnp.where((cc >= LANES) & (place < 2), 1 - place, place)
    same = (row_node == node) & (row_shot == 2 * (cc >> 8) + ((cc >> 5) & 1)) & (rr < 2 * data_rows)
    w0_ref[...] = jnp.where(same & (place < 3), dot(values, spread), 0.0).astype(BF16)

    widen = onehot((iota((LANES, CH), 0) & 31) == iota((LANES, CH), 1))
    kr = iota((LANES, LANES), 0)
    kc = iota((LANES, LANES), 1)
    same_shot = ((kr >> 5) & 1) == ((kc >> 5) & 1)
    sr = iota((3 * CH, LANES), 0)
    sc = iota((3 * CH, LANES), 1)
    for layer, ref, odd_taps in ((0, w1_ref, (1, 0, 2, 3)), (1, w2_ref, (1, 0, 3, 2))):
        base = 3 * layer
        tall = [
            dot_t(widen, cw_ref[(base + a) * 3 * CH : (base + a + 1) * 3 * CH, :]).astype(BF16)
            for a in range(3)
        ]
        for odd, (k_taps, n_taps) in enumerate((((0, 1, 2, 3), (0, 1, 3, 2)), (odd_taps, (1, 0, 2, 3)))):
            place = sum(jnp.where((sc >> 6) == y, n_taps[y], 0) for y in range(4))
            spread2 = onehot(((sr >> 5) == place) & ((sr & 31) == (sc & 31)))
            total = jnp.zeros((LANES, LANES), F32)
            for x in range(4):
                if k_taps[x] < 3:
                    total = jnp.where(((kr >> 6) == x) & same_shot, dot(tall[k_taps[x]], spread2), total)
            ref[odd] = total.astype(BF16)

    span = shift_ref.shape[0]
    window = span - 2 * HALO
    source = iota(shift_ref.shape, 0)
    source = jnp.where(source < window + HALO, source, source + window // 2 - HALO)
    shift_ref[...] = onehot(iota(shift_ref.shape, 1) == source)

    tile = onehot(iota((CH, LANES), 0) == (iota((CH, LANES), 1) & 31))
    wide_bias_ref[...] = sum(dot(term, tile) for term in split3(bias_ref[...]))


def band_kernel(dils, blocks, place_ref, *refs):
    b3_ref, b4_ref, ow_ref = refs[2:5]
    half = refs[0].shape[0] // 2
    cw_ref, out_w_ref = fetch((refs[0].at[half : 2 * half], refs[1]), refs[5:7], refs[7])
    widen = onehot((iota((LANES, CH), 0) & 31) == iota((LANES, CH), 1))

    er = iota((3 * CH, 3 * LANES), 0)
    ec = iota((3 * CH, 3 * LANES), 1)
    spread3 = onehot(((er >> 5) == (ec >> 8)) & ((er & 31) == (ec & 31)))
    row_lane = iota((LANES, 3 * LANES), 0)
    col_lane = iota((LANES, 3 * LANES), 1) & (LANES - 1)

    def shots_in(lane, block):
        couple = jnp.where(lane < HALF, couple_of(place_ref, 2 * block), couple_of(place_ref, 2 * block + 1))
        return QUAD * couple + ((lane >> 5) & (QUAD - 1))

    def expanded(layer, a):
        base = ((layer - 2) * 3 + a) * 3 * CH
        return dot(dot_t(widen, cw_ref[base : base + 3 * CH, :]).astype(BF16), spread3)

    for layer, ref in ((2, b3_ref), (3, b4_ref)):
        linked_taps = band_links(dils[layer], 0) if blocks == 1 else range(3)
        for out_block in range(blocks):
            for in_block in range(blocks):
                total = jnp.zeros((LANES, 3 * LANES), F32)
                for a in linked_taps:
                    reach = shots_in(col_lane, out_block) + (a - 1) * dils[layer]
                    total = total + jnp.where(shots_in(row_lane, in_block) == reach, expanded(layer, a), 0.0)
                for e in range(3):
                    ref[out_block * blocks + in_block, e * LANES : (e + 1) * LANES, :] = total[
                        :, e * LANES : (e + 1) * LANES
                    ].astype(BF16)

    rows = GROUP * COMPS
    pick = onehot((iota((rows, COMPS), 0) & (COMPS - 1)) == iota((rows, COMPS), 1))
    mine = dot(pick, out_w_ref[...]).astype(BF16)
    tile = onehot(iota((CH, LANES), 0) == (iota((CH, LANES), 1) & 31))
    same = (iota((rows, LANES), 0) >> 2) == (iota((rows, LANES), 1) >> 5)
    ow_ref[...] = jnp.where(same, dot(mine, tile), 0.0).astype(BF16)


def round_up(value, unit):
    return -(-value // unit) * unit


def shifted(value, dilation):
    span = value.shape[0]
    return jnp.concatenate(
        [
            pltpu.roll(value, dilation, axis=0).astype(BF16),
            value.astype(BF16),
            pltpu.roll(value, span - dilation, axis=0).astype(BF16),
        ],
        axis=1,
    )


class Shots:
    def __init__(
        self, dils, windows, step, couple, place_ref, recs, pick_ref, keep_ref, w0_ref, w1_ref, w2_ref,
        bias_ref, shift_ref, part_ref, x2_ref, rec_out_ref,
    ):
        self.dils, self.step, self.couple = dils, step, couple
        self.keep_ref, self.w0_ref, self.w1_ref, self.w2_ref = keep_ref, w0_ref, w1_ref, w2_ref
        self.bias_ref, self.shift_ref, self.x2_ref = bias_ref, shift_ref, x2_ref
        shots, rows, nodes = pick_ref.shape
        planes = shots // CORES
        self.slots = slots = x2_ref.shape[0]
        self.window = window = part_ref.shape[-1]
        self.rows, self.split = part_ref.shape[2], round_up(6 * slots, 16)
        self.span = window + 2 * HALO
        at = place_ref[1]
        self.right_ok = (at < windows - 1).astype(F32)
        self.left_ok = (at > 0).astype(F32)
        self.low_half = iota((self.span, HALF), 1) < CH * CORES

        lane = iota((nodes, 2 * window), 1)
        all_ok = jnp.where(
            lane < window, 1.0, jnp.where(lane < window + window // 2, self.right_ok, self.left_ok)
        ).astype(BF16)

        def put(part, swapped, value):
            for half in range(2):
                lanes = value[:, half * window : (half + 1) * window]
                part_ref[half, part, 0 : self.split] = lanes[0 : self.split]
                part_ref[half, swapped, self.split : rows] = lanes[self.split : rows]

        for x, rec_ref in enumerate(recs):
            n = 2 * couple + x % 2 + (planes if x >= 2 else 0)
            within = shot_of(place_ref, n, shots) & (QUAD - 1)
            edge = rec_ref[COMPS].astype(F32)
            for k in range(COMPS):
                turned = edge if k == 0 else pltpu.roll(edge, window - HALO * k, axis=1)
                both = jnp.concatenate([rec_ref[k], turned.astype(BF16)], axis=1)
                put(within * COMPS + k, (within ^ 2) * COMPS + k, dot(pick_ref[n], both))
            alive = dot(pick_ref[n], all_ok)
            for copy in range(2):
                first = QUAD * COMPS + QUAD * copy
                put(first + within, first + (within ^ 2), alive)

        self.half_rows = part_ref.shape[1] * self.rows
        self.part2 = part_ref.reshape(2 * self.half_rows, window)
        for q in range(slots):
            first = self.split + slots + q
            for half in range(2):
                pair = self.part2[pl.ds(first + (1 - half) * 8 * self.rows, 8, stride=self.rows), :]
                rec_out_ref[q, half * 8 : (half + 1) * 8] = pair

    def inside(self, value):
        w = self.window
        return jnp.concatenate(
            [value[0:w], value[w : w + HALO] * self.right_ok, value[w + HALO :] * self.left_ok], axis=0
        )

    def item_rows(self, q, b):
        start = (3 * (b // 2) * self.slots if b != 1 else self.split) + q
        halves = []
        for half in range(2):
            base = half * self.half_rows + start
            flags = base + QUAD * COMPS * self.rows
            pieces = [
                self.part2[pl.ds(base + a * self.slots, QUAD * COMPS, stride=self.rows), :] for a in range(3)
            ]
            for a in range(3):
                alive = self.part2[pl.ds(flags + a * self.slots, 2 * QUAD, stride=self.rows), :]
                pieces += [alive, alive]
            pieces.append(jnp.zeros((KROWS - 6 * QUAD * COMPS, self.window), F32))
            halves.append(jnp.concatenate(pieces, axis=0).astype(BF16))
        return jnp.concatenate(halves, axis=1)

    def items(self, group):
        return [(group * self.step + i, b) for i in range(self.step) for b in range(3)]

    def first_inputs(self, group):
        items = self.items(group)
        lhs = []
        for n in range(0, len(items), 2):
            some = jnp.concatenate([self.item_rows(q, b) for q, b in items[n : n + 2]], axis=0)
            moved = dot_t(self.shift_ref[...], some).astype(BF16)
            lhs += [moved[:, m : m + KROWS] for m in range(0, moved.shape[1], KROWS)]
        lifted = dot(jnp.concatenate(lhs, axis=0), self.w0_ref[...]).astype(BF16)
        return lifted[:, 0:LANES], lifted[:, LANES:]

    def taps_added(self, even, odd, dilation):
        mid = jnp.where(self.low_half, odd[:, 0:HALF], even[:, 0:HALF])
        late = jnp.where(self.low_half, odd[:, HALF:], even[:, HALF:])
        early = pltpu.roll(jnp.where(self.low_half, even[:, 0:HALF], odd[:, 0:HALF]), HALF // 2, axis=1)
        return (
            pltpu.roll(early, dilation, axis=0) + mid + pltpu.roll(late, self.span - dilation, axis=0)
        )

    def first_layer(self, group, even, odd):
        y_even, y_odd = dot(even, self.w1_ref[0]), dot(odd, self.w1_ref[1])
        x1 = []
        for n, (q, b) in enumerate(self.items(group)):
            at = slice(n * self.span, (n + 1) * self.span)
            old = jnp.where(self.low_half, odd[at, 0:HALF].astype(F32), even[at, 0:HALF].astype(F32))
            total = self.taps_added(y_even[at], y_odd[at], self.dils[0])
            new = jnp.maximum(total + self.bias_ref[0:1, 0:HALF], 0.0)
            x1.append(self.inside((old + new) * self.keep_ref[self.couple, b, q : q + 1, :]))
        even, odd, own = [], [], []
        for i in range(self.step):
            t0, t1, t2 = x1[3 * i : 3 * i + 3]
            t2 = t2.astype(BF16)
            even.append(jnp.concatenate([jnp.where(self.low_half, t0, t1).astype(BF16), t2], axis=1))
            odd.append(jnp.concatenate([jnp.where(self.low_half, t1, t0).astype(BF16), t2], axis=1))
            own.append(t1.astype(BF16))
        return jnp.concatenate(even, axis=0), jnp.concatenate(odd, axis=0), own

    def second_layer(self, group, even, odd, own):
        even, odd = dot(even, self.w2_ref[0]), dot(odd, self.w2_ref[1])
        for i in range(self.step):
            q = group * self.step + i
            at = slice(i * self.span, (i + 1) * self.span)
            total = self.taps_added(even[at], odd[at], self.dils[1])
            new = jnp.maximum(total + self.bias_ref[1:2, 0:HALF], 0.0)
            x2 = (own[i].astype(F32) + new) * self.keep_ref[self.couple, 1, q : q + 1, :]
            self.x2_ref[q] = shifted(self.inside(x2), self.dils[2])


def staged(work):
    inputs, middle = {}, {}
    for t in range(len(work) + 2):
        if t < len(work):
            stage, group = work[t]
            inputs[t] = stage.first_inputs(group)
        if 0 <= t - 1 < len(work):
            stage, group = work[t - 1]
            middle[t - 1] = stage.first_layer(group, *inputs.pop(t - 1))
        if 0 <= t - 2:
            stage, group = work[t - 2]
            stage.second_layer(group, *middle.pop(t - 2))
        yield t


def near_kernel(dils, windows, step, place_ref, *refs):
    pick_ref, keep_ref, w0_ref, w1_ref, w2_ref, bias_ref, shift_ref = refs[:7]
    x2_ref, rec_out_ref, part_ref = refs[7 + QUAD :]
    stage = Shots(
        dils, windows, step, 0, place_ref, refs[7 : 7 + QUAD], pick_ref, keep_ref, w0_ref, w1_ref, w2_ref,
        bias_ref, shift_ref, part_ref, x2_ref, rec_out_ref,
    )
    for _ in staged([(stage, group) for group in range(x2_ref.shape[0] // step)]):
        pass


def main_kernel(dils, windows, step, near, place_ref, *refs):
    shots = refs[0].shape[0]
    couples = shots // QUAD
    pick_ref, keep_ref, w0_ref, w1_ref, w2_ref, b3_ref, b4_ref, ow_ref, bias_ref, shift_ref = refs[:10]
    refs = refs[10:]
    rec_refs, refs = refs[: QUAD * (couples - near)], refs[QUAD * (couples - near) :]
    done_refs, refs = refs[: 2 * near], refs[2 * near :]
    out_ref, part_ref, x2_all, rec_all, x3_ref = refs
    blocks = couples // 2
    slots, window = out_ref.shape[1], out_ref.shape[3]
    span = window + 2 * HALO
    right_ok = (place_ref[1] < windows - 1).astype(F32)
    left_ok = (place_ref[1] > 0).astype(F32)

    stages = []
    x2_refs, rec_refs_out = list(done_refs[0::2]), list(done_refs[1::2])
    for c in range(near, couples):
        x2_refs.append(x2_all.at[c - near])
        rec_refs_out.append(rec_all.at[c - near])
        stages.append(
            Shots(
                dils, windows, step, c, place_ref, rec_refs[QUAD * (c - near) : QUAD * (c - near + 1)],
                pick_ref, keep_ref, w0_ref, w1_ref, w2_ref, bias_ref, shift_ref, part_ref.at[c - near],
                x2_refs[-1], rec_refs_out[-1],
            )
        )

    def receiver_layer(parts_of, weights, layer, block, group, out_rows):
        y = None
        for other in range(blocks):
            term = dot(jnp.concatenate(parts_of(other), axis=0), weights[block * blocks + other])
            y = term if y is None else y + term
        results = []
        for i, part in enumerate(parts_of(block)):
            q = group * step + i
            keep = jnp.concatenate([keep_ref[2 * block + c, 1, q : q + 1, :] for c in range(2)], axis=1)
            old = part[:, LANES : 2 * LANES].astype(F32)
            new = jnp.maximum(y[i * out_rows : (i + 1) * out_rows] + bias_ref[layer : layer + 1, :], 0.0)
            results.append((old + new) * keep)
        return results

    def third_layer(group):
        def parts_of(block):
            return [
                jnp.concatenate(
                    [
                        x2_refs[2 * block + c][group * step + i, :, e * HALF : (e + 1) * HALF]
                        for e in range(3)
                        for c in range(2)
                    ],
                    axis=1,
                )
                for i in range(step)
            ]

        for block in range(blocks):
            for i, value in enumerate(receiver_layer(parts_of, b3_ref, 2, block, group, span)):
                value = jnp.concatenate(
                    [
                        value[0:window],
                        value[window : window + HALO] * right_ok,
                        value[window + HALO :] * left_ok,
                    ],
                    axis=0,
                )
                x3_ref[block, group * step + i] = shifted(value, dils[3])[0:window]

    def last_layer(group):
        def parts_of(block):
            return [x3_ref[block, group * step + i] for i in range(step)]

        for block in range(blocks):
            for i, value in enumerate(receiver_layer(parts_of, b4_ref, 3, block, group, window)):
                q = group * step + i
                noise = dot_t(ow_ref[...], value.astype(BF16))
                record = jnp.concatenate([rec_refs_out[2 * block + c][q] for c in range(2)], axis=0)
                done = (record + noise).reshape(GROUP, COMPS, window)
                for c in range(2):
                    first = QUAD * couple_of(place_ref, 2 * block + c)
                    out_ref[pl.ds(first, QUAD), q] = done[c * QUAD : (c + 1) * QUAD]

    groups = slots // step
    work = [(stage, group) for group in range(groups) for stage in stages]
    lag = len(stages)
    for t in itertools.chain(staged(work), range(len(work) + 2, len(work) + 2 + 2 * lag)):
        done, rest = divmod(t - 2, lag)
        if rest == 0 and 0 <= done - 1 < groups:
            third_layer(done - 1)
        if rest == 0 and 0 <= done - 2 < groups:
            last_layer(done - 2)


def divisor(value, limit):
    return max(d for d in range(1, limit + 1) if value % d == 0)


def body(
    records,
    lift_weight,
    lift_bias,
    conv_weight,
    conv_bias,
    out_weight,
    live_count,
    trace_node,
    node_owner,
):
    _, comps, nodes, window = records.shape
    holders = lax.axis_size("gather")
    windows = lax.axis_size("tm")
    shots = holders * records.shape[0]
    couples = shots // QUAD
    blocks = couples // 2
    slots = (nodes + holders - 1) // holders
    dils = (1, 4, 2, 8)
    rows = round_up(6 * slots, 16) + round_up(3 * slots, 16)
    span = window + 2 * HALO

    planes = holders // CORES
    vmem = pl.BlockSpec(memory_space=pltpu.VMEM)
    smem = pl.BlockSpec(memory_space=pltpu.SMEM)
    hbm = pl.BlockSpec(memory_space=pltpu.HBM)
    like = jax.ShapeDtypeStruct

    def after(value, other):
        return lax.optimization_barrier((value, other))[0]

    def kernel(function, operands, specs, outs, scratch, limit, flops, name):
        return pl.pallas_call(
            function,
            out_shape=outs,
            in_specs=[smem] + specs,
            out_specs=jax.tree.map(lambda _: vmem, outs),
            scratch_shapes=scratch,
            compiler_params=pltpu.CompilerParams(vmem_limit_bytes=limit << 20),
            cost_estimate=pl.CostEstimate(flops=flops, bytes_accessed=1 << 10, transcendentals=0),
            name=name,
        )(place, *operands)

    def fetching(function, raw, memories, outs, name):
        shapes = [(a.shape[0] // 2, CH) if a is taps else a.shape for a in raw]
        scratch = [memory(shape, a.dtype) for memory, shape, a in zip(memories, shapes, raw)]
        scratch.append(pltpu.SemaphoreType.DMA((len(raw),)))
        raw = [pltpu.with_memory_space_constraint(a, pltpu.HBM) for a in raw]
        return kernel(function, raw, [hbm] * len(raw), outs, scratch, 16, 10**5, name)

    place = jnp.stack([lax.axis_index("gather"), lax.axis_index("tm")]).astype(jnp.int32)
    taps = jnp.transpose(conv_weight, (0, 3, 4, 1, 2)).reshape(-1, CH)

    own = records[0]
    even = lax.axis_index("tm") % 2 == 0
    pack = lambda part: jnp.transpose(part, (1, 0, 2)).reshape(nodes, comps * HALO)
    first, last = pack(own[:, :, :HALO]), pack(own[:, :, window - HALO :])
    got = []
    for begin in range(2):
        pairs = [(w, w + 1) for w in range(begin, windows - 1, 2)]
        pairs += [(b, a) for a, b in pairs]
        got.append(lax.ppermute(jnp.where(even == (begin == 0), last, first), "tm", pairs))
    right, left = jnp.where(even, got[0], got[1]), jnp.where(even, got[1], got[0])
    sent = jnp.concatenate([own, jnp.concatenate([right, left], axis=1)[None]], axis=0)

    w0, w1, w2, wide_bias, shift, pick, keep = fetching(
        functools.partial(prep_kernel, dils, slots),
        (live_count, trace_node, taps, jnp.transpose(lift_weight), lift_bias[None, :], conv_bias)
        + (node_owner[None, :],),
        [pltpu.SMEM] * 2 + [pltpu.VMEM] * 5,
        (
            like((KROWS, 2 * LANES), BF16),
            like((2, LANES, LANES), BF16),
            like((2, LANES, LANES), BF16),
            like((conv_bias.shape[0], LANES), F32),
            like((span, 2 * window), BF16),
            like((shots, rows, nodes), BF16),
            like((couples, 3, 16, HALF), F32),
        ),
        "weights",
    )
    sent = after(sent, wide_bias)

    def exchanged(block, distance):
        return lax.ppermute(block, "gather", [(g, g ^ distance) for g in range(holders)])

    near_blocks = [sent] + [exchanged(sent, d) for d in (CORES, 1, CORES + 1)]
    far = [exchanged(sent, CORES * r) for r in range(2, planes)]

    b3, b4, ow = fetching(
        functools.partial(band_kernel, dils, blocks),
        (taps, out_weight),
        [pltpu.VMEM] * 2,
        (
            like((blocks * blocks, 3 * LANES, LANES), BF16),
            like((blocks * blocks, 3 * LANES, LANES), BF16),
            like((GROUP * COMPS, LANES), BF16),
        ),
        "bands",
    )

    step = divisor(slots, 5)
    row_stride = round_up(rows, 16) + 8
    x2 = like((slots, span, 3 * HALF), BF16)
    held = like((slots, QUAD * COMPS, window), F32)
    parts = (2, PARTS, row_stride, window)
    operands = [after(pick, ow), keep, w0, w1, w2, wide_bias, shift, *near_blocks]
    near = kernel(
        functools.partial(near_kernel, dils, windows, step),
        operands,
        [vmem] * len(operands),
        (x2, held),
        [pltpu.VMEM(parts, F32)],
        24,
        10**5,
        "near",
    )

    operands = [pick, keep, w0, w1, w2, b3, b4, ow, wide_bias, shift]
    for r in range(0, len(far), 2):
        operands += far[r : r + 2] + [exchanged(after(block, near[1]), 1) for block in far[r : r + 2]]
    operands += near
    out = kernel(
        functools.partial(main_kernel, dils, windows, step, 1),
        operands,
        [vmem] * len(operands),
        like((shots, slots, comps, window), F32),
        [
            pltpu.VMEM((couples - 1, *parts), F32),
            pltpu.VMEM((couples - 1, *x2.shape), BF16),
            pltpu.VMEM((couples - 1, *held.shape), F32),
            pltpu.VMEM((blocks, slots, window, 3 * LANES), BF16),
        ],
        36,
        4 * 10**9,
        "layers",
    )
    return jnp.transpose(out, (0, 2, 1, 3))


def solution(mesh):
    return jax.shard_map(
        body,
        mesh=mesh,
        in_specs=(P("gather", None, None, "tm"), P(), P(), P(), P(), P(), P(), P(), P()),
        out_specs=P(None, None, "gather", "tm"),
        check_vma=False,
    )
```

```python
import functools
import itertools

import jax
import jax.numpy as jnp
from jax import lax
from jax.experimental import pallas as pl
from jax.experimental.pallas import tpu as pltpu
from jax.sharding import PartitionSpec as P

F32 = jnp.float32
BF16 = jnp.bfloat16
CH = 32
CORES = 2
COMPS = 4
GROUP = 8
LANES = GROUP * CH
HALO = 16
QUAD = 4
HALF = QUAD * CH
KROWS = 128
PARTS = QUAD * COMPS + 2 * QUAD


def iota(shape, dim):
    return lax.broadcasted_iota(jnp.int32, shape, dim)


def dot(a, b):
    return jnp.dot(a, b, preferred_element_type=F32)


def dot_t(a, b):
    return lax.dot_general(a, b, (((1,), (1,)), ((), ())), preferred_element_type=F32)


def onehot(cond):
    return cond.astype(F32).astype(BF16)


def band_links(dilation, offset):
    return [
        a
        for a in range(3)
        if any(s + GROUP * offset == t + (a - 1) * dilation for s in range(GROUP) for t in range(GROUP))
    ]


def split3(value):
    terms = []
    for _ in range(3):
        term = value.astype(BF16)
        terms.append(term)
        value = value - term.astype(F32)
    return terms


def shot_of(place_ref, n, shots):
    planes = shots // CORES
    plane = place_ref[0] // CORES
    core = place_ref[0] - CORES * plane
    return CORES * (plane ^ (n % planes)) + (core if n < planes else 1 - core)


def couple_of(place_ref, relative):
    return (place_ref[0] // (2 * CORES)) ^ relative


def table_kernel(dils, slots, place_ref, live_ref, trace_ref, owner_ref, pick_ref, keep_ref):
    shots, rows, nodes = pick_ref.shape
    split = round_up(6 * slots, 16)
    me = place_ref[0]

    mine = (owner_ref[...] == me).astype(F32)
    before = onehot(iota((nodes, nodes), 0) < iota((nodes, nodes), 1))
    rank = dot(jnp.broadcast_to(mine, (8, nodes)).astype(BF16), before)[0:1, :]
    node_ids = iota((1, nodes), 1).astype(F32)

    def nodes_of(slot_index):
        held = jnp.where((rank == slot_index.astype(F32)) & (mine > 0.5), 1.0, 0.0)
        node = jnp.sum(held * node_ids, axis=1, keepdims=True)
        there = jnp.sum(held, axis=1, keepdims=True)
        return jnp.where(there > 0.5, node, -1.0e6).astype(jnp.int32)

    row_id = iota((rows, nodes), 0)
    late = row_id >= split
    row_id = jnp.where(late, row_id - split, row_id)
    tap = jnp.zeros((rows, nodes), jnp.int32)
    for m in range(1, 7):
        tap = tap + (row_id >= m * slots).astype(jnp.int32)
    second = (tap >= 3).astype(jnp.int32)
    shift = dils[0] * (tap - 3 * second - 1) + jnp.where(late, 0, dils[1] * (2 * second - 1))
    target = nodes_of(row_id - slots * tap)
    target = jnp.where(tap >= jnp.where(late, 3, 6), -1000000, target + shift)

    node_lane = iota((rows, nodes), 1)
    for n in range(shots):
        s = shot_of(place_ref, n, shots)
        pick_ref[n] = onehot((node_lane == target - trace_ref[s, 0]) & (node_lane < live_ref[s]))

    slot_rows = keep_ref.shape[2]
    own_node = nodes_of(iota((slot_rows, nodes), 0))
    shot_lane = iota((slot_rows, HALF), 1) >> 5
    for c in range(shots // QUAD):
        base = QUAD * couple_of(place_ref, c)
        for b in range(3):
            first = jnp.zeros((slot_rows, HALF), jnp.int32)
            count = jnp.zeros((slot_rows, HALF), jnp.int32)
            for w in range(QUAD):
                at = shot_lane == (w if b == 1 else w ^ 2)
                first = jnp.where(at, trace_ref[base + w, 0], first)
                count = jnp.where(at, live_ref[base + w], count)
            trace = own_node + dils[1] * (b - 1) - first
            keep_ref[c, b] = ((trace >= 0) & (trace < count)).astype(F32)


def started(sources, places, sems):
    copies = [pltpu.make_async_copy(a, b, sems.at[n]) for n, (a, b) in enumerate(zip(sources, places))]
    for copy in copies:
        copy.start()
    return copies


def prep_kernel(dils, slots, place_ref, *refs):
    w0_ref, w1_ref, w2_ref, wide_bias_ref, shift_ref, pick_ref, keep_ref = refs[9:16]
    half = refs[2].shape[0] // 2
    passed = started((refs[7], refs[2].at[half : 2 * half], refs[8]), refs[16:19], refs[27])
    live_ref, trace_ref, cw_ref, lift_ref, lift_bias_ref, bias_ref, owner_ref = refs[19:26]
    sources = (*refs[:2], refs[2].at[0:half], *refs[3:7])
    for copy in started(sources, refs[19:26], refs[26]):
        copy.wait()
    table_kernel(dils, slots, place_ref, live_ref, trace_ref, owner_ref, pick_ref, keep_ref)

    rows8 = [lift_ref[...].astype(F32)] + [term.astype(F32) for term in split3(lift_bias_ref[...])]
    table = jnp.concatenate(rows8 + [jnp.zeros((1, CH), F32)], axis=0).astype(BF16)
    data_rows = 3 * QUAD * COMPS
    r8 = iota((KROWS, 8), 0)
    part = jnp.where(r8 < data_rows, r8 & (COMPS - 1), COMPS + ((r8 >> 2) & 3))
    values = dot(onehot((part == iota((KROWS, 8), 1)) & (r8 < 2 * data_rows)), table).astype(BF16)
    wide = iota((CH, 2 * LANES), 1)
    spread = onehot(iota((CH, 2 * LANES), 0) == (wide & 31))
    rr = iota((KROWS, 2 * LANES), 0)
    cc = iota((KROWS, 2 * LANES), 1)
    row_node = jnp.where(rr < data_rows, rr >> 4, (rr - data_rows) >> 4)
    row_shot = jnp.where(rr < data_rows, rr >> 2, rr) & (QUAD - 1)
    place = (cc >> 6) & 3
    node = jnp.where((cc >= LANES) & (place < 2), 1 - place, place)
    same = (row_node == node) & (row_shot == 2 * (cc >> 8) + ((cc >> 5) & 1)) & (rr < 2 * data_rows)
    w0_ref[...] = jnp.where(same & (place < 3), dot(values, spread), 0.0).astype(BF16)

    widen = onehot((iota((LANES, CH), 0) & 31) == iota((LANES, CH), 1))
    kr = iota((LANES, LANES), 0)
    kc = iota((LANES, LANES), 1)
    same_shot = ((kr >> 5) & 1) == ((kc >> 5) & 1)
    sr = iota((3 * CH, LANES), 0)
    sc = iota((3 * CH, LANES), 1)
    for layer, ref, odd_taps in ((0, w1_ref, (1, 0, 2, 3)), (1, w2_ref, (1, 0, 3, 2))):
        base = 3 * layer
        tall = [
            dot_t(widen, cw_ref[(base + a) * 3 * CH : (base + a + 1) * 3 * CH, :]).astype(BF16)
            for a in range(3)
        ]
        for odd, (k_taps, n_taps) in enumerate((((0, 1, 2, 3), (0, 1, 3, 2)), (odd_taps, (1, 0, 2, 3)))):
            place = sum(jnp.where((sc >> 6) == y, n_taps[y], 0) for y in range(4))
            spread2 = onehot(((sr >> 5) == place) & ((sr & 31) == (sc & 31)))
            total = jnp.zeros((LANES, LANES), F32)
            for x in range(4):
                if k_taps[x] < 3:
                    total = jnp.where(((kr >> 6) == x) & same_shot, dot(tall[k_taps[x]], spread2), total)
            ref[odd] = total.astype(BF16)

    span = shift_ref.shape[0]
    window = span - 2 * HALO
    source = iota(shift_ref.shape, 0)
    source = jnp.where(source < window + HALO, source, source + window // 2 - HALO)
    shift_ref[...] = onehot(iota(shift_ref.shape, 1) == source)

    tile = onehot(iota((CH, LANES), 0) == (iota((CH, LANES), 1) & 31))
    wide_bias_ref[...] = sum(dot(term, tile) for term in split3(bias_ref[...]))
    for copy in passed:
        copy.wait()


def band_kernel(dils, blocks, place_ref, *refs):
    cw_ref, out_w_ref, b3_ref, b4_ref, ow_ref = refs
    widen = onehot((iota((LANES, CH), 0) & 31) == iota((LANES, CH), 1))

    er = iota((3 * CH, 3 * LANES), 0)
    ec = iota((3 * CH, 3 * LANES), 1)
    spread3 = onehot(((er >> 5) == (ec >> 8)) & ((er & 31) == (ec & 31)))
    row_lane = iota((LANES, 3 * LANES), 0)
    col_lane = iota((LANES, 3 * LANES), 1) & (LANES - 1)

    def shots_in(lane, block):
        couple = jnp.where(lane < HALF, couple_of(place_ref, 2 * block), couple_of(place_ref, 2 * block + 1))
        return QUAD * couple + ((lane >> 5) & (QUAD - 1))

    def expanded(layer, a):
        base = ((layer - 2) * 3 + a) * 3 * CH
        return dot(dot_t(widen, cw_ref[base : base + 3 * CH, :]).astype(BF16), spread3)

    for layer, ref in ((2, b3_ref), (3, b4_ref)):
        linked_taps = band_links(dils[layer], 0) if blocks == 1 else range(3)
        for out_block in range(blocks):
            for in_block in range(blocks):
                total = jnp.zeros((LANES, 3 * LANES), F32)
                for a in linked_taps:
                    reach = shots_in(col_lane, out_block) + (a - 1) * dils[layer]
                    total = total + jnp.where(shots_in(row_lane, in_block) == reach, expanded(layer, a), 0.0)
                for e in range(3):
                    ref[out_block * blocks + in_block, e * LANES : (e + 1) * LANES, :] = total[
                        :, e * LANES : (e + 1) * LANES
                    ].astype(BF16)

    rows = GROUP * COMPS
    pick = onehot((iota((rows, COMPS), 0) & (COMPS - 1)) == iota((rows, COMPS), 1))
    mine = dot(pick, out_w_ref[...]).astype(BF16)
    tile = onehot(iota((CH, LANES), 0) == (iota((CH, LANES), 1) & 31))
    same = (iota((rows, LANES), 0) >> 2) == (iota((rows, LANES), 1) >> 5)
    ow_ref[...] = jnp.where(same, dot(mine, tile), 0.0).astype(BF16)


def round_up(value, unit):
    return -(-value // unit) * unit


def shifted(value, dilation):
    span = value.shape[0]
    return jnp.concatenate(
        [
            pltpu.roll(value, dilation, axis=0).astype(BF16),
            value.astype(BF16),
            pltpu.roll(value, span - dilation, axis=0).astype(BF16),
        ],
        axis=1,
    )


class Shots:
    def __init__(
        self, dils, windows, step, couple, place_ref, recs, pick_ref, keep_ref, w0_ref, w1_ref, w2_ref,
        bias_ref, shift_ref, part_ref, x2_ref, rec_out_ref,
    ):
        self.dils, self.step, self.couple = dils, step, couple
        self.keep_ref, self.w0_ref, self.w1_ref, self.w2_ref = keep_ref, w0_ref, w1_ref, w2_ref
        self.bias_ref, self.shift_ref, self.x2_ref = bias_ref, shift_ref, x2_ref
        shots, rows, nodes = pick_ref.shape
        planes = shots // CORES
        self.slots = slots = x2_ref.shape[0]
        self.window = window = part_ref.shape[-1]
        self.rows, self.split = part_ref.shape[2], round_up(6 * slots, 16)
        self.span = window + 2 * HALO
        at = place_ref[1]
        self.right_ok = (at < windows - 1).astype(F32)
        self.left_ok = (at > 0).astype(F32)
        self.low_half = iota((self.span, HALF), 1) < CH * CORES

        lane = iota((nodes, 2 * window), 1)
        all_ok = jnp.where(
            lane < window, 1.0, jnp.where(lane < window + window // 2, self.right_ok, self.left_ok)
        ).astype(BF16)

        def put(part, swapped, value):
            for half in range(2):
                lanes = value[:, half * window : (half + 1) * window]
                part_ref[half, part, 0 : self.split] = lanes[0 : self.split]
                part_ref[half, swapped, self.split : rows] = lanes[self.split : rows]

        for x, rec_ref in enumerate(recs):
            n = 2 * couple + x % 2 + (planes if x >= 2 else 0)
            within = shot_of(place_ref, n, shots) & (QUAD - 1)
            edge = rec_ref[COMPS].astype(F32)
            for k in range(COMPS):
                turned = edge if k == 0 else pltpu.roll(edge, window - HALO * k, axis=1)
                both = jnp.concatenate([rec_ref[k], turned.astype(BF16)], axis=1)
                put(within * COMPS + k, (within ^ 2) * COMPS + k, dot(pick_ref[n], both))
            alive = dot(pick_ref[n], all_ok)
            for copy in range(2):
                first = QUAD * COMPS + QUAD * copy
                put(first + within, first + (within ^ 2), alive)

        self.half_rows = part_ref.shape[1] * self.rows
        self.part2 = part_ref.reshape(2 * self.half_rows, window)
        for q in range(slots):
            first = self.split + slots + q
            for half in range(2):
                pair = self.part2[pl.ds(first + (1 - half) * 8 * self.rows, 8, stride=self.rows), :]
                rec_out_ref[q, half * 8 : (half + 1) * 8] = pair

    def inside(self, value):
        w = self.window
        return jnp.concatenate(
            [value[0:w], value[w : w + HALO] * self.right_ok, value[w + HALO :] * self.left_ok], axis=0
        )

    def item_rows(self, q, b):
        start = (3 * (b // 2) * self.slots if b != 1 else self.split) + q
        halves = []
        for half in range(2):
            base = half * self.half_rows + start
            flags = base + QUAD * COMPS * self.rows
            pieces = [
                self.part2[pl.ds(base + a * self.slots, QUAD * COMPS, stride=self.rows), :] for a in range(3)
            ]
            for a in range(3):
                alive = self.part2[pl.ds(flags + a * self.slots, 2 * QUAD, stride=self.rows), :]
                pieces += [alive, alive]
            pieces.append(jnp.zeros((KROWS - 6 * QUAD * COMPS, self.window), F32))
            halves.append(jnp.concatenate(pieces, axis=0).astype(BF16))
        return jnp.concatenate(halves, axis=1)

    def items(self, group):
        return [(group * self.step + i, b) for i in range(self.step) for b in range(3)]

    def first_inputs(self, group):
        items = self.items(group)
        lhs = []
        for n in range(0, len(items), 2):
            some = jnp.concatenate([self.item_rows(q, b) for q, b in items[n : n + 2]], axis=0)
            moved = dot_t(self.shift_ref[...], some).astype(BF16)
            lhs += [moved[:, m : m + KROWS] for m in range(0, moved.shape[1], KROWS)]
        lifted = dot(jnp.concatenate(lhs, axis=0), self.w0_ref[...]).astype(BF16)
        return lifted[:, 0:LANES], lifted[:, LANES:]

    def taps_added(self, even, odd, dilation):
        mid = jnp.where(self.low_half, odd[:, 0:HALF], even[:, 0:HALF])
        late = jnp.where(self.low_half, odd[:, HALF:], even[:, HALF:])
        early = pltpu.roll(jnp.where(self.low_half, even[:, 0:HALF], odd[:, 0:HALF]), HALF // 2, axis=1)
        return (
            pltpu.roll(early, dilation, axis=0) + mid + pltpu.roll(late, self.span - dilation, axis=0)
        )

    def first_layer(self, group, even, odd):
        y_even, y_odd = dot(even, self.w1_ref[0]), dot(odd, self.w1_ref[1])
        x1 = []
        for n, (q, b) in enumerate(self.items(group)):
            at = slice(n * self.span, (n + 1) * self.span)
            old = jnp.where(self.low_half, odd[at, 0:HALF].astype(F32), even[at, 0:HALF].astype(F32))
            total = self.taps_added(y_even[at], y_odd[at], self.dils[0])
            new = jnp.maximum(total + self.bias_ref[0:1, 0:HALF], 0.0)
            x1.append(self.inside((old + new) * self.keep_ref[self.couple, b, q : q + 1, :]))
        even, odd, own = [], [], []
        for i in range(self.step):
            t0, t1, t2 = x1[3 * i : 3 * i + 3]
            t2 = t2.astype(BF16)
            even.append(jnp.concatenate([jnp.where(self.low_half, t0, t1).astype(BF16), t2], axis=1))
            odd.append(jnp.concatenate([jnp.where(self.low_half, t1, t0).astype(BF16), t2], axis=1))
            own.append(t1.astype(BF16))
        return jnp.concatenate(even, axis=0), jnp.concatenate(odd, axis=0), own

    def second_layer(self, group, even, odd, own):
        even, odd = dot(even, self.w2_ref[0]), dot(odd, self.w2_ref[1])
        for i in range(self.step):
            q = group * self.step + i
            at = slice(i * self.span, (i + 1) * self.span)
            total = self.taps_added(even[at], odd[at], self.dils[1])
            new = jnp.maximum(total + self.bias_ref[1:2, 0:HALF], 0.0)
            x2 = (own[i].astype(F32) + new) * self.keep_ref[self.couple, 1, q : q + 1, :]
            self.x2_ref[q] = shifted(self.inside(x2), self.dils[2])


def staged(work):
    inputs, middle = {}, {}
    for t in range(len(work) + 2):
        if t < len(work):
            stage, group = work[t]
            inputs[t] = stage.first_inputs(group)
        if 0 <= t - 1 < len(work):
            stage, group = work[t - 1]
            middle[t - 1] = stage.first_layer(group, *inputs.pop(t - 1))
        if 0 <= t - 2:
            stage, group = work[t - 2]
            stage.second_layer(group, *middle.pop(t - 2))
        yield t


def near_kernel(dils, windows, step, place_ref, *refs):
    pick_ref, keep_ref, w0_ref, w1_ref, w2_ref, bias_ref, shift_ref = refs[:7]
    x2_ref, rec_out_ref, part_ref = refs[7 + QUAD :]
    stage = Shots(
        dils, windows, step, 0, place_ref, refs[7 : 7 + QUAD], pick_ref, keep_ref, w0_ref, w1_ref, w2_ref,
        bias_ref, shift_ref, part_ref, x2_ref, rec_out_ref,
    )
    for _ in staged([(stage, group) for group in range(x2_ref.shape[0] // step)]):
        pass


def main_kernel(dils, windows, step, near, place_ref, *refs):
    shots = refs[0].shape[0]
    couples = shots // QUAD
    pick_ref, keep_ref, w0_ref, w1_ref, w2_ref, b3_ref, b4_ref, ow_ref, bias_ref, shift_ref = refs[:10]
    refs = refs[10:]
    rec_refs, refs = refs[: QUAD * (couples - near)], refs[QUAD * (couples - near) :]
    done_refs, refs = refs[: 2 * near], refs[2 * near :]
    out_ref, part_ref, x2_all, rec_all, x3_ref = refs
    blocks = couples // 2
    slots, window = out_ref.shape[1], out_ref.shape[3]
    span = window + 2 * HALO
    right_ok = (place_ref[1] < windows - 1).astype(F32)
    left_ok = (place_ref[1] > 0).astype(F32)

    stages = []
    x2_refs, rec_refs_out = list(done_refs[0::2]), list(done_refs[1::2])
    for c in range(near, couples):
        x2_refs.append(x2_all.at[c - near])
        rec_refs_out.append(rec_all.at[c - near])
        stages.append(
            Shots(
                dils, windows, step, c, place_ref, rec_refs[QUAD * (c - near) : QUAD * (c - near + 1)],
                pick_ref, keep_ref, w0_ref, w1_ref, w2_ref, bias_ref, shift_ref, part_ref.at[c - near],
                x2_refs[-1], rec_refs_out[-1],
            )
        )

    def receiver_layer(parts_of, weights, layer, block, group, out_rows):
        y = None
        for other in range(blocks):
            term = dot(jnp.concatenate(parts_of(other), axis=0), weights[block * blocks + other])
            y = term if y is None else y + term
        results = []
        for i, part in enumerate(parts_of(block)):
            q = group * step + i
            keep = jnp.concatenate([keep_ref[2 * block + c, 1, q : q + 1, :] for c in range(2)], axis=1)
            old = part[:, LANES : 2 * LANES].astype(F32)
            new = jnp.maximum(y[i * out_rows : (i + 1) * out_rows] + bias_ref[layer : layer + 1, :], 0.0)
            results.append((old + new) * keep)
        return results

    def third_layer(group):
        def parts_of(block):
            return [
                jnp.concatenate(
                    [
                        x2_refs[2 * block + c][group * step + i, :, e * HALF : (e + 1) * HALF]
                        for e in range(3)
                        for c in range(2)
                    ],
                    axis=1,
                )
                for i in range(step)
            ]

        for block in range(blocks):
            for i, value in enumerate(receiver_layer(parts_of, b3_ref, 2, block, group, span)):
                value = jnp.concatenate(
                    [
                        value[0:window],
                        value[window : window + HALO] * right_ok,
                        value[window + HALO :] * left_ok,
                    ],
                    axis=0,
                )
                x3_ref[block, group * step + i] = shifted(value, dils[3])[0:window]

    def last_layer(group):
        def parts_of(block):
            return [x3_ref[block, group * step + i] for i in range(step)]

        for block in range(blocks):
            for i, value in enumerate(receiver_layer(parts_of, b4_ref, 3, block, group, window)):
                q = group * step + i
                noise = dot_t(ow_ref[...], value.astype(BF16))
                record = jnp.concatenate([rec_refs_out[2 * block + c][q] for c in range(2)], axis=0)
                done = (record + noise).reshape(GROUP, COMPS, window)
                for c in range(2):
                    first = QUAD * couple_of(place_ref, 2 * block + c)
                    out_ref[pl.ds(first, QUAD), q] = done[c * QUAD : (c + 1) * QUAD]

    groups = slots // step
    work = [(stage, group) for group in range(groups) for stage in stages]
    lag = len(stages)
    for t in itertools.chain(staged(work), range(len(work) + 2, len(work) + 2 + 2 * lag)):
        done, rest = divmod(t - 2, lag)
        if rest == 0 and 0 <= done - 1 < groups:
            third_layer(done - 1)
        if rest == 0 and 0 <= done - 2 < groups:
            last_layer(done - 2)


def divisor(value, limit):
    return max(d for d in range(1, limit + 1) if value % d == 0)


def body(
    records,
    lift_weight,
    lift_bias,
    conv_weight,
    conv_bias,
    out_weight,
    live_count,
    trace_node,
    node_owner,
):
    _, comps, nodes, window = records.shape
    holders = lax.axis_size("gather")
    windows = lax.axis_size("tm")
    shots = holders * records.shape[0]
    couples = shots // QUAD
    blocks = couples // 2
    slots = (nodes + holders - 1) // holders
    dils = (1, 4, 2, 8)
    rows = round_up(6 * slots, 16) + round_up(3 * slots, 16)
    span = window + 2 * HALO

    planes = holders // CORES
    vmem = pl.BlockSpec(memory_space=pltpu.VMEM)
    smem = pl.BlockSpec(memory_space=pltpu.SMEM)
    like = jax.ShapeDtypeStruct

    def after(value, other):
        return lax.optimization_barrier((value, other))[0]

    def kernel(function, operands, specs, outs, scratch, limit, flops, name):
        return pl.pallas_call(
            function,
            out_shape=outs,
            in_specs=[smem] + specs,
            out_specs=jax.tree.map(lambda _: vmem, outs),
            scratch_shapes=scratch,
            compiler_params=pltpu.CompilerParams(vmem_limit_bytes=limit << 20),
            cost_estimate=pl.CostEstimate(flops=flops, bytes_accessed=1 << 10, transcendentals=0),
            name=name,
        )(place, *operands)

    place = jnp.stack([lax.axis_index("gather"), lax.axis_index("tm")]).astype(jnp.int32)
    taps = jnp.transpose(conv_weight, (0, 3, 4, 1, 2)).reshape(-1, CH)

    own = records[0]
    even = lax.axis_index("tm") % 2 == 0
    pack = lambda part: jnp.transpose(part, (1, 0, 2)).reshape(nodes, comps * HALO)
    first, last = pack(own[:, :, :HALO]), pack(own[:, :, window - HALO :])
    got = []
    for begin in range(2):
        pairs = [(w, w + 1) for w in range(begin, windows - 1, 2)]
        pairs += [(b, a) for a, b in pairs]
        got.append(lax.ppermute(jnp.where(even == (begin == 0), last, first), "tm", pairs))
    small = [live_count, trace_node, taps, jnp.transpose(lift_weight), lift_bias[None, :], conv_bias]
    raw = small + [node_owner[None, :], own, out_weight]
    raw = [pltpu.with_memory_space_constraint(a, pltpu.HBM) for a in raw]
    half = (taps.shape[0] // 2, CH)
    scratch = [pltpu.SMEM(a.shape, a.dtype) for a in raw[:2]] + [pltpu.VMEM(half, BF16)]
    scratch += [pltpu.VMEM(a.shape, a.dtype) for a in raw[3:7]]
    w0, w1, w2, wide_bias, shift, pick, keep, own, late_taps, out_taps = kernel(
        functools.partial(prep_kernel, dils, slots),
        raw,
        [pl.BlockSpec(memory_space=pltpu.HBM)] * len(raw),
        (
            like((KROWS, 2 * LANES), BF16),
            like((2, LANES, LANES), BF16),
            like((2, LANES, LANES), BF16),
            like((conv_bias.shape[0], LANES), F32),
            like((span, 2 * window), BF16),
            like((shots, rows, nodes), BF16),
            like((couples, 3, 16, HALF), F32),
            like(own.shape, BF16),
            like(half, BF16),
            like(out_weight.shape, BF16),
        ),
        scratch + [pltpu.SemaphoreType.DMA((7,)), pltpu.SemaphoreType.DMA((3,))],
        16,
        10**5,
        "weights",
    )
    right, left = jnp.where(even, got[0], got[1]), jnp.where(even, got[1], got[0])
    sent = jnp.concatenate([own, jnp.concatenate([right, left], axis=1)[None]], axis=0)


    def exchanged(block, distance):
        return lax.ppermute(block, "gather", [(g, g ^ distance) for g in range(holders)])

    near_blocks = [sent, exchanged(sent, CORES)]
    far = [exchanged(sent, CORES * r) for r in range(2, planes)]
    near_blocks += [exchanged(block, 1) for block in near_blocks]

    b3, b4, ow = kernel(
        functools.partial(band_kernel, dils, blocks),
        [late_taps, out_taps],
        [vmem] * 2,
        (
            like((blocks * blocks, 3 * LANES, LANES), BF16),
            like((blocks * blocks, 3 * LANES, LANES), BF16),
            like((GROUP * COMPS, LANES), BF16),
        ),
        [],
        16,
        10**10,
        "bands",
    )

    step = divisor(slots, 5)
    row_stride = round_up(rows, 16) + 8
    x2 = like((slots, span, 3 * HALF), BF16)
    held = like((slots, QUAD * COMPS, window), F32)
    parts = (2, PARTS, row_stride, window)
    operands = [after(pick, ow), keep, w0, w1, w2, wide_bias, shift, *near_blocks]
    near = kernel(
        functools.partial(near_kernel, dils, windows, step),
        operands,
        [vmem] * len(operands),
        (x2, held),
        [pltpu.VMEM(parts, F32)],
        24,
        10**5,
        "near",
    )

    operands = [pick, keep, w0, w1, w2, b3, b4, ow, wide_bias, shift]
    for r in range(0, len(far), 2):
        operands += far[r : r + 2] + [exchanged(after(block, near[1]), 1) for block in far[r : r + 2]]
    operands += near
    out = kernel(
        functools.partial(main_kernel, dils, windows, step, 1),
        operands,
        [vmem] * len(operands),
        like((shots, slots, comps, window), F32),
        [
            pltpu.VMEM((couples - 1, *parts), F32),
            pltpu.VMEM((couples - 1, *x2.shape), BF16),
            pltpu.VMEM((couples - 1, *held.shape), F32),
            pltpu.VMEM((blocks, slots, window, 3 * LANES), BF16),
        ],
        36,
        4 * 10**9,
        "layers",
    )
    return jnp.transpose(out, (0, 2, 1, 3))


def solution(mesh):
    return jax.shard_map(
        body,
        mesh=mesh,
        in_specs=(P("gather", None, None, "tm"), P(), P(), P(), P(), P(), P(), P(), P()),
        out_specs=P(None, None, "gather", "tm"),
        check_vma=False,
    )
```

```python
import functools
import itertools

import jax
import jax.numpy as jnp
from jax import lax
from jax.experimental import pallas as pl
from jax.experimental.pallas import tpu as pltpu
from jax.sharding import PartitionSpec as P

F32 = jnp.float32
BF16 = jnp.bfloat16
CH = 32
CORES = 2
COMPS = 4
GROUP = 8
LANES = GROUP * CH
HALO = 16
QUAD = 4
HALF = QUAD * CH
KROWS = 128
PARTS = QUAD * COMPS + 2 * QUAD


def iota(shape, dim):
    return lax.broadcasted_iota(jnp.int32, shape, dim)


def dot(a, b):
    return jnp.dot(a, b, preferred_element_type=F32)


def dot_t(a, b):
    return lax.dot_general(a, b, (((1,), (1,)), ((), ())), preferred_element_type=F32)


def onehot(cond):
    return cond.astype(F32).astype(BF16)


def band_links(dilation, offset):
    return [
        a
        for a in range(3)
        if any(s + GROUP * offset == t + (a - 1) * dilation for s in range(GROUP) for t in range(GROUP))
    ]


def split3(value):
    terms = []
    for _ in range(3):
        term = value.astype(BF16)
        terms.append(term)
        value = value - term.astype(F32)
    return terms


def shot_of(place_ref, n, shots):
    planes = shots // CORES
    plane = place_ref[0] // CORES
    core = place_ref[0] - CORES * plane
    return CORES * (plane ^ (n % planes)) + (core if n < planes else 1 - core)


def couple_of(place_ref, relative):
    return (place_ref[0] // (2 * CORES)) ^ relative


def table_kernel(dils, slots, place_ref, live_ref, trace_ref, owner_ref, pick_ref, keep_ref):
    shots, rows, nodes = pick_ref.shape
    split = round_up(6 * slots, 16)
    me = place_ref[0]

    mine = (owner_ref[...] == me).astype(F32)
    before = onehot(iota((nodes, nodes), 0) < iota((nodes, nodes), 1))
    rank = dot(jnp.broadcast_to(mine, (8, nodes)).astype(BF16), before)[0:1, :]
    node_ids = iota((1, nodes), 1).astype(F32)

    def nodes_of(slot_index):
        held = jnp.where((rank == slot_index.astype(F32)) & (mine > 0.5), 1.0, 0.0)
        node = jnp.sum(held * node_ids, axis=1, keepdims=True)
        there = jnp.sum(held, axis=1, keepdims=True)
        return jnp.where(there > 0.5, node, -1.0e6).astype(jnp.int32)

    row_id = iota((rows, nodes), 0)
    late = row_id >= split
    row_id = jnp.where(late, row_id - split, row_id)
    tap = jnp.zeros((rows, nodes), jnp.int32)
    for m in range(1, 7):
        tap = tap + (row_id >= m * slots).astype(jnp.int32)
    second = (tap >= 3).astype(jnp.int32)
    shift = dils[0] * (tap - 3 * second - 1) + jnp.where(late, 0, dils[1] * (2 * second - 1))
    target = nodes_of(row_id - slots * tap)
    target = jnp.where(tap >= jnp.where(late, 3, 6), -1000000, target + shift)

    node_lane = iota((rows, nodes), 1)
    for n in range(shots):
        s = shot_of(place_ref, n, shots)
        pick_ref[n] = onehot((node_lane == target - trace_ref[s, 0]) & (node_lane < live_ref[s]))

    slot_rows = keep_ref.shape[2]
    own_node = nodes_of(iota((slot_rows, nodes), 0))
    shot_lane = iota((slot_rows, HALF), 1) >> 5
    for c in range(shots // QUAD):
        base = QUAD * couple_of(place_ref, c)
        for b in range(3):
            first = jnp.zeros((slot_rows, HALF), jnp.int32)
            count = jnp.zeros((slot_rows, HALF), jnp.int32)
            for w in range(QUAD):
                at = shot_lane == (w if b == 1 else w ^ 2)
                first = jnp.where(at, trace_ref[base + w, 0], first)
                count = jnp.where(at, live_ref[base + w], count)
            trace = own_node + dils[1] * (b - 1) - first
            keep_ref[c, b] = ((trace >= 0) & (trace < count)).astype(F32)


def started(sources, places, sems):
    copies = [pltpu.make_async_copy(a, b, sems.at[n]) for n, (a, b) in enumerate(zip(sources, places))]
    for copy in copies:
        copy.start()
    return copies


def prep_kernel(dils, slots, place_ref, *refs):
    w0_ref, w1_ref, w2_ref, wide_bias_ref, shift_ref, pick_ref, keep_ref = refs[9:16]
    half = refs[2].shape[0] // 2
    passed = started((refs[7], refs[2].at[half : 2 * half], refs[8]), refs[16:19], refs[27])
    live_ref, trace_ref, cw_ref, lift_ref, lift_bias_ref, bias_ref, owner_ref = refs[19:26]
    sources = (*refs[:2], refs[2].at[0:half], *refs[3:7])
    for copy in started(sources, refs[19:26], refs[26]):
        copy.wait()
    table_kernel(dils, slots, place_ref, live_ref, trace_ref, owner_ref, pick_ref, keep_ref)

    rows8 = [lift_ref[...].astype(F32)] + [term.astype(F32) for term in split3(lift_bias_ref[...])]
    table = jnp.concatenate(rows8 + [jnp.zeros((1, CH), F32)], axis=0).astype(BF16)
    data_rows = 3 * QUAD * COMPS
    r8 = iota((KROWS, 8), 0)
    part = jnp.where(r8 < data_rows, r8 & (COMPS - 1), COMPS + ((r8 >> 2) & 3))
    values = dot(onehot((part == iota((KROWS, 8), 1)) & (r8 < 2 * data_rows)), table).astype(BF16)
    wide = iota((CH, 2 * LANES), 1)
    spread = onehot(iota((CH, 2 * LANES), 0) == (wide & 31))
    rr = iota((KROWS, 2 * LANES), 0)
    cc = iota((KROWS, 2 * LANES), 1)
    row_node = jnp.where(rr < data_rows, rr >> 4, (rr - data_rows) >> 4)
    row_shot = jnp.where(rr < data_rows, rr >> 2, rr) & (QUAD - 1)
    place = (cc >> 6) & 3
    node = jnp.where((cc >= LANES) & (place < 2), 1 - place, place)
    same = (row_node == node) & (row_shot == 2 * (cc >> 8) + ((cc >> 5) & 1)) & (rr < 2 * data_rows)
    w0_ref[...] = jnp.where(same & (place < 3), dot(values, spread), 0.0).astype(BF16)

    widen = onehot((iota((LANES, CH), 0) & 31) == iota((LANES, CH), 1))
    kr = iota((LANES, LANES), 0)
    kc = iota((LANES, LANES), 1)
    same_shot = ((kr >> 5) & 1) == ((kc >> 5) & 1)
    sr = iota((3 * CH, LANES), 0)
    sc = iota((3 * CH, LANES), 1)
    for layer, ref, odd_taps in ((0, w1_ref, (1, 0, 2, 3)), (1, w2_ref, (1, 0, 3, 2))):
        base = 3 * layer
        tall = [
            dot_t(widen, cw_ref[(base + a) * 3 * CH : (base + a + 1) * 3 * CH, :]).astype(BF16)
            for a in range(3)
        ]
        for odd, (k_taps, n_taps) in enumerate((((0, 1, 2, 3), (0, 1, 3, 2)), (odd_taps, (1, 0, 2, 3)))):
            place = sum(jnp.where((sc >> 6) == y, n_taps[y], 0) for y in range(4))
            spread2 = onehot(((sr >> 5) == place) & ((sr & 31) == (sc & 31)))
            total = jnp.zeros((LANES, LANES), F32)
            for x in range(4):
                if k_taps[x] < 3:
                    total = jnp.where(((kr >> 6) == x) & same_shot, dot(tall[k_taps[x]], spread2), total)
            ref[odd] = total.astype(BF16)

    span = shift_ref.shape[0]
    window = span - 2 * HALO
    source = iota(shift_ref.shape, 0)
    source = jnp.where(source < window + HALO, source, source + window // 2 - HALO)
    shift_ref[...] = onehot(iota(shift_ref.shape, 1) == source)

    tile = onehot(iota((CH, LANES), 0) == (iota((CH, LANES), 1) & 31))
    wide_bias_ref[...] = sum(dot(term, tile) for term in split3(bias_ref[...]))
    for copy in passed:
        copy.wait()


def band_kernel(dils, blocks, place_ref, *refs):
    cw_ref, out_w_ref, b3_ref, b4_ref, ow_ref = refs
    widen = onehot((iota((LANES, CH), 0) & 31) == iota((LANES, CH), 1))

    er = iota((3 * CH, 3 * LANES), 0)
    ec = iota((3 * CH, 3 * LANES), 1)
    spread3 = onehot(((er >> 5) == (ec >> 8)) & ((er & 31) == (ec & 31)))
    row_lane = iota((LANES, 3 * LANES), 0)
    col_lane = iota((LANES, 3 * LANES), 1) & (LANES - 1)

    def shots_in(lane, block):
        couple = jnp.where(lane < HALF, couple_of(place_ref, 2 * block), couple_of(place_ref, 2 * block + 1))
        return QUAD * couple + ((lane >> 5) & (QUAD - 1))

    def expanded(layer, a):
        base = ((layer - 2) * 3 + a) * 3 * CH
        return dot(dot_t(widen, cw_ref[base : base + 3 * CH, :]).astype(BF16), spread3)

    for layer, ref in ((2, b3_ref), (3, b4_ref)):
        linked_taps = band_links(dils[layer], 0) if blocks == 1 else range(3)
        for out_block in range(blocks):
            for in_block in range(blocks):
                total = jnp.zeros((LANES, 3 * LANES), F32)
                for a in linked_taps:
                    reach = shots_in(col_lane, out_block) + (a - 1) * dils[layer]
                    total = total + jnp.where(shots_in(row_lane, in_block) == reach, expanded(layer, a), 0.0)
                for e in range(3):
                    ref[out_block * blocks + in_block, e * LANES : (e + 1) * LANES, :] = total[
                        :, e * LANES : (e + 1) * LANES
                    ].astype(BF16)

    rows = GROUP * COMPS
    pick = onehot((iota((rows, COMPS), 0) & (COMPS - 1)) == iota((rows, COMPS), 1))
    mine = dot(pick, out_w_ref[...]).astype(BF16)
    tile = onehot(iota((CH, LANES), 0) == (iota((CH, LANES), 1) & 31))
    same = (iota((rows, LANES), 0) >> 2) == (iota((rows, LANES), 1) >> 5)
    ow_ref[...] = jnp.where(same, dot(mine, tile), 0.0).astype(BF16)


def round_up(value, unit):
    return -(-value // unit) * unit


def shifted(value, dilation):
    span = value.shape[0]
    return jnp.concatenate(
        [
            pltpu.roll(value, dilation, axis=0).astype(BF16),
            value.astype(BF16),
            pltpu.roll(value, span - dilation, axis=0).astype(BF16),
        ],
        axis=1,
    )


class Shots:
    def __init__(
        self, dils, windows, step, couple, place_ref, recs, pick_ref, keep_ref, w0_ref, w1_ref, w2_ref,
        bias_ref, shift_ref, part_ref, x2_ref, rec_out_ref,
    ):
        self.dils, self.step, self.couple = dils, step, couple
        self.chunk = 3 * step if couple == 0 else 3
        self.keep_ref, self.w0_ref, self.w1_ref, self.w2_ref = keep_ref, w0_ref, w1_ref, w2_ref
        self.bias_ref, self.shift_ref, self.x2_ref = bias_ref, shift_ref, x2_ref
        shots, rows, nodes = pick_ref.shape
        planes = shots // CORES
        self.slots = slots = x2_ref.shape[0]
        self.window = window = part_ref.shape[-1]
        self.rows, self.split = part_ref.shape[2], round_up(6 * slots, 16)
        self.span = window + 2 * HALO
        at = place_ref[1]
        self.right_ok = (at < windows - 1).astype(F32)
        self.left_ok = (at > 0).astype(F32)
        self.low_half = iota((self.span, HALF), 1) < CH * CORES

        lane = iota((nodes, 2 * window), 1)
        all_ok = jnp.where(
            lane < window, 1.0, jnp.where(lane < window + window // 2, self.right_ok, self.left_ok)
        ).astype(BF16)

        def put(part, swapped, value):
            for half in range(2):
                lanes = value[:, half * window : (half + 1) * window]
                part_ref[half, part, 0 : self.split] = lanes[0 : self.split]
                part_ref[half, swapped, self.split : rows] = lanes[self.split : rows]

        for x, rec_ref in enumerate(recs):
            n = 2 * couple + x % 2 + (planes if x >= 2 else 0)
            within = shot_of(place_ref, n, shots) & (QUAD - 1)
            edge = rec_ref[COMPS].astype(F32)
            for k in range(COMPS):
                turned = edge if k == 0 else pltpu.roll(edge, window - HALO * k, axis=1)
                both = jnp.concatenate([rec_ref[k], turned.astype(BF16)], axis=1)
                put(within * COMPS + k, (within ^ 2) * COMPS + k, dot(pick_ref[n], both))
            alive = dot(pick_ref[n], all_ok)
            for copy in range(2):
                first = QUAD * COMPS + QUAD * copy
                put(first + within, first + (within ^ 2), alive)

        self.half_rows = part_ref.shape[1] * self.rows
        self.part2 = part_ref.reshape(2 * self.half_rows, window)
        for q in range(slots):
            first = self.split + slots + q
            for half in range(2):
                pair = self.part2[pl.ds(first + (1 - half) * 8 * self.rows, 8, stride=self.rows), :]
                rec_out_ref[q, half * 8 : (half + 1) * 8] = pair

    def inside(self, value):
        w = self.window
        return jnp.concatenate(
            [value[0:w], value[w : w + HALO] * self.right_ok, value[w + HALO :] * self.left_ok], axis=0
        )

    def item_rows(self, q, b):
        start = (3 * (b // 2) * self.slots if b != 1 else self.split) + q
        halves = []
        for half in range(2):
            base = half * self.half_rows + start
            flags = base + QUAD * COMPS * self.rows
            pieces = [
                self.part2[pl.ds(base + a * self.slots, QUAD * COMPS, stride=self.rows), :] for a in range(3)
            ]
            for a in range(3):
                alive = self.part2[pl.ds(flags + a * self.slots, 2 * QUAD, stride=self.rows), :]
                pieces += [alive, alive]
            pieces.append(jnp.zeros((KROWS - 6 * QUAD * COMPS, self.window), F32))
            halves.append(jnp.concatenate(pieces, axis=0).astype(BF16))
        return jnp.concatenate(halves, axis=1)

    def items(self, group):
        return [(group * self.step + i, b) for i in range(self.step) for b in range(3)]

    def first_inputs(self, group):
        items = self.items(group)
        lhs = []
        for n in range(0, len(items), 2):
            some = jnp.concatenate([self.item_rows(q, b) for q, b in items[n : n + 2]], axis=0)
            moved = dot_t(self.shift_ref[...], some).astype(BF16)
            lhs += [moved[:, m : m + KROWS] for m in range(0, moved.shape[1], KROWS)]
        lifted = [
            dot(jnp.concatenate(lhs[n : n + self.chunk], axis=0), self.w0_ref[...]).astype(BF16)
            for n in range(0, len(lhs), self.chunk)
        ]
        return tuple(jnp.concatenate([x[:, p : p + LANES] for x in lifted], axis=0) for p in (0, LANES))

    def taps_added(self, even, odd, dilation):
        mid = jnp.where(self.low_half, odd[:, 0:HALF], even[:, 0:HALF])
        late = jnp.where(self.low_half, odd[:, HALF:], even[:, HALF:])
        early = pltpu.roll(jnp.where(self.low_half, even[:, 0:HALF], odd[:, 0:HALF]), HALF // 2, axis=1)
        return (
            pltpu.roll(early, dilation, axis=0) + mid + pltpu.roll(late, self.span - dilation, axis=0)
        )

    def first_layer(self, group, even, odd):
        y_even, y_odd = dot(even, self.w1_ref[0]), dot(odd, self.w1_ref[1])
        x1 = []
        for n, (q, b) in enumerate(self.items(group)):
            at = slice(n * self.span, (n + 1) * self.span)
            old = jnp.where(self.low_half, odd[at, 0:HALF].astype(F32), even[at, 0:HALF].astype(F32))
            total = self.taps_added(y_even[at], y_odd[at], self.dils[0])
            new = jnp.maximum(total + self.bias_ref[0:1, 0:HALF], 0.0)
            x1.append(self.inside((old + new) * self.keep_ref[self.couple, b, q : q + 1, :]))
        even, odd, own = [], [], []
        for i in range(self.step):
            t0, t1, t2 = x1[3 * i : 3 * i + 3]
            t2 = t2.astype(BF16)
            even.append(jnp.concatenate([jnp.where(self.low_half, t0, t1).astype(BF16), t2], axis=1))
            odd.append(jnp.concatenate([jnp.where(self.low_half, t1, t0).astype(BF16), t2], axis=1))
            own.append(t1.astype(BF16))
        return jnp.concatenate(even, axis=0), jnp.concatenate(odd, axis=0), own

    def second_layer(self, group, even, odd, own):
        even, odd = dot(even, self.w2_ref[0]), dot(odd, self.w2_ref[1])
        for i in range(self.step):
            q = group * self.step + i
            at = slice(i * self.span, (i + 1) * self.span)
            total = self.taps_added(even[at], odd[at], self.dils[1])
            new = jnp.maximum(total + self.bias_ref[1:2, 0:HALF], 0.0)
            x2 = (own[i].astype(F32) + new) * self.keep_ref[self.couple, 1, q : q + 1, :]
            self.x2_ref[q] = shifted(self.inside(x2), self.dils[2])


def staged(work):
    inputs, middle = {}, {}
    for t in range(len(work) + 2):
        if t < len(work):
            stage, group = work[t]
            inputs[t] = stage.first_inputs(group)
        if 0 <= t - 1 < len(work):
            stage, group = work[t - 1]
            middle[t - 1] = stage.first_layer(group, *inputs.pop(t - 1))
        if 0 <= t - 2:
            stage, group = work[t - 2]
            stage.second_layer(group, *middle.pop(t - 2))
        yield t


def near_kernel(dils, windows, step, place_ref, *refs):
    pick_ref, keep_ref, w0_ref, w1_ref, w2_ref, bias_ref, shift_ref = refs[:7]
    x2_ref, rec_out_ref, part_ref = refs[7 + QUAD :]
    stage = Shots(
        dils, windows, step, 0, place_ref, refs[7 : 7 + QUAD], pick_ref, keep_ref, w0_ref, w1_ref, w2_ref,
        bias_ref, shift_ref, part_ref, x2_ref, rec_out_ref,
    )
    for _ in staged([(stage, group) for group in range(x2_ref.shape[0] // step)]):
        pass


def main_kernel(dils, windows, step, near, place_ref, *refs):
    shots = refs[0].shape[0]
    couples = shots // QUAD
    pick_ref, keep_ref, w0_ref, w1_ref, w2_ref, b3_ref, b4_ref, ow_ref, bias_ref, shift_ref = refs[:10]
    refs = refs[10:]
    rec_refs, refs = refs[: QUAD * (couples - near)], refs[QUAD * (couples - near) :]
    done_refs, refs = refs[: 2 * near], refs[2 * near :]
    out_ref, part_ref, x2_all, rec_all, x3_ref = refs
    blocks = couples // 2
    slots, window = out_ref.shape[1], out_ref.shape[3]
    span = window + 2 * HALO
    right_ok = (place_ref[1] < windows - 1).astype(F32)
    left_ok = (place_ref[1] > 0).astype(F32)

    stages = []
    x2_refs, rec_refs_out = list(done_refs[0::2]), list(done_refs[1::2])
    for c in range(near, couples):
        x2_refs.append(x2_all.at[c - near])
        rec_refs_out.append(rec_all.at[c - near])
        stages.append(
            Shots(
                dils, windows, step, c, place_ref, rec_refs[QUAD * (c - near) : QUAD * (c - near + 1)],
                pick_ref, keep_ref, w0_ref, w1_ref, w2_ref, bias_ref, shift_ref, part_ref.at[c - near],
                x2_refs[-1], rec_refs_out[-1],
            )
        )

    def receiver_layer(parts_of, weights, layer, block, group, out_rows):
        y = None
        for other in range(blocks):
            term = dot(jnp.concatenate(parts_of(other), axis=0), weights[block * blocks + other])
            y = term if y is None else y + term
        results = []
        for i, part in enumerate(parts_of(block)):
            q = group * step + i
            keep = jnp.concatenate([keep_ref[2 * block + c, 1, q : q + 1, :] for c in range(2)], axis=1)
            old = part[:, LANES : 2 * LANES].astype(F32)
            new = jnp.maximum(y[i * out_rows : (i + 1) * out_rows] + bias_ref[layer : layer + 1, :], 0.0)
            results.append((old + new) * keep)
        return results

    def third_layer(group):
        def parts_of(block):
            return [
                jnp.concatenate(
                    [
                        x2_refs[2 * block + c][group * step + i, :, e * HALF : (e + 1) * HALF]
                        for e in range(3)
                        for c in range(2)
                    ],
                    axis=1,
                )
                for i in range(step)
            ]

        for block in range(blocks):
            for i, value in enumerate(receiver_layer(parts_of, b3_ref, 2, block, group, span)):
                value = jnp.concatenate(
                    [
                        value[0:window],
                        value[window : window + HALO] * right_ok,
                        value[window + HALO :] * left_ok,
                    ],
                    axis=0,
                )
                x3_ref[block, group * step + i] = shifted(value, dils[3])[0:window]

    def last_layer(group):
        def parts_of(block):
            return [x3_ref[block, group * step + i] for i in range(step)]

        for block in range(blocks):
            for i, value in enumerate(receiver_layer(parts_of, b4_ref, 3, block, group, window)):
                q = group * step + i
                noise = dot_t(ow_ref[...], value.astype(BF16))
                record = jnp.concatenate([rec_refs_out[2 * block + c][q] for c in range(2)], axis=0)
                done = (record + noise).reshape(GROUP, COMPS, window)
                for c in range(2):
                    first = QUAD * couple_of(place_ref, 2 * block + c)
                    out_ref[pl.ds(first, QUAD), q] = done[c * QUAD : (c + 1) * QUAD]

    groups = slots // step
    work = [(stage, group) for group in range(groups) for stage in stages]
    lag = len(stages)
    for t in itertools.chain(staged(work), range(len(work) + 2, len(work) + 2 + 2 * lag)):
        done, rest = divmod(t - 2, lag)
        if rest == 0 and 0 <= done - 1 < groups:
            third_layer(done - 1)
        if rest == 0 and 0 <= done - 2 < groups:
            last_layer(done - 2)


def divisor(value, limit):
    return max(d for d in range(1, limit + 1) if value % d == 0)


def body(
    records,
    lift_weight,
    lift_bias,
    conv_weight,
    conv_bias,
    out_weight,
    live_count,
    trace_node,
    node_owner,
):
    _, comps, nodes, window = records.shape
    holders = lax.axis_size("gather")
    windows = lax.axis_size("tm")
    shots = holders * records.shape[0]
    couples = shots // QUAD
    blocks = couples // 2
    slots = (nodes + holders - 1) // holders
    dils = (1, 4, 2, 8)
    rows = round_up(6 * slots, 16) + round_up(3 * slots, 16)
    span = window + 2 * HALO

    planes = holders // CORES
    vmem = pl.BlockSpec(memory_space=pltpu.VMEM)
    smem = pl.BlockSpec(memory_space=pltpu.SMEM)
    like = jax.ShapeDtypeStruct

    def after(value, other):
        return lax.optimization_barrier((value, other))[0]

    def kernel(function, operands, specs, outs, scratch, limit, flops, name):
        return pl.pallas_call(
            function,
            out_shape=outs,
            in_specs=[smem] + specs,
            out_specs=jax.tree.map(lambda _: vmem, outs),
            scratch_shapes=scratch,
            compiler_params=pltpu.CompilerParams(vmem_limit_bytes=limit << 20),
            cost_estimate=pl.CostEstimate(flops=flops, bytes_accessed=1 << 10, transcendentals=0),
            name=name,
        )(place, *operands)

    place = jnp.stack([lax.axis_index("gather"), lax.axis_index("tm")]).astype(jnp.int32)
    taps = jnp.transpose(conv_weight, (0, 3, 4, 1, 2)).reshape(-1, CH)

    own = records[0]
    even = lax.axis_index("tm") % 2 == 0
    pack = lambda part: jnp.transpose(part, (1, 0, 2)).reshape(nodes, comps * HALO)
    first, last = pack(own[:, :, :HALO]), pack(own[:, :, window - HALO :])
    got = []
    for begin in range(2):
        pairs = [(w, w + 1) for w in range(begin, windows - 1, 2)]
        pairs += [(b, a) for a, b in pairs]
        got.append(lax.ppermute(jnp.where(even == (begin == 0), last, first), "tm", pairs))
    small = [live_count, trace_node, taps, jnp.transpose(lift_weight), lift_bias[None, :], conv_bias]
    raw = small + [node_owner[None, :], own, out_weight]
    raw = [pltpu.with_memory_space_constraint(a, pltpu.HBM) for a in raw]
    half = (taps.shape[0] // 2, CH)
    scratch = [pltpu.SMEM(a.shape, a.dtype) for a in raw[:2]] + [pltpu.VMEM(half, BF16)]
    scratch += [pltpu.VMEM(a.shape, a.dtype) for a in raw[3:7]]
    w0, w1, w2, wide_bias, shift, pick, keep, own, late_taps, out_taps = kernel(
        functools.partial(prep_kernel, dils, slots),
        raw,
        [pl.BlockSpec(memory_space=pltpu.HBM)] * len(raw),
        (
            like((KROWS, 2 * LANES), BF16),
            like((2, LANES, LANES), BF16),
            like((2, LANES, LANES), BF16),
            like((conv_bias.shape[0], LANES), F32),
            like((span, 2 * window), BF16),
            like((shots, rows, nodes), BF16),
            like((couples, 3, 16, HALF), F32),
            like(own.shape, BF16),
            like(half, BF16),
            like(out_weight.shape, BF16),
        ),
        scratch + [pltpu.SemaphoreType.DMA((7,)), pltpu.SemaphoreType.DMA((3,))],
        16,
        10**5,
        "weights",
    )
    right, left = jnp.where(even, got[0], got[1]), jnp.where(even, got[1], got[0])
    sent = jnp.concatenate([own, jnp.concatenate([right, left], axis=1)[None]], axis=0)


    def exchanged(block, distance):
        return lax.ppermute(block, "gather", [(g, g ^ distance) for g in range(holders)])

    near_blocks = [sent, exchanged(sent, CORES)]
    far = [exchanged(sent, CORES * r) for r in range(2, planes)]
    near_blocks += [exchanged(block, 1) for block in near_blocks]

    b3, b4, ow = kernel(
        functools.partial(band_kernel, dils, blocks),
        [late_taps, out_taps],
        [vmem] * 2,
        (
            like((blocks * blocks, 3 * LANES, LANES), BF16),
            like((blocks * blocks, 3 * LANES, LANES), BF16),
            like((GROUP * COMPS, LANES), BF16),
        ),
        [],
        16,
        10**10,
        "bands",
    )

    step = divisor(slots, 5)
    row_stride = round_up(rows, 16) + 8
    x2 = like((slots, span, 3 * HALF), BF16)
    held = like((slots, QUAD * COMPS, window), F32)
    parts = (2, PARTS, row_stride, window)
    operands = [after(pick, ow), keep, w0, w1, w2, wide_bias, shift, *near_blocks]
    near = kernel(
        functools.partial(near_kernel, dils, windows, slots),
        operands,
        [vmem] * len(operands),
        (x2, held),
        [pltpu.VMEM(parts, F32)],
        24,
        10**5,
        "near",
    )

    operands = [pick, keep, w0, w1, w2, b3, b4, ow, wide_bias, shift]
    for r in range(0, len(far), 2):
        operands += far[r : r + 2] + [exchanged(after(block, near[1]), 1) for block in far[r : r + 2]]
    operands += near
    out = kernel(
        functools.partial(main_kernel, dils, windows, step, 1),
        operands,
        [vmem] * len(operands),
        like((shots, slots, comps, window), F32),
        [
            pltpu.VMEM((couples - 1, *parts), F32),
            pltpu.VMEM((couples - 1, *x2.shape), BF16),
            pltpu.VMEM((couples - 1, *held.shape), F32),
            pltpu.VMEM((blocks, slots, window, 3 * LANES), BF16),
        ],
        36,
        4 * 10**9,
        "layers",
    )
    return jnp.transpose(out, (0, 2, 1, 3))


def solution(mesh):
    return jax.shard_map(
        body,
        mesh=mesh,
        in_specs=(P("gather", None, None, "tm"), P(), P(), P(), P(), P(), P(), P(), P()),
        out_specs=P(None, None, "gather", "tm"),
        check_vma=False,
    )
```

```python
import functools
import itertools

import jax
import jax.numpy as jnp
from jax import lax
from jax.experimental import pallas as pl
from jax.experimental.pallas import tpu as pltpu
from jax.sharding import PartitionSpec as P

F32 = jnp.float32
BF16 = jnp.bfloat16
CH = 32
CORES = 2
COMPS = 4
GROUP = 8
LANES = GROUP * CH
HALO = 16
QUAD = 4
HALF = QUAD * CH
KROWS = 128
PARTS = QUAD * COMPS + 2 * QUAD


def iota(shape, dim):
    return lax.broadcasted_iota(jnp.int32, shape, dim)


def dot(a, b):
    return jnp.dot(a, b, preferred_element_type=F32)


def dot_t(a, b):
    return lax.dot_general(a, b, (((1,), (1,)), ((), ())), preferred_element_type=F32)


def onehot(cond):
    return cond.astype(F32).astype(BF16)


def band_links(dilation, offset):
    return [
        a
        for a in range(3)
        if any(s + GROUP * offset == t + (a - 1) * dilation for s in range(GROUP) for t in range(GROUP))
    ]


def split3(value):
    terms = []
    for _ in range(3):
        term = value.astype(BF16)
        terms.append(term)
        value = value - term.astype(F32)
    return terms


def shot_of(place_ref, n, shots):
    planes = shots // CORES
    plane = place_ref[0] // CORES
    core = place_ref[0] - CORES * plane
    return CORES * (plane ^ (n % planes)) + (core if n < planes else 1 - core)


def couple_of(place_ref, relative):
    return (place_ref[0] // (2 * CORES)) ^ relative


def table_kernel(dils, slots, place_ref, live_ref, trace_ref, owner_ref, pick_ref, keep_ref):
    shots, rows, nodes = pick_ref.shape
    split = round_up(6 * slots, 16)
    me = place_ref[0]

    mine = (owner_ref[...] == me).astype(F32)
    before = onehot(iota((nodes, nodes), 0) < iota((nodes, nodes), 1))
    rank = dot(jnp.broadcast_to(mine, (8, nodes)).astype(BF16), before)[0:1, :]
    node_ids = iota((1, nodes), 1).astype(F32)

    def nodes_of(slot_index):
        held = jnp.where((rank == slot_index.astype(F32)) & (mine > 0.5), 1.0, 0.0)
        node = jnp.sum(held * node_ids, axis=1, keepdims=True)
        there = jnp.sum(held, axis=1, keepdims=True)
        return jnp.where(there > 0.5, node, -1.0e6).astype(jnp.int32)

    row_id = iota((rows, nodes), 0)
    late = row_id >= split
    row_id = jnp.where(late, row_id - split, row_id)
    tap = jnp.zeros((rows, nodes), jnp.int32)
    for m in range(1, 7):
        tap = tap + (row_id >= m * slots).astype(jnp.int32)
    second = (tap >= 3).astype(jnp.int32)
    shift = dils[0] * (tap - 3 * second - 1) + jnp.where(late, 0, dils[1] * (2 * second - 1))
    target = nodes_of(row_id - slots * tap)
    target = jnp.where(tap >= jnp.where(late, 3, 6), -1000000, target + shift)

    node_lane = iota((rows, nodes), 1)
    for n in range(shots):
        s = shot_of(place_ref, n, shots)
        pick_ref[n] = onehot((node_lane == target - trace_ref[s, 0]) & (node_lane < live_ref[s]))

    slot_rows = keep_ref.shape[2]
    own_node = nodes_of(iota((slot_rows, nodes), 0))
    shot_lane = iota((slot_rows, HALF), 1) >> 5
    for c in range(shots // QUAD):
        base = QUAD * couple_of(place_ref, c)
        for b in range(3):
            first = jnp.zeros((slot_rows, HALF), jnp.int32)
            count = jnp.zeros((slot_rows, HALF), jnp.int32)
            for w in range(QUAD):
                at = shot_lane == (w if b == 1 else w ^ 2)
                first = jnp.where(at, trace_ref[base + w, 0], first)
                count = jnp.where(at, live_ref[base + w], count)
            trace = own_node + dils[1] * (b - 1) - first
            keep_ref[c, b] = ((trace >= 0) & (trace < count)).astype(F32)


def started(sources, places, sems):
    copies = [pltpu.make_async_copy(a, b, sems.at[n]) for n, (a, b) in enumerate(zip(sources, places))]
    for copy in copies:
        copy.start()
    return copies


def prep_kernel(dils, slots, place_ref, *refs):
    w0_ref, w1_ref, w2_ref, wide_bias_ref, shift_ref, pick_ref, keep_ref = refs[9:16]
    half = refs[2].shape[0] // 2
    passed = started((refs[7], refs[2].at[half : 2 * half], refs[8]), refs[16:19], refs[27])
    live_ref, trace_ref, cw_ref, lift_ref, lift_bias_ref, bias_ref, owner_ref = refs[19:26]
    sources = (*refs[:2], refs[2].at[0:half], *refs[3:7])
    for copy in started(sources, refs[19:26], refs[26]):
        copy.wait()
    table_kernel(dils, slots, place_ref, live_ref, trace_ref, owner_ref, pick_ref, keep_ref)

    rows8 = [lift_ref[...].astype(F32)] + [term.astype(F32) for term in split3(lift_bias_ref[...])]
    table = jnp.concatenate(rows8 + [jnp.zeros((1, CH), F32)], axis=0).astype(BF16)
    data_rows = 3 * QUAD * COMPS
    r8 = iota((KROWS, 8), 0)
    part = jnp.where(r8 < data_rows, r8 & (COMPS - 1), COMPS + ((r8 >> 2) & 3))
    values = dot(onehot((part == iota((KROWS, 8), 1)) & (r8 < 2 * data_rows)), table).astype(BF16)
    wide = iota((CH, 2 * LANES), 1)
    spread = onehot(iota((CH, 2 * LANES), 0) == (wide & 31))
    rr = iota((KROWS, 2 * LANES), 0)
    cc = iota((KROWS, 2 * LANES), 1)
    row_node = jnp.where(rr < data_rows, rr >> 4, (rr - data_rows) >> 4)
    row_shot = jnp.where(rr < data_rows, rr >> 2, rr) & (QUAD - 1)
    place = (cc >> 6) & 3
    node = jnp.where((cc >= LANES) & (place < 2), 1 - place, place)
    same = (row_node == node) & (row_shot == 2 * (cc >> 8) + ((cc >> 5) & 1)) & (rr < 2 * data_rows)
    w0_ref[...] = jnp.where(same & (place < 3), dot(values, spread), 0.0).astype(BF16)

    widen = onehot((iota((LANES, CH), 0) & 31) == iota((LANES, CH), 1))
    kr = iota((LANES, LANES), 0)
    kc = iota((LANES, LANES), 1)
    same_shot = ((kr >> 5) & 1) == ((kc >> 5) & 1)
    sr = iota((3 * CH, LANES), 0)
    sc = iota((3 * CH, LANES), 1)
    for layer, ref, odd_taps in ((0, w1_ref, (1, 0, 2, 3)), (1, w2_ref, (1, 0, 3, 2))):
        base = 3 * layer
        tall = [
            dot_t(widen, cw_ref[(base + a) * 3 * CH : (base + a + 1) * 3 * CH, :]).astype(BF16)
            for a in range(3)
        ]
        for odd, (k_taps, n_taps) in enumerate((((0, 1, 2, 3), (0, 1, 3, 2)), (odd_taps, (1, 0, 2, 3)))):
            place = sum(jnp.where((sc >> 6) == y, n_taps[y], 0) for y in range(4))
            spread2 = onehot(((sr >> 5) == place) & ((sr & 31) == (sc & 31)))
            total = jnp.zeros((LANES, LANES), F32)
            for x in range(4):
                if k_taps[x] < 3:
                    total = jnp.where(((kr >> 6) == x) & same_shot, dot(tall[k_taps[x]], spread2), total)
            ref[odd] = total.astype(BF16)

    span = shift_ref.shape[0]
    window = span - 2 * HALO
    source = iota(shift_ref.shape, 0)
    source = jnp.where(source < window + HALO, source, source + window // 2 - HALO)
    shift_ref[...] = onehot(iota(shift_ref.shape, 1) == source)

    tile = onehot(iota((CH, LANES), 0) == (iota((CH, LANES), 1) & 31))
    wide_bias_ref[...] = sum(dot(term, tile) for term in split3(bias_ref[...]))
    for copy in passed:
        copy.wait()


def band_kernel(dils, blocks, place_ref, *refs):
    cw_ref, out_w_ref, b3_ref, b4_ref, ow_ref = refs
    widen = onehot((iota((LANES, CH), 0) & 31) == iota((LANES, CH), 1))

    er = iota((3 * CH, 3 * LANES), 0)
    ec = iota((3 * CH, 3 * LANES), 1)
    spread3 = onehot(((er >> 5) == (ec >> 8)) & ((er & 31) == (ec & 31)))
    row_lane = iota((LANES, 3 * LANES), 0)
    col_lane = iota((LANES, 3 * LANES), 1) & (LANES - 1)

    def shots_in(lane, block):
        couple = jnp.where(lane < HALF, couple_of(place_ref, 2 * block), couple_of(place_ref, 2 * block + 1))
        return QUAD * couple + ((lane >> 5) & (QUAD - 1))

    def expanded(layer, a):
        base = ((layer - 2) * 3 + a) * 3 * CH
        return dot(dot_t(widen, cw_ref[base : base + 3 * CH, :]).astype(BF16), spread3)

    for layer, ref in ((2, b3_ref), (3, b4_ref)):
        linked_taps = band_links(dils[layer], 0) if blocks == 1 else range(3)
        for out_block in range(blocks):
            for in_block in range(blocks):
                total = jnp.zeros((LANES, 3 * LANES), F32)
                for a in linked_taps:
                    reach = shots_in(col_lane, out_block) + (a - 1) * dils[layer]
                    total = total + jnp.where(shots_in(row_lane, in_block) == reach, expanded(layer, a), 0.0)
                for e in range(3):
                    ref[out_block * blocks + in_block, e * LANES : (e + 1) * LANES, :] = total[
                        :, e * LANES : (e + 1) * LANES
                    ].astype(BF16)

    rows = GROUP * COMPS
    pick = onehot((iota((rows, COMPS), 0) & (COMPS - 1)) == iota((rows, COMPS), 1))
    mine = dot(pick, out_w_ref[...]).astype(BF16)
    tile = onehot(iota((CH, LANES), 0) == (iota((CH, LANES), 1) & 31))
    same = (iota((rows, LANES), 0) >> 2) == (iota((rows, LANES), 1) >> 5)
    ow_ref[...] = jnp.where(same, dot(mine, tile), 0.0).astype(BF16)


def round_up(value, unit):
    return -(-value // unit) * unit


def shifted(value, dilation):
    span = value.shape[0]
    return jnp.concatenate(
        [
            pltpu.roll(value, dilation, axis=0).astype(BF16),
            value.astype(BF16),
            pltpu.roll(value, span - dilation, axis=0).astype(BF16),
        ],
        axis=1,
    )


class Shots:
    def __init__(
        self, dils, windows, step, couple, place_ref, recs, pick_ref, keep_ref, w0_ref, w1_ref, w2_ref,
        bias_ref, shift_ref, part_ref, x2_ref, rec_out_ref,
    ):
        self.dils, self.step, self.couple = dils, step, couple
        self.finished = lambda q: None
        self.keep_ref, self.w0_ref, self.w1_ref, self.w2_ref = keep_ref, w0_ref, w1_ref, w2_ref
        self.bias_ref, self.shift_ref, self.x2_ref = bias_ref, shift_ref, x2_ref
        shots, rows, nodes = pick_ref.shape
        planes = shots // CORES
        self.slots = slots = x2_ref.shape[0]
        self.window = window = part_ref.shape[-1]
        self.rows, self.split = part_ref.shape[2], round_up(6 * slots, 16)
        self.span = window + 2 * HALO
        at = place_ref[1]
        self.right_ok = (at < windows - 1).astype(F32)
        self.left_ok = (at > 0).astype(F32)
        self.low_half = iota((self.span, HALF), 1) < CH * CORES

        lane = iota((nodes, 2 * window), 1)
        all_ok = jnp.where(
            lane < window, 1.0, jnp.where(lane < window + window // 2, self.right_ok, self.left_ok)
        ).astype(BF16)

        def put(part, swapped, value):
            for half in range(2):
                lanes = value[:, half * window : (half + 1) * window]
                part_ref[half, part, 0 : self.split] = lanes[0 : self.split]
                part_ref[half, swapped, self.split : rows] = lanes[self.split : rows]

        for x, rec_ref in enumerate(recs):
            n = 2 * couple + x % 2 + (planes if x >= 2 else 0)
            within = shot_of(place_ref, n, shots) & (QUAD - 1)
            edge = rec_ref[COMPS].astype(F32)
            for k in range(COMPS):
                turned = edge if k == 0 else pltpu.roll(edge, window - HALO * k, axis=1)
                both = jnp.concatenate([rec_ref[k], turned.astype(BF16)], axis=1)
                put(within * COMPS + k, (within ^ 2) * COMPS + k, dot(pick_ref[n], both))
            alive = dot(pick_ref[n], all_ok)
            for copy in range(2):
                first = QUAD * COMPS + QUAD * copy
                put(first + within, first + (within ^ 2), alive)

        self.half_rows = part_ref.shape[1] * self.rows
        self.part2 = part_ref.reshape(2 * self.half_rows, window)
        for q in range(slots):
            first = self.split + slots + q
            for half in range(2):
                pair = self.part2[pl.ds(first + (1 - half) * 8 * self.rows, 8, stride=self.rows), :]
                rec_out_ref[q, half * 8 : (half + 1) * 8] = pair

    def inside(self, value):
        w = self.window
        return jnp.concatenate(
            [value[0:w], value[w : w + HALO] * self.right_ok, value[w + HALO :] * self.left_ok], axis=0
        )

    def item_rows(self, q, b):
        start = (3 * (b // 2) * self.slots if b != 1 else self.split) + q
        halves = []
        for half in range(2):
            base = half * self.half_rows + start
            flags = base + QUAD * COMPS * self.rows
            pieces = [
                self.part2[pl.ds(base + a * self.slots, QUAD * COMPS, stride=self.rows), :] for a in range(3)
            ]
            for a in range(3):
                alive = self.part2[pl.ds(flags + a * self.slots, 2 * QUAD, stride=self.rows), :]
                pieces += [alive, alive]
            pieces.append(jnp.zeros((KROWS - 6 * QUAD * COMPS, self.window), F32))
            halves.append(jnp.concatenate(pieces, axis=0).astype(BF16))
        return jnp.concatenate(halves, axis=1)

    def items(self, group):
        return [(group * self.step + i, b) for i in range(self.step) for b in range(3)]

    def first_inputs(self, group):
        items = self.items(group)
        lhs = []
        for n in range(0, len(items), 2):
            some = jnp.concatenate([self.item_rows(q, b) for q, b in items[n : n + 2]], axis=0)
            moved = dot_t(self.shift_ref[...], some).astype(BF16)
            lhs += [moved[:, m : m + KROWS] for m in range(0, moved.shape[1], KROWS)]
        lifted = dot(jnp.concatenate(lhs, axis=0), self.w0_ref[...]).astype(BF16)
        return lifted[:, 0:LANES], lifted[:, LANES:]

    def taps_added(self, even, odd, dilation):
        mid = jnp.where(self.low_half, odd[:, 0:HALF], even[:, 0:HALF])
        late = jnp.where(self.low_half, odd[:, HALF:], even[:, HALF:])
        early = pltpu.roll(jnp.where(self.low_half, even[:, 0:HALF], odd[:, 0:HALF]), HALF // 2, axis=1)
        return (
            pltpu.roll(early, dilation, axis=0) + mid + pltpu.roll(late, self.span - dilation, axis=0)
        )

    def first_layer(self, group, even, odd):
        y_even, y_odd = dot(even, self.w1_ref[0]), dot(odd, self.w1_ref[1])
        x1 = []
        for n, (q, b) in enumerate(self.items(group)):
            at = slice(n * self.span, (n + 1) * self.span)
            old = jnp.where(self.low_half, odd[at, 0:HALF].astype(F32), even[at, 0:HALF].astype(F32))
            total = self.taps_added(y_even[at], y_odd[at], self.dils[0])
            new = jnp.maximum(total + self.bias_ref[0:1, 0:HALF], 0.0)
            x1.append(self.inside((old + new) * self.keep_ref[self.couple, b, q : q + 1, :]))
        even, odd, own = [], [], []
        for i in range(self.step):
            t0, t1, t2 = x1[3 * i : 3 * i + 3]
            t2 = t2.astype(BF16)
            even.append(jnp.concatenate([jnp.where(self.low_half, t0, t1).astype(BF16), t2], axis=1))
            odd.append(jnp.concatenate([jnp.where(self.low_half, t1, t0).astype(BF16), t2], axis=1))
            own.append(t1.astype(BF16))
        return jnp.concatenate(even, axis=0), jnp.concatenate(odd, axis=0), own

    def second_layer(self, group, even, odd, own):
        even, odd = dot(even, self.w2_ref[0]), dot(odd, self.w2_ref[1])
        for i in range(self.step):
            q = group * self.step + i
            at = slice(i * self.span, (i + 1) * self.span)
            total = self.taps_added(even[at], odd[at], self.dils[1])
            new = jnp.maximum(total + self.bias_ref[1:2, 0:HALF], 0.0)
            x2 = (own[i].astype(F32) + new) * self.keep_ref[self.couple, 1, q : q + 1, :]
            self.x2_ref[q] = shifted(self.inside(x2), self.dils[2])
            self.finished(q)


def staged(work):
    inputs, middle = {}, {}
    for t in range(len(work) + 2):
        if t < len(work):
            stage, group = work[t]
            inputs[t] = stage.first_inputs(group)
        if 0 <= t - 1 < len(work):
            stage, group = work[t - 1]
            middle[t - 1] = stage.first_layer(group, *inputs.pop(t - 1))
        if 0 <= t - 2:
            stage, group = work[t - 2]
            stage.second_layer(group, *middle.pop(t - 2))
        yield t


def near_kernel(dils, windows, step, place_ref, *refs):
    pick_ref, keep_ref, w0_ref, w1_ref, w2_ref, bias_ref, shift_ref = refs[:7]
    x2_out_ref, rec_out_ref, part_ref, x2_ref, sems = refs[7 + QUAD :]
    stage = Shots(
        dils, windows, step, 0, place_ref, refs[7 : 7 + QUAD], pick_ref, keep_ref, w0_ref, w1_ref, w2_ref,
        bias_ref, shift_ref, part_ref, x2_ref, rec_out_ref,
    )
    copies = [pltpu.make_async_copy(x2_ref.at[q], x2_out_ref.at[q], sems.at[q]) for q in range(x2_ref.shape[0])]
    stage.finished = lambda q: copies[q].start()
    for _ in staged([(stage, group) for group in range(x2_ref.shape[0] // step)]):
        pass
    for copy in copies:
        copy.wait()


def main_kernel(dils, windows, step, near, place_ref, *refs):
    shots = refs[0].shape[0]
    couples = shots // QUAD
    pick_ref, keep_ref, w0_ref, w1_ref, w2_ref, b3_ref, b4_ref, ow_ref, bias_ref, shift_ref = refs[:10]
    refs = refs[10:]
    rec_refs, refs = refs[: QUAD * (couples - near)], refs[QUAD * (couples - near) :]
    done_refs, refs = refs[: 2 * near], refs[2 * near :]
    out_ref, part_ref, x2_all, rec_all, x3_ref, x2_near, b3_in, b4_in, sems = refs
    late = [(done_refs[0], x2_near), (b3_ref, b3_in), (b4_ref, b4_in)]
    late_copies = started([a for a, _ in late], [b for _, b in late], sems)
    done_refs = (x2_near, *done_refs[1:])
    b3_ref, b4_ref = b3_in, b4_in
    blocks = couples // 2
    slots, window = out_ref.shape[1], out_ref.shape[3]
    span = window + 2 * HALO
    right_ok = (place_ref[1] < windows - 1).astype(F32)
    left_ok = (place_ref[1] > 0).astype(F32)

    stages = []
    x2_refs, rec_refs_out = list(done_refs[0::2]), list(done_refs[1::2])
    for c in range(near, couples):
        x2_refs.append(x2_all.at[c - near])
        rec_refs_out.append(rec_all.at[c - near])
        stages.append(
            Shots(
                dils, windows, step, c, place_ref, rec_refs[QUAD * (c - near) : QUAD * (c - near + 1)],
                pick_ref, keep_ref, w0_ref, w1_ref, w2_ref, bias_ref, shift_ref, part_ref.at[c - near],
                x2_refs[-1], rec_refs_out[-1],
            )
        )

    def receiver_layer(parts_of, weights, layer, block, group, out_rows):
        y = None
        for other in range(blocks):
            term = dot(jnp.concatenate(parts_of(other), axis=0), weights[block * blocks + other])
            y = term if y is None else y + term
        results = []
        for i, part in enumerate(parts_of(block)):
            q = group * step + i
            keep = jnp.concatenate([keep_ref[2 * block + c, 1, q : q + 1, :] for c in range(2)], axis=1)
            old = part[:, LANES : 2 * LANES].astype(F32)
            new = jnp.maximum(y[i * out_rows : (i + 1) * out_rows] + bias_ref[layer : layer + 1, :], 0.0)
            results.append((old + new) * keep)
        return results

    def third_layer(group):
        def parts_of(block):
            return [
                jnp.concatenate(
                    [
                        x2_refs[2 * block + c][group * step + i, :, e * HALF : (e + 1) * HALF]
                        for e in range(3)
                        for c in range(2)
                    ],
                    axis=1,
                )
                for i in range(step)
            ]

        for block in range(blocks):
            for i, value in enumerate(receiver_layer(parts_of, b3_ref, 2, block, group, span)):
                value = jnp.concatenate(
                    [
                        value[0:window],
                        value[window : window + HALO] * right_ok,
                        value[window + HALO :] * left_ok,
                    ],
                    axis=0,
                )
                x3_ref[block, group * step + i] = shifted(value, dils[3])[0:window]

    def last_layer(group):
        def parts_of(block):
            return [x3_ref[block, group * step + i] for i in range(step)]

        for block in range(blocks):
            for i, value in enumerate(receiver_layer(parts_of, b4_ref, 3, block, group, window)):
                q = group * step + i
                noise = dot_t(ow_ref[...], value.astype(BF16))
                record = jnp.concatenate([rec_refs_out[2 * block + c][q] for c in range(2)], axis=0)
                done = (record + noise).reshape(GROUP, COMPS, window)
                for c in range(2):
                    first = QUAD * couple_of(place_ref, 2 * block + c)
                    out_ref[pl.ds(first, QUAD), q] = done[c * QUAD : (c + 1) * QUAD]

    groups = slots // step
    work = [(stage, group) for group in range(groups) for stage in stages]
    lag = len(stages)
    for t in itertools.chain(staged(work), range(len(work) + 2, len(work) + 2 + 2 * lag)):
        done, rest = divmod(t - 2, lag)
        if rest == 0 and done == 1:
            for copy in late_copies:
                copy.wait()
        if rest == 0 and 0 <= done - 1 < groups:
            third_layer(done - 1)
        if rest == 0 and 0 <= done - 2 < groups:
            last_layer(done - 2)


def divisor(value, limit):
    return max(d for d in range(1, limit + 1) if value % d == 0)


def body(
    records,
    lift_weight,
    lift_bias,
    conv_weight,
    conv_bias,
    out_weight,
    live_count,
    trace_node,
    node_owner,
):
    _, comps, nodes, window = records.shape
    holders = lax.axis_size("gather")
    windows = lax.axis_size("tm")
    shots = holders * records.shape[0]
    couples = shots // QUAD
    blocks = couples // 2
    slots = (nodes + holders - 1) // holders
    dils = (1, 4, 2, 8)
    rows = round_up(6 * slots, 16) + round_up(3 * slots, 16)
    span = window + 2 * HALO

    planes = holders // CORES
    vmem = pl.BlockSpec(memory_space=pltpu.VMEM)
    smem = pl.BlockSpec(memory_space=pltpu.SMEM)
    anywhere = pl.BlockSpec(memory_space=pl.ANY)
    like = jax.ShapeDtypeStruct

    def after(value, other):
        return lax.optimization_barrier((value, other))[0]

    def kernel(function, operands, specs, outs, scratch, limit, flops, name, out_specs=None):
        return pl.pallas_call(
            function,
            out_shape=outs,
            in_specs=[smem] + specs,
            out_specs=out_specs or jax.tree.map(lambda _: vmem, outs),
            scratch_shapes=scratch,
            compiler_params=pltpu.CompilerParams(vmem_limit_bytes=limit << 20),
            cost_estimate=pl.CostEstimate(flops=flops, bytes_accessed=1 << 10, transcendentals=0),
            name=name,
        )(place, *operands)

    place = jnp.stack([lax.axis_index("gather"), lax.axis_index("tm")]).astype(jnp.int32)
    taps = jnp.transpose(conv_weight, (0, 3, 4, 1, 2)).reshape(-1, CH)

    own = records[0]
    even = lax.axis_index("tm") % 2 == 0
    pack = lambda part: jnp.transpose(part, (1, 0, 2)).reshape(nodes, comps * HALO)
    first, last = pack(own[:, :, :HALO]), pack(own[:, :, window - HALO :])
    got = []
    for begin in range(2):
        pairs = [(w, w + 1) for w in range(begin, windows - 1, 2)]
        pairs += [(b, a) for a, b in pairs]
        got.append(lax.ppermute(jnp.where(even == (begin == 0), last, first), "tm", pairs))
    small = [live_count, trace_node, taps, jnp.transpose(lift_weight), lift_bias[None, :], conv_bias]
    raw = small + [node_owner[None, :], own, out_weight]
    raw = [pltpu.with_memory_space_constraint(a, pltpu.HBM) for a in raw]
    half = (taps.shape[0] // 2, CH)
    scratch = [pltpu.SMEM(a.shape, a.dtype) for a in raw[:2]] + [pltpu.VMEM(half, BF16)]
    scratch += [pltpu.VMEM(a.shape, a.dtype) for a in raw[3:7]]
    w0, w1, w2, wide_bias, shift, pick, keep, own, late_taps, out_taps = kernel(
        functools.partial(prep_kernel, dils, slots),
        raw,
        [pl.BlockSpec(memory_space=pltpu.HBM)] * len(raw),
        (
            like((KROWS, 2 * LANES), BF16),
            like((2, LANES, LANES), BF16),
            like((2, LANES, LANES), BF16),
            like((conv_bias.shape[0], LANES), F32),
            like((span, 2 * window), BF16),
            like((shots, rows, nodes), BF16),
            like((couples, 3, 16, HALF), F32),
            like(own.shape, BF16),
            like(half, BF16),
            like(out_weight.shape, BF16),
        ),
        scratch + [pltpu.SemaphoreType.DMA((7,)), pltpu.SemaphoreType.DMA((3,))],
        16,
        10**5,
        "weights",
    )
    right, left = jnp.where(even, got[0], got[1]), jnp.where(even, got[1], got[0])
    sent = jnp.concatenate([own, jnp.concatenate([right, left], axis=1)[None]], axis=0)


    def exchanged(block, distance):
        return lax.ppermute(block, "gather", [(g, g ^ distance) for g in range(holders)])

    near_blocks = [sent, exchanged(sent, CORES)]
    far = [exchanged(sent, CORES * r) for r in range(2, planes)]
    near_blocks += [exchanged(block, 1) for block in near_blocks]

    b3, b4, ow = kernel(
        functools.partial(band_kernel, dils, blocks),
        [late_taps, out_taps],
        [vmem] * 2,
        (
            like((blocks * blocks, 3 * LANES, LANES), BF16),
            like((blocks * blocks, 3 * LANES, LANES), BF16),
            like((GROUP * COMPS, LANES), BF16),
        ),
        [],
        16,
        10**10,
        "bands",
    )

    step = divisor(slots, 5)
    row_stride = round_up(rows, 16) + 8
    x2 = like((slots, span, 3 * HALF), BF16)
    held = like((slots, QUAD * COMPS, window), F32)
    parts = (2, PARTS, row_stride, window)
    operands = [after(pick, ow), keep, w0, w1, w2, wide_bias, shift, *near_blocks]
    near = kernel(
        functools.partial(near_kernel, dils, windows, step),
        operands,
        [vmem] * len(operands),
        (x2, held),
        [pltpu.VMEM(parts, F32), pltpu.VMEM(x2.shape, BF16), pltpu.SemaphoreType.DMA((slots,))],
        24,
        10**5,
        "near",
        (anywhere, vmem),
    )

    operands = [pick, keep, w0, w1, w2, b3, b4, ow, wide_bias, shift]
    for r in range(0, len(far), 2):
        operands += far[r : r + 2] + [exchanged(after(block, near[1]), 1) for block in far[r : r + 2]]
    operands += near
    specs = [anywhere if any(a is b for b in (b3, b4, near[0])) else vmem for a in operands]
    out = kernel(
        functools.partial(main_kernel, dils, windows, step, 1),
        operands,
        specs,
        like((shots, slots, comps, window), F32),
        [
            pltpu.VMEM((couples - 1, *parts), F32),
            pltpu.VMEM((couples - 1, *x2.shape), BF16),
            pltpu.VMEM((couples - 1, *held.shape), F32),
            pltpu.VMEM((blocks, slots, window, 3 * LANES), BF16),
            pltpu.VMEM(x2.shape, BF16),
            pltpu.VMEM(b3.shape, BF16),
            pltpu.VMEM(b4.shape, BF16),
            pltpu.SemaphoreType.DMA((3,)),
        ],
        36,
        4 * 10**9,
        "layers",
    )
    return jnp.transpose(out, (0, 2, 1, 3))


def solution(mesh):
    return jax.shard_map(
        body,
        mesh=mesh,
        in_specs=(P("gather", None, None, "tm"), P(), P(), P(), P(), P(), P(), P(), P()),
        out_specs=P(None, None, "gather", "tm"),
        check_vma=False,
    )
```

```python
import functools

import jax
import jax.numpy as jnp
from jax import lax
from jax.experimental import pallas as pl
from jax.experimental.pallas import tpu as pltpu
from jax.sharding import PartitionSpec as P

F32 = jnp.float32
BF16 = jnp.bfloat16
CH = 32
CORES = 2
COMPS = 4
GROUP = 8
LANES = GROUP * CH
HALO = 16
QUAD = 4
HALF = QUAD * CH
KROWS = 128
PARTS = QUAD * COMPS + 2 * QUAD


def iota(shape, dim):
    return lax.broadcasted_iota(jnp.int32, shape, dim)


def dot(a, b):
    return jnp.dot(a, b, preferred_element_type=F32)


def dot_t(a, b):
    return lax.dot_general(a, b, (((1,), (1,)), ((), ())), preferred_element_type=F32)


def onehot(cond):
    return cond.astype(F32).astype(BF16)


def band_links(dilation, offset):
    return [
        a
        for a in range(3)
        if any(s + GROUP * offset == t + (a - 1) * dilation for s in range(GROUP) for t in range(GROUP))
    ]


def split3(value):
    terms = []
    for _ in range(3):
        term = value.astype(BF16)
        terms.append(term)
        value = value - term.astype(F32)
    return terms


def shot_of(place_ref, n, shots):
    planes = shots // CORES
    plane = place_ref[0] // CORES
    core = place_ref[0] - CORES * plane
    return CORES * (plane ^ (n % planes)) + (core if n < planes else 1 - core)


def couple_of(place_ref, relative):
    return (place_ref[0] // (2 * CORES)) ^ relative


def table_kernel(dils, slots, place_ref, live_ref, trace_ref, owner_ref, pick_ref, keep_ref):
    shots, rows, nodes = pick_ref.shape
    split = round_up(6 * slots, 16)
    me = place_ref[0]

    mine = (owner_ref[...] == me).astype(F32)
    before = onehot(iota((nodes, nodes), 0) < iota((nodes, nodes), 1))
    rank = dot(jnp.broadcast_to(mine, (8, nodes)).astype(BF16), before)[0:1, :]
    node_ids = iota((1, nodes), 1).astype(F32)

    def nodes_of(slot_index):
        held = jnp.where((rank == slot_index.astype(F32)) & (mine > 0.5), 1.0, 0.0)
        node = jnp.sum(held * node_ids, axis=1, keepdims=True)
        there = jnp.sum(held, axis=1, keepdims=True)
        return jnp.where(there > 0.5, node, -1.0e6).astype(jnp.int32)

    row_id = iota((rows, nodes), 0)
    late = row_id >= split
    row_id = jnp.where(late, row_id - split, row_id)
    tap = jnp.zeros((rows, nodes), jnp.int32)
    for m in range(1, 7):
        tap = tap + (row_id >= m * slots).astype(jnp.int32)
    second = (tap >= 3).astype(jnp.int32)
    shift = dils[0] * (tap - 3 * second - 1) + jnp.where(late, 0, dils[1] * (2 * second - 1))
    target = nodes_of(row_id - slots * tap)
    target = jnp.where(tap >= jnp.where(late, 3, 6), -1000000, target + shift)

    node_lane = iota((rows, nodes), 1)
    for n in range(shots):
        s = shot_of(place_ref, n, shots)
        pick_ref[n] = onehot((node_lane == target - trace_ref[s, 0]) & (node_lane < live_ref[s]))

    slot_rows = keep_ref.shape[2]
    own_node = nodes_of(iota((slot_rows, nodes), 0))
    shot_lane = iota((slot_rows, HALF), 1) >> 5
    for c in range(shots // QUAD):
        base = QUAD * couple_of(place_ref, c)
        for b in range(3):
            first = jnp.zeros((slot_rows, HALF), jnp.int32)
            count = jnp.zeros((slot_rows, HALF), jnp.int32)
            for w in range(QUAD):
                at = shot_lane == (w if b == 1 else w ^ 2)
                first = jnp.where(at, trace_ref[base + w, 0], first)
                count = jnp.where(at, live_ref[base + w], count)
            trace = own_node + dils[1] * (b - 1) - first
            keep_ref[c, b] = ((trace >= 0) & (trace < count)).astype(F32)


def started(sources, places, sems):
    copies = [pltpu.make_async_copy(a, b, sems.at[n]) for n, (a, b) in enumerate(zip(sources, places))]
    for copy in copies:
        copy.start()
    return copies


def prep_kernel(dils, slots, place_ref, *refs):
    w0_ref, w1_ref, w2_ref, wide_bias_ref, shift_ref, pick_ref, keep_ref = refs[9:16]
    half = refs[2].shape[0] // 2
    passed = started((refs[7], refs[2].at[half : 2 * half], refs[8]), refs[16:19], refs[27])
    live_ref, trace_ref, cw_ref, lift_ref, lift_bias_ref, bias_ref, owner_ref = refs[19:26]
    sources = (*refs[:2], refs[2].at[0:half], *refs[3:7])
    for copy in started(sources, refs[19:26], refs[26]):
        copy.wait()
    table_kernel(dils, slots, place_ref, live_ref, trace_ref, owner_ref, pick_ref, keep_ref)

    rows8 = [lift_ref[...].astype(F32)] + [term.astype(F32) for term in split3(lift_bias_ref[...])]
    table = jnp.concatenate(rows8 + [jnp.zeros((1, CH), F32)], axis=0).astype(BF16)
    data_rows = 3 * QUAD * COMPS
    r8 = iota((KROWS, 8), 0)
    part = jnp.where(r8 < data_rows, r8 & (COMPS - 1), COMPS + ((r8 >> 2) & 3))
    values = dot(onehot((part == iota((KROWS, 8), 1)) & (r8 < 2 * data_rows)), table).astype(BF16)
    wide = iota((CH, 2 * LANES), 1)
    spread = onehot(iota((CH, 2 * LANES), 0) == (wide & 31))
    rr = iota((KROWS, 2 * LANES), 0)
    cc = iota((KROWS, 2 * LANES), 1)
    row_node = jnp.where(rr < data_rows, rr >> 4, (rr - data_rows) >> 4)
    row_shot = jnp.where(rr < data_rows, rr >> 2, rr) & (QUAD - 1)
    place = (cc >> 6) & 3
    node = jnp.where((cc >= LANES) & (place < 2), 1 - place, place)
    same = (row_node == node) & (row_shot == 2 * (cc >> 8) + ((cc >> 5) & 1)) & (rr < 2 * data_rows)
    w0_ref[...] = jnp.where(same & (place < 3), dot(values, spread), 0.0).astype(BF16)

    widen = onehot((iota((LANES, CH), 0) & 31) == iota((LANES, CH), 1))
    kr = iota((LANES, LANES), 0)
    kc = iota((LANES, LANES), 1)
    same_shot = ((kr >> 5) & 1) == ((kc >> 5) & 1)
    sr = iota((3 * CH, LANES), 0)
    sc = iota((3 * CH, LANES), 1)
    for layer, ref, odd_taps in ((0, w1_ref, (1, 0, 2, 3)), (1, w2_ref, (1, 0, 3, 2))):
        base = 3 * layer
        tall = [
            dot_t(widen, cw_ref[(base + a) * 3 * CH : (base + a + 1) * 3 * CH, :]).astype(BF16)
            for a in range(3)
        ]
        for odd, (k_taps, n_taps) in enumerate((((0, 1, 2, 3), (0, 1, 3, 2)), (odd_taps, (1, 0, 2, 3)))):
            place = sum(jnp.where((sc >> 6) == y, n_taps[y], 0) for y in range(4))
            spread2 = onehot(((sr >> 5) == place) & ((sr & 31) == (sc & 31)))
            total = jnp.zeros((LANES, LANES), F32)
            for x in range(4):
                if k_taps[x] < 3:
                    total = jnp.where(((kr >> 6) == x) & same_shot, dot(tall[k_taps[x]], spread2), total)
            ref[odd] = total.astype(BF16)

    span = shift_ref.shape[0]
    window = span - 2 * HALO
    source = iota(shift_ref.shape, 0)
    source = jnp.where(source < window + HALO, source, source + window // 2 - HALO)
    shift_ref[...] = onehot(iota(shift_ref.shape, 1) == source)

    tile = onehot(iota((CH, LANES), 0) == (iota((CH, LANES), 1) & 31))
    wide_bias_ref[...] = sum(dot(term, tile) for term in split3(bias_ref[...]))
    for copy in passed:
        copy.wait()


def band_kernel(dils, blocks, place_ref, *refs):
    cw_ref, out_w_ref, b3_ref, b4_ref, ow_ref = refs
    widen = onehot((iota((LANES, CH), 0) & 31) == iota((LANES, CH), 1))

    er = iota((3 * CH, 3 * LANES), 0)
    ec = iota((3 * CH, 3 * LANES), 1)
    spread3 = onehot(((er >> 5) == (ec >> 8)) & ((er & 31) == (ec & 31)))
    row_lane = iota((LANES, 3 * LANES), 0)
    col_lane = iota((LANES, 3 * LANES), 1) & (LANES - 1)

    def shots_in(lane, block):
        couple = jnp.where(lane < HALF, couple_of(place_ref, 2 * block), couple_of(place_ref, 2 * block + 1))
        return QUAD * couple + ((lane >> 5) & (QUAD - 1))

    def expanded(layer, a):
        base = ((layer - 2) * 3 + a) * 3 * CH
        return dot(dot_t(widen, cw_ref[base : base + 3 * CH, :]).astype(BF16), spread3)

    for layer, ref in ((2, b3_ref), (3, b4_ref)):
        linked_taps = band_links(dils[layer], 0) if blocks == 1 else range(3)
        for out_block in range(blocks):
            for in_block in range(blocks):
                total = jnp.zeros((LANES, 3 * LANES), F32)
                for a in linked_taps:
                    reach = shots_in(col_lane, out_block) + (a - 1) * dils[layer]
                    total = total + jnp.where(shots_in(row_lane, in_block) == reach, expanded(layer, a), 0.0)
                for e in range(3):
                    ref[out_block * blocks + in_block, e * LANES : (e + 1) * LANES, :] = total[
                        :, e * LANES : (e + 1) * LANES
                    ].astype(BF16)

    rows = GROUP * COMPS
    pick = onehot((iota((rows, COMPS), 0) & (COMPS - 1)) == iota((rows, COMPS), 1))
    mine = dot(pick, out_w_ref[...]).astype(BF16)
    tile = onehot(iota((CH, LANES), 0) == (iota((CH, LANES), 1) & 31))
    same = (iota((rows, LANES), 0) >> 2) == (iota((rows, LANES), 1) >> 5)
    ow_ref[...] = jnp.where(same, dot(mine, tile), 0.0).astype(BF16)


def round_up(value, unit):
    return -(-value // unit) * unit


def shifted(value, dilation):
    span = value.shape[0]
    return jnp.concatenate(
        [
            pltpu.roll(value, dilation, axis=0).astype(BF16),
            value.astype(BF16),
            pltpu.roll(value, span - dilation, axis=0).astype(BF16),
        ],
        axis=1,
    )


class Shots:
    def __init__(
        self, dils, windows, step, couple, place_ref, recs, pick_ref, keep_ref, w0_ref, w1_ref, w2_ref,
        bias_ref, shift_ref, part_ref, x2_ref, rec_out_ref,
    ):
        self.dils, self.step, self.couple = dils, step, couple
        self.keep_ref, self.w0_ref, self.w1_ref, self.w2_ref = keep_ref, w0_ref, w1_ref, w2_ref
        self.bias_ref, self.shift_ref, self.x2_ref = bias_ref, shift_ref, x2_ref
        shots, rows, nodes = pick_ref.shape
        planes = shots // CORES
        self.slots = slots = x2_ref.shape[0]
        self.window = window = part_ref.shape[-1]
        self.rows, self.split = part_ref.shape[2], round_up(6 * slots, 16)
        self.span = window + 2 * HALO
        at = place_ref[1]
        self.right_ok = (at < windows - 1).astype(F32)
        self.left_ok = (at > 0).astype(F32)
        self.low_half = iota((self.span, HALF), 1) < CH * CORES

        lane = iota((nodes, 2 * window), 1)
        all_ok = jnp.where(
            lane < window, 1.0, jnp.where(lane < window + window // 2, self.right_ok, self.left_ok)
        ).astype(BF16)

        def put(part, swapped, value):
            for half in range(2):
                lanes = value[:, half * window : (half + 1) * window]
                part_ref[half, part, 0 : self.split] = lanes[0 : self.split]
                part_ref[half, swapped, self.split : rows] = lanes[self.split : rows]

        for x, rec_ref in enumerate(recs):
            n = 2 * couple + x % 2 + (planes if x >= 2 else 0)
            within = shot_of(place_ref, n, shots) & (QUAD - 1)
            edge = rec_ref[COMPS].astype(F32)
            for k in range(COMPS):
                turned = edge if k == 0 else pltpu.roll(edge, window - HALO * k, axis=1)
                both = jnp.concatenate([rec_ref[k], turned.astype(BF16)], axis=1)
                put(within * COMPS + k, (within ^ 2) * COMPS + k, dot(pick_ref[n], both))
            alive = dot(pick_ref[n], all_ok)
            for copy in range(2):
                first = QUAD * COMPS + QUAD * copy
                put(first + within, first + (within ^ 2), alive)

        self.half_rows = part_ref.shape[1] * self.rows
        self.part2 = part_ref.reshape(2 * self.half_rows, window)
        for q in range(slots):
            first = self.split + slots + q
            for half in range(2):
                pair = self.part2[pl.ds(first + (1 - half) * 8 * self.rows, 8, stride=self.rows), :]
                rec_out_ref[q, half * 8 : (half + 1) * 8] = pair

    def inside(self, value):
        w = self.window
        return jnp.concatenate(
            [value[0:w], value[w : w + HALO] * self.right_ok, value[w + HALO :] * self.left_ok], axis=0
        )

    def item_rows(self, q, b):
        start = (3 * (b // 2) * self.slots if b != 1 else self.split) + q
        halves = []
        for half in range(2):
            base = half * self.half_rows + start
            flags = base + QUAD * COMPS * self.rows
            pieces = [
                self.part2[pl.ds(base + a * self.slots, QUAD * COMPS, stride=self.rows), :] for a in range(3)
            ]
            for a in range(3):
                alive = self.part2[pl.ds(flags + a * self.slots, 2 * QUAD, stride=self.rows), :]
                pieces += [alive, alive]
            pieces.append(jnp.zeros((KROWS - 6 * QUAD * COMPS, self.window), F32))
            halves.append(jnp.concatenate(pieces, axis=0).astype(BF16))
        return jnp.concatenate(halves, axis=1)

    def items(self, group):
        return [(group * self.step + i, b) for i in range(self.step) for b in range(3)]

    def first_inputs(self, group):
        items = self.items(group)
        lhs = []
        for n in range(0, len(items), 2):
            some = jnp.concatenate([self.item_rows(q, b) for q, b in items[n : n + 2]], axis=0)
            moved = dot_t(self.shift_ref[...], some).astype(BF16)
            lhs += [moved[:, m : m + KROWS] for m in range(0, moved.shape[1], KROWS)]
        lifted = dot(jnp.concatenate(lhs, axis=0), self.w0_ref[...]).astype(BF16)
        return lifted[:, 0:LANES], lifted[:, LANES:]

    def taps_added(self, even, odd, dilation):
        mid = jnp.where(self.low_half, odd[:, 0:HALF], even[:, 0:HALF])
        late = jnp.where(self.low_half, odd[:, HALF:], even[:, HALF:])
        early = pltpu.roll(jnp.where(self.low_half, even[:, 0:HALF], odd[:, 0:HALF]), HALF // 2, axis=1)
        return (
            pltpu.roll(early, dilation, axis=0) + mid + pltpu.roll(late, self.span - dilation, axis=0)
        )

    def first_layer(self, group, even, odd):
        y_even, y_odd = dot(even, self.w1_ref[0]), dot(odd, self.w1_ref[1])
        x1 = []
        for n, (q, b) in enumerate(self.items(group)):
            at = slice(n * self.span, (n + 1) * self.span)
            old = jnp.where(self.low_half, odd[at, 0:HALF].astype(F32), even[at, 0:HALF].astype(F32))
            total = self.taps_added(y_even[at], y_odd[at], self.dils[0])
            new = jnp.maximum(total + self.bias_ref[0:1, 0:HALF], 0.0)
            x1.append(self.inside((old + new) * self.keep_ref[self.couple, b, pl.ds(q, 1), :]))
        even, odd, own = [], [], []
        for i in range(self.step):
            t0, t1, t2 = x1[3 * i : 3 * i + 3]
            t2 = t2.astype(BF16)
            even.append(jnp.concatenate([jnp.where(self.low_half, t0, t1).astype(BF16), t2], axis=1))
            odd.append(jnp.concatenate([jnp.where(self.low_half, t1, t0).astype(BF16), t2], axis=1))
            own.append(t1.astype(BF16))
        return jnp.concatenate(even, axis=0), jnp.concatenate(odd, axis=0), own

    def layers(self, group):
        self.second_layer(group, *self.first_layer(group, *self.first_inputs(group)))

    def second_layer(self, group, even, odd, own):
        even, odd = dot(even, self.w2_ref[0]), dot(odd, self.w2_ref[1])
        for i in range(self.step):
            q = group * self.step + i
            at = slice(i * self.span, (i + 1) * self.span)
            total = self.taps_added(even[at], odd[at], self.dils[1])
            new = jnp.maximum(total + self.bias_ref[1:2, 0:HALF], 0.0)
            x2 = (own[i].astype(F32) + new) * self.keep_ref[self.couple, 1, pl.ds(q, 1), :]
            self.x2_ref[q] = shifted(self.inside(x2), self.dils[2])


def in_groups(count, step, function):
    lax.fori_loop(0, count // step, lambda group, _: (function(group), 0)[1], 0)


def near_kernel(dils, windows, step, place_ref, *refs):
    pick_ref, keep_ref, w0_ref, w1_ref, w2_ref, bias_ref, shift_ref = refs[:7]
    x2_ref, rec_out_ref, part_ref = refs[7 + QUAD :]
    stage = Shots(
        dils, windows, step, 0, place_ref, refs[7 : 7 + QUAD], pick_ref, keep_ref, w0_ref, w1_ref, w2_ref,
        bias_ref, shift_ref, part_ref, x2_ref, rec_out_ref,
    )
    in_groups(x2_ref.shape[0], step, stage.layers)


def main_kernel(dils, windows, step, near, place_ref, *refs):
    shots = refs[0].shape[0]
    couples = shots // QUAD
    pick_ref, keep_ref, w0_ref, w1_ref, w2_ref, b3_ref, b4_ref, ow_ref, bias_ref, shift_ref = refs[:10]
    refs = refs[10:]
    rec_refs, refs = refs[: QUAD * (couples - near)], refs[QUAD * (couples - near) :]
    done_refs, refs = refs[: 2 * near], refs[2 * near :]
    out_ref, part_ref, x2_all, rec_all, x3_ref = refs
    blocks = couples // 2
    slots, window = out_ref.shape[1], out_ref.shape[3]
    span = window + 2 * HALO
    right_ok = (place_ref[1] < windows - 1).astype(F32)
    left_ok = (place_ref[1] > 0).astype(F32)

    stages = []
    x2_refs, rec_refs_out = list(done_refs[0::2]), list(done_refs[1::2])
    for c in range(near, couples):
        x2_refs.append(x2_all.at[c - near])
        rec_refs_out.append(rec_all.at[c - near])
        stages.append(
            Shots(
                dils, windows, step, c, place_ref, rec_refs[QUAD * (c - near) : QUAD * (c - near + 1)],
                pick_ref, keep_ref, w0_ref, w1_ref, w2_ref, bias_ref, shift_ref, part_ref.at[c - near],
                x2_refs[-1], rec_refs_out[-1],
            )
        )

    def receiver_layer(parts_of, weights, layer, block, group, out_rows):
        y = None
        for other in range(blocks):
            term = dot(jnp.concatenate(parts_of(other), axis=0), weights[block * blocks + other])
            y = term if y is None else y + term
        results = []
        for i, part in enumerate(parts_of(block)):
            q = group * step + i
            keep = jnp.concatenate([keep_ref[2 * block + c, 1, pl.ds(q, 1), :] for c in range(2)], axis=1)
            old = part[:, LANES : 2 * LANES].astype(F32)
            new = jnp.maximum(y[i * out_rows : (i + 1) * out_rows] + bias_ref[layer : layer + 1, :], 0.0)
            results.append((old + new) * keep)
        return results

    def third_layer(group):
        def parts_of(block):
            return [
                jnp.concatenate(
                    [
                        x2_refs[2 * block + c][group * step + i, :, e * HALF : (e + 1) * HALF]
                        for e in range(3)
                        for c in range(2)
                    ],
                    axis=1,
                )
                for i in range(step)
            ]

        for block in range(blocks):
            for i, value in enumerate(receiver_layer(parts_of, b3_ref, 2, block, group, span)):
                value = jnp.concatenate(
                    [
                        value[0:window],
                        value[window : window + HALO] * right_ok,
                        value[window + HALO :] * left_ok,
                    ],
                    axis=0,
                )
                x3_ref[block, group * step + i] = shifted(value, dils[3])[0:window]

    def last_layer(group):
        def parts_of(block):
            return [x3_ref[block, group * step + i] for i in range(step)]

        for block in range(blocks):
            for i, value in enumerate(receiver_layer(parts_of, b4_ref, 3, block, group, window)):
                q = group * step + i
                noise = dot_t(ow_ref[...], value.astype(BF16))
                record = jnp.concatenate([rec_refs_out[2 * block + c][q] for c in range(2)], axis=0)
                done = (record + noise).reshape(GROUP, COMPS, window)
                for c in range(2):
                    first = QUAD * couple_of(place_ref, 2 * block + c)
                    out_ref[pl.ds(first, QUAD), q] = done[c * QUAD : (c + 1) * QUAD]

    for stage in stages:
        in_groups(slots, step, stage.layers)
    step = divisor(slots, 5)
    in_groups(slots, step, third_layer)
    in_groups(slots, step, last_layer)


def divisor(value, limit):
    return max(d for d in range(1, limit + 1) if value % d == 0)


def body(
    records,
    lift_weight,
    lift_bias,
    conv_weight,
    conv_bias,
    out_weight,
    live_count,
    trace_node,
    node_owner,
):
    _, comps, nodes, window = records.shape
    holders = lax.axis_size("gather")
    windows = lax.axis_size("tm")
    shots = holders * records.shape[0]
    couples = shots // QUAD
    blocks = couples // 2
    slots = (nodes + holders - 1) // holders
    dils = (1, 4, 2, 8)
    rows = round_up(6 * slots, 16) + round_up(3 * slots, 16)
    span = window + 2 * HALO

    planes = holders // CORES
    vmem = pl.BlockSpec(memory_space=pltpu.VMEM)
    smem = pl.BlockSpec(memory_space=pltpu.SMEM)
    like = jax.ShapeDtypeStruct

    def after(value, other):
        return lax.optimization_barrier((value, other))[0]

    def kernel(function, operands, specs, outs, scratch, limit, flops, name):
        return pl.pallas_call(
            function,
            out_shape=outs,
            in_specs=[smem] + specs,
            out_specs=jax.tree.map(lambda _: vmem, outs),
            scratch_shapes=scratch,
            compiler_params=pltpu.CompilerParams(vmem_limit_bytes=limit << 20),
            cost_estimate=pl.CostEstimate(flops=flops, bytes_accessed=1 << 10, transcendentals=0),
            name=name,
        )(place, *operands)

    place = jnp.stack([lax.axis_index("gather"), lax.axis_index("tm")]).astype(jnp.int32)
    taps = jnp.transpose(conv_weight, (0, 3, 4, 1, 2)).reshape(-1, CH)

    own = records[0]
    even = lax.axis_index("tm") % 2 == 0
    pack = lambda part: jnp.transpose(part, (1, 0, 2)).reshape(nodes, comps * HALO)
    first, last = pack(own[:, :, :HALO]), pack(own[:, :, window - HALO :])
    got = []
    for begin in range(2):
        pairs = [(w, w + 1) for w in range(begin, windows - 1, 2)]
        pairs += [(b, a) for a, b in pairs]
        got.append(lax.ppermute(jnp.where(even == (begin == 0), last, first), "tm", pairs))
    small = [live_count, trace_node, taps, jnp.transpose(lift_weight), lift_bias[None, :], conv_bias]
    raw = small + [node_owner[None, :], own, out_weight]
    raw = [pltpu.with_memory_space_constraint(a, pltpu.HBM) for a in raw]
    half = (taps.shape[0] // 2, CH)
    scratch = [pltpu.SMEM(a.shape, a.dtype) for a in raw[:2]] + [pltpu.VMEM(half, BF16)]
    scratch += [pltpu.VMEM(a.shape, a.dtype) for a in raw[3:7]]
    w0, w1, w2, wide_bias, shift, pick, keep, own, late_taps, out_taps = kernel(
        functools.partial(prep_kernel, dils, slots),
        raw,
        [pl.BlockSpec(memory_space=pltpu.HBM)] * len(raw),
        (
            like((KROWS, 2 * LANES), BF16),
            like((2, LANES, LANES), BF16),
            like((2, LANES, LANES), BF16),
            like((conv_bias.shape[0], LANES), F32),
            like((span, 2 * window), BF16),
            like((shots, rows, nodes), BF16),
            like((couples, 3, 16, HALF), F32),
            like(own.shape, BF16),
            like(half, BF16),
            like(out_weight.shape, BF16),
        ),
        scratch + [pltpu.SemaphoreType.DMA((7,)), pltpu.SemaphoreType.DMA((3,))],
        16,
        10**5,
        "weights",
    )
    right, left = jnp.where(even, got[0], got[1]), jnp.where(even, got[1], got[0])
    sent = jnp.concatenate([own, jnp.concatenate([right, left], axis=1)[None]], axis=0)


    def exchanged(block, distance):
        return lax.ppermute(block, "gather", [(g, g ^ distance) for g in range(holders)])

    near_blocks = [sent, exchanged(sent, CORES)]
    far = [exchanged(sent, CORES * r) for r in range(2, planes)]
    near_blocks += [exchanged(block, 1) for block in near_blocks]

    b3, b4, ow = kernel(
        functools.partial(band_kernel, dils, blocks),
        [late_taps, out_taps],
        [vmem] * 2,
        (
            like((blocks * blocks, 3 * LANES, LANES), BF16),
            like((blocks * blocks, 3 * LANES, LANES), BF16),
            like((GROUP * COMPS, LANES), BF16),
        ),
        [],
        16,
        10**10,
        "bands",
    )

    step = divisor(slots, 5)
    row_stride = round_up(rows, 16) + 8
    x2 = like((slots, span, 3 * HALF), BF16)
    held = like((slots, QUAD * COMPS, window), F32)
    parts = (2, PARTS, row_stride, window)
    operands = [after(pick, ow), keep, w0, w1, w2, wide_bias, shift, *near_blocks]
    near = kernel(
        functools.partial(near_kernel, dils, windows, divisor(slots, 2)),
        operands,
        [vmem] * len(operands),
        (x2, held),
        [pltpu.VMEM(parts, F32)],
        24,
        10**5,
        "near",
    )

    operands = [pick, keep, w0, w1, w2, b3, b4, ow, wide_bias, shift]
    for r in range(0, len(far), 2):
        operands += far[r : r + 2] + [exchanged(after(block, near[1]), 1) for block in far[r : r + 2]]
    operands += near
    out = kernel(
        functools.partial(main_kernel, dils, windows, step, 1),
        operands,
        [vmem] * len(operands),
        like((shots, slots, comps, window), F32),
        [
            pltpu.VMEM((couples - 1, *parts), F32),
            pltpu.VMEM((couples - 1, *x2.shape), BF16),
            pltpu.VMEM((couples - 1, *held.shape), F32),
            pltpu.VMEM((blocks, slots, window, 3 * LANES), BF16),
        ],
        36,
        4 * 10**9,
        "layers",
    )
    return jnp.transpose(out, (0, 2, 1, 3))


def solution(mesh):
    return jax.shard_map(
        body,
        mesh=mesh,
        in_specs=(P("gather", None, None, "tm"), P(), P(), P(), P(), P(), P(), P(), P()),
        out_specs=P(None, None, "gather", "tm"),
        check_vma=False,
    )
```

```python
import collections
import functools
import itertools

import jax
import jax.numpy as jnp
from jax import lax
from jax.experimental import pallas as pl
from jax.experimental.pallas import tpu as pltpu
from jax.sharding import PartitionSpec as P

F32 = jnp.float32
BF16 = jnp.bfloat16
CH = 32
CORES = 2
COMPS = 4
GROUP = 8
LANES = GROUP * CH
HALO = 16
QUAD = 4
HALF = QUAD * CH
KROWS = 128
PARTS = QUAD * COMPS + 2 * QUAD


def iota(shape, dim):
    return lax.broadcasted_iota(jnp.int32, shape, dim)


def dot(a, b):
    return jnp.dot(a, b, preferred_element_type=F32)


def dot_t(a, b):
    return lax.dot_general(a, b, (((1,), (1,)), ((), ())), preferred_element_type=F32)


def onehot(cond):
    return cond.astype(F32).astype(BF16)


def band_links(dilation, offset):
    return [
        a
        for a in range(3)
        if any(s + GROUP * offset == t + (a - 1) * dilation for s in range(GROUP) for t in range(GROUP))
    ]


def split3(value):
    terms = []
    for _ in range(3):
        term = value.astype(BF16)
        terms.append(term)
        value = value - term.astype(F32)
    return terms


def shot_of(place_ref, n, shots):
    planes = shots // CORES
    plane = place_ref[0] // CORES
    core = place_ref[0] - CORES * plane
    return CORES * (plane ^ (n % planes)) + (core if n < planes else 1 - core)


def couple_of(place_ref, relative):
    return (place_ref[0] // (2 * CORES)) ^ relative


def table_kernel(dils, slots, place_ref, live_ref, trace_ref, owner_ref, pick_ref, keep_ref):
    shots, rows, nodes = pick_ref.shape
    split = round_up(6 * slots, 16)
    me = place_ref[0]

    mine = (owner_ref[...] == me).astype(F32)
    before = onehot(iota((nodes, nodes), 0) < iota((nodes, nodes), 1))
    rank = dot(jnp.broadcast_to(mine, (8, nodes)).astype(BF16), before)[0:1, :]
    node_ids = iota((1, nodes), 1).astype(F32)

    def nodes_of(slot_index):
        held = jnp.where((rank == slot_index.astype(F32)) & (mine > 0.5), 1.0, 0.0)
        node = jnp.sum(held * node_ids, axis=1, keepdims=True)
        there = jnp.sum(held, axis=1, keepdims=True)
        return jnp.where(there > 0.5, node, -1.0e6).astype(jnp.int32)

    row_id = iota((rows, nodes), 0)
    late = row_id >= split
    row_id = jnp.where(late, row_id - split, row_id)
    tap = jnp.zeros((rows, nodes), jnp.int32)
    for m in range(1, 7):
        tap = tap + (row_id >= m * slots).astype(jnp.int32)
    second = (tap >= 3).astype(jnp.int32)
    shift = dils[0] * (tap - 3 * second - 1) + jnp.where(late, 0, dils[1] * (2 * second - 1))
    target = nodes_of(row_id - slots * tap)
    target = jnp.where(tap >= jnp.where(late, 3, 6), -1000000, target + shift)

    node_lane = iota((rows, nodes), 1)
    for n in range(shots):
        s = shot_of(place_ref, n, shots)
        pick_ref[n] = onehot((node_lane == target - trace_ref[s, 0]) & (node_lane < live_ref[s]))

    slot_rows = keep_ref.shape[2]
    own_node = nodes_of(iota((slot_rows, nodes), 0))
    shot_lane = iota((slot_rows, HALF), 1) >> 5
    for c in range(shots // QUAD):
        base = QUAD * couple_of(place_ref, c)
        for b in range(3):
            first = jnp.zeros((slot_rows, HALF), jnp.int32)
            count = jnp.zeros((slot_rows, HALF), jnp.int32)
            for w in range(QUAD):
                at = shot_lane == (w if b == 1 else w ^ 2)
                first = jnp.where(at, trace_ref[base + w, 0], first)
                count = jnp.where(at, live_ref[base + w], count)
            trace = own_node + dils[1] * (b - 1) - first
            keep_ref[c, b] = ((trace >= 0) & (trace < count)).astype(F32)


def started(sources, places, sems):
    copies = [pltpu.make_async_copy(a, b, sems.at[n]) for n, (a, b) in enumerate(zip(sources, places))]
    for copy in copies:
        copy.start()
    return copies


def prep_kernel(dils, slots, place_ref, *refs):
    w0_ref, w1_ref, w2_ref, wide_bias_ref, shift_ref, pick_ref, keep_ref = refs[9:16]
    half = refs[2].shape[0] // 2
    passed = started((refs[7], refs[2].at[half : 2 * half], refs[8]), refs[16:19], refs[27])
    live_ref, trace_ref, cw_ref, lift_ref, lift_bias_ref, bias_ref, owner_ref = refs[19:26]
    sources = (*refs[:2], refs[2].at[0:half], *refs[3:7])
    for copy in started(sources, refs[19:26], refs[26]):
        copy.wait()
    table_kernel(dils, slots, place_ref, live_ref, trace_ref, owner_ref, pick_ref, keep_ref)

    rows8 = [lift_ref[...].astype(F32)] + [term.astype(F32) for term in split3(lift_bias_ref[...])]
    table = jnp.concatenate(rows8 + [jnp.zeros((1, CH), F32)], axis=0).astype(BF16)
    data_rows = 3 * QUAD * COMPS
    r8 = iota((KROWS, 8), 0)
    part = jnp.where(r8 < data_rows, r8 & (COMPS - 1), COMPS + ((r8 >> 2) & 3))
    values = dot(onehot((part == iota((KROWS, 8), 1)) & (r8 < 2 * data_rows)), table).astype(BF16)
    wide = iota((CH, 2 * LANES), 1)
    spread = onehot(iota((CH, 2 * LANES), 0) == (wide & 31))
    rr = iota((KROWS, 2 * LANES), 0)
    cc = iota((KROWS, 2 * LANES), 1)
    row_node = jnp.where(rr < data_rows, rr >> 4, (rr - data_rows) >> 4)
    row_shot = jnp.where(rr < data_rows, rr >> 2, rr) & (QUAD - 1)
    place = (cc >> 6) & 3
    node = jnp.where((cc >= LANES) & (place < 2), 1 - place, place)
    same = (row_node == node) & (row_shot == 2 * (cc >> 8) + ((cc >> 5) & 1)) & (rr < 2 * data_rows)
    w0_ref[...] = jnp.where(same & (place < 3), dot(values, spread), 0.0).astype(BF16)

    widen = onehot((iota((LANES, CH), 0) & 31) == iota((LANES, CH), 1))
    kr = iota((LANES, LANES), 0)
    kc = iota((LANES, LANES), 1)
    same_shot = ((kr >> 5) & 1) == ((kc >> 5) & 1)
    sr = iota((3 * CH, LANES), 0)
    sc = iota((3 * CH, LANES), 1)
    for layer, ref, odd_taps in ((0, w1_ref, (1, 0, 2, 3)), (1, w2_ref, (1, 0, 3, 2))):
        base = 3 * layer
        tall = [
            dot_t(widen, cw_ref[(base + a) * 3 * CH : (base + a + 1) * 3 * CH, :]).astype(BF16)
            for a in range(3)
        ]
        for odd, (k_taps, n_taps) in enumerate((((0, 1, 2, 3), (0, 1, 3, 2)), (odd_taps, (1, 0, 2, 3)))):
            place = sum(jnp.where((sc >> 6) == y, n_taps[y], 0) for y in range(4))
            spread2 = onehot(((sr >> 5) == place) & ((sr & 31) == (sc & 31)))
            total = jnp.zeros((LANES, LANES), F32)
            for x in range(4):
                if k_taps[x] < 3:
                    total = jnp.where(((kr >> 6) == x) & same_shot, dot(tall[k_taps[x]], spread2), total)
            ref[odd] = total.astype(BF16)

    span = shift_ref.shape[0]
    window = span - 2 * HALO
    source = iota(shift_ref.shape, 0)
    source = jnp.where(source < window + HALO, source, source + window // 2 - HALO)
    shift_ref[...] = onehot(iota(shift_ref.shape, 1) == source)

    tile = onehot(iota((CH, LANES), 0) == (iota((CH, LANES), 1) & 31))
    wide_bias_ref[...] = sum(dot(term, tile) for term in split3(bias_ref[...]))
    for copy in passed:
        copy.wait()


def band_kernel(dils, blocks, place_ref, *refs):
    cw_ref, out_w_ref, b3_ref, b4_ref, ow_ref = refs
    widen = onehot((iota((LANES, CH), 0) & 31) == iota((LANES, CH), 1))

    er = iota((3 * CH, 3 * LANES), 0)
    ec = iota((3 * CH, 3 * LANES), 1)
    spread3 = onehot(((er >> 5) == (ec >> 8)) & ((er & 31) == (ec & 31)))
    row_lane = iota((LANES, 3 * LANES), 0)
    col_lane = iota((LANES, 3 * LANES), 1) & (LANES - 1)

    def shots_in(lane, block):
        couple = jnp.where(lane < HALF, couple_of(place_ref, 2 * block), couple_of(place_ref, 2 * block + 1))
        return QUAD * couple + ((lane >> 5) & (QUAD - 1))

    def expanded(layer, a):
        base = ((layer - 2) * 3 + a) * 3 * CH
        return dot(dot_t(widen, cw_ref[base : base + 3 * CH, :]).astype(BF16), spread3)

    for layer, ref in ((2, b3_ref), (3, b4_ref)):
        linked_taps = band_links(dils[layer], 0) if blocks == 1 else range(3)
        for out_block in range(blocks):
            for in_block in range(blocks):
                total = jnp.zeros((LANES, 3 * LANES), F32)
                for a in linked_taps:
                    reach = shots_in(col_lane, out_block) + (a - 1) * dils[layer]
                    total = total + jnp.where(shots_in(row_lane, in_block) == reach, expanded(layer, a), 0.0)
                for e in range(3):
                    ref[out_block * blocks + in_block, e * LANES : (e + 1) * LANES, :] = total[
                        :, e * LANES : (e + 1) * LANES
                    ].astype(BF16)

    rows = GROUP * COMPS
    pick = onehot((iota((rows, COMPS), 0) & (COMPS - 1)) == iota((rows, COMPS), 1))
    mine = dot(pick, out_w_ref[...]).astype(BF16)
    tile = onehot(iota((CH, LANES), 0) == (iota((CH, LANES), 1) & 31))
    same = (iota((rows, LANES), 0) >> 2) == (iota((rows, LANES), 1) >> 5)
    ow_ref[...] = jnp.where(same, dot(mine, tile), 0.0).astype(BF16)


def round_up(value, unit):
    return -(-value // unit) * unit


def shifted(value, dilation):
    span = value.shape[0]
    return jnp.concatenate(
        [
            pltpu.roll(value, dilation, axis=0).astype(BF16),
            value.astype(BF16),
            pltpu.roll(value, span - dilation, axis=0).astype(BF16),
        ],
        axis=1,
    )


class Shots:
    def __init__(
        self, dils, windows, step, couple, place_ref, recs, pick_ref, keep_ref, w0_ref, w1_ref, w2_ref,
        bias_ref, shift_ref, part_ref, x2_ref, rec_out_ref,
    ):
        self.dils, self.step, self.couple = dils, step, couple
        self.lifted, self.middle = collections.defaultdict(list), {}
        self.keep_ref, self.w0_ref, self.w1_ref, self.w2_ref = keep_ref, w0_ref, w1_ref, w2_ref
        self.bias_ref, self.shift_ref, self.x2_ref = bias_ref, shift_ref, x2_ref
        shots, rows, nodes = pick_ref.shape
        planes = shots // CORES
        self.slots = slots = x2_ref.shape[0]
        self.window = window = part_ref.shape[-1]
        self.rows, self.split = part_ref.shape[2], round_up(6 * slots, 16)
        self.span = window + 2 * HALO
        at = place_ref[1]
        self.right_ok = (at < windows - 1).astype(F32)
        self.left_ok = (at > 0).astype(F32)
        self.low_half = iota((self.span, HALF), 1) < CH * CORES

        lane = iota((nodes, 2 * window), 1)
        all_ok = jnp.where(
            lane < window, 1.0, jnp.where(lane < window + window // 2, self.right_ok, self.left_ok)
        ).astype(BF16)

        def put(part, swapped, value):
            for half in range(2):
                lanes = value[:, half * window : (half + 1) * window]
                part_ref[half, part, 0 : self.split] = lanes[0 : self.split]
                part_ref[half, swapped, self.split : rows] = lanes[self.split : rows]

        for x, rec_ref in enumerate(recs):
            n = 2 * couple + x % 2 + (planes if x >= 2 else 0)
            within = shot_of(place_ref, n, shots) & (QUAD - 1)
            edge = rec_ref[COMPS].astype(F32)
            for k in range(COMPS):
                turned = edge if k == 0 else pltpu.roll(edge, window - HALO * k, axis=1)
                both = jnp.concatenate([rec_ref[k], turned.astype(BF16)], axis=1)
                put(within * COMPS + k, (within ^ 2) * COMPS + k, dot(pick_ref[n], both))
            alive = dot(pick_ref[n], all_ok)
            for copy in range(2):
                first = QUAD * COMPS + QUAD * copy
                put(first + within, first + (within ^ 2), alive)

        self.half_rows = part_ref.shape[1] * self.rows
        self.part2 = part_ref.reshape(2 * self.half_rows, window)
        for q in range(slots):
            first = self.split + slots + q
            for half in range(2):
                pair = self.part2[pl.ds(first + (1 - half) * 8 * self.rows, 8, stride=self.rows), :]
                rec_out_ref[q, half * 8 : (half + 1) * 8] = pair

    def inside(self, value):
        w = self.window
        return jnp.concatenate(
            [value[0:w], value[w : w + HALO] * self.right_ok, value[w + HALO :] * self.left_ok], axis=0
        )

    def item_rows(self, q, b):
        start = (3 * (b // 2) * self.slots if b != 1 else self.split) + q
        halves = []
        for half in range(2):
            base = half * self.half_rows + start
            flags = base + QUAD * COMPS * self.rows
            pieces = [
                self.part2[pl.ds(base + a * self.slots, QUAD * COMPS, stride=self.rows), :] for a in range(3)
            ]
            for a in range(3):
                alive = self.part2[pl.ds(flags + a * self.slots, 2 * QUAD, stride=self.rows), :]
                pieces += [alive, alive]
            pieces.append(jnp.zeros((KROWS - 6 * QUAD * COMPS, self.window), F32))
            halves.append(jnp.concatenate(pieces, axis=0).astype(BF16))
        return jnp.concatenate(halves, axis=1)

    def items(self, group):
        return [(group * self.step + i, b) for i in range(self.step) for b in range(3)]

    def first_inputs(self, group):
        items = self.items(group)
        for n in range(0, len(items), 2):
            some = jnp.concatenate([self.item_rows(q, b) for q, b in items[n : n + 2]], axis=0)
            moved = dot_t(self.shift_ref[...], some).astype(BF16)
            lhs = [moved[:, m : m + KROWS] for m in range(0, moved.shape[1], KROWS)]
            lifted = dot(jnp.concatenate(lhs, axis=0), self.w0_ref[...]).astype(BF16)
            self.lifted[group].append((lifted[:, 0:LANES], lifted[:, LANES:]))
            yield

    def taps_added(self, even, odd, dilation):
        mid = jnp.where(self.low_half, odd[:, 0:HALF], even[:, 0:HALF])
        late = jnp.where(self.low_half, odd[:, HALF:], even[:, HALF:])
        early = pltpu.roll(jnp.where(self.low_half, even[:, 0:HALF], odd[:, 0:HALF]), HALF // 2, axis=1)
        return (
            pltpu.roll(early, dilation, axis=0) + mid + pltpu.roll(late, self.span - dilation, axis=0)
        )

    def first_layer(self, group):
        x1 = []
        items = self.items(group)
        for n, (even, odd) in enumerate(self.lifted.pop(group)):
            y_even, y_odd = dot(even, self.w1_ref[0]), dot(odd, self.w1_ref[1])
            for m, (q, b) in enumerate(items[2 * n : 2 * n + 2]):
                at = slice(m * self.span, (m + 1) * self.span)
                old = jnp.where(self.low_half, odd[at, 0:HALF].astype(F32), even[at, 0:HALF].astype(F32))
                total = self.taps_added(y_even[at], y_odd[at], self.dils[0])
                new = jnp.maximum(total + self.bias_ref[0:1, 0:HALF], 0.0)
                x1.append(self.inside((old + new) * self.keep_ref[self.couple, b, q : q + 1, :]))
            yield
        even, odd, own = [], [], []
        for i in range(self.step):
            t0, t1, t2 = x1[3 * i : 3 * i + 3]
            t2 = t2.astype(BF16)
            even.append(jnp.concatenate([jnp.where(self.low_half, t0, t1).astype(BF16), t2], axis=1))
            odd.append(jnp.concatenate([jnp.where(self.low_half, t1, t0).astype(BF16), t2], axis=1))
            own.append(t1.astype(BF16))
        self.middle[group] = (jnp.concatenate(even, axis=0), jnp.concatenate(odd, axis=0), own)

    def second_layer(self, group):
        even, odd, own = self.middle.pop(group)
        even, odd = dot(even, self.w2_ref[0]), dot(odd, self.w2_ref[1])
        yield
        for i in range(self.step):
            q = group * self.step + i
            at = slice(i * self.span, (i + 1) * self.span)
            total = self.taps_added(even[at], odd[at], self.dils[1])
            new = jnp.maximum(total + self.bias_ref[1:2, 0:HALF], 0.0)
            x2 = (own[i].astype(F32) + new) * self.keep_ref[self.couple, 1, q : q + 1, :]
            self.x2_ref[q] = shifted(self.inside(x2), self.dils[2])
            yield


def in_turns(steps):
    for _ in itertools.zip_longest(*steps):
        pass


def shot_steps(work, t):
    at = lambda lag: work[t - lag] if 0 <= t - lag < len(work) else None
    steps = [(stage.second_layer, group) for stage, group in filter(None, [at(2)])]
    steps += [(stage.first_layer, group) for stage, group in filter(None, [at(1)])]
    steps += [(stage.first_inputs, group) for stage, group in filter(None, [at(0)])]
    return [function(group) for function, group in steps]


def near_kernel(dils, windows, step, place_ref, *refs):
    pick_ref, keep_ref, w0_ref, w1_ref, w2_ref, bias_ref, shift_ref = refs[:7]
    x2_ref, rec_out_ref, part_ref = refs[7 + QUAD :]
    stage = Shots(
        dils, windows, step, 0, place_ref, refs[7 : 7 + QUAD], pick_ref, keep_ref, w0_ref, w1_ref, w2_ref,
        bias_ref, shift_ref, part_ref, x2_ref, rec_out_ref,
    )
    work = [(stage, group) for group in range(x2_ref.shape[0] // step)]
    for t in range(len(work) + 2):
        in_turns(shot_steps(work, t))


def main_kernel(dils, windows, step, near, place_ref, *refs):
    shots = refs[0].shape[0]
    couples = shots // QUAD
    pick_ref, keep_ref, w0_ref, w1_ref, w2_ref, b3_ref, b4_ref, ow_ref, bias_ref, shift_ref = refs[:10]
    refs = refs[10:]
    rec_refs, refs = refs[: QUAD * (couples - near)], refs[QUAD * (couples - near) :]
    done_refs, refs = refs[: 2 * near], refs[2 * near :]
    out_ref, part_ref, x2_all, rec_all, x3_ref = refs
    blocks = couples // 2
    slots, window = out_ref.shape[1], out_ref.shape[3]
    span = window + 2 * HALO
    right_ok = (place_ref[1] < windows - 1).astype(F32)
    left_ok = (place_ref[1] > 0).astype(F32)

    stages = []
    x2_refs, rec_refs_out = list(done_refs[0::2]), list(done_refs[1::2])
    for c in range(near, couples):
        x2_refs.append(x2_all.at[c - near])
        rec_refs_out.append(rec_all.at[c - near])
        stages.append(
            Shots(
                dils, windows, step, c, place_ref, rec_refs[QUAD * (c - near) : QUAD * (c - near + 1)],
                pick_ref, keep_ref, w0_ref, w1_ref, w2_ref, bias_ref, shift_ref, part_ref.at[c - near],
                x2_refs[-1], rec_refs_out[-1],
            )
        )

    def receiver_layer(parts_of, weights, layer, block, group, out_rows):
        y = None
        for other in range(blocks):
            term = dot(jnp.concatenate(parts_of(other), axis=0), weights[block * blocks + other])
            y = term if y is None else y + term
        for i, part in enumerate(parts_of(block)):
            q = group * step + i
            keep = jnp.concatenate([keep_ref[2 * block + c, 1, q : q + 1, :] for c in range(2)], axis=1)
            old = part[:, LANES : 2 * LANES].astype(F32)
            new = jnp.maximum(y[i * out_rows : (i + 1) * out_rows] + bias_ref[layer : layer + 1, :], 0.0)
            yield (old + new) * keep

    def third_layer(group):
        def parts_of(block):
            return [
                jnp.concatenate(
                    [
                        x2_refs[2 * block + c][group * step + i, :, e * HALF : (e + 1) * HALF]
                        for e in range(3)
                        for c in range(2)
                    ],
                    axis=1,
                )
                for i in range(step)
            ]

        for block in range(blocks):
            for i, value in enumerate(receiver_layer(parts_of, b3_ref, 2, block, group, span)):
                value = jnp.concatenate(
                    [
                        value[0:window],
                        value[window : window + HALO] * right_ok,
                        value[window + HALO :] * left_ok,
                    ],
                    axis=0,
                )
                x3_ref[block, group * step + i] = shifted(value, dils[3])[0:window]
                yield

    def last_layer(group):
        def parts_of(block):
            return [x3_ref[block, group * step + i] for i in range(step)]

        for block in range(blocks):
            for i, value in enumerate(receiver_layer(parts_of, b4_ref, 3, block, group, window)):
                q = group * step + i
                noise = dot_t(ow_ref[...], value.astype(BF16))
                record = jnp.concatenate([rec_refs_out[2 * block + c][q] for c in range(2)], axis=0)
                done = (record + noise).reshape(GROUP, COMPS, window)
                for c in range(2):
                    first = QUAD * couple_of(place_ref, 2 * block + c)
                    out_ref[pl.ds(first, QUAD), q] = done[c * QUAD : (c + 1) * QUAD]
                yield

    groups = slots // step
    work = [(stage, group) for group in range(groups) for stage in stages]
    lag = len(stages)
    for t in range(len(work) + 2 + 2 * lag):
        done, rest = divmod(t - 2, lag)
        late = []
        if rest == 0 and 0 <= done - 2 < groups:
            late.append(last_layer(done - 2))
        if rest == 0 and 0 <= done - 1 < groups:
            late.append(third_layer(done - 1))
        in_turns(late + shot_steps(work, t))


def divisor(value, limit):
    return max(d for d in range(1, limit + 1) if value % d == 0)


def body(
    records,
    lift_weight,
    lift_bias,
    conv_weight,
    conv_bias,
    out_weight,
    live_count,
    trace_node,
    node_owner,
):
    _, comps, nodes, window = records.shape
    holders = lax.axis_size("gather")
    windows = lax.axis_size("tm")
    shots = holders * records.shape[0]
    couples = shots // QUAD
    blocks = couples // 2
    slots = (nodes + holders - 1) // holders
    dils = (1, 4, 2, 8)
    rows = round_up(6 * slots, 16) + round_up(3 * slots, 16)
    span = window + 2 * HALO

    planes = holders // CORES
    vmem = pl.BlockSpec(memory_space=pltpu.VMEM)
    smem = pl.BlockSpec(memory_space=pltpu.SMEM)
    like = jax.ShapeDtypeStruct

    def after(value, other):
        return lax.optimization_barrier((value, other))[0]

    def kernel(function, operands, specs, outs, scratch, limit, flops, name):
        return pl.pallas_call(
            function,
            out_shape=outs,
            in_specs=[smem] + specs,
            out_specs=jax.tree.map(lambda _: vmem, outs),
            scratch_shapes=scratch,
            compiler_params=pltpu.CompilerParams(vmem_limit_bytes=limit << 20),
            cost_estimate=pl.CostEstimate(flops=flops, bytes_accessed=1 << 10, transcendentals=0),
            name=name,
        )(place, *operands)

    place = jnp.stack([lax.axis_index("gather"), lax.axis_index("tm")]).astype(jnp.int32)
    taps = jnp.transpose(conv_weight, (0, 3, 4, 1, 2)).reshape(-1, CH)

    own = records[0]
    even = lax.axis_index("tm") % 2 == 0
    pack = lambda part: jnp.transpose(part, (1, 0, 2)).reshape(nodes, comps * HALO)
    first, last = pack(own[:, :, :HALO]), pack(own[:, :, window - HALO :])
    got = []
    for begin in range(2):
        pairs = [(w, w + 1) for w in range(begin, windows - 1, 2)]
        pairs += [(b, a) for a, b in pairs]
        got.append(lax.ppermute(jnp.where(even == (begin == 0), last, first), "tm", pairs))
    small = [live_count, trace_node, taps, jnp.transpose(lift_weight), lift_bias[None, :], conv_bias]
    raw = small + [node_owner[None, :], own, out_weight]
    raw = [pltpu.with_memory_space_constraint(a, pltpu.HBM) for a in raw]
    half = (taps.shape[0] // 2, CH)
    scratch = [pltpu.SMEM(a.shape, a.dtype) for a in raw[:2]] + [pltpu.VMEM(half, BF16)]
    scratch += [pltpu.VMEM(a.shape, a.dtype) for a in raw[3:7]]
    w0, w1, w2, wide_bias, shift, pick, keep, own, late_taps, out_taps = kernel(
        functools.partial(prep_kernel, dils, slots),
        raw,
        [pl.BlockSpec(memory_space=pltpu.HBM)] * len(raw),
        (
            like((KROWS, 2 * LANES), BF16),
            like((2, LANES, LANES), BF16),
            like((2, LANES, LANES), BF16),
            like((conv_bias.shape[0], LANES), F32),
            like((span, 2 * window), BF16),
            like((shots, rows, nodes), BF16),
            like((couples, 3, 16, HALF), F32),
            like(own.shape, BF16),
            like(half, BF16),
            like(out_weight.shape, BF16),
        ),
        scratch + [pltpu.SemaphoreType.DMA((7,)), pltpu.SemaphoreType.DMA((3,))],
        16,
        10**5,
        "weights",
    )
    right, left = jnp.where(even, got[0], got[1]), jnp.where(even, got[1], got[0])
    sent = jnp.concatenate([own, jnp.concatenate([right, left], axis=1)[None]], axis=0)


    def exchanged(block, distance):
        return lax.ppermute(block, "gather", [(g, g ^ distance) for g in range(holders)])

    near_blocks = [sent, exchanged(sent, CORES)]
    far = [exchanged(sent, CORES * r) for r in range(2, planes)]
    near_blocks += [exchanged(block, 1) for block in near_blocks]

    b3, b4, ow = kernel(
        functools.partial(band_kernel, dils, blocks),
        [late_taps, out_taps],
        [vmem] * 2,
        (
            like((blocks * blocks, 3 * LANES, LANES), BF16),
            like((blocks * blocks, 3 * LANES, LANES), BF16),
            like((GROUP * COMPS, LANES), BF16),
        ),
        [],
        16,
        10**10,
        "bands",
    )

    step = divisor(slots, 2)
    row_stride = round_up(rows, 16) + 8
    x2 = like((slots, span, 3 * HALF), BF16)
    held = like((slots, QUAD * COMPS, window), F32)
    parts = (2, PARTS, row_stride, window)
    operands = [after(pick, ow), keep, w0, w1, w2, wide_bias, shift, *near_blocks]
    near = kernel(
        functools.partial(near_kernel, dils, windows, step),
        operands,
        [vmem] * len(operands),
        (x2, held),
        [pltpu.VMEM(parts, F32)],
        24,
        10**5,
        "near",
    )

    operands = [pick, keep, w0, w1, w2, b3, b4, ow, wide_bias, shift]
    for r in range(0, len(far), 2):
        operands += far[r : r + 2] + [exchanged(after(block, near[1]), 1) for block in far[r : r + 2]]
    operands += near
    out = kernel(
        functools.partial(main_kernel, dils, windows, step, 1),
        operands,
        [vmem] * len(operands),
        like((shots, slots, comps, window), F32),
        [
            pltpu.VMEM((couples - 1, *parts), F32),
            pltpu.VMEM((couples - 1, *x2.shape), BF16),
            pltpu.VMEM((couples - 1, *held.shape), F32),
            pltpu.VMEM((blocks, slots, window, 3 * LANES), BF16),
        ],
        36,
        4 * 10**9,
        "layers",
    )
    return jnp.transpose(out, (0, 2, 1, 3))


def solution(mesh):
    return jax.shard_map(
        body,
        mesh=mesh,
        in_specs=(P("gather", None, None, "tm"), P(), P(), P(), P(), P(), P(), P(), P()),
        out_specs=P(None, None, "gather", "tm"),
        check_vma=False,
    )
```

```python
import functools
import itertools

import jax
import jax.numpy as jnp
from jax import lax
from jax.experimental import pallas as pl
from jax.experimental.pallas import tpu as pltpu
from jax.sharding import PartitionSpec as P

F32 = jnp.float32
BF16 = jnp.bfloat16
CH = 32
CORES = 2
COMPS = 4
GROUP = 8
LANES = GROUP * CH
HALO = 16
QUAD = 4
HALF = QUAD * CH
KROWS = 128
PARTS = QUAD * COMPS + 2 * QUAD


def iota(shape, dim):
    return lax.broadcasted_iota(jnp.int32, shape, dim)


def dot(a, b):
    return jnp.dot(a, b, preferred_element_type=F32)


def dot_t(a, b):
    return lax.dot_general(a, b, (((1,), (1,)), ((), ())), preferred_element_type=F32)


def onehot(cond):
    return cond.astype(F32).astype(BF16)


def band_links(dilation, offset):
    return [
        a
        for a in range(3)
        if any(s + GROUP * offset == t + (a - 1) * dilation for s in range(GROUP) for t in range(GROUP))
    ]


def split3(value):
    terms = []
    for _ in range(3):
        term = value.astype(BF16)
        terms.append(term)
        value = value - term.astype(F32)
    return terms


def shot_of(place_ref, n, shots):
    planes = shots // CORES
    plane = place_ref[0] // CORES
    core = place_ref[0] - CORES * plane
    return CORES * (plane ^ (n % planes)) + (core if n < planes else 1 - core)


def couple_of(place_ref, relative):
    return (place_ref[0] // (2 * CORES)) ^ relative


def table_kernel(dils, slots, place_ref, live_ref, trace_ref, owner_ref, pick_ref, keep_ref):
    shots, rows, nodes = pick_ref.shape
    split = round_up(6 * slots, 16)
    me = place_ref[0]

    mine = (owner_ref[...] == me).astype(F32)
    before = onehot(iota((nodes, nodes), 0) < iota((nodes, nodes), 1))
    rank = dot(jnp.broadcast_to(mine, (8, nodes)).astype(BF16), before)[0:1, :]
    node_ids = iota((1, nodes), 1).astype(F32)

    def nodes_of(slot_index):
        held = jnp.where((rank == slot_index.astype(F32)) & (mine > 0.5), 1.0, 0.0)
        node = jnp.sum(held * node_ids, axis=1, keepdims=True)
        there = jnp.sum(held, axis=1, keepdims=True)
        return jnp.where(there > 0.5, node, -1.0e6).astype(jnp.int32)

    row_id = iota((rows, nodes), 0)
    late = row_id >= split
    row_id = jnp.where(late, row_id - split, row_id)
    tap = jnp.zeros((rows, nodes), jnp.int32)
    for m in range(1, 7):
        tap = tap + (row_id >= m * slots).astype(jnp.int32)
    second = (tap >= 3).astype(jnp.int32)
    shift = dils[0] * (tap - 3 * second - 1) + jnp.where(late, 0, dils[1] * (2 * second - 1))
    target = nodes_of(row_id - slots * tap)
    target = jnp.where(tap >= jnp.where(late, 3, 6), -1000000, target + shift)

    node_lane = iota((rows, nodes), 1)
    for n in range(shots):
        s = shot_of(place_ref, n, shots)
        pick_ref[n] = onehot((node_lane == target - trace_ref[s, 0]) & (node_lane < live_ref[s]))

    slot_rows = keep_ref.shape[2]
    own_node = nodes_of(iota((slot_rows, nodes), 0))
    shot_lane = iota((slot_rows, HALF), 1) >> 5
    for c in range(shots // QUAD):
        base = QUAD * couple_of(place_ref, c)
        for b in range(3):
            first = jnp.zeros((slot_rows, HALF), jnp.int32)
            count = jnp.zeros((slot_rows, HALF), jnp.int32)
            for w in range(QUAD):
                at = shot_lane == (w if b == 1 else w ^ 2)
                first = jnp.where(at, trace_ref[base + w, 0], first)
                count = jnp.where(at, live_ref[base + w], count)
            trace = own_node + dils[1] * (b - 1) - first
            keep_ref[c, b] = ((trace >= 0) & (trace < count)).astype(F32)


def started(sources, places, sems):
    copies = [pltpu.make_async_copy(a, b, sems.at[n]) for n, (a, b) in enumerate(zip(sources, places))]
    for copy in copies:
        copy.start()
    return copies


def prep_kernel(dils, slots, place_ref, *refs):
    w0_ref, w1_ref, w2_ref, wide_bias_ref, shift_ref, pick_ref, keep_ref = refs[9:16]
    half = refs[2].shape[0] // 2
    passed = started((refs[7], refs[2].at[half : 2 * half], refs[8]), refs[16:19], refs[27])
    live_ref, trace_ref, cw_ref, lift_ref, lift_bias_ref, bias_ref, owner_ref = refs[19:26]
    sources = (*refs[:2], refs[2].at[0:half], *refs[3:7])
    for copy in started(sources, refs[19:26], refs[26]):
        copy.wait()
    table_kernel(dils, slots, place_ref, live_ref, trace_ref, owner_ref, pick_ref, keep_ref)

    rows8 = [lift_ref[...].astype(F32)] + [term.astype(F32) for term in split3(lift_bias_ref[...])]
    table = jnp.concatenate(rows8 + [jnp.zeros((1, CH), F32)], axis=0).astype(BF16)
    data_rows = 3 * QUAD * COMPS
    r8 = iota((KROWS, 8), 0)
    part = jnp.where(r8 < data_rows, r8 & (COMPS - 1), COMPS + ((r8 >> 2) & 3))
    values = dot(onehot((part == iota((KROWS, 8), 1)) & (r8 < 2 * data_rows)), table).astype(BF16)
    wide = iota((CH, 2 * LANES), 1)
    spread = onehot(iota((CH, 2 * LANES), 0) == (wide & 31))
    rr = iota((KROWS, 2 * LANES), 0)
    cc = iota((KROWS, 2 * LANES), 1)
    row_node = jnp.where(rr < data_rows, rr >> 4, (rr - data_rows) >> 4)
    row_shot = jnp.where(rr < data_rows, rr >> 2, rr) & (QUAD - 1)
    place = (cc >> 6) & 3
    node = jnp.where((cc >= LANES) & (place < 2), 1 - place, place)
    same = (row_node == node) & (row_shot == 2 * (cc >> 8) + ((cc >> 5) & 1)) & (rr < 2 * data_rows)
    w0_ref[...] = jnp.where(same & (place < 3), dot(values, spread), 0.0).astype(BF16)

    widen = onehot((iota((LANES, CH), 0) & 31) == iota((LANES, CH), 1))
    kr = iota((LANES, LANES), 0)
    kc = iota((LANES, LANES), 1)
    same_shot = ((kr >> 5) & 1) == ((kc >> 5) & 1)
    sr = iota((3 * CH, LANES), 0)
    sc = iota((3 * CH, LANES), 1)
    for layer, ref, odd_taps in ((0, w1_ref, (1, 0, 2, 3)), (1, w2_ref, (1, 0, 3, 2))):
        base = 3 * layer
        tall = [
            dot_t(widen, cw_ref[(base + a) * 3 * CH : (base + a + 1) * 3 * CH, :]).astype(BF16)
            for a in range(3)
        ]
        for odd, (k_taps, n_taps) in enumerate((((0, 1, 2, 3), (0, 1, 3, 2)), (odd_taps, (1, 0, 2, 3)))):
            place = sum(jnp.where((sc >> 6) == y, n_taps[y], 0) for y in range(4))
            spread2 = onehot(((sr >> 5) == place) & ((sr & 31) == (sc & 31)))
            total = jnp.zeros((LANES, LANES), F32)
            for x in range(4):
                if k_taps[x] < 3:
                    total = jnp.where(((kr >> 6) == x) & same_shot, dot(tall[k_taps[x]], spread2), total)
            ref[odd] = total.astype(BF16)

    span = shift_ref.shape[0]
    window = span - 2 * HALO
    source = iota(shift_ref.shape, 0)
    source = jnp.where(source < window + HALO, source, source + window // 2 - HALO)
    shift_ref[...] = onehot(iota(shift_ref.shape, 1) == source)

    tile = onehot(iota((CH, LANES), 0) == (iota((CH, LANES), 1) & 31))
    wide_bias_ref[...] = sum(dot(term, tile) for term in split3(bias_ref[...]))
    for copy in passed:
        copy.wait()


def band_kernel(dils, blocks, place_ref, *refs):
    cw_ref, out_w_ref, b3_ref, b4_ref, ow_ref = refs
    widen = onehot((iota((LANES, CH), 0) & 31) == iota((LANES, CH), 1))

    er = iota((3 * CH, 3 * LANES), 0)
    ec = iota((3 * CH, 3 * LANES), 1)
    spread3 = onehot(((er >> 5) == (ec >> 8)) & ((er & 31) == (ec & 31)))
    row_lane = iota((LANES, 3 * LANES), 0)
    col_lane = iota((LANES, 3 * LANES), 1) & (LANES - 1)

    def shots_in(lane, block):
        couple = jnp.where(lane < HALF, couple_of(place_ref, 2 * block), couple_of(place_ref, 2 * block + 1))
        return QUAD * couple + ((lane >> 5) & (QUAD - 1))

    def expanded(layer, a):
        base = ((layer - 2) * 3 + a) * 3 * CH
        return dot(dot_t(widen, cw_ref[base : base + 3 * CH, :]).astype(BF16), spread3)

    for layer, ref in ((2, b3_ref), (3, b4_ref)):
        linked_taps = band_links(dils[layer], 0) if blocks == 1 else range(3)
        for out_block in range(blocks):
            for in_block in range(blocks):
                total = jnp.zeros((LANES, 3 * LANES), F32)
                for a in linked_taps:
                    reach = shots_in(col_lane, out_block) + (a - 1) * dils[layer]
                    total = total + jnp.where(shots_in(row_lane, in_block) == reach, expanded(layer, a), 0.0)
                for e in range(3):
                    ref[out_block * blocks + in_block, e * LANES : (e + 1) * LANES, :] = total[
                        :, e * LANES : (e + 1) * LANES
                    ].astype(BF16)

    rows = GROUP * COMPS
    pick = onehot((iota((rows, COMPS), 0) & (COMPS - 1)) == iota((rows, COMPS), 1))
    mine = dot(pick, out_w_ref[...]).astype(BF16)
    tile = onehot(iota((CH, LANES), 0) == (iota((CH, LANES), 1) & 31))
    same = (iota((rows, LANES), 0) >> 2) == (iota((rows, LANES), 1) >> 5)
    ow_ref[...] = jnp.where(same, dot(mine, tile), 0.0).astype(BF16)


def round_up(value, unit):
    return -(-value // unit) * unit


def shifted(value, dilation):
    span = value.shape[0]
    return jnp.concatenate(
        [
            pltpu.roll(value, dilation, axis=0).astype(BF16),
            value.astype(BF16),
            pltpu.roll(value, span - dilation, axis=0).astype(BF16),
        ],
        axis=1,
    )


class Shots:
    def __init__(
        self, dils, windows, step, couple, place_ref, recs, pick_ref, keep_ref, w0_ref, w1_ref, w2_ref,
        bias_ref, shift_ref, part_ref, x2_ref, rec_out_ref,
    ):
        self.dils, self.step, self.couple = dils, step, couple
        self.keep_ref, self.w0_ref, self.w1_ref, self.w2_ref = keep_ref, w0_ref, w1_ref, w2_ref
        self.bias_ref, self.shift_ref, self.x2_ref = bias_ref, shift_ref, x2_ref
        shots, rows, nodes = pick_ref.shape
        planes = shots // CORES
        self.slots = slots = x2_ref.shape[0]
        self.window = window = part_ref.shape[-1]
        self.rows, self.split = part_ref.shape[2], round_up(6 * slots, 16)
        self.span = window + 2 * HALO
        at = place_ref[1]
        self.right_ok = (at < windows - 1).astype(F32)
        self.left_ok = (at > 0).astype(F32)
        self.low_half = iota((self.span, HALF), 1) < CH * CORES

        lane = iota((nodes, 2 * window), 1)
        all_ok = jnp.where(
            lane < window, 1.0, jnp.where(lane < window + window // 2, self.right_ok, self.left_ok)
        ).astype(BF16)

        def put(part, swapped, value):
            for half in range(2):
                lanes = value[:, half * window : (half + 1) * window]
                part_ref[half, part, 0 : self.split] = lanes[0 : self.split]
                part_ref[half, swapped, self.split : rows] = lanes[self.split : rows]

        for x, rec_ref in enumerate(recs):
            n = 2 * couple + x % 2 + (planes if x >= 2 else 0)
            within = shot_of(place_ref, n, shots) & (QUAD - 1)
            edge = rec_ref[COMPS].astype(F32)
            for k in range(COMPS):
                turned = edge if k == 0 else pltpu.roll(edge, window - HALO * k, axis=1)
                both = jnp.concatenate([rec_ref[k], turned.astype(BF16)], axis=1)
                put(within * COMPS + k, (within ^ 2) * COMPS + k, dot(pick_ref[n], both))
            alive = dot(pick_ref[n], all_ok)
            for copy in range(2):
                first = QUAD * COMPS + QUAD * copy
                put(first + within, first + (within ^ 2), alive)

        self.half_rows = part_ref.shape[1] * self.rows
        self.part2 = part_ref.reshape(2 * self.half_rows, window)
        for q in range(slots):
            first = self.split + slots + q
            for half in range(2):
                pair = self.part2[pl.ds(first + (1 - half) * 8 * self.rows, 8, stride=self.rows), :]
                rec_out_ref[q, half * 8 : (half + 1) * 8] = pair

    def inside(self, value):
        w = self.window
        return jnp.concatenate(
            [value[0:w], value[w : w + HALO] * self.right_ok, value[w + HALO :] * self.left_ok], axis=0
        )

    def item_rows(self, q, b):
        start = (3 * (b // 2) * self.slots if b != 1 else self.split) + q
        halves = []
        for half in range(2):
            base = half * self.half_rows + start
            flags = base + QUAD * COMPS * self.rows
            pieces = [
                self.part2[pl.ds(base + a * self.slots, QUAD * COMPS, stride=self.rows), :] for a in range(3)
            ]
            for a in range(3):
                alive = self.part2[pl.ds(flags + a * self.slots, 2 * QUAD, stride=self.rows), :]
                pieces += [alive, alive]
            pieces.append(jnp.zeros((KROWS - 6 * QUAD * COMPS, self.window), F32))
            halves.append(jnp.concatenate(pieces, axis=0).astype(BF16))
        return jnp.concatenate(halves, axis=1)

    def items(self, group):
        return [(group * self.step + i, b) for i in range(self.step) for b in range(3)]

    def first_inputs(self, group):
        items = self.items(group)
        lhs = []
        for n in range(0, len(items), 2):
            some = jnp.concatenate([self.item_rows(q, b) for q, b in items[n : n + 2]], axis=0)
            moved = dot_t(self.shift_ref[...], some).astype(BF16)
            lhs += [moved[:, m : m + KROWS] for m in range(0, moved.shape[1], KROWS)]
        lifted = dot(jnp.concatenate(lhs, axis=0), self.w0_ref[...]).astype(BF16)
        return lifted[:, 0:LANES], lifted[:, LANES:]

    def taps_added(self, even, odd, dilation):
        mid = jnp.where(self.low_half, odd[:, 0:HALF], even[:, 0:HALF])
        late = jnp.where(self.low_half, odd[:, HALF:], even[:, HALF:])
        early = pltpu.roll(jnp.where(self.low_half, even[:, 0:HALF], odd[:, 0:HALF]), HALF // 2, axis=1)
        return (
            pltpu.roll(early, dilation, axis=0) + mid + pltpu.roll(late, self.span - dilation, axis=0)
        )

    def first_layer(self, group, even, odd):
        y_even, y_odd = dot(even, self.w1_ref[0]), dot(odd, self.w1_ref[1])
        x1 = []
        for n, (q, b) in enumerate(self.items(group)):
            at = slice(n * self.span, (n + 1) * self.span)
            old = jnp.where(self.low_half, odd[at, 0:HALF].astype(F32), even[at, 0:HALF].astype(F32))
            total = self.taps_added(y_even[at], y_odd[at], self.dils[0])
            new = jnp.maximum(total + self.bias_ref[0:1, 0:HALF], 0.0)
            x1.append(self.inside((old + new) * self.keep_ref[self.couple, b, q : q + 1, :]))
        even, odd, own = [], [], []
        for i in range(self.step):
            t0, t1, t2 = x1[3 * i : 3 * i + 3]
            t2 = t2.astype(BF16)
            even.append(jnp.concatenate([jnp.where(self.low_half, t0, t1).astype(BF16), t2], axis=1))
            odd.append(jnp.concatenate([jnp.where(self.low_half, t1, t0).astype(BF16), t2], axis=1))
            own.append(t1.astype(BF16))
        return jnp.concatenate(even, axis=0), jnp.concatenate(odd, axis=0), own

    def second_layer(self, group, even, odd, own):
        even, odd = dot(even, self.w2_ref[0]), dot(odd, self.w2_ref[1])
        for i in range(self.step):
            q = group * self.step + i
            at = slice(i * self.span, (i + 1) * self.span)
            total = self.taps_added(even[at], odd[at], self.dils[1])
            new = jnp.maximum(total + self.bias_ref[1:2, 0:HALF], 0.0)
            x2 = (own[i].astype(F32) + new) * self.keep_ref[self.couple, 1, q : q + 1, :]
            self.x2_ref[q] = shifted(self.inside(x2), self.dils[2])


def staged(work):
    inputs, middle = {}, {}
    for t in range(len(work) + 2):
        if t < len(work):
            stage, group = work[t]
            inputs[t] = stage.first_inputs(group)
        if 0 <= t - 1 < len(work):
            stage, group = work[t - 1]
            middle[t - 1] = stage.first_layer(group, *inputs.pop(t - 1))
        if 0 <= t - 2:
            stage, group = work[t - 2]
            stage.second_layer(group, *middle.pop(t - 2))
        yield t


def near_kernel(dils, windows, step, place_ref, *refs):
    pick_ref, keep_ref, w0_ref, w1_ref, w2_ref, bias_ref, shift_ref = refs[:7]
    recs = [refs[7], refs[8], refs[9].at[0], refs[9].at[1]]
    x2_ref, rec_out_ref, part_ref = refs[10:]
    stage = Shots(
        dils, windows, step, 0, place_ref, recs, pick_ref, keep_ref, w0_ref, w1_ref, w2_ref,
        bias_ref, shift_ref, part_ref, x2_ref, rec_out_ref,
    )
    for _ in staged([(stage, group) for group in range(x2_ref.shape[0] // step)]):
        pass


def main_kernel(dils, windows, step, near, place_ref, *refs):
    shots = refs[0].shape[0]
    couples = shots // QUAD
    pick_ref, keep_ref, w0_ref, w1_ref, w2_ref, b3_ref, b4_ref, ow_ref, bias_ref, shift_ref = refs[:10]
    refs = refs[10:]
    rec_refs, refs = refs[: QUAD * (couples - near)], refs[QUAD * (couples - near) :]
    done_refs, refs = refs[: 2 * near], refs[2 * near :]
    out_ref, part_ref, x2_all, rec_all, x3_ref = refs
    blocks = couples // 2
    slots, window = out_ref.shape[1], out_ref.shape[3]
    span = window + 2 * HALO
    right_ok = (place_ref[1] < windows - 1).astype(F32)
    left_ok = (place_ref[1] > 0).astype(F32)

    stages = []
    x2_refs, rec_refs_out = list(done_refs[0::2]), list(done_refs[1::2])
    for c in range(near, couples):
        x2_refs.append(x2_all.at[c - near])
        rec_refs_out.append(rec_all.at[c - near])
        stages.append(
            Shots(
                dils, windows, step, c, place_ref, rec_refs[QUAD * (c - near) : QUAD * (c - near + 1)],
                pick_ref, keep_ref, w0_ref, w1_ref, w2_ref, bias_ref, shift_ref, part_ref.at[c - near],
                x2_refs[-1], rec_refs_out[-1],
            )
        )

    def receiver_layer(parts_of, weights, layer, block, group, out_rows):
        y = None
        for other in range(blocks):
            term = dot(jnp.concatenate(parts_of(other), axis=0), weights[block * blocks + other])
            y = term if y is None else y + term
        results = []
        for i, part in enumerate(parts_of(block)):
            q = group * step + i
            keep = jnp.concatenate([keep_ref[2 * block + c, 1, q : q + 1, :] for c in range(2)], axis=1)
            old = part[:, LANES : 2 * LANES].astype(F32)
            new = jnp.maximum(y[i * out_rows : (i + 1) * out_rows] + bias_ref[layer : layer + 1, :], 0.0)
            results.append((old + new) * keep)
        return results

    def third_layer(group):
        def parts_of(block):
            return [
                jnp.concatenate(
                    [
                        x2_refs[2 * block + c][group * step + i, :, e * HALF : (e + 1) * HALF]
                        for e in range(3)
                        for c in range(2)
                    ],
                    axis=1,
                )
                for i in range(step)
            ]

        for block in range(blocks):
            for i, value in enumerate(receiver_layer(parts_of, b3_ref, 2, block, group, span)):
                value = jnp.concatenate(
                    [
                        value[0:window],
                        value[window : window + HALO] * right_ok,
                        value[window + HALO :] * left_ok,
                    ],
                    axis=0,
                )
                x3_ref[block, group * step + i] = shifted(value, dils[3])[0:window]

    def last_layer(group):
        def parts_of(block):
            return [x3_ref[block, group * step + i] for i in range(step)]

        for block in range(blocks):
            for i, value in enumerate(receiver_layer(parts_of, b4_ref, 3, block, group, window)):
                q = group * step + i
                noise = dot_t(ow_ref[...], value.astype(BF16))
                record = jnp.concatenate([rec_refs_out[2 * block + c][q] for c in range(2)], axis=0)
                done = (record + noise).reshape(GROUP, COMPS, window)
                for c in range(2):
                    first = QUAD * couple_of(place_ref, 2 * block + c)
                    out_ref[pl.ds(first, QUAD), q] = done[c * QUAD : (c + 1) * QUAD]

    groups = slots // step
    work = [(stage, group) for group in range(groups) for stage in stages]
    lag = len(stages)
    for t in itertools.chain(staged(work), range(len(work) + 2, len(work) + 2 + 2 * lag)):
        done, rest = divmod(t - 2, lag)
        if rest == 0 and 0 <= done - 1 < groups:
            third_layer(done - 1)
        if rest == 0 and 0 <= done - 2 < groups:
            last_layer(done - 2)


def divisor(value, limit):
    return max(d for d in range(1, limit + 1) if value % d == 0)


def body(
    records,
    lift_weight,
    lift_bias,
    conv_weight,
    conv_bias,
    out_weight,
    live_count,
    trace_node,
    node_owner,
):
    _, comps, nodes, window = records.shape
    holders = lax.axis_size("gather")
    windows = lax.axis_size("tm")
    shots = holders * records.shape[0]
    couples = shots // QUAD
    blocks = couples // 2
    slots = (nodes + holders - 1) // holders
    dils = (1, 4, 2, 8)
    rows = round_up(6 * slots, 16) + round_up(3 * slots, 16)
    span = window + 2 * HALO

    planes = holders // CORES
    vmem = pl.BlockSpec(memory_space=pltpu.VMEM)
    smem = pl.BlockSpec(memory_space=pltpu.SMEM)
    like = jax.ShapeDtypeStruct

    def after(value, other):
        return lax.optimization_barrier((value, other))[0]

    def kernel(function, operands, specs, outs, scratch, limit, flops, name):
        return pl.pallas_call(
            function,
            out_shape=outs,
            in_specs=[smem] + specs,
            out_specs=jax.tree.map(lambda _: vmem, outs),
            scratch_shapes=scratch,
            compiler_params=pltpu.CompilerParams(vmem_limit_bytes=limit << 20),
            cost_estimate=pl.CostEstimate(flops=flops, bytes_accessed=1 << 10, transcendentals=0),
            name=name,
        )(place, *operands)

    place = jnp.stack([lax.axis_index("gather"), lax.axis_index("tm")]).astype(jnp.int32)
    taps = jnp.transpose(conv_weight, (0, 3, 4, 1, 2)).reshape(-1, CH)

    own = records[0]
    even = lax.axis_index("tm") % 2 == 0
    pack = lambda part: jnp.transpose(part, (1, 0, 2)).reshape(nodes, comps * HALO)
    first, last = pack(own[:, :, :HALO]), pack(own[:, :, window - HALO :])
    got = []
    for begin in range(2):
        pairs = [(w, w + 1) for w in range(begin, windows - 1, 2)]
        pairs += [(b, a) for a, b in pairs]
        got.append(lax.ppermute(jnp.where(even == (begin == 0), last, first), "tm", pairs))
    small = [live_count, trace_node, taps, jnp.transpose(lift_weight), lift_bias[None, :], conv_bias]
    raw = small + [node_owner[None, :], own, out_weight]
    raw = [pltpu.with_memory_space_constraint(a, pltpu.HBM) for a in raw]
    half = (taps.shape[0] // 2, CH)
    scratch = [pltpu.SMEM(a.shape, a.dtype) for a in raw[:2]] + [pltpu.VMEM(half, BF16)]
    scratch += [pltpu.VMEM(a.shape, a.dtype) for a in raw[3:7]]
    w0, w1, w2, wide_bias, shift, pick, keep, own, late_taps, out_taps = kernel(
        functools.partial(prep_kernel, dils, slots),
        raw,
        [pl.BlockSpec(memory_space=pltpu.HBM)] * len(raw),
        (
            like((KROWS, 2 * LANES), BF16),
            like((2, LANES, LANES), BF16),
            like((2, LANES, LANES), BF16),
            like((conv_bias.shape[0], LANES), F32),
            like((span, 2 * window), BF16),
            like((shots, rows, nodes), BF16),
            like((couples, 3, 16, HALF), F32),
            like(own.shape, BF16),
            like(half, BF16),
            like(out_weight.shape, BF16),
        ),
        scratch + [pltpu.SemaphoreType.DMA((7,)), pltpu.SemaphoreType.DMA((3,))],
        16,
        10**5,
        "weights",
    )
    right, left = jnp.where(even, got[0], got[1]), jnp.where(even, got[1], got[0])
    sent = jnp.concatenate([own, jnp.concatenate([right, left], axis=1)[None]], axis=0)


    def exchanged(block, distance):
        return lax.ppermute(block, "gather", [(g, g ^ distance) for g in range(holders)])

    near_blocks = [sent, exchanged(sent, CORES)]
    far = [exchanged(sent, CORES * r) for r in range(2, planes)]
    near_blocks.append(exchanged(jnp.stack(near_blocks), 1))

    b3, b4, ow = kernel(
        functools.partial(band_kernel, dils, blocks),
        [late_taps, out_taps],
        [vmem] * 2,
        (
            like((blocks * blocks, 3 * LANES, LANES), BF16),
            like((blocks * blocks, 3 * LANES, LANES), BF16),
            like((GROUP * COMPS, LANES), BF16),
        ),
        [],
        16,
        10**10,
        "bands",
    )

    step = divisor(slots, 5)
    row_stride = round_up(rows, 16) + 8
    x2 = like((slots, span, 3 * HALF), BF16)
    held = like((slots, QUAD * COMPS, window), F32)
    parts = (2, PARTS, row_stride, window)
    operands = [after(pick, ow), keep, w0, w1, w2, wide_bias, shift, *near_blocks]
    near = kernel(
        functools.partial(near_kernel, dils, windows, step),
        operands,
        [vmem] * len(operands),
        (x2, held),
        [pltpu.VMEM(parts, F32)],
        24,
        10**5,
        "near",
    )

    operands = [pick, keep, w0, w1, w2, b3, b4, ow, wide_bias, shift]
    for r in range(0, len(far), 2):
        operands += far[r : r + 2] + [exchanged(after(block, near[1]), 1) for block in far[r : r + 2]]
    operands += near
    out = kernel(
        functools.partial(main_kernel, dils, windows, step, 1),
        operands,
        [vmem] * len(operands),
        like((shots, slots, comps, window), F32),
        [
            pltpu.VMEM((couples - 1, *parts), F32),
            pltpu.VMEM((couples - 1, *x2.shape), BF16),
            pltpu.VMEM((couples - 1, *held.shape), F32),
            pltpu.VMEM((blocks, slots, window, 3 * LANES), BF16),
        ],
        36,
        4 * 10**9,
        "layers",
    )
    return jnp.transpose(out, (0, 2, 1, 3))


def solution(mesh):
    return jax.shard_map(
        body,
        mesh=mesh,
        in_specs=(P("gather", None, None, "tm"), P(), P(), P(), P(), P(), P(), P(), P()),
        out_specs=P(None, None, "gather", "tm"),
        check_vma=False,
    )
```

```python
import functools
import itertools

import jax
import jax.numpy as jnp
from jax import lax
from jax.experimental import pallas as pl
from jax.experimental.pallas import tpu as pltpu
from jax.sharding import PartitionSpec as P

F32 = jnp.float32
BF16 = jnp.bfloat16
CH = 32
CORES = 2
COMPS = 4
GROUP = 8
LANES = GROUP * CH
HALO = 16
QUAD = 4
HALF = QUAD * CH
KROWS = 128
LIFTED = ((0, 0), (0, 1), (1, 1), (1, 0), (0, 2), (1, 2))
PARTS = QUAD * COMPS + 2 * QUAD


def iota(shape, dim):
    return lax.broadcasted_iota(jnp.int32, shape, dim)


def dot(a, b):
    return jnp.dot(a, b, preferred_element_type=F32)


def dot_t(a, b):
    return lax.dot_general(a, b, (((1,), (1,)), ((), ())), preferred_element_type=F32)


def onehot(cond):
    return cond.astype(F32).astype(BF16)


def band_links(dilation, offset):
    return [
        a
        for a in range(3)
        if any(s + GROUP * offset == t + (a - 1) * dilation for s in range(GROUP) for t in range(GROUP))
    ]


def split3(value):
    terms = []
    for _ in range(3):
        term = value.astype(BF16)
        terms.append(term)
        value = value - term.astype(F32)
    return terms


def shot_of(place_ref, n, shots):
    planes = shots // CORES
    plane = place_ref[0] // CORES
    core = place_ref[0] - CORES * plane
    return CORES * (plane ^ (n % planes)) + (core if n < planes else 1 - core)


def couple_of(place_ref, relative):
    return (place_ref[0] // (2 * CORES)) ^ relative


def table_kernel(dils, slots, place_ref, live_ref, trace_ref, owner_ref, pick_ref, keep_ref):
    shots, rows, nodes = pick_ref.shape
    split = round_up(6 * slots, 16)
    me = place_ref[0]

    mine = (owner_ref[...] == me).astype(F32)
    before = onehot(iota((nodes, nodes), 0) < iota((nodes, nodes), 1))
    rank = dot(jnp.broadcast_to(mine, (8, nodes)).astype(BF16), before)[0:1, :]
    node_ids = iota((1, nodes), 1).astype(F32)

    def nodes_of(slot_index):
        held = jnp.where((rank == slot_index.astype(F32)) & (mine > 0.5), 1.0, 0.0)
        node = jnp.sum(held * node_ids, axis=1, keepdims=True)
        there = jnp.sum(held, axis=1, keepdims=True)
        return jnp.where(there > 0.5, node, -1.0e6).astype(jnp.int32)

    row_id = iota((rows, nodes), 0)
    late = row_id >= split
    row_id = jnp.where(late, row_id - split, row_id)
    tap = jnp.zeros((rows, nodes), jnp.int32)
    for m in range(1, 7):
        tap = tap + (row_id >= m * slots).astype(jnp.int32)
    second = (tap >= 3).astype(jnp.int32)
    shift = dils[0] * (tap - 3 * second - 1) + jnp.where(late, 0, dils[1] * (2 * second - 1))
    target = nodes_of(row_id - slots * tap)
    target = jnp.where(tap >= jnp.where(late, 3, 6), -1000000, target + shift)

    node_lane = iota((rows, nodes), 1)
    for n in range(shots):
        s = shot_of(place_ref, n, shots)
        pick_ref[n] = onehot((node_lane == target - trace_ref[s, 0]) & (node_lane < live_ref[s]))

    slot_rows = keep_ref.shape[2]
    own_node = nodes_of(iota((slot_rows, nodes), 0))
    shot_lane = iota((slot_rows, HALF), 1) >> 5
    for c in range(shots // QUAD):
        base = QUAD * couple_of(place_ref, c)
        for b in range(3):
            first = jnp.zeros((slot_rows, HALF), jnp.int32)
            count = jnp.zeros((slot_rows, HALF), jnp.int32)
            for w in range(QUAD):
                at = shot_lane == (w if b == 1 else w ^ 2)
                first = jnp.where(at, trace_ref[base + w, 0], first)
                count = jnp.where(at, live_ref[base + w], count)
            trace = own_node + dils[1] * (b - 1) - first
            keep_ref[c, b] = ((trace >= 0) & (trace < count)).astype(F32)


def started(sources, places, sems):
    copies = [pltpu.make_async_copy(a, b, sems.at[n]) for n, (a, b) in enumerate(zip(sources, places))]
    for copy in copies:
        copy.start()
    return copies


def prep_kernel(dils, slots, place_ref, *refs):
    w0_ref, w1_ref, w2_ref, wide_bias_ref, shift_ref, pick_ref, keep_ref = refs[9:16]
    half = refs[2].shape[0] // 2
    passed = started((refs[7], refs[2].at[half : 2 * half], refs[8]), refs[16:19], refs[27])
    live_ref, trace_ref, cw_ref, lift_ref, lift_bias_ref, bias_ref, owner_ref = refs[19:26]
    sources = (*refs[:2], refs[2].at[0:half], *refs[3:7])
    for copy in started(sources, refs[19:26], refs[26]):
        copy.wait()
    table_kernel(dils, slots, place_ref, live_ref, trace_ref, owner_ref, pick_ref, keep_ref)

    rows8 = [lift_ref[...].astype(F32)] + [term.astype(F32) for term in split3(lift_bias_ref[...])]
    table = jnp.concatenate(rows8 + [jnp.zeros((1, CH), F32)], axis=0).astype(BF16)
    data_rows = 3 * QUAD * COMPS
    r8 = iota((KROWS, 8), 0)
    part = jnp.where(r8 < data_rows, r8 & (COMPS - 1), COMPS + ((r8 >> 2) & 3))
    values = dot(onehot((part == iota((KROWS, 8), 1)) & (r8 < 2 * data_rows)), table).astype(BF16)
    wide = iota((CH, 3 * HALF), 1)
    spread = onehot(iota((CH, 3 * HALF), 0) == (wide & 31))
    rr = iota((KROWS, 3 * HALF), 0)
    cc = iota((KROWS, 3 * HALF), 1)
    row_node = jnp.where(rr < data_rows, rr >> 4, (rr - data_rows) >> 4)
    row_shot = jnp.where(rr < data_rows, rr >> 2, rr) & (QUAD - 1)
    node = sum(jnp.where((cc >> 6) == y, LIFTED[y][1], 0) for y in range(6))
    pair = sum(jnp.where((cc >> 6) == y, LIFTED[y][0], 0) for y in range(6))
    same = (row_node == node) & (row_shot == 2 * pair + ((cc >> 5) & 1)) & (rr < 2 * data_rows)
    w0_ref[...] = jnp.where(same, dot(values, spread), 0.0).astype(BF16)

    widen = onehot((iota((LANES, CH), 0) & 31) == iota((LANES, CH), 1))
    kr = iota((LANES, LANES), 0)
    kc = iota((LANES, LANES), 1)
    same_shot = ((kr >> 5) & 1) == ((kc >> 5) & 1)
    sr = iota((3 * CH, LANES), 0)
    sc = iota((3 * CH, LANES), 1)
    for layer, ref in ((0, w1_ref), (1, w2_ref)):
        base = 3 * layer
        tall = [
            dot_t(widen, cw_ref[(base + a) * 3 * CH : (base + a + 1) * 3 * CH, :]).astype(BF16)
            for a in range(3)
        ]
        for odd, (k_taps, n_taps) in enumerate((((0, 1, 2, 3), (0, 1, 3, 2)), ((1, 0, 3, 2), (1, 0, 2, 3)))):
            place = sum(jnp.where((sc >> 6) == y, n_taps[y], 0) for y in range(4))
            spread2 = onehot(((sr >> 5) == place) & ((sr & 31) == (sc & 31)))
            total = jnp.zeros((LANES, LANES), F32)
            for x in range(4):
                if k_taps[x] < 3:
                    total = jnp.where(((kr >> 6) == x) & same_shot, dot(tall[k_taps[x]], spread2), total)
            ref[odd] = total.astype(BF16)

    span = shift_ref.shape[0]
    window = span - 2 * HALO
    source = iota(shift_ref.shape, 0)
    source = jnp.where(source < window + HALO, source, source + window // 2 - HALO)
    shift_ref[...] = onehot(iota(shift_ref.shape, 1) == source)

    tile = onehot(iota((CH, LANES), 0) == (iota((CH, LANES), 1) & 31))
    wide_bias_ref[...] = sum(dot(term, tile) for term in split3(bias_ref[...]))
    for copy in passed:
        copy.wait()


def band_kernel(dils, blocks, place_ref, *refs):
    cw_ref, out_w_ref, b3_ref, b4_ref, ow_ref = refs
    widen = onehot((iota((LANES, CH), 0) & 31) == iota((LANES, CH), 1))

    er = iota((3 * CH, 3 * LANES), 0)
    ec = iota((3 * CH, 3 * LANES), 1)
    spread3 = onehot(((er >> 5) == (ec >> 8)) & ((er & 31) == (ec & 31)))
    row_lane = iota((LANES, 3 * LANES), 0)
    col_lane = iota((LANES, 3 * LANES), 1) & (LANES - 1)

    def shots_in(lane, block):
        couple = jnp.where(lane < HALF, couple_of(place_ref, 2 * block), couple_of(place_ref, 2 * block + 1))
        return QUAD * couple + ((lane >> 5) & (QUAD - 1))

    def expanded(layer, a):
        base = ((layer - 2) * 3 + a) * 3 * CH
        return dot(dot_t(widen, cw_ref[base : base + 3 * CH, :]).astype(BF16), spread3)

    for layer, ref in ((2, b3_ref), (3, b4_ref)):
        linked_taps = band_links(dils[layer], 0) if blocks == 1 else range(3)
        for out_block in range(blocks):
            for in_block in range(blocks):
                total = jnp.zeros((LANES, 3 * LANES), F32)
                for a in linked_taps:
                    reach = shots_in(col_lane, out_block) + (a - 1) * dils[layer]
                    total = total + jnp.where(shots_in(row_lane, in_block) == reach, expanded(layer, a), 0.0)
                for e in range(3):
                    ref[out_block * blocks + in_block, e * LANES : (e + 1) * LANES, :] = total[
                        :, e * LANES : (e + 1) * LANES
                    ].astype(BF16)

    rows = GROUP * COMPS
    pick = onehot((iota((rows, COMPS), 0) & (COMPS - 1)) == iota((rows, COMPS), 1))
    mine = dot(pick, out_w_ref[...]).astype(BF16)
    tile = onehot(iota((CH, LANES), 0) == (iota((CH, LANES), 1) & 31))
    same = (iota((rows, LANES), 0) >> 2) == (iota((rows, LANES), 1) >> 5)
    ow_ref[...] = jnp.where(same, dot(mine, tile), 0.0).astype(BF16)


def round_up(value, unit):
    return -(-value // unit) * unit


def shifted(value, dilation):
    span = value.shape[0]
    return jnp.concatenate(
        [
            pltpu.roll(value, dilation, axis=0).astype(BF16),
            value.astype(BF16),
            pltpu.roll(value, span - dilation, axis=0).astype(BF16),
        ],
        axis=1,
    )


class Shots:
    def __init__(
        self, dils, windows, step, couple, place_ref, recs, pick_ref, keep_ref, w0_ref, w1_ref, w2_ref,
        bias_ref, shift_ref, part_ref, x2_ref, rec_out_ref,
    ):
        self.dils, self.step, self.couple = dils, step, couple
        self.keep_ref, self.w0_ref, self.w1_ref, self.w2_ref = keep_ref, w0_ref, w1_ref, w2_ref
        self.bias_ref, self.shift_ref, self.x2_ref = bias_ref, shift_ref, x2_ref
        shots, rows, nodes = pick_ref.shape
        planes = shots // CORES
        self.slots = slots = x2_ref.shape[0]
        self.window = window = part_ref.shape[-1]
        self.rows, self.split = part_ref.shape[2], round_up(6 * slots, 16)
        self.span = window + 2 * HALO
        at = place_ref[1]
        self.right_ok = (at < windows - 1).astype(F32)
        self.left_ok = (at > 0).astype(F32)
        self.low_half = iota((self.span, HALF), 1) < CH * CORES

        lane = iota((nodes, 2 * window), 1)
        all_ok = jnp.where(
            lane < window, 1.0, jnp.where(lane < window + window // 2, self.right_ok, self.left_ok)
        ).astype(BF16)

        def put(part, swapped, value):
            for half in range(2):
                lanes = value[:, half * window : (half + 1) * window]
                part_ref[half, part, 0 : self.split] = lanes[0 : self.split]
                part_ref[half, swapped, self.split : rows] = lanes[self.split : rows]

        for x, rec_ref in enumerate(recs):
            n = 2 * couple + x % 2 + (planes if x >= 2 else 0)
            within = shot_of(place_ref, n, shots) & (QUAD - 1)
            edge = rec_ref[COMPS].astype(F32)
            for k in range(COMPS):
                turned = edge if k == 0 else pltpu.roll(edge, window - HALO * k, axis=1)
                both = jnp.concatenate([rec_ref[k], turned.astype(BF16)], axis=1)
                put(within * COMPS + k, (within ^ 2) * COMPS + k, dot(pick_ref[n], both))
            alive = dot(pick_ref[n], all_ok)
            for copy in range(2):
                first = QUAD * COMPS + QUAD * copy
                put(first + within, first + (within ^ 2), alive)

        self.half_rows = part_ref.shape[1] * self.rows
        self.part2 = part_ref.reshape(2 * self.half_rows, window)
        for q in range(slots):
            first = self.split + slots + q
            for half in range(2):
                pair = self.part2[pl.ds(first + (1 - half) * 8 * self.rows, 8, stride=self.rows), :]
                rec_out_ref[q, half * 8 : (half + 1) * 8] = pair

    def inside(self, value):
        w = self.window
        return jnp.concatenate(
            [value[0:w], value[w : w + HALO] * self.right_ok, value[w + HALO :] * self.left_ok], axis=0
        )

    def item_rows(self, q, b):
        start = (3 * (b // 2) * self.slots if b != 1 else self.split) + q
        halves = []
        for half in range(2):
            base = half * self.half_rows + start
            flags = base + QUAD * COMPS * self.rows
            pieces = [
                self.part2[pl.ds(base + a * self.slots, QUAD * COMPS, stride=self.rows), :] for a in range(3)
            ]
            for a in range(3):
                alive = self.part2[pl.ds(flags + a * self.slots, 2 * QUAD, stride=self.rows), :]
                pieces += [alive, alive]
            pieces.append(jnp.zeros((KROWS - 6 * QUAD * COMPS, self.window), F32))
            halves.append(jnp.concatenate(pieces, axis=0).astype(BF16))
        return jnp.concatenate(halves, axis=1)

    def items(self, group):
        return [(group * self.step + i, b) for i in range(self.step) for b in range(3)]

    def first_inputs(self, group):
        items = self.items(group)
        lhs = []
        for n in range(0, len(items), 2):
            some = jnp.concatenate([self.item_rows(q, b) for q, b in items[n : n + 2]], axis=0)
            moved = dot_t(self.shift_ref[...], some).astype(BF16)
            lhs += [moved[:, m : m + KROWS] for m in range(0, moved.shape[1], KROWS)]
        lifted = dot(jnp.concatenate(lhs, axis=0), self.w0_ref[...]).astype(BF16)
        own, other, shared = (lifted[:, m * HALF : (m + 1) * HALF] for m in range(3))
        return jnp.concatenate([own, shared], axis=1), jnp.concatenate([other, shared], axis=1)

    def taps_added(self, even, odd, dilation):
        mid = jnp.where(self.low_half, odd[:, 0:HALF], even[:, 0:HALF])
        late = jnp.where(self.low_half, odd[:, HALF:], even[:, HALF:])
        early = pltpu.roll(jnp.where(self.low_half, even[:, 0:HALF], odd[:, 0:HALF]), HALF // 2, axis=1)
        return (
            pltpu.roll(early, dilation, axis=0) + mid + pltpu.roll(late, self.span - dilation, axis=0)
        )

    def first_layer(self, group, even, odd):
        y_even, y_odd = dot(even, self.w1_ref[0]), dot(odd, self.w1_ref[1])
        x1 = []
        for n, (q, b) in enumerate(self.items(group)):
            at = slice(n * self.span, (n + 1) * self.span)
            old = jnp.where(self.low_half, odd[at, 0:HALF].astype(F32), even[at, 0:HALF].astype(F32))
            total = self.taps_added(y_even[at], y_odd[at], self.dils[0])
            new = jnp.maximum(total + self.bias_ref[0:1, 0:HALF], 0.0)
            x1.append(self.inside((old + new) * self.keep_ref[self.couple, b, q : q + 1, :]))
        even, odd, own = [], [], []
        for i in range(self.step):
            t0, t1, t2 = x1[3 * i : 3 * i + 3]
            t2 = t2.astype(BF16)
            even.append(jnp.concatenate([jnp.where(self.low_half, t0, t1).astype(BF16), t2], axis=1))
            odd.append(jnp.concatenate([jnp.where(self.low_half, t1, t0).astype(BF16), t2], axis=1))
            own.append(t1.astype(BF16))
        return jnp.concatenate(even, axis=0), jnp.concatenate(odd, axis=0), own

    def second_layer(self, group, even, odd, own):
        even, odd = dot(even, self.w2_ref[0]), dot(odd, self.w2_ref[1])
        for i in range(self.step):
            q = group * self.step + i
            at = slice(i * self.span, (i + 1) * self.span)
            total = self.taps_added(even[at], odd[at], self.dils[1])
            new = jnp.maximum(total + self.bias_ref[1:2, 0:HALF], 0.0)
            x2 = (own[i].astype(F32) + new) * self.keep_ref[self.couple, 1, q : q + 1, :]
            self.x2_ref[q] = shifted(self.inside(x2), self.dils[2])


def staged(work):
    inputs, middle = {}, {}
    for t in range(len(work) + 2):
        if t < len(work):
            stage, group = work[t]
            inputs[t] = stage.first_inputs(group)
        if 0 <= t - 1 < len(work):
            stage, group = work[t - 1]
            middle[t - 1] = stage.first_layer(group, *inputs.pop(t - 1))
        if 0 <= t - 2:
            stage, group = work[t - 2]
            stage.second_layer(group, *middle.pop(t - 2))
        yield t


def near_kernel(dils, windows, step, place_ref, *refs):
    pick_ref, keep_ref, w0_ref, w1_ref, w2_ref, bias_ref, shift_ref = refs[:7]
    recs = [refs[7], refs[8], refs[9].at[0], refs[9].at[1]]
    x2_ref, rec_out_ref, part_ref = refs[10:]
    stage = Shots(
        dils, windows, step, 0, place_ref, recs, pick_ref, keep_ref, w0_ref, w1_ref, w2_ref,
        bias_ref, shift_ref, part_ref, x2_ref, rec_out_ref,
    )
    for _ in staged([(stage, group) for group in range(x2_ref.shape[0] // step)]):
        pass


def main_kernel(dils, windows, step, near, place_ref, *refs):
    shots = refs[0].shape[0]
    couples = shots // QUAD
    pick_ref, keep_ref, w0_ref, w1_ref, w2_ref, b3_ref, b4_ref, ow_ref, bias_ref, shift_ref = refs[:10]
    refs = refs[10:]
    rec_refs, refs = refs[: QUAD * (couples - near)], refs[QUAD * (couples - near) :]
    done_refs, refs = refs[: 2 * near], refs[2 * near :]
    out_ref, part_ref, x2_all, rec_all, x3_ref = refs
    blocks = couples // 2
    slots, window = out_ref.shape[1], out_ref.shape[3]
    span = window + 2 * HALO
    right_ok = (place_ref[1] < windows - 1).astype(F32)
    left_ok = (place_ref[1] > 0).astype(F32)

    stages = []
    x2_refs, rec_refs_out = list(done_refs[0::2]), list(done_refs[1::2])
    for c in range(near, couples):
        x2_refs.append(x2_all.at[c - near])
        rec_refs_out.append(rec_all.at[c - near])
        stages.append(
            Shots(
                dils, windows, step, c, place_ref, rec_refs[QUAD * (c - near) : QUAD * (c - near + 1)],
                pick_ref, keep_ref, w0_ref, w1_ref, w2_ref, bias_ref, shift_ref, part_ref.at[c - near],
                x2_refs[-1], rec_refs_out[-1],
            )
        )

    def receiver_layer(parts_of, weights, layer, block, group, out_rows):
        y = None
        for other in range(blocks):
            term = dot(jnp.concatenate(parts_of(other), axis=0), weights[block * blocks + other])
            y = term if y is None else y + term
        results = []
        for i, part in enumerate(parts_of(block)):
            q = group * step + i
            keep = jnp.concatenate([keep_ref[2 * block + c, 1, q : q + 1, :] for c in range(2)], axis=1)
            old = part[:, LANES : 2 * LANES].astype(F32)
            new = jnp.maximum(y[i * out_rows : (i + 1) * out_rows] + bias_ref[layer : layer + 1, :], 0.0)
            results.append((old + new) * keep)
        return results

    def third_layer(group):
        def parts_of(block):
            return [
                jnp.concatenate(
                    [
                        x2_refs[2 * block + c][group * step + i, :, e * HALF : (e + 1) * HALF]
                        for e in range(3)
                        for c in range(2)
                    ],
                    axis=1,
                )
                for i in range(step)
            ]

        for block in range(blocks):
            for i, value in enumerate(receiver_layer(parts_of, b3_ref, 2, block, group, span)):
                value = jnp.concatenate(
                    [
                        value[0:window],
                        value[window : window + HALO] * right_ok,
                        value[window + HALO :] * left_ok,
                    ],
                    axis=0,
                )
                x3_ref[block, group * step + i] = shifted(value, dils[3])[0:window]

    def last_layer(group):
        def parts_of(block):
            return [x3_ref[block, group * step + i] for i in range(step)]

        for block in range(blocks):
            for i, value in enumerate(receiver_layer(parts_of, b4_ref, 3, block, group, window)):
                q = group * step + i
                noise = dot_t(ow_ref[...], value.astype(BF16))
                record = jnp.concatenate([rec_refs_out[2 * block + c][q] for c in range(2)], axis=0)
                done = (record + noise).reshape(GROUP, COMPS, window)
                for c in range(2):
                    first = QUAD * couple_of(place_ref, 2 * block + c)
                    out_ref[pl.ds(first, QUAD), q] = done[c * QUAD : (c + 1) * QUAD]

    groups = slots // step
    work = [(stage, group) for group in range(groups) for stage in stages]
    lag = len(stages)
    for t in itertools.chain(staged(work), range(len(work) + 2, len(work) + 2 + 2 * lag)):
        done, rest = divmod(t - 2, lag)
        if rest == 0 and 0 <= done - 1 < groups:
            third_layer(done - 1)
        if rest == 0 and 0 <= done - 2 < groups:
            last_layer(done - 2)


def divisor(value, limit):
    return max(d for d in range(1, limit + 1) if value % d == 0)


def body(
    records,
    lift_weight,
    lift_bias,
    conv_weight,
    conv_bias,
    out_weight,
    live_count,
    trace_node,
    node_owner,
):
    _, comps, nodes, window = records.shape
    holders = lax.axis_size("gather")
    windows = lax.axis_size("tm")
    shots = holders * records.shape[0]
    couples = shots // QUAD
    blocks = couples // 2
    slots = (nodes + holders - 1) // holders
    dils = (1, 4, 2, 8)
    rows = round_up(6 * slots, 16) + round_up(3 * slots, 16)
    span = window + 2 * HALO

    planes = holders // CORES
    vmem = pl.BlockSpec(memory_space=pltpu.VMEM)
    smem = pl.BlockSpec(memory_space=pltpu.SMEM)
    like = jax.ShapeDtypeStruct

    def after(value, other):
        return lax.optimization_barrier((value, other))[0]

    def kernel(function, operands, specs, outs, scratch, limit, flops, name):
        return pl.pallas_call(
            function,
            out_shape=outs,
            in_specs=[smem] + specs,
            out_specs=jax.tree.map(lambda _: vmem, outs),
            scratch_shapes=scratch,
            compiler_params=pltpu.CompilerParams(vmem_limit_bytes=limit << 20),
            cost_estimate=pl.CostEstimate(flops=flops, bytes_accessed=1 << 10, transcendentals=0),
            name=name,
        )(place, *operands)

    place = jnp.stack([lax.axis_index("gather"), lax.axis_index("tm")]).astype(jnp.int32)
    taps = jnp.transpose(conv_weight, (0, 3, 4, 1, 2)).reshape(-1, CH)

    own = records[0]
    even = lax.axis_index("tm") % 2 == 0
    pack = lambda part: jnp.transpose(part, (1, 0, 2)).reshape(nodes, comps * HALO)
    first, last = pack(own[:, :, :HALO]), pack(own[:, :, window - HALO :])
    got = []
    for begin in range(2):
        pairs = [(w, w + 1) for w in range(begin, windows - 1, 2)]
        pairs += [(b, a) for a, b in pairs]
        got.append(lax.ppermute(jnp.where(even == (begin == 0), last, first), "tm", pairs))
    small = [live_count, trace_node, taps, jnp.transpose(lift_weight), lift_bias[None, :], conv_bias]
    raw = small + [node_owner[None, :], own, out_weight]
    raw = [pltpu.with_memory_space_constraint(a, pltpu.HBM) for a in raw]
    half = (taps.shape[0] // 2, CH)
    scratch = [pltpu.SMEM(a.shape, a.dtype) for a in raw[:2]] + [pltpu.VMEM(half, BF16)]
    scratch += [pltpu.VMEM(a.shape, a.dtype) for a in raw[3:7]]
    w0, w1, w2, wide_bias, shift, pick, keep, own, late_taps, out_taps = kernel(
        functools.partial(prep_kernel, dils, slots),
        raw,
        [pl.BlockSpec(memory_space=pltpu.HBM)] * len(raw),
        (
            like((KROWS, 3 * HALF), BF16),
            like((2, LANES, LANES), BF16),
            like((2, LANES, LANES), BF16),
            like((conv_bias.shape[0], LANES), F32),
            like((span, 2 * window), BF16),
            like((shots, rows, nodes), BF16),
            like((couples, 3, 16, HALF), F32),
            like(own.shape, BF16),
            like(half, BF16),
            like(out_weight.shape, BF16),
        ),
        scratch + [pltpu.SemaphoreType.DMA((7,)), pltpu.SemaphoreType.DMA((3,))],
        16,
        10**5,
        "weights",
    )
    right, left = jnp.where(even, got[0], got[1]), jnp.where(even, got[1], got[0])
    sent = jnp.concatenate([own, jnp.concatenate([right, left], axis=1)[None]], axis=0)


    def exchanged(block, distance):
        return lax.ppermute(block, "gather", [(g, g ^ distance) for g in range(holders)])

    near_blocks = [sent, exchanged(sent, CORES)]
    far = [exchanged(sent, CORES * r) for r in range(2, planes)]
    near_blocks.append(exchanged(jnp.stack(near_blocks), 1))

    b3, b4, ow = kernel(
        functools.partial(band_kernel, dils, blocks),
        [late_taps, out_taps],
        [vmem] * 2,
        (
            like((blocks * blocks, 3 * LANES, LANES), BF16),
            like((blocks * blocks, 3 * LANES, LANES), BF16),
            like((GROUP * COMPS, LANES), BF16),
        ),
        [],
        16,
        10**10,
        "bands",
    )

    step = divisor(slots, 5)
    row_stride = round_up(rows, 16) + 8
    x2 = like((slots, span, 3 * HALF), BF16)
    held = like((slots, QUAD * COMPS, window), F32)
    parts = (2, PARTS, row_stride, window)
    operands = [after(pick, ow), keep, w0, w1, w2, wide_bias, shift, *near_blocks]
    near = kernel(
        functools.partial(near_kernel, dils, windows, step),
        operands,
        [vmem] * len(operands),
        (x2, held),
        [pltpu.VMEM(parts, F32)],
        24,
        10**5,
        "near",
    )

    operands = [pick, keep, w0, w1, w2, b3, b4, ow, wide_bias, shift]
    for r in range(0, len(far), 2):
        operands += far[r : r + 2] + [exchanged(after(block, near[1]), 1) for block in far[r : r + 2]]
    operands += near
    out = kernel(
        functools.partial(main_kernel, dils, windows, step, 1),
        operands,
        [vmem] * len(operands),
        like((shots, slots, comps, window), F32),
        [
            pltpu.VMEM((couples - 1, *parts), F32),
            pltpu.VMEM((couples - 1, *x2.shape), BF16),
            pltpu.VMEM((couples - 1, *held.shape), F32),
            pltpu.VMEM((blocks, slots, window, 3 * LANES), BF16),
        ],
        36,
        4 * 10**9,
        "layers",
    )
    return jnp.transpose(out, (0, 2, 1, 3))


def solution(mesh):
    return jax.shard_map(
        body,
        mesh=mesh,
        in_specs=(P("gather", None, None, "tm"), P(), P(), P(), P(), P(), P(), P(), P()),
        out_specs=P(None, None, "gather", "tm"),
        check_vma=False,
    )
```

```python
import functools
import itertools

import jax
import jax.numpy as jnp
from jax import lax
from jax.experimental import pallas as pl
from jax.experimental.pallas import tpu as pltpu
from jax.sharding import PartitionSpec as P

F32 = jnp.float32
BF16 = jnp.bfloat16
CH = 32
CORES = 2
COMPS = 4
GROUP = 8
LANES = GROUP * CH
HALO = 16
QUAD = 4
HALF = QUAD * CH
KROWS = 128
LIFTED = ((0, 0), (0, 1), (1, 1), (1, 0), (0, 2), (1, 2))
PARTS = QUAD * COMPS + 2 * QUAD


def iota(shape, dim):
    return lax.broadcasted_iota(jnp.int32, shape, dim)


def dot(a, b):
    return jnp.dot(a, b, preferred_element_type=F32)


def dot_t(a, b):
    return lax.dot_general(a, b, (((1,), (1,)), ((), ())), preferred_element_type=F32)


def onehot(cond):
    return cond.astype(F32).astype(BF16)


def band_links(dilation, offset):
    return [
        a
        for a in range(3)
        if any(s + GROUP * offset == t + (a - 1) * dilation for s in range(GROUP) for t in range(GROUP))
    ]


def split3(value):
    terms = []
    for _ in range(3):
        term = value.astype(BF16)
        terms.append(term)
        value = value - term.astype(F32)
    return terms


def shot_of(place_ref, n, shots):
    planes = shots // CORES
    plane = place_ref[0] // CORES
    core = place_ref[0] - CORES * plane
    return CORES * (plane ^ (n % planes)) + (core if n < planes else 1 - core)


def couple_of(place_ref, relative):
    return (place_ref[0] // (2 * CORES)) ^ relative


def table_kernel(dils, slots, place_ref, live_ref, trace_ref, owner_ref, pick_ref, keep_ref):
    shots, rows, nodes = pick_ref.shape
    split = round_up(6 * slots, 16)
    me = place_ref[0]

    mine = (owner_ref[...] == me).astype(F32)
    before = onehot(iota((nodes, nodes), 0) < iota((nodes, nodes), 1))
    rank = dot(jnp.broadcast_to(mine, (8, nodes)).astype(BF16), before)[0:1, :]
    node_ids = iota((1, nodes), 1).astype(F32)

    def nodes_of(slot_index):
        held = jnp.where((rank == slot_index.astype(F32)) & (mine > 0.5), 1.0, 0.0)
        node = jnp.sum(held * node_ids, axis=1, keepdims=True)
        there = jnp.sum(held, axis=1, keepdims=True)
        return jnp.where(there > 0.5, node, -1.0e6).astype(jnp.int32)

    row_id = iota((rows, nodes), 0)
    late = row_id >= split
    row_id = jnp.where(late, row_id - split, row_id)
    tap = jnp.zeros((rows, nodes), jnp.int32)
    for m in range(1, 7):
        tap = tap + (row_id >= m * slots).astype(jnp.int32)
    second = (tap >= 3).astype(jnp.int32)
    shift = dils[0] * (tap - 3 * second - 1) + jnp.where(late, 0, dils[1] * (2 * second - 1))
    target = nodes_of(row_id - slots * tap)
    target = jnp.where(tap >= jnp.where(late, 3, 6), -1000000, target + shift)

    node_lane = iota((rows, nodes), 1)
    for n in range(shots):
        s = shot_of(place_ref, n, shots)
        pick_ref[n] = onehot((node_lane == target - trace_ref[s, 0]) & (node_lane < live_ref[s]))

    slot_rows = keep_ref.shape[2]
    own_node = nodes_of(iota((slot_rows, nodes), 0))
    shot_lane = iota((slot_rows, HALF), 1) >> 5
    for c in range(shots // QUAD):
        base = QUAD * couple_of(place_ref, c)
        for b in range(3):
            first = jnp.zeros((slot_rows, HALF), jnp.int32)
            count = jnp.zeros((slot_rows, HALF), jnp.int32)
            for w in range(QUAD):
                at = shot_lane == (w if b == 1 else w ^ 2)
                first = jnp.where(at, trace_ref[base + w, 0], first)
                count = jnp.where(at, live_ref[base + w], count)
            trace = own_node + dils[1] * (b - 1) - first
            keep_ref[c, b] = ((trace >= 0) & (trace < count)).astype(F32)


def started(sources, places, sems):
    copies = [pltpu.make_async_copy(a, b, sems.at[n]) for n, (a, b) in enumerate(zip(sources, places))]
    for copy in copies:
        copy.start()
    return copies


def prep_kernel(dils, slots, place_ref, *refs):
    w0_ref, w1_ref, w2_ref, wide_bias_ref, shift_ref, pick_ref, keep_ref = refs[9:16]
    half = refs[2].shape[0] // 2
    passed = started((refs[7], refs[2].at[half : 2 * half], refs[8]), refs[16:19], refs[27])
    live_ref, trace_ref, cw_ref, lift_ref, lift_bias_ref, bias_ref, owner_ref = refs[19:26]
    sources = (*refs[:2], refs[2].at[0:half], *refs[3:7])
    for copy in started(sources, refs[19:26], refs[26]):
        copy.wait()
    table_kernel(dils, slots, place_ref, live_ref, trace_ref, owner_ref, pick_ref, keep_ref)

    rows8 = [lift_ref[...].astype(F32)] + [term.astype(F32) for term in split3(lift_bias_ref[...])]
    table = jnp.concatenate(rows8 + [jnp.zeros((1, CH), F32)], axis=0).astype(BF16)
    data_rows = 3 * QUAD * COMPS
    r8 = iota((KROWS, 8), 0)
    part = jnp.where(r8 < data_rows, r8 & (COMPS - 1), COMPS + ((r8 >> 2) & 3))
    values = dot(onehot((part == iota((KROWS, 8), 1)) & (r8 < 2 * data_rows)), table).astype(BF16)
    wide = iota((CH, 3 * HALF), 1)
    spread = onehot(iota((CH, 3 * HALF), 0) == (wide & 31))
    rr = iota((KROWS, 3 * HALF), 0)
    cc = iota((KROWS, 3 * HALF), 1)
    row_node = jnp.where(rr < data_rows, rr >> 4, (rr - data_rows) >> 4)
    row_shot = jnp.where(rr < data_rows, rr >> 2, rr) & (QUAD - 1)
    node = sum(jnp.where((cc >> 6) == y, LIFTED[y][1], 0) for y in range(6))
    pair = sum(jnp.where((cc >> 6) == y, LIFTED[y][0], 0) for y in range(6))
    same = (row_node == node) & (row_shot == 2 * pair + ((cc >> 5) & 1)) & (rr < 2 * data_rows)
    w0_ref[...] = jnp.where(same, dot(values, spread), 0.0).astype(BF16)

    widen = onehot((iota((LANES, CH), 0) & 31) == iota((LANES, CH), 1))
    kr = iota((LANES, LANES), 0)
    kc = iota((LANES, LANES), 1)
    same_shot = ((kr >> 5) & 1) == ((kc >> 5) & 1)
    sr = iota((3 * CH, LANES), 0)
    sc = iota((3 * CH, LANES), 1)
    for layer, ref in ((0, w1_ref), (1, w2_ref)):
        base = 3 * layer
        tall = [
            dot_t(widen, cw_ref[(base + a) * 3 * CH : (base + a + 1) * 3 * CH, :]).astype(BF16)
            for a in range(3)
        ]
        for odd, (k_taps, n_taps) in enumerate((((0, 1, 2, 3), (0, 1, 3, 2)), ((1, 0, 3, 2), (1, 0, 2, 3)))):
            place = sum(jnp.where((sc >> 6) == y, n_taps[y], 0) for y in range(4))
            spread2 = onehot(((sr >> 5) == place) & ((sr & 31) == (sc & 31)))
            total = jnp.zeros((LANES, LANES), F32)
            for x in range(4):
                if k_taps[x] < 3:
                    total = jnp.where(((kr >> 6) == x) & same_shot, dot(tall[k_taps[x]], spread2), total)
            ref[odd] = total.astype(BF16)

    span = shift_ref.shape[0]
    window = span - 2 * HALO
    source = iota(shift_ref.shape, 0)
    source = jnp.where(source < window + HALO, source, source + window // 2 - HALO)
    shift_ref[...] = onehot(iota(shift_ref.shape, 1) == source)

    tile = onehot(iota((CH, LANES), 0) == (iota((CH, LANES), 1) & 31))
    wide_bias_ref[...] = sum(dot(term, tile) for term in split3(bias_ref[...]))
    for copy in passed:
        copy.wait()


def band_kernel(dils, blocks, place_ref, *refs):
    cw_ref, out_w_ref, b3_ref, b4_ref, ow_ref = refs
    widen = onehot((iota((LANES, CH), 0) & 31) == iota((LANES, CH), 1))

    er = iota((3 * CH, 3 * LANES), 0)
    ec = iota((3 * CH, 3 * LANES), 1)
    spread3 = onehot(((er >> 5) == (ec >> 8)) & ((er & 31) == (ec & 31)))
    row_lane = iota((LANES, 3 * LANES), 0)
    col_lane = iota((LANES, 3 * LANES), 1) & (LANES - 1)

    def shots_in(lane, block):
        couple = jnp.where(lane < HALF, couple_of(place_ref, 2 * block), couple_of(place_ref, 2 * block + 1))
        return QUAD * couple + ((lane >> 5) & (QUAD - 1))

    def expanded(layer, a):
        base = ((layer - 2) * 3 + a) * 3 * CH
        return dot(dot_t(widen, cw_ref[base : base + 3 * CH, :]).astype(BF16), spread3)

    for layer, ref in ((2, b3_ref), (3, b4_ref)):
        linked_taps = band_links(dils[layer], 0) if blocks == 1 else range(3)
        for out_block in range(blocks):
            for in_block in range(blocks):
                total = jnp.zeros((LANES, 3 * LANES), F32)
                for a in linked_taps:
                    reach = shots_in(col_lane, out_block) + (a - 1) * dils[layer]
                    total = total + jnp.where(shots_in(row_lane, in_block) == reach, expanded(layer, a), 0.0)
                for e in range(3):
                    ref[out_block * blocks + in_block, e * LANES : (e + 1) * LANES, :] = total[
                        :, e * LANES : (e + 1) * LANES
                    ].astype(BF16)

    rows = GROUP * COMPS
    pick = onehot((iota((rows, COMPS), 0) & (COMPS - 1)) == iota((rows, COMPS), 1))
    mine = dot(pick, out_w_ref[...]).astype(BF16)
    tile = onehot(iota((CH, LANES), 0) == (iota((CH, LANES), 1) & 31))
    same = (iota((rows, LANES), 0) >> 2) == (iota((rows, LANES), 1) >> 5)
    ow_ref[...] = jnp.where(same, dot(mine, tile), 0.0).astype(BF16)


def round_up(value, unit):
    return -(-value // unit) * unit


def shifted(value, dilation):
    span = value.shape[0]
    return jnp.concatenate(
        [
            pltpu.roll(value, dilation, axis=0).astype(BF16),
            value.astype(BF16),
            pltpu.roll(value, span - dilation, axis=0).astype(BF16),
        ],
        axis=1,
    )


class Shots:
    def __init__(
        self, dils, windows, step, couple, place_ref, recs, pick_ref, keep_ref, w0_ref, w1_ref, w2_ref,
        bias_ref, shift_ref, part_ref, x2_ref, rec_out_ref,
    ):
        self.dils, self.step, self.couple = dils, step, couple
        self.keep_ref, self.w0_ref, self.w1_ref, self.w2_ref = keep_ref, w0_ref, w1_ref, w2_ref
        self.bias_ref, self.shift_ref, self.x2_ref = bias_ref, shift_ref, x2_ref
        shots, rows, nodes = pick_ref.shape
        planes = shots // CORES
        self.slots = slots = x2_ref.shape[0]
        self.window = window = part_ref.shape[-1]
        self.rows, self.split = part_ref.shape[2], round_up(6 * slots, 16)
        self.span = window + 2 * HALO
        at = place_ref[1]
        self.right_ok = (at < windows - 1).astype(F32)
        self.left_ok = (at > 0).astype(F32)
        self.low_half = iota((self.span, HALF), 1) < CH * CORES

        lane = iota((nodes, 2 * window), 1)
        all_ok = jnp.where(
            lane < window, 1.0, jnp.where(lane < window + window // 2, self.right_ok, self.left_ok)
        ).astype(BF16)

        def put(part, swapped, value):
            for half in range(2):
                lanes = value[:, half * window : (half + 1) * window]
                part_ref[half, part, 0 : self.split] = lanes[0 : self.split]
                part_ref[half, swapped, self.split : rows] = lanes[self.split : rows]

        for x, rec_ref in enumerate(recs):
            n = 2 * couple + x % 2 + (planes if x >= 2 else 0)
            within = shot_of(place_ref, n, shots) & (QUAD - 1)
            edge = rec_ref[COMPS].astype(F32)
            for k in range(COMPS):
                turned = edge if k == 0 else pltpu.roll(edge, window - HALO * k, axis=1)
                both = jnp.concatenate([rec_ref[k], turned.astype(BF16)], axis=1)
                put(within * COMPS + k, (within ^ 2) * COMPS + k, dot(pick_ref[n], both))
            alive = dot(pick_ref[n], all_ok)
            for copy in range(2):
                first = QUAD * COMPS + QUAD * copy
                put(first + within, first + (within ^ 2), alive)

        self.half_rows = part_ref.shape[1] * self.rows
        self.part2 = part_ref.reshape(2 * self.half_rows, window)
        for q in range(slots):
            first = self.split + slots + q
            for half in range(2):
                pair = self.part2[pl.ds(first + (1 - half) * 8 * self.rows, 8, stride=self.rows), :]
                rec_out_ref[q, half * 8 : (half + 1) * 8] = pair

    def inside(self, value):
        w = self.window
        return jnp.concatenate(
            [value[0:w], value[w : w + HALO] * self.right_ok, value[w + HALO :] * self.left_ok], axis=0
        )

    def item_rows(self, q, b):
        start = (3 * (b // 2) * self.slots if b != 1 else self.split) + q
        halves = []
        for half in range(2):
            base = half * self.half_rows + start
            flags = base + QUAD * COMPS * self.rows
            pieces = [
                self.part2[pl.ds(base + a * self.slots, QUAD * COMPS, stride=self.rows), :] for a in range(3)
            ]
            for a in range(3):
                alive = self.part2[pl.ds(flags + a * self.slots, 2 * QUAD, stride=self.rows), :]
                pieces += [alive, alive]
            pieces.append(jnp.zeros((KROWS - 6 * QUAD * COMPS, self.window), F32))
            halves.append(jnp.concatenate(pieces, axis=0).astype(BF16))
        return jnp.concatenate(halves, axis=1)

    def items(self, group):
        return [(group * self.step + i, b) for i in range(self.step) for b in range(3)]

    def first_inputs(self, group):
        items = self.items(group)
        lhs = []
        for n in range(0, len(items), 2):
            some = jnp.concatenate([self.item_rows(q, b) for q, b in items[n : n + 2]], axis=0)
            moved = dot_t(self.shift_ref[...], some).astype(BF16)
            lhs += [moved[:, m : m + KROWS] for m in range(0, moved.shape[1], KROWS)]
        lifted = dot(jnp.concatenate(lhs, axis=0), self.w0_ref[...]).astype(BF16)
        own, other, shared = (lifted[:, m * HALF : (m + 1) * HALF] for m in range(3))
        return jnp.concatenate([own, shared], axis=1), jnp.concatenate([other, shared], axis=1)

    def taps_added(self, even, odd, dilation):
        mid = jnp.where(self.low_half, odd[:, 0:HALF], even[:, 0:HALF])
        late = jnp.where(self.low_half, odd[:, HALF:], even[:, HALF:])
        early = pltpu.roll(jnp.where(self.low_half, even[:, 0:HALF], odd[:, 0:HALF]), HALF // 2, axis=1)
        return (
            pltpu.roll(early, dilation, axis=0) + mid + pltpu.roll(late, self.span - dilation, axis=0)
        )

    def first_layer(self, group, even, odd):
        y_even, y_odd = dot(even, self.w1_ref[0]), dot(odd, self.w1_ref[1])
        x1 = []
        for n, (q, b) in enumerate(self.items(group)):
            at = slice(n * self.span, (n + 1) * self.span)
            old = jnp.where(self.low_half, odd[at, 0:HALF].astype(F32), even[at, 0:HALF].astype(F32))
            total = self.taps_added(y_even[at], y_odd[at], self.dils[0])
            new = jnp.maximum(total + self.bias_ref[0:1, 0:HALF], 0.0)
            x1.append(self.inside((old + new) * self.keep_ref[self.couple, b, q : q + 1, :]))
        even, odd, own = [], [], []
        for i in range(self.step):
            t0, t1, t2 = x1[3 * i : 3 * i + 3]
            t2 = t2.astype(BF16)
            even.append(jnp.concatenate([jnp.where(self.low_half, t0, t1).astype(BF16), t2], axis=1))
            odd.append(jnp.concatenate([jnp.where(self.low_half, t1, t0).astype(BF16), t2], axis=1))
            own.append(t1.astype(BF16))
        return jnp.concatenate(even, axis=0), jnp.concatenate(odd, axis=0), own

    def second_layer(self, group, even, odd, own):
        even, odd = dot(even, self.w2_ref[0]), dot(odd, self.w2_ref[1])
        for i in range(self.step):
            q = group * self.step + i
            at = slice(i * self.span, (i + 1) * self.span)
            total = self.taps_added(even[at], odd[at], self.dils[1])
            new = jnp.maximum(total + self.bias_ref[1:2, 0:HALF], 0.0)
            x2 = (own[i].astype(F32) + new) * self.keep_ref[self.couple, 1, q : q + 1, :]
            self.x2_ref[q] = shifted(self.inside(x2), self.dils[2])


def staged(work):
    inputs, middle = {}, {}
    for t in range(len(work) + 2):
        if t < len(work):
            stage, group = work[t]
            inputs[t] = stage.first_inputs(group)
        if 0 <= t - 1 < len(work):
            stage, group = work[t - 1]
            middle[t - 1] = stage.first_layer(group, *inputs.pop(t - 1))
        if 0 <= t - 2:
            stage, group = work[t - 2]
            stage.second_layer(group, *middle.pop(t - 2))
        yield t


def near_kernel(dils, windows, step, place_ref, *refs):
    pick_ref, keep_ref, w0_ref, w1_ref, w2_ref, bias_ref, shift_ref = refs[:7]
    recs = [refs[7], refs[8], refs[9].at[0], refs[9].at[1]]
    x2_ref, rec_out_ref, part_ref = refs[10:]
    stage = Shots(
        dils, windows, step, 0, place_ref, recs, pick_ref, keep_ref, w0_ref, w1_ref, w2_ref,
        bias_ref, shift_ref, part_ref, x2_ref, rec_out_ref,
    )
    for _ in staged([(stage, group) for group in range(x2_ref.shape[0] // step)]):
        pass


def main_kernel(dils, windows, step, near, place_ref, *refs):
    shots = refs[0].shape[0]
    couples = shots // QUAD
    pick_ref, keep_ref, w0_ref, w1_ref, w2_ref, b3_ref, b4_ref, ow_ref, bias_ref, shift_ref = refs[:10]
    refs = refs[10:]
    rec_refs, refs = refs[: QUAD * (couples - near)], refs[QUAD * (couples - near) :]
    done_refs, refs = refs[: 2 * near], refs[2 * near :]
    out_ref, part_ref, x2_all, rec_all, x3_ref = refs
    blocks = couples // 2
    slots, window = out_ref.shape[1], out_ref.shape[3]
    span = window + 2 * HALO
    right_ok = (place_ref[1] < windows - 1).astype(F32)
    left_ok = (place_ref[1] > 0).astype(F32)

    stages = []
    x2_refs, rec_refs_out = list(done_refs[0::2]), list(done_refs[1::2])
    for c in range(near, couples):
        x2_refs.append(x2_all.at[c - near])
        rec_refs_out.append(rec_all.at[c - near])
        stages.append(
            Shots(
                dils, windows, step, c, place_ref, rec_refs[QUAD * (c - near) : QUAD * (c - near + 1)],
                pick_ref, keep_ref, w0_ref, w1_ref, w2_ref, bias_ref, shift_ref, part_ref.at[c - near],
                x2_refs[-1], rec_refs_out[-1],
            )
        )

    def receiver_layer(parts_of, weights, layer, block, group, out_rows):
        y = None
        for other in range(blocks):
            term = dot(jnp.concatenate(parts_of(other), axis=0), weights[block * blocks + other])
            y = term if y is None else y + term
        results = []
        for i, part in enumerate(parts_of(block)):
            q = group * step + i
            keep = jnp.concatenate([keep_ref[2 * block + c, 1, q : q + 1, :] for c in range(2)], axis=1)
            old = part[:, LANES : 2 * LANES].astype(F32)
            new = jnp.maximum(y[i * out_rows : (i + 1) * out_rows] + bias_ref[layer : layer + 1, :], 0.0)
            results.append((old + new) * keep)
        return results

    def third_layer(group):
        def parts_of(block):
            return [
                jnp.concatenate(
                    [
                        x2_refs[2 * block + c][group * step + i, :, e * HALF : (e + 1) * HALF]
                        for e in range(3)
                        for c in range(2)
                    ],
                    axis=1,
                )
                for i in range(step)
            ]

        for block in range(blocks):
            for i, value in enumerate(receiver_layer(parts_of, b3_ref, 2, block, group, span)):
                value = jnp.concatenate(
                    [
                        value[0:window],
                        value[window : window + HALO] * right_ok,
                        value[window + HALO :] * left_ok,
                    ],
                    axis=0,
                )
                x3_ref[block, group * step + i] = shifted(value, dils[3])[0:window]

    def last_layer(group):
        def parts_of(block):
            return [x3_ref[block, group * step + i] for i in range(step)]

        for block in range(blocks):
            for i, value in enumerate(receiver_layer(parts_of, b4_ref, 3, block, group, window)):
                q = group * step + i
                noise = dot_t(ow_ref[...], value.astype(BF16))
                record = jnp.concatenate([rec_refs_out[2 * block + c][q] for c in range(2)], axis=0)
                done = (record + noise).reshape(GROUP, COMPS, window)
                for c in range(2):
                    first = QUAD * couple_of(place_ref, 2 * block + c)
                    out_ref[pl.ds(first, QUAD), q] = done[c * QUAD : (c + 1) * QUAD]

    groups = slots // step
    work = [(stage, group) for group in range(groups) for stage in stages]
    lag = len(stages)
    for t in itertools.chain(staged(work), range(len(work) + 2, len(work) + 2 + 2 * lag)):
        done, rest = divmod(t - 2, lag)
        if rest == 0 and 0 <= done - 1 < groups:
            third_layer(done - 1)
        if rest == 0 and 0 <= done - 2 < groups:
            last_layer(done - 2)


def divisor(value, limit):
    return max(d for d in range(1, limit + 1) if value % d == 0)


def body(
    records,
    lift_weight,
    lift_bias,
    conv_weight,
    conv_bias,
    out_weight,
    live_count,
    trace_node,
    node_owner,
):
    _, comps, nodes, window = records.shape
    holders = lax.axis_size("gather")
    windows = lax.axis_size("tm")
    shots = holders * records.shape[0]
    couples = shots // QUAD
    blocks = couples // 2
    slots = (nodes + holders - 1) // holders
    dils = (1, 4, 2, 8)
    rows = round_up(6 * slots, 16) + round_up(3 * slots, 16)
    span = window + 2 * HALO

    planes = holders // CORES
    vmem = pl.BlockSpec(memory_space=pltpu.VMEM)
    smem = pl.BlockSpec(memory_space=pltpu.SMEM)
    like = jax.ShapeDtypeStruct

    def after(value, other):
        return lax.optimization_barrier((value, other))[0]

    def kernel(function, operands, specs, outs, scratch, limit, flops, name):
        return pl.pallas_call(
            function,
            out_shape=outs,
            in_specs=[smem] + specs,
            out_specs=jax.tree.map(lambda _: vmem, outs),
            scratch_shapes=scratch,
            compiler_params=pltpu.CompilerParams(vmem_limit_bytes=limit << 20),
            cost_estimate=pl.CostEstimate(flops=flops, bytes_accessed=1 << 10, transcendentals=0),
            name=name,
        )(place, *operands)

    place = jnp.stack([lax.axis_index("gather"), lax.axis_index("tm")]).astype(jnp.int32)
    taps = jnp.transpose(conv_weight, (0, 3, 4, 1, 2)).reshape(-1, CH)

    own = records[0]
    even = lax.axis_index("tm") % 2 == 0
    pack = lambda part: jnp.transpose(part, (1, 0, 2)).reshape(nodes, comps * HALO)
    first, last = pack(own[:, :, :HALO]), pack(own[:, :, window - HALO :])
    got = []
    for begin in range(2):
        pairs = [(w, w + 1) for w in range(begin, windows - 1, 2)]
        pairs += [(b, a) for a, b in pairs]
        got.append(lax.ppermute(jnp.where(even == (begin == 0), last, first), "tm", pairs))
    small = [live_count, trace_node, taps, jnp.transpose(lift_weight), lift_bias[None, :], conv_bias]
    raw = small + [node_owner[None, :], own, out_weight]
    raw = [pltpu.with_memory_space_constraint(a, pltpu.HBM) for a in raw]
    half = (taps.shape[0] // 2, CH)
    scratch = [pltpu.SMEM(a.shape, a.dtype) for a in raw[:2]] + [pltpu.VMEM(half, BF16)]
    scratch += [pltpu.VMEM(a.shape, a.dtype) for a in raw[3:7]]
    w0, w1, w2, wide_bias, shift, pick, keep, own, late_taps, out_taps = kernel(
        functools.partial(prep_kernel, dils, slots),
        raw,
        [pl.BlockSpec(memory_space=pltpu.HBM)] * len(raw),
        (
            like((KROWS, 3 * HALF), BF16),
            like((2, LANES, LANES), BF16),
            like((2, LANES, LANES), BF16),
            like((conv_bias.shape[0], LANES), F32),
            like((span, 2 * window), BF16),
            like((shots, rows, nodes), BF16),
            like((couples, 3, 16, HALF), F32),
            like(own.shape, BF16),
            like(half, BF16),
            like(out_weight.shape, BF16),
        ),
        scratch + [pltpu.SemaphoreType.DMA((7,)), pltpu.SemaphoreType.DMA((3,))],
        16,
        10**5,
        "weights",
    )
    right, left = jnp.where(even, got[0], got[1]), jnp.where(even, got[1], got[0])
    sent = jnp.concatenate([own, jnp.concatenate([right, left], axis=1)[None]], axis=0)


    def exchanged(block, distance):
        return lax.ppermute(block, "gather", [(g, g ^ distance) for g in range(holders)])

    near_blocks = [sent, exchanged(sent, CORES)]
    far = [exchanged(sent, CORES * r) for r in range(2, planes)]
    near_blocks.append(exchanged(jnp.stack(near_blocks), 1))

    b3, b4, ow = kernel(
        functools.partial(band_kernel, dils, blocks),
        [late_taps, out_taps],
        [vmem] * 2,
        (
            like((blocks * blocks, 3 * LANES, LANES), BF16),
            like((blocks * blocks, 3 * LANES, LANES), BF16),
            like((GROUP * COMPS, LANES), BF16),
        ),
        [],
        16,
        10**10,
        "bands",
    )

    step = divisor(slots, 5)
    row_stride = round_up(rows, 16) + 8
    x2 = like((slots, span, 3 * HALF), BF16)
    held = like((slots, QUAD * COMPS, window), F32)
    parts = (2, PARTS + 1, row_stride, window)
    operands = [after(pick, ow), keep, w0, w1, w2, wide_bias, shift, *near_blocks]
    near = kernel(
        functools.partial(near_kernel, dils, windows, step),
        operands,
        [vmem] * len(operands),
        (x2, held),
        [pltpu.VMEM(parts, F32)],
        24,
        10**5,
        "near",
    )

    operands = [pick, keep, w0, w1, w2, b3, b4, ow, wide_bias, shift]
    for r in range(0, len(far), 2):
        operands += far[r : r + 2] + [exchanged(after(block, near[1]), 1) for block in far[r : r + 2]]
    operands += near
    out = kernel(
        functools.partial(main_kernel, dils, windows, step, 1),
        operands,
        [vmem] * len(operands),
        like((shots, slots, comps, window), F32),
        [
            pltpu.VMEM((couples - 1, *parts), F32),
            pltpu.VMEM((couples - 1, *x2.shape), BF16),
            pltpu.VMEM((couples - 1, *held.shape), F32),
            pltpu.VMEM((blocks, slots, window, 3 * LANES), BF16),
        ],
        36,
        4 * 10**9,
        "layers",
    )
    return jnp.transpose(out, (0, 2, 1, 3))


def solution(mesh):
    return jax.shard_map(
        body,
        mesh=mesh,
        in_specs=(P("gather", None, None, "tm"), P(), P(), P(), P(), P(), P(), P(), P()),
        out_specs=P(None, None, "gather", "tm"),
        check_vma=False,
    )
```

```python
import functools
import itertools

import jax
import jax.numpy as jnp
from jax import lax
from jax.experimental import pallas as pl
from jax.experimental.pallas import tpu as pltpu
from jax.sharding import PartitionSpec as P

F32 = jnp.float32
BF16 = jnp.bfloat16
CH = 32
CORES = 2
COMPS = 4
GROUP = 8
LANES = GROUP * CH
HALO = 16
QUAD = 4
HALF = QUAD * CH
KROWS = 128
LIFTED = ((0, 0), (0, 1), (1, 1), (1, 0), (0, 2), (1, 2))
PARTS = QUAD * COMPS + 2 * QUAD


def iota(shape, dim):
    return lax.broadcasted_iota(jnp.int32, shape, dim)


def dot(a, b):
    return jnp.dot(a, b, preferred_element_type=F32)


def dot_t(a, b):
    return lax.dot_general(a, b, (((1,), (1,)), ((), ())), preferred_element_type=F32)


def onehot(cond):
    return cond.astype(F32).astype(BF16)


def band_links(dilation, offset):
    return [
        a
        for a in range(3)
        if any(s + GROUP * offset == t + (a - 1) * dilation for s in range(GROUP) for t in range(GROUP))
    ]


def split3(value):
    terms = []
    for _ in range(3):
        term = value.astype(BF16)
        terms.append(term)
        value = value - term.astype(F32)
    return terms


def shot_of(place_ref, n, shots):
    planes = shots // CORES
    plane = place_ref[0] // CORES
    core = place_ref[0] - CORES * plane
    return CORES * (plane ^ (n % planes)) + (core if n < planes else 1 - core)


def couple_of(place_ref, relative):
    return (place_ref[0] // (2 * CORES)) ^ relative


def table_kernel(dils, slots, place_ref, live_ref, trace_ref, owner_ref, pick_ref, keep_ref):
    shots, rows, nodes = pick_ref.shape
    split = round_up(6 * slots, 16)
    me = place_ref[0]

    mine = (owner_ref[...] == me).astype(F32)
    before = onehot(iota((nodes, nodes), 0) < iota((nodes, nodes), 1))
    rank = dot(jnp.broadcast_to(mine, (8, nodes)).astype(BF16), before)[0:1, :]
    node_ids = iota((1, nodes), 1).astype(F32)

    def nodes_of(slot_index):
        held = jnp.where((rank == slot_index.astype(F32)) & (mine > 0.5), 1.0, 0.0)
        node = jnp.sum(held * node_ids, axis=1, keepdims=True)
        there = jnp.sum(held, axis=1, keepdims=True)
        return jnp.where(there > 0.5, node, -1.0e6).astype(jnp.int32)

    row_id = iota((rows, nodes), 0)
    late = row_id >= split
    row_id = jnp.where(late, row_id - split, row_id)
    tap = jnp.zeros((rows, nodes), jnp.int32)
    for m in range(1, 7):
        tap = tap + (row_id >= m * slots).astype(jnp.int32)
    second = (tap >= 3).astype(jnp.int32)
    shift = dils[0] * (tap - 3 * second - 1) + jnp.where(late, 0, dils[1] * (2 * second - 1))
    target = nodes_of(row_id - slots * tap)
    target = jnp.where(tap >= jnp.where(late, 3, 6), -1000000, target + shift)

    node_lane = iota((rows, nodes), 1)
    for n in range(shots):
        s = shot_of(place_ref, n, shots)
        pick_ref[n] = onehot((node_lane == target - trace_ref[s, 0]) & (node_lane < live_ref[s]))

    slot_rows = keep_ref.shape[2]
    own_node = nodes_of(iota((slot_rows, nodes), 0))
    shot_lane = iota((slot_rows, HALF), 1) >> 5
    for c in range(shots // QUAD):
        base = QUAD * couple_of(place_ref, c)
        for b in range(3):
            first = jnp.zeros((slot_rows, HALF), jnp.int32)
            count = jnp.zeros((slot_rows, HALF), jnp.int32)
            for w in range(QUAD):
                at = shot_lane == (w if b == 1 else w ^ 2)
                first = jnp.where(at, trace_ref[base + w, 0], first)
                count = jnp.where(at, live_ref[base + w], count)
            trace = own_node + dils[1] * (b - 1) - first
            keep_ref[c, b] = ((trace >= 0) & (trace < count)).astype(F32)


def started(sources, places, sems):
    copies = [pltpu.make_async_copy(a, b, sems.at[n]) for n, (a, b) in enumerate(zip(sources, places))]
    for copy in copies:
        copy.start()
    return copies


def prep_kernel(dils, slots, place_ref, *refs):
    w0_ref, w1_ref, w2_ref, wide_bias_ref, shift_ref, pick_ref, keep_ref = refs[9:16]
    half = refs[2].shape[0] // 2
    passed = started((refs[7], refs[2].at[half : 2 * half], refs[8]), refs[16:19], refs[27])
    live_ref, trace_ref, cw_ref, lift_ref, lift_bias_ref, bias_ref, owner_ref = refs[19:26]
    sources = (*refs[:2], refs[2].at[0:half], *refs[3:7])
    for copy in started(sources, refs[19:26], refs[26]):
        copy.wait()
    table_kernel(dils, slots, place_ref, live_ref, trace_ref, owner_ref, pick_ref, keep_ref)

    rows8 = [lift_ref[...].astype(F32)] + [term.astype(F32) for term in split3(lift_bias_ref[...])]
    table = jnp.concatenate(rows8 + [jnp.zeros((1, CH), F32)], axis=0).astype(BF16)
    data_rows = 3 * QUAD * COMPS
    r8 = iota((KROWS, 8), 0)
    part = jnp.where(r8 < data_rows, r8 & (COMPS - 1), COMPS + ((r8 >> 2) & 3))
    values = dot(onehot((part == iota((KROWS, 8), 1)) & (r8 < 2 * data_rows)), table).astype(BF16)
    wide = iota((CH, 3 * HALF), 1)
    spread = onehot(iota((CH, 3 * HALF), 0) == (wide & 31))
    rr = iota((KROWS, 3 * HALF), 0)
    cc = iota((KROWS, 3 * HALF), 1)
    row_node = jnp.where(rr < data_rows, rr >> 4, (rr - data_rows) >> 4)
    row_shot = jnp.where(rr < data_rows, rr >> 2, rr) & (QUAD - 1)
    node = sum(jnp.where((cc >> 6) == y, LIFTED[y][1], 0) for y in range(6))
    pair = sum(jnp.where((cc >> 6) == y, LIFTED[y][0], 0) for y in range(6))
    same = (row_node == node) & (row_shot == 2 * pair + ((cc >> 5) & 1)) & (rr < 2 * data_rows)
    w0_ref[...] = jnp.where(same, dot(values, spread), 0.0).astype(BF16)

    widen = onehot((iota((LANES, CH), 0) & 31) == iota((LANES, CH), 1))
    kr = iota((LANES, LANES), 0)
    kc = iota((LANES, LANES), 1)
    same_shot = ((kr >> 5) & 1) == ((kc >> 5) & 1)
    sr = iota((3 * CH, LANES), 0)
    sc = iota((3 * CH, LANES), 1)
    for layer, ref in ((0, w1_ref), (1, w2_ref)):
        base = 3 * layer
        tall = [
            dot_t(widen, cw_ref[(base + a) * 3 * CH : (base + a + 1) * 3 * CH, :]).astype(BF16)
            for a in range(3)
        ]
        for odd, (k_taps, n_taps) in enumerate((((0, 1, 2, 3), (0, 1, 3, 2)), ((1, 0, 3, 2), (1, 0, 2, 3)))):
            place = sum(jnp.where((sc >> 6) == y, n_taps[y], 0) for y in range(4))
            spread2 = onehot(((sr >> 5) == place) & ((sr & 31) == (sc & 31)))
            total = jnp.zeros((LANES, LANES), F32)
            for x in range(4):
                if k_taps[x] < 3:
                    total = jnp.where(((kr >> 6) == x) & same_shot, dot(tall[k_taps[x]], spread2), total)
            ref[odd] = total.astype(BF16)

    span = shift_ref.shape[0]
    window = span - 2 * HALO
    source = iota(shift_ref.shape, 0)
    source = jnp.where(source < window + HALO, source, source + window // 2 - HALO)
    shift_ref[...] = onehot(iota(shift_ref.shape, 1) == source)

    tile = onehot(iota((CH, LANES), 0) == (iota((CH, LANES), 1) & 31))
    wide_bias_ref[...] = sum(dot(term, tile) for term in split3(bias_ref[...]))
    for copy in passed:
        copy.wait()


def band_kernel(dils, blocks, place_ref, *refs):
    cw_ref, out_w_ref, b3_ref, b4_ref, ow_ref = refs
    widen = onehot((iota((LANES, CH), 0) & 31) == iota((LANES, CH), 1))

    er = iota((3 * CH, 3 * LANES), 0)
    ec = iota((3 * CH, 3 * LANES), 1)
    spread3 = onehot(((er >> 5) == (ec >> 8)) & ((er & 31) == (ec & 31)))
    row_lane = iota((LANES, 3 * LANES), 0)
    col_lane = iota((LANES, 3 * LANES), 1) & (LANES - 1)

    def shots_in(lane, block):
        couple = jnp.where(lane < HALF, couple_of(place_ref, 2 * block), couple_of(place_ref, 2 * block + 1))
        return QUAD * couple + ((lane >> 5) & (QUAD - 1))

    def expanded(layer, a):
        base = ((layer - 2) * 3 + a) * 3 * CH
        return dot(dot_t(widen, cw_ref[base : base + 3 * CH, :]).astype(BF16), spread3)

    for layer, ref in ((2, b3_ref), (3, b4_ref)):
        linked_taps = band_links(dils[layer], 0) if blocks == 1 else range(3)
        for out_block in range(blocks):
            for in_block in range(blocks):
                total = jnp.zeros((LANES, 3 * LANES), F32)
                for a in linked_taps:
                    reach = shots_in(col_lane, out_block) + (a - 1) * dils[layer]
                    total = total + jnp.where(shots_in(row_lane, in_block) == reach, expanded(layer, a), 0.0)
                for e in range(3):
                    ref[out_block * blocks + in_block, e * LANES : (e + 1) * LANES, :] = total[
                        :, e * LANES : (e + 1) * LANES
                    ].astype(BF16)

    rows = GROUP * COMPS
    pick = onehot((iota((rows, COMPS), 0) & (COMPS - 1)) == iota((rows, COMPS), 1))
    mine = dot(pick, out_w_ref[...]).astype(BF16)
    tile = onehot(iota((CH, LANES), 0) == (iota((CH, LANES), 1) & 31))
    same = (iota((rows, LANES), 0) >> 2) == (iota((rows, LANES), 1) >> 5)
    ow_ref[...] = jnp.where(same, dot(mine, tile), 0.0).astype(BF16)


def round_up(value, unit):
    return -(-value // unit) * unit


def shifted(value, dilation):
    span = value.shape[0]
    return jnp.concatenate(
        [
            pltpu.roll(value, dilation, axis=0).astype(BF16),
            value.astype(BF16),
            pltpu.roll(value, span - dilation, axis=0).astype(BF16),
        ],
        axis=1,
    )


class Shots:
    def __init__(
        self, dils, windows, step, couple, place_ref, recs, pick_ref, keep_ref, w0_ref, w1_ref, w2_ref,
        bias_ref, shift_ref, part_ref, x2_ref, rec_out_ref,
    ):
        self.dils, self.step, self.couple = dils, step, couple
        self.keep_ref, self.w0_ref, self.w1_ref, self.w2_ref = keep_ref, w0_ref, w1_ref, w2_ref
        self.bias_ref, self.shift_ref, self.x2_ref = bias_ref, shift_ref, x2_ref
        shots, rows, nodes = pick_ref.shape
        planes = shots // CORES
        self.slots = slots = x2_ref.shape[0]
        self.window = window = part_ref.shape[-1]
        self.rows, self.split = part_ref.shape[2], round_up(6 * slots, 16)
        self.span = window + 2 * HALO
        at = place_ref[1]
        self.right_ok = (at < windows - 1).astype(F32)
        self.left_ok = (at > 0).astype(F32)
        self.low_half = iota((self.span, HALF), 1) < CH * CORES

        lane = iota((nodes, 2 * window), 1)
        all_ok = jnp.where(
            lane < window, 1.0, jnp.where(lane < window + window // 2, self.right_ok, self.left_ok)
        ).astype(BF16)

        def put(part, swapped, value):
            for half in range(2):
                lanes = value[:, half * window : (half + 1) * window]
                part_ref[half, part, 0 : self.split] = lanes[0 : self.split]
                part_ref[half, swapped, self.split : rows] = lanes[self.split : rows]

        for x, rec_ref in enumerate(recs):
            n = 2 * couple + x % 2 + (planes if x >= 2 else 0)
            within = shot_of(place_ref, n, shots) & (QUAD - 1)
            edge = rec_ref[COMPS].astype(F32)
            for k in range(COMPS):
                turned = edge if k == 0 else pltpu.roll(edge, window - HALO * k, axis=1)
                both = jnp.concatenate([rec_ref[k], turned.astype(BF16)], axis=1)
                put(within * COMPS + k, (within ^ 2) * COMPS + k, dot(pick_ref[n], both))
            alive = dot(pick_ref[n], all_ok)
            for copy in range(2):
                first = QUAD * COMPS + QUAD * copy
                put(first + within, first + (within ^ 2), alive)

        self.half_rows = part_ref.shape[1] * self.rows
        self.part2 = part_ref.reshape(2 * self.half_rows, window)
        for q in range(slots):
            first = self.split + slots + q
            for half in range(2):
                pair = self.part2[pl.ds(first + (1 - half) * 8 * self.rows, 8, stride=self.rows), :]
                rec_out_ref[q, half * 8 : (half + 1) * 8] = pair

    def inside(self, value):
        w = self.window
        return jnp.concatenate(
            [value[0:w], value[w : w + HALO] * self.right_ok, value[w + HALO :] * self.left_ok], axis=0
        )

    def item_rows(self, q, b):
        start = (3 * (b // 2) * self.slots if b != 1 else self.split) + q
        halves = []
        for half in range(2):
            base = half * self.half_rows + start
            flags = base + QUAD * COMPS * self.rows
            pieces = [
                self.part2[pl.ds(base + a * self.slots, QUAD * COMPS, stride=self.rows), :] for a in range(3)
            ]
            for a in range(3):
                alive = self.part2[pl.ds(flags + a * self.slots, 2 * QUAD, stride=self.rows), :]
                pieces += [alive, alive]
            pieces.append(jnp.zeros((KROWS - 6 * QUAD * COMPS, self.window), F32))
            halves.append(jnp.concatenate(pieces, axis=0).astype(BF16))
        return jnp.concatenate(halves, axis=1)

    def items(self, group):
        return [(group * self.step + i, b) for i in range(self.step) for b in range(3)]

    def first_inputs(self, group):
        items = self.items(group)
        lhs = []
        for n in range(0, len(items), 2):
            some = jnp.concatenate([self.item_rows(q, b) for q, b in items[n : n + 2]], axis=0)
            moved = dot_t(self.shift_ref[...], some).astype(BF16)
            lhs += [moved[:, m : m + KROWS] for m in range(0, moved.shape[1], KROWS)]
        lifted = dot(jnp.concatenate(lhs, axis=0), self.w0_ref[...]).astype(BF16)
        own, other, shared = (lifted[:, m * HALF : (m + 1) * HALF] for m in range(3))
        return jnp.concatenate([own, shared], axis=1), jnp.concatenate([other, shared], axis=1)

    def taps_added(self, even, odd, dilation):
        mid = jnp.where(self.low_half, odd[:, 0:HALF], even[:, 0:HALF])
        late = jnp.where(self.low_half, odd[:, HALF:], even[:, HALF:])
        early = pltpu.roll(jnp.where(self.low_half, even[:, 0:HALF], odd[:, 0:HALF]), HALF // 2, axis=1)
        return (
            pltpu.roll(early, dilation, axis=0) + mid + pltpu.roll(late, self.span - dilation, axis=0)
        )

    def first_layer(self, group, even, odd):
        y_even, y_odd = dot(even, self.w1_ref[0]), dot(odd, self.w1_ref[1])
        x1 = []
        for n, (q, b) in enumerate(self.items(group)):
            at = slice(n * self.span, (n + 1) * self.span)
            old = jnp.where(self.low_half, odd[at, 0:HALF].astype(F32), even[at, 0:HALF].astype(F32))
            total = self.taps_added(y_even[at], y_odd[at], self.dils[0])
            new = jnp.maximum(total + self.bias_ref[0:1, 0:HALF], 0.0)
            x1.append(self.inside((old + new) * self.keep_ref[self.couple, b, q : q + 1, :]))
        even, odd, own = [], [], []
        for i in range(self.step):
            t0, t1, t2 = x1[3 * i : 3 * i + 3]
            t2 = t2.astype(BF16)
            even.append(jnp.concatenate([jnp.where(self.low_half, t0, t1).astype(BF16), t2], axis=1))
            odd.append(jnp.concatenate([jnp.where(self.low_half, t1, t0).astype(BF16), t2], axis=1))
            own.append(t1.astype(BF16))
        return jnp.concatenate(even, axis=0), jnp.concatenate(odd, axis=0), own

    def second_layer(self, group, even, odd, own):
        even, odd = dot(even, self.w2_ref[0]), dot(odd, self.w2_ref[1])
        for i in range(self.step):
            q = group * self.step + i
            at = slice(i * self.span, (i + 1) * self.span)
            total = self.taps_added(even[at], odd[at], self.dils[1])
            new = jnp.maximum(total + self.bias_ref[1:2, 0:HALF], 0.0)
            x2 = (own[i].astype(F32) + new) * self.keep_ref[self.couple, 1, q : q + 1, :]
            self.x2_ref[q] = shifted(self.inside(x2), self.dils[2])


def staged(work):
    inputs, middle = {}, {}
    for t in range(len(work) + 2):
        if 0 <= t - 2:
            stage, group = work[t - 2]
            stage.second_layer(group, *middle.pop(t - 2))
        if 0 <= t - 1 < len(work):
            stage, group = work[t - 1]
            middle[t - 1] = stage.first_layer(group, *inputs.pop(t - 1))
        if t < len(work):
            stage, group = work[t]
            inputs[t] = stage.first_inputs(group)
        yield t


def near_kernel(dils, windows, step, place_ref, *refs):
    pick_ref, keep_ref, w0_ref, w1_ref, w2_ref, bias_ref, shift_ref = refs[:7]
    recs = [refs[7], refs[8], refs[9].at[0], refs[9].at[1]]
    x2_ref, rec_out_ref, part_ref = refs[10:]
    stage = Shots(
        dils, windows, step, 0, place_ref, recs, pick_ref, keep_ref, w0_ref, w1_ref, w2_ref,
        bias_ref, shift_ref, part_ref, x2_ref, rec_out_ref,
    )
    for _ in staged([(stage, group) for group in range(x2_ref.shape[0] // step)]):
        pass


def main_kernel(dils, windows, step, near, place_ref, *refs):
    shots = refs[0].shape[0]
    couples = shots // QUAD
    pick_ref, keep_ref, w0_ref, w1_ref, w2_ref, b3_ref, b4_ref, ow_ref, bias_ref, shift_ref = refs[:10]
    refs = refs[10:]
    rec_refs, refs = refs[: QUAD * (couples - near)], refs[QUAD * (couples - near) :]
    done_refs, refs = refs[: 2 * near], refs[2 * near :]
    out_ref, part_ref, x2_all, rec_all, x3_ref = refs
    blocks = couples // 2
    slots, window = out_ref.shape[1], out_ref.shape[3]
    span = window + 2 * HALO
    right_ok = (place_ref[1] < windows - 1).astype(F32)
    left_ok = (place_ref[1] > 0).astype(F32)

    stages = []
    x2_refs, rec_refs_out = list(done_refs[0::2]), list(done_refs[1::2])
    for c in range(near, couples):
        x2_refs.append(x2_all.at[c - near])
        rec_refs_out.append(rec_all.at[c - near])
        stages.append(
            Shots(
                dils, windows, step, c, place_ref, rec_refs[QUAD * (c - near) : QUAD * (c - near + 1)],
                pick_ref, keep_ref, w0_ref, w1_ref, w2_ref, bias_ref, shift_ref, part_ref.at[c - near],
                x2_refs[-1], rec_refs_out[-1],
            )
        )

    def receiver_layer(parts_of, weights, layer, block, group, out_rows):
        y = None
        for other in range(blocks):
            term = dot(jnp.concatenate(parts_of(other), axis=0), weights[block * blocks + other])
            y = term if y is None else y + term
        results = []
        for i, part in enumerate(parts_of(block)):
            q = group * step + i
            keep = jnp.concatenate([keep_ref[2 * block + c, 1, q : q + 1, :] for c in range(2)], axis=1)
            old = part[:, LANES : 2 * LANES].astype(F32)
            new = jnp.maximum(y[i * out_rows : (i + 1) * out_rows] + bias_ref[layer : layer + 1, :], 0.0)
            results.append((old + new) * keep)
        return results

    def third_layer(group):
        def parts_of(block):
            return [
                jnp.concatenate(
                    [
                        x2_refs[2 * block + c][group * step + i, :, e * HALF : (e + 1) * HALF]
                        for e in range(3)
                        for c in range(2)
                    ],
                    axis=1,
                )
                for i in range(step)
            ]

        for block in range(blocks):
            for i, value in enumerate(receiver_layer(parts_of, b3_ref, 2, block, group, span)):
                value = jnp.concatenate(
                    [
                        value[0:window],
                        value[window : window + HALO] * right_ok,
                        value[window + HALO :] * left_ok,
                    ],
                    axis=0,
                )
                x3_ref[block, group * step + i] = shifted(value, dils[3])[0:window]

    def last_layer(group):
        def parts_of(block):
            return [x3_ref[block, group * step + i] for i in range(step)]

        for block in range(blocks):
            for i, value in enumerate(receiver_layer(parts_of, b4_ref, 3, block, group, window)):
                q = group * step + i
                noise = dot_t(ow_ref[...], value.astype(BF16))
                record = jnp.concatenate([rec_refs_out[2 * block + c][q] for c in range(2)], axis=0)
                done = (record + noise).reshape(GROUP, COMPS, window)
                for c in range(2):
                    first = QUAD * couple_of(place_ref, 2 * block + c)
                    out_ref[pl.ds(first, QUAD), q] = done[c * QUAD : (c + 1) * QUAD]

    groups = slots // step
    work = [(stage, group) for group in range(groups) for stage in stages]
    lag = len(stages)
    for t in itertools.chain(staged(work), range(len(work) + 2, len(work) + 2 + 2 * lag)):
        done, rest = divmod(t - 2, lag)
        if rest == 0 and 0 <= done - 1 < groups:
            third_layer(done - 1)
        if rest == 0 and 0 <= done - 2 < groups:
            last_layer(done - 2)


def divisor(value, limit):
    return max(d for d in range(1, limit + 1) if value % d == 0)


def body(
    records,
    lift_weight,
    lift_bias,
    conv_weight,
    conv_bias,
    out_weight,
    live_count,
    trace_node,
    node_owner,
):
    _, comps, nodes, window = records.shape
    holders = lax.axis_size("gather")
    windows = lax.axis_size("tm")
    shots = holders * records.shape[0]
    couples = shots // QUAD
    blocks = couples // 2
    slots = (nodes + holders - 1) // holders
    dils = (1, 4, 2, 8)
    rows = round_up(6 * slots, 16) + round_up(3 * slots, 16)
    span = window + 2 * HALO

    planes = holders // CORES
    vmem = pl.BlockSpec(memory_space=pltpu.VMEM)
    smem = pl.BlockSpec(memory_space=pltpu.SMEM)
    like = jax.ShapeDtypeStruct

    def after(value, other):
        return lax.optimization_barrier((value, other))[0]

    def kernel(function, operands, specs, outs, scratch, limit, flops, name):
        return pl.pallas_call(
            function,
            out_shape=outs,
            in_specs=[smem] + specs,
            out_specs=jax.tree.map(lambda _: vmem, outs),
            scratch_shapes=scratch,
            compiler_params=pltpu.CompilerParams(vmem_limit_bytes=limit << 20),
            cost_estimate=pl.CostEstimate(flops=flops, bytes_accessed=1 << 10, transcendentals=0),
            name=name,
        )(place, *operands)

    place = jnp.stack([lax.axis_index("gather"), lax.axis_index("tm")]).astype(jnp.int32)
    taps = jnp.transpose(conv_weight, (0, 3, 4, 1, 2)).reshape(-1, CH)

    own = records[0]
    even = lax.axis_index("tm") % 2 == 0
    pack = lambda part: jnp.transpose(part, (1, 0, 2)).reshape(nodes, comps * HALO)
    first, last = pack(own[:, :, :HALO]), pack(own[:, :, window - HALO :])
    got = []
    for begin in range(2):
        pairs = [(w, w + 1) for w in range(begin, windows - 1, 2)]
        pairs += [(b, a) for a, b in pairs]
        got.append(lax.ppermute(jnp.where(even == (begin == 0), last, first), "tm", pairs))
    small = [live_count, trace_node, taps, jnp.transpose(lift_weight), lift_bias[None, :], conv_bias]
    raw = small + [node_owner[None, :], own, out_weight]
    raw = [pltpu.with_memory_space_constraint(a, pltpu.HBM) for a in raw]
    half = (taps.shape[0] // 2, CH)
    scratch = [pltpu.SMEM(a.shape, a.dtype) for a in raw[:2]] + [pltpu.VMEM(half, BF16)]
    scratch += [pltpu.VMEM(a.shape, a.dtype) for a in raw[3:7]]
    w0, w1, w2, wide_bias, shift, pick, keep, own, late_taps, out_taps = kernel(
        functools.partial(prep_kernel, dils, slots),
        raw,
        [pl.BlockSpec(memory_space=pltpu.HBM)] * len(raw),
        (
            like((KROWS, 3 * HALF), BF16),
            like((2, LANES, LANES), BF16),
            like((2, LANES, LANES), BF16),
            like((conv_bias.shape[0], LANES), F32),
            like((span, 2 * window), BF16),
            like((shots, rows, nodes), BF16),
            like((couples, 3, 16, HALF), F32),
            like(own.shape, BF16),
            like(half, BF16),
            like(out_weight.shape, BF16),
        ),
        scratch + [pltpu.SemaphoreType.DMA((7,)), pltpu.SemaphoreType.DMA((3,))],
        16,
        10**5,
        "weights",
    )
    right, left = jnp.where(even, got[0], got[1]), jnp.where(even, got[1], got[0])
    sent = jnp.concatenate([own, jnp.concatenate([right, left], axis=1)[None]], axis=0)


    def exchanged(block, distance):
        return lax.ppermute(block, "gather", [(g, g ^ distance) for g in range(holders)])

    near_blocks = [sent, exchanged(sent, CORES)]
    far = [exchanged(sent, CORES * r) for r in range(2, planes)]
    near_blocks.append(exchanged(jnp.stack(near_blocks), 1))

    b3, b4, ow = kernel(
        functools.partial(band_kernel, dils, blocks),
        [late_taps, out_taps],
        [vmem] * 2,
        (
            like((blocks * blocks, 3 * LANES, LANES), BF16),
            like((blocks * blocks, 3 * LANES, LANES), BF16),
            like((GROUP * COMPS, LANES), BF16),
        ),
        [],
        16,
        10**10,
        "bands",
    )

    step = divisor(slots, 5)
    row_stride = round_up(rows, 16) + 8
    x2 = like((slots, span, 3 * HALF), BF16)
    held = like((slots, QUAD * COMPS, window), F32)
    parts = (2, PARTS + 1, row_stride, window)
    operands = [after(pick, ow), keep, w0, w1, w2, wide_bias, shift, *near_blocks]
    near = kernel(
        functools.partial(near_kernel, dils, windows, step),
        operands,
        [vmem] * len(operands),
        (x2, held),
        [pltpu.VMEM(parts, F32)],
        24,
        10**5,
        "near",
    )

    operands = [pick, keep, w0, w1, w2, b3, b4, ow, wide_bias, shift]
    for r in range(0, len(far), 2):
        operands += far[r : r + 2] + [exchanged(after(block, near[1]), 1) for block in far[r : r + 2]]
    operands += near
    out = kernel(
        functools.partial(main_kernel, dils, windows, step, 1),
        operands,
        [vmem] * len(operands),
        like((shots, slots, comps, window), F32),
        [
            pltpu.VMEM((couples - 1, *parts), F32),
            pltpu.VMEM((couples - 1, *x2.shape), BF16),
            pltpu.VMEM((couples - 1, *held.shape), F32),
            pltpu.VMEM((blocks, slots, window, 3 * LANES), BF16),
        ],
        36,
        4 * 10**9,
        "layers",
    )
    return jnp.transpose(out, (0, 2, 1, 3))


def solution(mesh):
    return jax.shard_map(
        body,
        mesh=mesh,
        in_specs=(P("gather", None, None, "tm"), P(), P(), P(), P(), P(), P(), P(), P()),
        out_specs=P(None, None, "gather", "tm"),
        check_vma=False,
    )
```

```python
import functools
import itertools

import jax
import jax.numpy as jnp
from jax import lax
from jax.experimental import pallas as pl
from jax.experimental.pallas import tpu as pltpu
from jax.sharding import PartitionSpec as P

F32 = jnp.float32
BF16 = jnp.bfloat16
CH = 32
CORES = 2
COMPS = 4
GROUP = 8
LANES = GROUP * CH
HALO = 16
QUAD = 4
HALF = QUAD * CH
KROWS = 128
LIFTED = ((0, 0), (0, 1), (1, 1), (1, 0), (0, 2), (1, 2))
PARTS = QUAD * COMPS + 2 * QUAD


def iota(shape, dim):
    return lax.broadcasted_iota(jnp.int32, shape, dim)


def dot(a, b):
    return jnp.dot(a, b, preferred_element_type=F32)


def dot_t(a, b):
    return lax.dot_general(a, b, (((1,), (1,)), ((), ())), preferred_element_type=F32)


def onehot(cond):
    return cond.astype(F32).astype(BF16)


def band_links(dilation, offset):
    return [
        a
        for a in range(3)
        if any(s + GROUP * offset == t + (a - 1) * dilation for s in range(GROUP) for t in range(GROUP))
    ]


def split3(value):
    terms = []
    for _ in range(3):
        term = value.astype(BF16)
        terms.append(term)
        value = value - term.astype(F32)
    return terms


def shot_of(place_ref, n, shots):
    planes = shots // CORES
    plane = place_ref[0] // CORES
    core = place_ref[0] - CORES * plane
    return CORES * (plane ^ (n % planes)) + (core if n < planes else 1 - core)


def couple_of(place_ref, relative):
    return (place_ref[0] // (2 * CORES)) ^ relative


def table_kernel(dils, slots, place_ref, live_ref, trace_ref, owner_ref, pick_ref, keep_ref):
    shots, rows, nodes = pick_ref.shape
    split = round_up(6 * slots, 16)
    me = place_ref[0]

    mine = (owner_ref[...] == me).astype(F32)
    before = onehot(iota((nodes, nodes), 0) < iota((nodes, nodes), 1))
    rank = dot(jnp.broadcast_to(mine, (8, nodes)).astype(BF16), before)[0:1, :]
    node_ids = iota((1, nodes), 1).astype(F32)

    def nodes_of(slot_index):
        held = jnp.where((rank == slot_index.astype(F32)) & (mine > 0.5), 1.0, 0.0)
        node = jnp.sum(held * node_ids, axis=1, keepdims=True)
        there = jnp.sum(held, axis=1, keepdims=True)
        return jnp.where(there > 0.5, node, -1.0e6).astype(jnp.int32)

    row_id = iota((rows, nodes), 0)
    late = row_id >= split
    row_id = jnp.where(late, row_id - split, row_id)
    tap = jnp.zeros((rows, nodes), jnp.int32)
    for m in range(1, 7):
        tap = tap + (row_id >= m * slots).astype(jnp.int32)
    second = (tap >= 3).astype(jnp.int32)
    shift = dils[0] * (tap - 3 * second - 1) + jnp.where(late, 0, dils[1] * (2 * second - 1))
    target = nodes_of(row_id - slots * tap)
    target = jnp.where(tap >= jnp.where(late, 3, 6), -1000000, target + shift)

    node_lane = iota((rows, nodes), 1)
    for n in range(shots):
        s = shot_of(place_ref, n, shots)
        pick_ref[n] = onehot((node_lane == target - trace_ref[s, 0]) & (node_lane < live_ref[s]))

    slot_rows = keep_ref.shape[2]
    own_node = nodes_of(iota((slot_rows, nodes), 0))
    shot_lane = iota((slot_rows, HALF), 1) >> 5
    for c in range(shots // QUAD):
        base = QUAD * couple_of(place_ref, c)
        for b in range(3):
            first = jnp.zeros((slot_rows, HALF), jnp.int32)
            count = jnp.zeros((slot_rows, HALF), jnp.int32)
            for w in range(QUAD):
                at = shot_lane == (w if b == 1 else w ^ 2)
                first = jnp.where(at, trace_ref[base + w, 0], first)
                count = jnp.where(at, live_ref[base + w], count)
            trace = own_node + dils[1] * (b - 1) - first
            keep_ref[c, b] = ((trace >= 0) & (trace < count)).astype(F32)


def started(sources, places, sems):
    copies = [pltpu.make_async_copy(a, b, sems.at[n]) for n, (a, b) in enumerate(zip(sources, places))]
    for copy in copies:
        copy.start()
    return copies


def prep_kernel(dils, slots, place_ref, *refs):
    w0_ref, w1_ref, w2_ref, wide_bias_ref, shift_ref, pick_ref, keep_ref = refs[9:16]
    half = refs[2].shape[0] // 2
    passed = started((refs[7], refs[2].at[half : 2 * half], refs[8]), refs[16:19], refs[27])
    live_ref, trace_ref, cw_ref, lift_ref, lift_bias_ref, bias_ref, owner_ref = refs[19:26]
    sources = (*refs[:2], refs[2].at[0:half], *refs[3:7])
    for copy in started(sources, refs[19:26], refs[26]):
        copy.wait()
    table_kernel(dils, slots, place_ref, live_ref, trace_ref, owner_ref, pick_ref, keep_ref)

    rows8 = [lift_ref[...].astype(F32)] + [term.astype(F32) for term in split3(lift_bias_ref[...])]
    table = jnp.concatenate(rows8 + [jnp.zeros((1, CH), F32)], axis=0).astype(BF16)
    data_rows = 3 * QUAD * COMPS
    r8 = iota((KROWS, 8), 0)
    part = jnp.where(r8 < data_rows, r8 & (COMPS - 1), COMPS + ((r8 >> 2) & 3))
    values = dot(onehot((part == iota((KROWS, 8), 1)) & (r8 < 2 * data_rows)), table).astype(BF16)
    wide = iota((CH, 3 * HALF), 1)
    spread = onehot(iota((CH, 3 * HALF), 0) == (wide & 31))
    rr = iota((KROWS, 3 * HALF), 0)
    cc = iota((KROWS, 3 * HALF), 1)
    row_node = jnp.where(rr < data_rows, rr >> 4, (rr - data_rows) >> 4)
    row_shot = jnp.where(rr < data_rows, rr >> 2, rr) & (QUAD - 1)
    node = sum(jnp.where((cc >> 6) == y, LIFTED[y][1], 0) for y in range(6))
    pair = sum(jnp.where((cc >> 6) == y, LIFTED[y][0], 0) for y in range(6))
    same = (row_node == node) & (row_shot == 2 * pair + ((cc >> 5) & 1)) & (rr < 2 * data_rows)
    w0_ref[...] = jnp.where(same, dot(values, spread), 0.0).astype(BF16)

    widen = onehot((iota((LANES, CH), 0) & 31) == iota((LANES, CH), 1))
    kr = iota((LANES, LANES), 0)
    kc = iota((LANES, LANES), 1)
    same_shot = ((kr >> 5) & 1) == ((kc >> 5) & 1)
    sr = iota((3 * CH, LANES), 0)
    sc = iota((3 * CH, LANES), 1)
    for layer, ref in ((0, w1_ref), (1, w2_ref)):
        base = 3 * layer
        tall = [
            dot_t(widen, cw_ref[(base + a) * 3 * CH : (base + a + 1) * 3 * CH, :]).astype(BF16)
            for a in range(3)
        ]
        for odd, (k_taps, n_taps) in enumerate((((0, 1, 2, 3), (0, 1, 3, 2)), ((1, 0, 3, 2), (1, 0, 2, 3)))):
            place = sum(jnp.where((sc >> 6) == y, n_taps[y], 0) for y in range(4))
            spread2 = onehot(((sr >> 5) == place) & ((sr & 31) == (sc & 31)))
            total = jnp.zeros((LANES, LANES), F32)
            for x in range(4):
                if k_taps[x] < 3:
                    total = jnp.where(((kr >> 6) == x) & same_shot, dot(tall[k_taps[x]], spread2), total)
            ref[odd] = total.astype(BF16)

    span = shift_ref.shape[0]
    window = span - 2 * HALO
    source = iota(shift_ref.shape, 0)
    source = jnp.where(source < window + HALO, source, source + window // 2 - HALO)
    shift_ref[...] = onehot(iota(shift_ref.shape, 1) == source)

    tile = onehot(iota((CH, LANES), 0) == (iota((CH, LANES), 1) & 31))
    wide_bias_ref[...] = sum(dot(term, tile) for term in split3(bias_ref[...]))
    for copy in passed:
        copy.wait()


def band_kernel(dils, blocks, place_ref, *refs):
    cw_ref, out_w_ref, b3_ref, b4_ref, ow_ref = refs
    widen = onehot((iota((LANES, CH), 0) & 31) == iota((LANES, CH), 1))

    er = iota((3 * CH, 3 * LANES), 0)
    ec = iota((3 * CH, 3 * LANES), 1)
    spread3 = onehot(((er >> 5) == (ec >> 8)) & ((er & 31) == (ec & 31)))
    row_lane = iota((LANES, 3 * LANES), 0)
    col_lane = iota((LANES, 3 * LANES), 1) & (LANES - 1)

    def shots_in(lane, block):
        couple = jnp.where(lane < HALF, couple_of(place_ref, 2 * block), couple_of(place_ref, 2 * block + 1))
        return QUAD * couple + ((lane >> 5) & (QUAD - 1))

    def expanded(layer, a):
        base = ((layer - 2) * 3 + a) * 3 * CH
        return dot(dot_t(widen, cw_ref[base : base + 3 * CH, :]).astype(BF16), spread3)

    for layer, ref in ((2, b3_ref), (3, b4_ref)):
        linked_taps = band_links(dils[layer], 0) if blocks == 1 else range(3)
        for out_block in range(blocks):
            for in_block in range(blocks):
                total = jnp.zeros((LANES, 3 * LANES), F32)
                for a in linked_taps:
                    reach = shots_in(col_lane, out_block) + (a - 1) * dils[layer]
                    total = total + jnp.where(shots_in(row_lane, in_block) == reach, expanded(layer, a), 0.0)
                for e in range(3):
                    ref[out_block * blocks + in_block, e * LANES : (e + 1) * LANES, :] = total[
                        :, e * LANES : (e + 1) * LANES
                    ].astype(BF16)

    rows = GROUP * COMPS
    pick = onehot((iota((rows, COMPS), 0) & (COMPS - 1)) == iota((rows, COMPS), 1))
    mine = dot(pick, out_w_ref[...]).astype(BF16)
    tile = onehot(iota((CH, LANES), 0) == (iota((CH, LANES), 1) & 31))
    same = (iota((rows, LANES), 0) >> 2) == (iota((rows, LANES), 1) >> 5)
    ow_ref[...] = jnp.where(same, dot(mine, tile), 0.0).astype(BF16)


def round_up(value, unit):
    return -(-value // unit) * unit


def shifted(value, dilation):
    span = value.shape[0]
    return jnp.concatenate(
        [
            pltpu.roll(value, dilation, axis=0).astype(BF16),
            value.astype(BF16),
            pltpu.roll(value, span - dilation, axis=0).astype(BF16),
        ],
        axis=1,
    )


class Shots:
    def __init__(
        self, dils, windows, step, couple, place_ref, recs, pick_ref, keep_ref, w0_ref, w1_ref, w2_ref,
        bias_ref, shift_ref, part_ref, x2_ref, rec_out_ref,
    ):
        self.dils, self.step, self.couple = dils, step, couple
        self.keep_ref, self.w0_ref, self.w1_ref, self.w2_ref = keep_ref, w0_ref, w1_ref, w2_ref
        self.bias_ref, self.shift_ref, self.x2_ref = bias_ref, shift_ref, x2_ref
        shots, rows, nodes = pick_ref.shape
        planes = shots // CORES
        self.slots = slots = x2_ref.shape[0]
        self.window = window = part_ref.shape[-1]
        self.rows, self.split = part_ref.shape[2], round_up(6 * slots, 16)
        self.span = window + 2 * HALO
        at = place_ref[1]
        self.right_ok = (at < windows - 1).astype(F32)
        self.left_ok = (at > 0).astype(F32)
        self.low_half = iota((self.span, HALF), 1) < CH * CORES

        lane = iota((nodes, 2 * window), 1)
        all_ok = jnp.where(
            lane < window, 1.0, jnp.where(lane < window + window // 2, self.right_ok, self.left_ok)
        ).astype(BF16)

        def put(part, swapped, value):
            for half in range(2):
                lanes = value[:, half * window : (half + 1) * window]
                part_ref[half, part, 0 : self.split] = lanes[0 : self.split]
                part_ref[half, swapped, self.split : rows] = lanes[self.split : rows]

        for x, rec_ref in enumerate(recs):
            n = 2 * couple + x % 2 + (planes if x >= 2 else 0)
            within = shot_of(place_ref, n, shots) & (QUAD - 1)
            edge = rec_ref[COMPS].astype(F32)
            for k in range(COMPS):
                turned = edge if k == 0 else pltpu.roll(edge, window - HALO * k, axis=1)
                both = jnp.concatenate([rec_ref[k], turned.astype(BF16)], axis=1)
                put(within * COMPS + k, (within ^ 2) * COMPS + k, dot(pick_ref[n], both))
            alive = dot(pick_ref[n], all_ok)
            for copy in range(2):
                first = QUAD * COMPS + QUAD * copy
                put(first + within, first + (within ^ 2), alive)

        self.half_rows = part_ref.shape[1] * self.rows
        self.part2 = part_ref.reshape(2 * self.half_rows, window)
        for q in range(slots):
            first = self.split + slots + q
            for half in range(2):
                pair = self.part2[pl.ds(first + (1 - half) * 8 * self.rows, 8, stride=self.rows), :]
                rec_out_ref[q, half * 8 : (half + 1) * 8] = pair

    def inside(self, value):
        w = self.window
        return jnp.concatenate(
            [value[0:w], value[w : w + HALO] * self.right_ok, value[w + HALO :] * self.left_ok], axis=0
        )

    def item_rows(self, q, b):
        start = (3 * (b // 2) * self.slots if b != 1 else self.split) + q
        halves = []
        for half in range(2):
            base = half * self.half_rows + start
            flags = base + QUAD * COMPS * self.rows
            pieces = [
                self.part2[pl.ds(base + a * self.slots, QUAD * COMPS, stride=self.rows), :] for a in range(3)
            ]
            for a in range(3):
                alive = self.part2[pl.ds(flags + a * self.slots, 2 * QUAD, stride=self.rows), :]
                pieces += [alive, alive]
            pieces.append(jnp.zeros((KROWS - 6 * QUAD * COMPS, self.window), F32))
            halves.append(jnp.concatenate(pieces, axis=0).astype(BF16))
        return jnp.concatenate(halves, axis=1)

    def items(self, group):
        return [(group * self.step + i, b) for i in range(self.step) for b in range(3)]

    def first_inputs(self, group):
        items = self.items(group)
        lhs = []
        for n in range(0, len(items), 2):
            some = jnp.concatenate([self.item_rows(q, b) for q, b in items[n : n + 2]], axis=0)
            moved = dot_t(self.shift_ref[...], some).astype(BF16)
            lhs += [moved[:, m : m + KROWS] for m in range(0, moved.shape[1], KROWS)]
        lifted = dot(jnp.concatenate(lhs, axis=0), self.w0_ref[...]).astype(BF16)
        own, other, shared = (lifted[:, m * HALF : (m + 1) * HALF] for m in range(3))
        return jnp.concatenate([own, shared], axis=1), jnp.concatenate([other, shared], axis=1)

    def taps_added(self, even, odd, dilation):
        mid = jnp.where(self.low_half, odd[:, 0:HALF], even[:, 0:HALF])
        late = jnp.where(self.low_half, odd[:, HALF:], even[:, HALF:])
        early = pltpu.roll(jnp.where(self.low_half, even[:, 0:HALF], odd[:, 0:HALF]), HALF // 2, axis=1)
        return (
            pltpu.roll(early, dilation, axis=0) + mid + pltpu.roll(late, self.span - dilation, axis=0)
        )

    def first_layer(self, group, even, odd):
        y_even, y_odd = dot(even, self.w1_ref[0]), dot(odd, self.w1_ref[1])
        x1 = []
        for n, (q, b) in enumerate(self.items(group)):
            at = slice(n * self.span, (n + 1) * self.span)
            old = jnp.where(self.low_half, odd[at, 0:HALF].astype(F32), even[at, 0:HALF].astype(F32))
            total = self.taps_added(y_even[at], y_odd[at], self.dils[0])
            new = jnp.maximum(total + self.bias_ref[0:1, 0:HALF], 0.0)
            x1.append(self.inside((old + new) * self.keep_ref[self.couple, b, q : q + 1, :]))
        even, odd, own = [], [], []
        for i in range(self.step):
            t0, t1, t2 = x1[3 * i : 3 * i + 3]
            t2 = t2.astype(BF16)
            even.append(jnp.concatenate([jnp.where(self.low_half, t0, t1).astype(BF16), t2], axis=1))
            odd.append(jnp.concatenate([jnp.where(self.low_half, t1, t0).astype(BF16), t2], axis=1))
            own.append(t1.astype(BF16))
        return jnp.concatenate(even, axis=0), jnp.concatenate(odd, axis=0), own

    def second_layer(self, group, even, odd, own):
        even, odd = dot(even, self.w2_ref[0]), dot(odd, self.w2_ref[1])
        for i in range(self.step):
            q = group * self.step + i
            at = slice(i * self.span, (i + 1) * self.span)
            total = self.taps_added(even[at], odd[at], self.dils[1])
            new = jnp.maximum(total + self.bias_ref[1:2, 0:HALF], 0.0)
            x2 = (own[i].astype(F32) + new) * self.keep_ref[self.couple, 1, q : q + 1, :]
            self.x2_ref[q] = shifted(self.inside(x2), self.dils[2])


def staged(work):
    inputs, middle = {}, {}
    for t in range(len(work) + 2):
        yield t
        if 0 <= t - 2:
            stage, group = work[t - 2]
            stage.second_layer(group, *middle.pop(t - 2))
        if 0 <= t - 1 < len(work):
            stage, group = work[t - 1]
            middle[t - 1] = stage.first_layer(group, *inputs.pop(t - 1))
        if t < len(work):
            stage, group = work[t]
            inputs[t] = stage.first_inputs(group)


def near_kernel(dils, windows, step, place_ref, *refs):
    pick_ref, keep_ref, w0_ref, w1_ref, w2_ref, bias_ref, shift_ref = refs[:7]
    recs = [refs[7], refs[8], refs[9].at[0], refs[9].at[1]]
    x2_ref, rec_out_ref, part_ref = refs[10:]
    stage = Shots(
        dils, windows, step, 0, place_ref, recs, pick_ref, keep_ref, w0_ref, w1_ref, w2_ref,
        bias_ref, shift_ref, part_ref, x2_ref, rec_out_ref,
    )
    for _ in staged([(stage, group) for group in range(x2_ref.shape[0] // step)]):
        pass


def main_kernel(dils, windows, step, near, place_ref, *refs):
    shots = refs[0].shape[0]
    couples = shots // QUAD
    pick_ref, keep_ref, w0_ref, w1_ref, w2_ref, b3_ref, b4_ref, ow_ref, bias_ref, shift_ref = refs[:10]
    refs = refs[10:]
    rec_refs, refs = refs[: QUAD * (couples - near)], refs[QUAD * (couples - near) :]
    done_refs, refs = refs[: 2 * near], refs[2 * near :]
    out_ref, part_ref, x2_all, rec_all, x3_ref = refs
    blocks = couples // 2
    slots, window = out_ref.shape[1], out_ref.shape[3]
    span = window + 2 * HALO
    right_ok = (place_ref[1] < windows - 1).astype(F32)
    left_ok = (place_ref[1] > 0).astype(F32)

    stages = []
    x2_refs, rec_refs_out = list(done_refs[0::2]), list(done_refs[1::2])
    for c in range(near, couples):
        x2_refs.append(x2_all.at[c - near])
        rec_refs_out.append(rec_all.at[c - near])
        stages.append(
            Shots(
                dils, windows, step, c, place_ref, rec_refs[QUAD * (c - near) : QUAD * (c - near + 1)],
                pick_ref, keep_ref, w0_ref, w1_ref, w2_ref, bias_ref, shift_ref, part_ref.at[c - near],
                x2_refs[-1], rec_refs_out[-1],
            )
        )

    def receiver_layer(parts_of, weights, layer, block, group, out_rows):
        y = None
        for other in range(blocks):
            term = dot(jnp.concatenate(parts_of(other), axis=0), weights[block * blocks + other])
            y = term if y is None else y + term
        results = []
        for i, part in enumerate(parts_of(block)):
            q = group * step + i
            keep = jnp.concatenate([keep_ref[2 * block + c, 1, q : q + 1, :] for c in range(2)], axis=1)
            old = part[:, LANES : 2 * LANES].astype(F32)
            new = jnp.maximum(y[i * out_rows : (i + 1) * out_rows] + bias_ref[layer : layer + 1, :], 0.0)
            results.append((old + new) * keep)
        return results

    def third_layer(group):
        def parts_of(block):
            return [
                jnp.concatenate(
                    [
                        x2_refs[2 * block + c][group * step + i, :, e * HALF : (e + 1) * HALF]
                        for e in range(3)
                        for c in range(2)
                    ],
                    axis=1,
                )
                for i in range(step)
            ]

        for block in range(blocks):
            for i, value in enumerate(receiver_layer(parts_of, b3_ref, 2, block, group, span)):
                value = jnp.concatenate(
                    [
                        value[0:window],
                        value[window : window + HALO] * right_ok,
                        value[window + HALO :] * left_ok,
                    ],
                    axis=0,
                )
                x3_ref[block, group * step + i] = shifted(value, dils[3])[0:window]

    def last_layer(group):
        def parts_of(block):
            return [x3_ref[block, group * step + i] for i in range(step)]

        for block in range(blocks):
            for i, value in enumerate(receiver_layer(parts_of, b4_ref, 3, block, group, window)):
                q = group * step + i
                noise = dot_t(ow_ref[...], value.astype(BF16))
                record = jnp.concatenate([rec_refs_out[2 * block + c][q] for c in range(2)], axis=0)
                done = (record + noise).reshape(GROUP, COMPS, window)
                for c in range(2):
                    first = QUAD * couple_of(place_ref, 2 * block + c)
                    out_ref[pl.ds(first, QUAD), q] = done[c * QUAD : (c + 1) * QUAD]

    groups = slots // step
    work = [(stage, group) for group in range(groups) for stage in stages]
    lag = len(stages)
    for t in itertools.chain(staged(work), range(len(work) + 2, len(work) + 2 + 2 * lag)):
        done, rest = divmod(t - 2, lag)
        if rest == 0 and 0 <= done - 2 < groups:
            last_layer(done - 2)
        if rest == 0 and 0 <= done - 1 < groups:
            third_layer(done - 1)


def divisor(value, limit):
    return max(d for d in range(1, limit + 1) if value % d == 0)


def body(
    records,
    lift_weight,
    lift_bias,
    conv_weight,
    conv_bias,
    out_weight,
    live_count,
    trace_node,
    node_owner,
):
    _, comps, nodes, window = records.shape
    holders = lax.axis_size("gather")
    windows = lax.axis_size("tm")
    shots = holders * records.shape[0]
    couples = shots // QUAD
    blocks = couples // 2
    slots = (nodes + holders - 1) // holders
    dils = (1, 4, 2, 8)
    rows = round_up(6 * slots, 16) + round_up(3 * slots, 16)
    span = window + 2 * HALO

    planes = holders // CORES
    vmem = pl.BlockSpec(memory_space=pltpu.VMEM)
    smem = pl.BlockSpec(memory_space=pltpu.SMEM)
    like = jax.ShapeDtypeStruct

    def after(value, other):
        return lax.optimization_barrier((value, other))[0]

    def kernel(function, operands, specs, outs, scratch, limit, flops, name):
        return pl.pallas_call(
            function,
            out_shape=outs,
            in_specs=[smem] + specs,
            out_specs=jax.tree.map(lambda _: vmem, outs),
            scratch_shapes=scratch,
            compiler_params=pltpu.CompilerParams(vmem_limit_bytes=limit << 20),
            cost_estimate=pl.CostEstimate(flops=flops, bytes_accessed=1 << 10, transcendentals=0),
            name=name,
        )(place, *operands)

    place = jnp.stack([lax.axis_index("gather"), lax.axis_index("tm")]).astype(jnp.int32)
    taps = jnp.transpose(conv_weight, (0, 3, 4, 1, 2)).reshape(-1, CH)

    own = records[0]
    even = lax.axis_index("tm") % 2 == 0
    pack = lambda part: jnp.transpose(part, (1, 0, 2)).reshape(nodes, comps * HALO)
    first, last = pack(own[:, :, :HALO]), pack(own[:, :, window - HALO :])
    got = []
    for begin in range(2):
        pairs = [(w, w + 1) for w in range(begin, windows - 1, 2)]
        pairs += [(b, a) for a, b in pairs]
        got.append(lax.ppermute(jnp.where(even == (begin == 0), last, first), "tm", pairs))
    small = [live_count, trace_node, taps, jnp.transpose(lift_weight), lift_bias[None, :], conv_bias]
    raw = small + [node_owner[None, :], own, out_weight]
    raw = [pltpu.with_memory_space_constraint(a, pltpu.HBM) for a in raw]
    half = (taps.shape[0] // 2, CH)
    scratch = [pltpu.SMEM(a.shape, a.dtype) for a in raw[:2]] + [pltpu.VMEM(half, BF16)]
    scratch += [pltpu.VMEM(a.shape, a.dtype) for a in raw[3:7]]
    w0, w1, w2, wide_bias, shift, pick, keep, own, late_taps, out_taps = kernel(
        functools.partial(prep_kernel, dils, slots),
        raw,
        [pl.BlockSpec(memory_space=pltpu.HBM)] * len(raw),
        (
            like((KROWS, 3 * HALF), BF16),
            like((2, LANES, LANES), BF16),
            like((2, LANES, LANES), BF16),
            like((conv_bias.shape[0], LANES), F32),
            like((span, 2 * window), BF16),
            like((shots, rows, nodes), BF16),
            like((couples, 3, 16, HALF), F32),
            like(own.shape, BF16),
            like(half, BF16),
            like(out_weight.shape, BF16),
        ),
        scratch + [pltpu.SemaphoreType.DMA((7,)), pltpu.SemaphoreType.DMA((3,))],
        16,
        10**5,
        "weights",
    )
    right, left = jnp.where(even, got[0], got[1]), jnp.where(even, got[1], got[0])
    sent = jnp.concatenate([own, jnp.concatenate([right, left], axis=1)[None]], axis=0)


    def exchanged(block, distance):
        return lax.ppermute(block, "gather", [(g, g ^ distance) for g in range(holders)])

    near_blocks = [sent, exchanged(sent, CORES)]
    far = [exchanged(sent, CORES * r) for r in range(2, planes)]
    near_blocks.append(exchanged(jnp.stack(near_blocks), 1))

    b3, b4, ow = kernel(
        functools.partial(band_kernel, dils, blocks),
        [late_taps, out_taps],
        [vmem] * 2,
        (
            like((blocks * blocks, 3 * LANES, LANES), BF16),
            like((blocks * blocks, 3 * LANES, LANES), BF16),
            like((GROUP * COMPS, LANES), BF16),
        ),
        [],
        16,
        10**10,
        "bands",
    )

    step = divisor(slots, 5)
    row_stride = round_up(rows, 16) + 8
    x2 = like((slots, span, 3 * HALF), BF16)
    held = like((slots, QUAD * COMPS, window), F32)
    parts = (2, PARTS + 1, row_stride, window)
    operands = [after(pick, ow), keep, w0, w1, w2, wide_bias, shift, *near_blocks]
    near = kernel(
        functools.partial(near_kernel, dils, windows, step),
        operands,
        [vmem] * len(operands),
        (x2, held),
        [pltpu.VMEM(parts, F32)],
        24,
        10**5,
        "near",
    )

    operands = [pick, keep, w0, w1, w2, b3, b4, ow, wide_bias, shift]
    for r in range(0, len(far), 2):
        operands += far[r : r + 2] + [exchanged(after(block, near[1]), 1) for block in far[r : r + 2]]
    operands += near
    out = kernel(
        functools.partial(main_kernel, dils, windows, step, 1),
        operands,
        [vmem] * len(operands),
        like((shots, slots, comps, window), F32),
        [
            pltpu.VMEM((couples - 1, *parts), F32),
            pltpu.VMEM((couples - 1, *x2.shape), BF16),
            pltpu.VMEM((couples - 1, *held.shape), F32),
            pltpu.VMEM((blocks, slots, window, 3 * LANES), BF16),
        ],
        36,
        4 * 10**9,
        "layers",
    )
    return jnp.transpose(out, (0, 2, 1, 3))


def solution(mesh):
    return jax.shard_map(
        body,
        mesh=mesh,
        in_specs=(P("gather", None, None, "tm"), P(), P(), P(), P(), P(), P(), P(), P()),
        out_specs=P(None, None, "gather", "tm"),
        check_vma=False,
    )
```

```python
import functools
import itertools

import jax
import jax.numpy as jnp
from jax import lax
from jax.experimental import pallas as pl
from jax.experimental.pallas import tpu as pltpu
from jax.sharding import PartitionSpec as P

F32 = jnp.float32
BF16 = jnp.bfloat16
CH = 32
CORES = 2
COMPS = 4
GROUP = 8
LANES = GROUP * CH
HALO = 16
QUAD = 4
HALF = QUAD * CH
KROWS = 128
LIFTED = ((0, 0), (0, 1), (1, 1), (1, 0), (0, 2), (1, 2))
PARTS = QUAD * COMPS + 2 * QUAD


def iota(shape, dim):
    return lax.broadcasted_iota(jnp.int32, shape, dim)


def dot(a, b):
    return jnp.dot(a, b, preferred_element_type=F32)


def dot_t(a, b):
    return lax.dot_general(a, b, (((1,), (1,)), ((), ())), preferred_element_type=F32)


def onehot(cond):
    return cond.astype(F32).astype(BF16)


def band_links(dilation, offset):
    return [
        a
        for a in range(3)
        if any(s + GROUP * offset == t + (a - 1) * dilation for s in range(GROUP) for t in range(GROUP))
    ]


def split3(value):
    terms = []
    for _ in range(3):
        term = value.astype(BF16)
        terms.append(term)
        value = value - term.astype(F32)
    return terms


def shot_of(place_ref, n, shots):
    planes = shots // CORES
    plane = place_ref[0] // CORES
    core = place_ref[0] - CORES * plane
    return CORES * (plane ^ (n % planes)) + (core if n < planes else 1 - core)


def couple_of(place_ref, relative):
    return (place_ref[0] // (2 * CORES)) ^ relative


def table_kernel(dils, slots, place_ref, live_ref, trace_ref, owner_ref, pick_ref, keep_ref):
    shots, rows, nodes = pick_ref.shape
    split = round_up(6 * slots, 16)
    me = place_ref[0]

    mine = (owner_ref[...] == me).astype(F32)
    before = onehot(iota((nodes, nodes), 0) < iota((nodes, nodes), 1))
    rank = dot(jnp.broadcast_to(mine, (8, nodes)).astype(BF16), before)[0:1, :]
    node_ids = iota((1, nodes), 1).astype(F32)

    def nodes_of(slot_index):
        held = jnp.where((rank == slot_index.astype(F32)) & (mine > 0.5), 1.0, 0.0)
        node = jnp.sum(held * node_ids, axis=1, keepdims=True)
        there = jnp.sum(held, axis=1, keepdims=True)
        return jnp.where(there > 0.5, node, -1.0e6).astype(jnp.int32)

    row_id = iota((rows, nodes), 0)
    late = row_id >= split
    row_id = jnp.where(late, row_id - split, row_id)
    tap = jnp.zeros((rows, nodes), jnp.int32)
    for m in range(1, 7):
        tap = tap + (row_id >= m * slots).astype(jnp.int32)
    second = (tap >= 3).astype(jnp.int32)
    shift = dils[0] * (tap - 3 * second - 1) + jnp.where(late, 0, dils[1] * (2 * second - 1))
    target = nodes_of(row_id - slots * tap)
    target = jnp.where(tap >= jnp.where(late, 3, 6), -1000000, target + shift)

    node_lane = iota((rows, nodes), 1)
    for n in range(shots):
        s = shot_of(place_ref, n, shots)
        pick_ref[n] = onehot((node_lane == target - trace_ref[s, 0]) & (node_lane < live_ref[s]))

    slot_rows = keep_ref.shape[2]
    own_node = nodes_of(iota((slot_rows, nodes), 0))
    shot_lane = iota((slot_rows, HALF), 1) >> 5
    for c in range(shots // QUAD):
        base = QUAD * couple_of(place_ref, c)
        for b in range(3):
            first = jnp.zeros((slot_rows, HALF), jnp.int32)
            count = jnp.zeros((slot_rows, HALF), jnp.int32)
            for w in range(QUAD):
                at = shot_lane == (w if b == 1 else w ^ 2)
                first = jnp.where(at, trace_ref[base + w, 0], first)
                count = jnp.where(at, live_ref[base + w], count)
            trace = own_node + dils[1] * (b - 1) - first
            keep_ref[c, b] = ((trace >= 0) & (trace < count)).astype(F32)


def started(sources, places, sems):
    copies = [pltpu.make_async_copy(a, b, sems.at[n]) for n, (a, b) in enumerate(zip(sources, places))]
    for copy in copies:
        copy.start()
    return copies


def prep_kernel(dils, slots, place_ref, *refs):
    w0_ref, w1_ref, w2_ref, wide_bias_ref, shift_ref, pick_ref, keep_ref = refs[9:16]
    half = refs[2].shape[0] // 2
    passed = started((refs[7], refs[2].at[half : 2 * half], refs[8]), refs[16:19], refs[27])
    live_ref, trace_ref, cw_ref, lift_ref, lift_bias_ref, bias_ref, owner_ref = refs[19:26]
    sources = (*refs[:2], refs[2].at[0:half], *refs[3:7])
    for copy in started(sources, refs[19:26], refs[26]):
        copy.wait()
    table_kernel(dils, slots, place_ref, live_ref, trace_ref, owner_ref, pick_ref, keep_ref)

    rows8 = [lift_ref[...].astype(F32)] + [term.astype(F32) for term in split3(lift_bias_ref[...])]
    table = jnp.concatenate(rows8 + [jnp.zeros((1, CH), F32)], axis=0).astype(BF16)
    data_rows = 3 * QUAD * COMPS
    r8 = iota((KROWS, 8), 0)
    part = jnp.where(r8 < data_rows, r8 & (COMPS - 1), COMPS + ((r8 >> 2) & 3))
    values = dot(onehot((part == iota((KROWS, 8), 1)) & (r8 < 2 * data_rows)), table).astype(BF16)
    wide = iota((CH, 3 * HALF), 1)
    spread = onehot(iota((CH, 3 * HALF), 0) == (wide & 31))
    rr = iota((KROWS, 3 * HALF), 0)
    cc = iota((KROWS, 3 * HALF), 1)
    row_node = jnp.where(rr < data_rows, rr >> 4, (rr - data_rows) >> 4)
    row_shot = jnp.where(rr < data_rows, rr >> 2, rr) & (QUAD - 1)
    node = sum(jnp.where((cc >> 6) == y, LIFTED[y][1], 0) for y in range(6))
    pair = sum(jnp.where((cc >> 6) == y, LIFTED[y][0], 0) for y in range(6))
    same = (row_node == node) & (row_shot == 2 * pair + ((cc >> 5) & 1)) & (rr < 2 * data_rows)
    w0_ref[...] = jnp.where(same, dot(values, spread), 0.0).astype(BF16)

    widen = onehot((iota((LANES, CH), 0) & 31) == iota((LANES, CH), 1))
    kr = iota((LANES, LANES), 0)
    kc = iota((LANES, LANES), 1)
    same_shot = ((kr >> 5) & 1) == ((kc >> 5) & 1)
    sr = iota((3 * CH, LANES), 0)
    sc = iota((3 * CH, LANES), 1)
    for layer, ref in ((0, w1_ref), (1, w2_ref)):
        base = 3 * layer
        tall = [
            dot_t(widen, cw_ref[(base + a) * 3 * CH : (base + a + 1) * 3 * CH, :]).astype(BF16)
            for a in range(3)
        ]
        for odd, (k_taps, n_taps) in enumerate((((0, 1, 2, 3), (0, 1, 3, 2)), ((1, 0, 3, 2), (1, 0, 2, 3)))):
            place = sum(jnp.where((sc >> 6) == y, n_taps[y], 0) for y in range(4))
            spread2 = onehot(((sr >> 5) == place) & ((sr & 31) == (sc & 31)))
            total = jnp.zeros((LANES, LANES), F32)
            for x in range(4):
                if k_taps[x] < 3:
                    total = jnp.where(((kr >> 6) == x) & same_shot, dot(tall[k_taps[x]], spread2), total)
            ref[odd] = total.astype(BF16)

    span = shift_ref.shape[0]
    window = span - 2 * HALO
    source = iota(shift_ref.shape, 0)
    source = jnp.where(source < window + HALO, source, source + window // 2 - HALO)
    shift_ref[...] = onehot(iota(shift_ref.shape, 1) == source)

    tile = onehot(iota((CH, LANES), 0) == (iota((CH, LANES), 1) & 31))
    wide_bias_ref[...] = sum(dot(term, tile) for term in split3(bias_ref[...]))
    for copy in passed:
        copy.wait()


def band_kernel(dils, blocks, place_ref, *refs):
    cw_ref, out_w_ref, b3_ref, b4_ref, ow_ref = refs
    widen = onehot((iota((LANES, CH), 0) & 31) == iota((LANES, CH), 1))

    er = iota((3 * CH, 3 * LANES), 0)
    ec = iota((3 * CH, 3 * LANES), 1)
    spread3 = onehot(((er >> 5) == (ec >> 8)) & ((er & 31) == (ec & 31)))
    row_lane = iota((LANES, 3 * LANES), 0)
    col_lane = iota((LANES, 3 * LANES), 1) & (LANES - 1)

    def shots_in(lane, block):
        couple = jnp.where(lane < HALF, couple_of(place_ref, 2 * block), couple_of(place_ref, 2 * block + 1))
        return QUAD * couple + ((lane >> 5) & (QUAD - 1))

    def expanded(layer, a):
        base = ((layer - 2) * 3 + a) * 3 * CH
        return dot(dot_t(widen, cw_ref[base : base + 3 * CH, :]).astype(BF16), spread3)

    for layer, ref in ((2, b3_ref), (3, b4_ref)):
        linked_taps = band_links(dils[layer], 0) if blocks == 1 else range(3)
        for out_block in range(blocks):
            for in_block in range(blocks):
                total = jnp.zeros((LANES, 3 * LANES), F32)
                for a in linked_taps:
                    reach = shots_in(col_lane, out_block) + (a - 1) * dils[layer]
                    total = total + jnp.where(shots_in(row_lane, in_block) == reach, expanded(layer, a), 0.0)
                for e in range(3):
                    ref[out_block * blocks + in_block, e * LANES : (e + 1) * LANES, :] = total[
                        :, e * LANES : (e + 1) * LANES
                    ].astype(BF16)

    rows = GROUP * COMPS
    pick = onehot((iota((rows, COMPS), 0) & (COMPS - 1)) == iota((rows, COMPS), 1))
    mine = dot(pick, out_w_ref[...]).astype(BF16)
    tile = onehot(iota((CH, LANES), 0) == (iota((CH, LANES), 1) & 31))
    same = (iota((rows, LANES), 0) >> 2) == (iota((rows, LANES), 1) >> 5)
    ow_ref[...] = jnp.where(same, dot(mine, tile), 0.0).astype(BF16)


def round_up(value, unit):
    return -(-value // unit) * unit


def shifted(value, dilation):
    span = value.shape[0]
    return jnp.concatenate(
        [
            pltpu.roll(value, dilation, axis=0).astype(BF16),
            value.astype(BF16),
            pltpu.roll(value, span - dilation, axis=0).astype(BF16),
        ],
        axis=1,
    )


class Shots:
    def __init__(
        self, dils, windows, step, couple, place_ref, recs, pick_ref, keep_ref, w0_ref, w1_ref, w2_ref,
        bias_ref, shift_ref, part_ref, x2_ref, rec_out_ref,
    ):
        self.dils, self.step, self.couple = dils, step, couple
        self.keep_ref, self.w0_ref, self.w1_ref, self.w2_ref = keep_ref, w0_ref, w1_ref, w2_ref
        self.bias_ref, self.shift_ref, self.x2_ref = bias_ref, shift_ref, x2_ref
        shots, rows, nodes = pick_ref.shape
        planes = shots // CORES
        self.slots = slots = x2_ref.shape[0]
        self.window = window = part_ref.shape[-1]
        self.rows, self.split = part_ref.shape[2], round_up(6 * slots, 16)
        self.span = window + 2 * HALO
        at = place_ref[1]
        self.right_ok = (at < windows - 1).astype(F32)
        self.left_ok = (at > 0).astype(F32)
        self.low_half = iota((self.span, HALF), 1) < CH * CORES

        lane = iota((nodes, 2 * window), 1)
        all_ok = jnp.where(
            lane < window, 1.0, jnp.where(lane < window + window // 2, self.right_ok, self.left_ok)
        ).astype(BF16)

        def put(part, swapped, value):
            for half in range(2):
                lanes = value[:, half * window : (half + 1) * window]
                part_ref[half, part, 0 : self.split] = lanes[0 : self.split]
                part_ref[half, swapped, self.split : rows] = lanes[self.split : rows]

        for x, rec_ref in enumerate(recs):
            n = 2 * couple + x % 2 + (planes if x >= 2 else 0)
            within = shot_of(place_ref, n, shots) & (QUAD - 1)
            edge = rec_ref[COMPS].astype(F32)
            for k in range(COMPS):
                turned = edge if k == 0 else pltpu.roll(edge, window - HALO * k, axis=1)
                both = jnp.concatenate([rec_ref[k], turned.astype(BF16)], axis=1)
                put(within * COMPS + k, (within ^ 2) * COMPS + k, dot(pick_ref[n], both))
            alive = dot(pick_ref[n], all_ok)
            for copy in range(2):
                first = QUAD * COMPS + QUAD * copy
                put(first + within, first + (within ^ 2), alive)

        self.half_rows = part_ref.shape[1] * self.rows
        self.part2 = part_ref.reshape(2 * self.half_rows, window)
        for q in range(slots):
            first = self.split + slots + q
            for half in range(2):
                pair = self.part2[pl.ds(first + (1 - half) * 8 * self.rows, 8, stride=self.rows), :]
                rec_out_ref[q, half * 8 : (half + 1) * 8] = pair

    def inside(self, value):
        w = self.window
        return jnp.concatenate(
            [value[0:w], value[w : w + HALO] * self.right_ok, value[w + HALO :] * self.left_ok], axis=0
        )

    def item_rows(self, q, b):
        start = (3 * (b // 2) * self.slots if b != 1 else self.split) + q
        halves = []
        for half in range(2):
            base = half * self.half_rows + start
            flags = base + QUAD * COMPS * self.rows
            pieces = [
                self.part2[pl.ds(base + a * self.slots, QUAD * COMPS, stride=self.rows), :] for a in range(3)
            ]
            for a in range(3):
                alive = self.part2[pl.ds(flags + a * self.slots, 2 * QUAD, stride=self.rows), :]
                pieces += [alive, alive]
            pieces.append(jnp.zeros((KROWS - 6 * QUAD * COMPS, self.window), F32))
            halves.append(jnp.concatenate(pieces, axis=0).astype(BF16))
        return jnp.concatenate(halves, axis=1)

    def items(self, group):
        return [(group * self.step + i, b) for i in range(self.step) for b in range(3)]

    def first_inputs(self, group):
        items = self.items(group)
        lhs = []
        for n in range(0, len(items), 2):
            some = jnp.concatenate([self.item_rows(q, b) for q, b in items[n : n + 2]], axis=0)
            moved = dot_t(self.shift_ref[...], some).astype(BF16)
            lhs += [moved[:, m : m + KROWS] for m in range(0, moved.shape[1], KROWS)]
        lifted = dot(jnp.concatenate(lhs, axis=0), self.w0_ref[...]).astype(BF16)
        own, other, shared = (lifted[:, m * HALF : (m + 1) * HALF] for m in range(3))
        return jnp.concatenate([own, shared], axis=1), jnp.concatenate([other, shared], axis=1)

    def taps_added(self, even, odd, dilation):
        mid = jnp.where(self.low_half, odd[:, 0:HALF], even[:, 0:HALF])
        late = jnp.where(self.low_half, odd[:, HALF:], even[:, HALF:])
        early = pltpu.roll(jnp.where(self.low_half, even[:, 0:HALF], odd[:, 0:HALF]), HALF // 2, axis=1)
        return (
            pltpu.roll(early, dilation, axis=0) + mid + pltpu.roll(late, self.span - dilation, axis=0)
        )

    def first_layer(self, group, even, odd):
        y_even, y_odd = dot(even, self.w1_ref[0]), dot(odd, self.w1_ref[1])
        x1 = []
        for n, (q, b) in enumerate(self.items(group)):
            at = slice(n * self.span, (n + 1) * self.span)
            old = jnp.where(self.low_half, odd[at, 0:HALF].astype(F32), even[at, 0:HALF].astype(F32))
            total = self.taps_added(y_even[at], y_odd[at], self.dils[0])
            new = jnp.maximum(total + self.bias_ref[0:1, 0:HALF], 0.0)
            x1.append(self.inside((old + new) * self.keep_ref[self.couple, b, q : q + 1, :]))
        even, odd, own = [], [], []
        for i in range(self.step):
            t0, t1, t2 = x1[3 * i : 3 * i + 3]
            t2 = t2.astype(BF16)
            even.append(jnp.concatenate([jnp.where(self.low_half, t0, t1).astype(BF16), t2], axis=1))
            odd.append(jnp.concatenate([jnp.where(self.low_half, t1, t0).astype(BF16), t2], axis=1))
            own.append(t1.astype(BF16))
        return jnp.concatenate(even, axis=0), jnp.concatenate(odd, axis=0), own

    def second_layer(self, group, even, odd, own):
        even, odd = dot(even, self.w2_ref[0]), dot(odd, self.w2_ref[1])
        for i in range(self.step):
            q = group * self.step + i
            at = slice(i * self.span, (i + 1) * self.span)
            total = self.taps_added(even[at], odd[at], self.dils[1])
            new = jnp.maximum(total + self.bias_ref[1:2, 0:HALF], 0.0)
            x2 = (own[i].astype(F32) + new) * self.keep_ref[self.couple, 1, q : q + 1, :]
            self.x2_ref[q] = shifted(self.inside(x2), self.dils[2])


def staged(work):
    inputs, middle = {}, {}
    for t in range(len(work) + 2):
        if 0 <= t - 2:
            stage, group = work[t - 2]
            stage.second_layer(group, *middle.pop(t - 2))
        if 0 <= t - 1 < len(work):
            stage, group = work[t - 1]
            middle[t - 1] = stage.first_layer(group, *inputs.pop(t - 1))
        if t < len(work):
            stage, group = work[t]
            inputs[t] = stage.first_inputs(group)
        yield t


def near_kernel(dils, windows, step, place_ref, *refs):
    pick_ref, keep_ref, w0_ref, w1_ref, w2_ref, bias_ref, shift_ref = refs[:7]
    recs = [refs[7], refs[8], refs[9].at[0], refs[9].at[1]]
    x2_ref, rec_out_ref, part_ref = refs[10:]
    stage = Shots(
        dils, windows, step, 0, place_ref, recs, pick_ref, keep_ref, w0_ref, w1_ref, w2_ref,
        bias_ref, shift_ref, part_ref, x2_ref, rec_out_ref,
    )
    for _ in staged([(stage, group) for group in range(x2_ref.shape[0] // step)]):
        pass


def main_kernel(dils, windows, step, near, place_ref, *refs):
    shots = refs[0].shape[0]
    couples = shots // QUAD
    pick_ref, keep_ref, w0_ref, w1_ref, w2_ref, b3_ref, b4_ref, ow_ref, bias_ref, shift_ref = refs[:10]
    refs = refs[10:]
    rec_refs, refs = refs[: QUAD * (couples - near)], refs[QUAD * (couples - near) :]
    done_refs, refs = refs[: 2 * near], refs[2 * near :]
    out_ref, part_ref, x2_all, rec_all, x3_ref = refs
    blocks = couples // 2
    slots, window = out_ref.shape[1], out_ref.shape[3]
    span = window + 2 * HALO
    right_ok = (place_ref[1] < windows - 1).astype(F32)
    left_ok = (place_ref[1] > 0).astype(F32)

    stages = []
    x2_refs, rec_refs_out = list(done_refs[0::2]), list(done_refs[1::2])
    for c in range(near, couples):
        x2_refs.append(x2_all.at[c - near])
        rec_refs_out.append(rec_all.at[c - near])
        stages.append(
            Shots(
                dils, windows, step, c, place_ref, rec_refs[QUAD * (c - near) : QUAD * (c - near + 1)],
                pick_ref, keep_ref, w0_ref, w1_ref, w2_ref, bias_ref, shift_ref, part_ref.at[c - near],
                x2_refs[-1], rec_refs_out[-1],
            )
        )

    def receiver_layer(parts_of, weights, layer, block, group, out_rows):
        y = None
        for other in range(blocks):
            term = dot(jnp.concatenate(parts_of(other), axis=0), weights[block * blocks + other])
            y = term if y is None else y + term
        results = []
        for i, part in enumerate(parts_of(block)):
            q = group * step + i
            keep = jnp.concatenate([keep_ref[2 * block + c, 1, q : q + 1, :] for c in range(2)], axis=1)
            old = part[:, LANES : 2 * LANES].astype(F32)
            new = jnp.maximum(y[i * out_rows : (i + 1) * out_rows] + bias_ref[layer : layer + 1, :], 0.0)
            results.append((old + new) * keep)
        return results

    def third_layer(group):
        def parts_of(block):
            return [
                jnp.concatenate(
                    [
                        x2_refs[2 * block + c][group * step + i, :, e * HALF : (e + 1) * HALF]
                        for e in range(3)
                        for c in range(2)
                    ],
                    axis=1,
                )
                for i in range(step)
            ]

        for block in range(blocks):
            for i, value in enumerate(receiver_layer(parts_of, b3_ref, 2, block, group, span)):
                value = jnp.concatenate(
                    [
                        value[0:window],
                        value[window : window + HALO] * right_ok,
                        value[window + HALO :] * left_ok,
                    ],
                    axis=0,
                )
                x3_ref[block, group * step + i] = shifted(value, dils[3])[0:window]

    def last_layer(group):
        def parts_of(block):
            return [x3_ref[block, group * step + i] for i in range(step)]

        for block in range(blocks):
            for i, value in enumerate(receiver_layer(parts_of, b4_ref, 3, block, group, window)):
                q = group * step + i
                noise = dot_t(ow_ref[...], value.astype(BF16))
                record = jnp.concatenate([rec_refs_out[2 * block + c][q] for c in range(2)], axis=0)
                done = (record + noise).reshape(GROUP, COMPS, window)
                for c in range(2):
                    first = QUAD * couple_of(place_ref, 2 * block + c)
                    out_ref[pl.ds(first, QUAD), q] = done[c * QUAD : (c + 1) * QUAD]

    groups = slots // step
    work = [(stage, group) for group in range(groups) for stage in stages]
    lag = len(stages)
    for t in itertools.chain(staged(work), range(len(work) + 2, len(work) + 2 + 2 * lag)):
        done, rest = divmod(t - 2, lag)
        if rest == 0 and 0 <= done - 1 < groups:
            third_layer(done - 1)
        if rest == 0 and 0 <= done - 2 < groups:
            last_layer(done - 2)


def divisor(value, limit):
    return max(d for d in range(1, limit + 1) if value % d == 0)


def body(
    records,
    lift_weight,
    lift_bias,
    conv_weight,
    conv_bias,
    out_weight,
    live_count,
    trace_node,
    node_owner,
):
    _, comps, nodes, window = records.shape
    holders = lax.axis_size("gather")
    windows = lax.axis_size("tm")
    shots = holders * records.shape[0]
    couples = shots // QUAD
    blocks = couples // 2
    slots = (nodes + holders - 1) // holders
    dils = (1, 4, 2, 8)
    rows = round_up(6 * slots, 16) + round_up(3 * slots, 16)
    span = window + 2 * HALO

    planes = holders // CORES
    vmem = pl.BlockSpec(memory_space=pltpu.VMEM)
    smem = pl.BlockSpec(memory_space=pltpu.SMEM)
    like = jax.ShapeDtypeStruct

    def after(value, other):
        return lax.optimization_barrier((value, other))[0]

    def kernel(function, operands, specs, outs, scratch, limit, flops, name):
        return pl.pallas_call(
            function,
            out_shape=outs,
            in_specs=[smem] + specs,
            out_specs=jax.tree.map(lambda _: vmem, outs),
            scratch_shapes=scratch,
            compiler_params=pltpu.CompilerParams(vmem_limit_bytes=limit << 20),
            cost_estimate=pl.CostEstimate(flops=flops, bytes_accessed=1 << 10, transcendentals=0),
            name=name,
        )(place, *operands)

    place = jnp.stack([lax.axis_index("gather"), lax.axis_index("tm")]).astype(jnp.int32)
    taps = jnp.transpose(conv_weight, (0, 3, 4, 1, 2)).reshape(-1, CH)

    own = records[0]
    even = lax.axis_index("tm") % 2 == 0
    pack = lambda part: jnp.transpose(part, (1, 0, 2)).reshape(nodes, comps * HALO)
    first, last = pack(own[:, :, :HALO]), pack(own[:, :, window - HALO :])
    got = []
    for begin in range(2):
        pairs = [(w, w + 1) for w in range(begin, windows - 1, 2)]
        pairs += [(b, a) for a, b in pairs]
        got.append(lax.ppermute(jnp.where(even == (begin == 0), last, first), "tm", pairs))
    small = [live_count, trace_node, taps, jnp.transpose(lift_weight), lift_bias[None, :], conv_bias]
    raw = small + [node_owner[None, :], own, out_weight]
    raw = [pltpu.with_memory_space_constraint(a, pltpu.HBM) for a in raw]
    half = (taps.shape[0] // 2, CH)
    scratch = [pltpu.SMEM(a.shape, a.dtype) for a in raw[:2]] + [pltpu.VMEM(half, BF16)]
    scratch += [pltpu.VMEM(a.shape, a.dtype) for a in raw[3:7]]
    w0, w1, w2, wide_bias, shift, pick, keep, own, late_taps, out_taps = kernel(
        functools.partial(prep_kernel, dils, slots),
        raw,
        [pl.BlockSpec(memory_space=pltpu.HBM)] * len(raw),
        (
            like((KROWS, 3 * HALF), BF16),
            like((2, LANES, LANES), BF16),
            like((2, LANES, LANES), BF16),
            like((conv_bias.shape[0], LANES), F32),
            like((span, 2 * window), BF16),
            like((shots, rows, nodes), BF16),
            like((couples, 3, 16, HALF), F32),
            like(own.shape, BF16),
            like(half, BF16),
            like(out_weight.shape, BF16),
        ),
        scratch + [pltpu.SemaphoreType.DMA((7,)), pltpu.SemaphoreType.DMA((3,))],
        16,
        10**5,
        "weights",
    )
    right, left = jnp.where(even, got[0], got[1]), jnp.where(even, got[1], got[0])
    sent = jnp.concatenate([own, jnp.concatenate([right, left], axis=1)[None]], axis=0)


    def exchanged(block, distance):
        return lax.ppermute(block, "gather", [(g, g ^ distance) for g in range(holders)])

    near_blocks = [sent, exchanged(sent, CORES)]
    far = [exchanged(sent, CORES * r) for r in range(2, planes)]
    near_blocks.append(exchanged(jnp.stack(near_blocks), 1))

    b3, b4, ow = kernel(
        functools.partial(band_kernel, dils, blocks),
        [late_taps, out_taps],
        [vmem] * 2,
        (
            like((blocks * blocks, 3 * LANES, LANES), BF16),
            like((blocks * blocks, 3 * LANES, LANES), BF16),
            like((GROUP * COMPS, LANES), BF16),
        ),
        [],
        16,
        10**10,
        "bands",
    )

    step = divisor(slots, 5)
    row_stride = round_up(rows, 16) + 8
    x2 = like((slots, span, 3 * HALF), BF16)
    held = like((slots, QUAD * COMPS, window), F32)
    parts = (2, PARTS + 1, row_stride, window)
    operands = [pick, keep, w0, w1, w2, wide_bias, shift, *near_blocks]
    near = kernel(
        functools.partial(near_kernel, dils, windows, step),
        operands,
        [vmem] * len(operands),
        (x2, held),
        [pltpu.VMEM(parts, F32)],
        24,
        10**5,
        "near",
    )

    operands = [pick, keep, w0, w1, w2, b3, b4, ow, wide_bias, shift]
    for r in range(0, len(far), 2):
        operands += far[r : r + 2] + [exchanged(after(block, near[1]), 1) for block in far[r : r + 2]]
    operands += near
    out = kernel(
        functools.partial(main_kernel, dils, windows, step, 1),
        operands,
        [vmem] * len(operands),
        like((shots, slots, comps, window), F32),
        [
            pltpu.VMEM((couples - 1, *parts), F32),
            pltpu.VMEM((couples - 1, *x2.shape), BF16),
            pltpu.VMEM((couples - 1, *held.shape), F32),
            pltpu.VMEM((blocks, slots, window, 3 * LANES), BF16),
        ],
        36,
        4 * 10**9,
        "layers",
    )
    return jnp.transpose(out, (0, 2, 1, 3))


def solution(mesh):
    return jax.shard_map(
        body,
        mesh=mesh,
        in_specs=(P("gather", None, None, "tm"), P(), P(), P(), P(), P(), P(), P(), P()),
        out_specs=P(None, None, "gather", "tm"),
        check_vma=False,
    )
```
